32 devices in a mesh: gx: 2 (over x), gy: 4 (over y, core), gz: 4 (over z).
Axes of the slice: x: 2, y: 2, z: 4, core: 2. Of those that a mesh axis runs over, the one named last changes fastest.
Arguments:
- residual_in: float32 [2, 4, 4, 128, 768], P('gx', 'gy', 'gz'), as said below
- schur: float32 [2, 4, 4, 768, 768], P('gx', 'gy', 'gz'), as said below
- modes: float32 [2, 4, 4, 6, 768], P('gx', 'gy', 'gz'), may hold values from -0.875 to 0.875
- coarse_inv: float32 [2, 4, 24, 24], P('gx', 'gy', 'gz'), as said below
Outputs:
- multipliers: float32 [2, 4, 4, 128, 768], P('gx', 'gy', 'gz')
- residual: float32 [2, 4, 4, 128, 768], P('gx', 'gy', 'gz')
The draws below stay inside these ranges and needn't reach their ends.
Inputs may be any that keep to these rules, and one draw needn't show every extreme that they name: `residual_in`: each multiplier has the same value on both sides of its face. `schur`: every subdomain's matrix is symmetric positive definite. `coarse_inv`: every coarse block is symmetric positive definite.
All inputs are finite; a program needn't handle non-finite values.
Results may differ from the reference program's by a relative error of at most 0.0003.
Values sent between devices are 32-bit elements; how exact they have to be, the bound alone decides.
No kernel may reach another device: no remote copies, remote signals or barrier semaphores. Data moves between devices by JAX's collectives and lax.ppermute only.
A program may use at most 64 MiB of HBM per device.

```python
import jax
import jax.numpy as jnp
from jax import lax

FACE = 128
IF = 768
LOADS = 128
MODES = 6
ITERS = 4
CN = 24
N_GX = 2
N_GY = 4
N_GZ = 4


def draw_residual_in(key, part):
    shape = (N_GX, N_GY, N_GZ, 3, LOADS, FACE)
    base = jax.random.normal(key, shape, jnp.float32)
    face_x = base[:, :, :, 0]
    face_y = base[:, :, :, 1]
    face_z = base[:, :, :, 2]
    pieces = [face_x, jnp.roll(face_x, -1, axis=0), face_y, jnp.roll(face_y, -1, axis=1), face_z, jnp.roll(face_z, -1, axis=2)]
    return jnp.concatenate(pieces, axis=-1)


def draw_schur(key, part):
    key_diag = jax.random.fold_in(key, 11)
    key_off = jax.random.fold_in(key, 12)
    diag = jnp.exp(jax.random.uniform(key_diag, (N_GX, N_GY, N_GZ, IF), jnp.float32, jnp.log(2.0), jnp.log(5.0)))
    shape = (N_GX, N_GY, N_GZ, IF, IF)
    noise = jax.random.normal(key_off, shape, jnp.float32)
    noise = noise * IF ** (-0.5)
    sym = 0.5 * (noise + jnp.swapaxes(noise, -1, -2))
    return sym + diag[..., None] * jnp.eye(IF, dtype=jnp.float32)


def draw_coarse_inv(key, part):
    key_diag = jax.random.fold_in(key, 21)
    key_off = jax.random.fold_in(key, 22)
    diag = jnp.exp(jax.random.uniform(key_diag, (N_GX, N_GY, CN), jnp.float32, jnp.log(1.5), jnp.log(4.0)))
    shape = (N_GX, N_GY, CN, CN)
    noise = jax.random.normal(key_off, shape, jnp.float32)
    noise = noise * (0.7 * CN ** (-0.5))
    sym = 0.5 * (noise + jnp.swapaxes(noise, -1, -2))
    return sym + diag[..., None] * jnp.eye(CN, dtype=jnp.float32)


def shard_levels(key, shape, shards, least, high):
    factor_of, own = 1.0, jax.random.fold_in(key, 6)
    for axis_at, shards_of in shards:
        heights = jnp.exp(jax.random.uniform(jax.random.fold_in(own, axis_at), (shards_of,), jnp.float32, least / len(shards), high / len(shards)))
        factor_of = factor_of * jnp.repeat(heights, shape[axis_at] // shards_of).reshape([-1 if axis == axis_at else 1 for axis in range(len(shape))])
    return factor_of


def bell_draw(own_key, shape, deviation, bound, shards=(), kind=jnp.bfloat16):
    factor_of = shard_levels(own_key, shape, shards, -0.22, 0.18) if shards else 1.0
    drawn = jax.random.normal(own_key, shape, jnp.float32) * deviation * factor_of
    return jnp.minimum(jnp.maximum(drawn, -bound), bound).astype(kind)


def setup_inputs(seed: int = 0) -> dict:
    key_of = jax.random.split(jax.random.key(seed), 5)
    residual_in = draw_residual_in(jax.random.fold_in(key_of[4], 71), 0)
    schur = draw_schur(jax.random.fold_in(key_of[4], 71), 0)
    modes = bell_draw(key_of[2], (N_GX, N_GY, N_GZ, MODES, IF), (IF // 16) ** -0.5, 0.875, ((0, 2), (1, 4), (2, 4)), jnp.float32)
    coarse_inv = draw_coarse_inv(jax.random.fold_in(key_of[4], 71), 0)
    return dict(residual_in=residual_in, schur=schur, modes=modes, coarse_inv=coarse_inv)


def face_signs(face):
    return jnp.repeat(jnp.array([1.0, -1.0, 1.0, -1.0, 1.0, -1.0], dtype=jnp.float32), face)


def subdomain_product(pair):
    matrix, vector = pair
    return jnp.einsum('rj,ij->ri', vector, matrix, precision=lax.Precision.HIGHEST)


def assemble(values):
    parts = []
    for axis_id in range(3):
        low_face = values[..., 2 * axis_id * FACE:(2 * axis_id + 1) * FACE]
        high_face = values[..., (2 * axis_id + 1) * FACE:(2 * axis_id + 2) * FACE]
        from_low = jnp.roll(high_face, 1, axis=axis_id)
        from_high = jnp.roll(low_face, -1, axis=axis_id)
        parts.append(low_face - from_low)
        parts.append(from_high - high_face)
    return jnp.concatenate(parts, axis=-1)


def operate(field, schur, modes, coarse_inv):
    sign = face_signs(FACE)
    u = sign * field
    shape = u.shape
    flat_schur = schur.reshape(-1, IF, IF)
    flat_u = u.reshape(-1, LOADS, IF)
    local = lax.map(subdomain_product, (flat_schur, flat_u)).reshape(shape)
    loads = jnp.einsum('xyzmj,xyzrj->xyzmr', modes, u, precision=lax.Precision.HIGHEST)
    column = loads.reshape(N_GX, N_GY, CN, LOADS)
    amp = jnp.einsum('xyab,xybr->xyar', coarse_inv, column, precision=lax.Precision.HIGHEST)
    amp = amp.reshape(N_GX, N_GY, N_GZ, MODES, LOADS)
    coarse_term = jnp.einsum('xyzmr,xyzmj->xyzrj', amp, modes, precision=lax.Precision.HIGHEST)
    return assemble(local + coarse_term)


def inner_dot(left, right):
    return 0.5 * jnp.sum(left * right, axis=(0, 1, 2, 4))


def reference(residual_in, schur, modes, coarse_inv):
    resid = residual_in
    mult = jnp.zeros_like(residual_in)
    image = operate(resid, schur, modes, coarse_inv)
    norm_now = inner_dot(resid, resid)
    alpha = norm_now / inner_dot(resid, image)
    direction = resid
    along = image
    for step in range(ITERS):
        mult = mult + alpha[:, None] * direction
        resid = resid - alpha[:, None] * along
        if step + 1 < ITERS:
            image = operate(resid, schur, modes, coarse_inv)
            norm_next = inner_dot(resid, resid)
            curv = inner_dot(resid, image)
            ratio = norm_next / norm_now
            alpha = norm_next / (curv - ratio * norm_next / alpha)
            direction = resid + ratio[:, None] * direction
            along = image + ratio[:, None] * along
            norm_now = norm_next
    return mult, resid
```

```python
import functools

import jax
import jax.numpy as jnp
from jax import lax
from jax.experimental import pallas as pl
from jax.experimental.pallas import tpu as pltpu
from jax.sharding import PartitionSpec as P

F32 = jnp.float32
BF16 = jnp.bfloat16
HI = lax.Precision.HIGHEST
MODE_PAD = 8
DOT_PAD = 8


def call(kernel, outs, *args, flops=0):
    nbytes = sum(a.size * a.dtype.itemsize for a in args)
    nbytes += sum(o.size * o.dtype.itemsize for o in outs)
    return pl.pallas_call(
        kernel,
        out_shape=outs,
        in_specs=[pl.BlockSpec(memory_space=pltpu.VMEM)] * len(args),
        out_specs=[pl.BlockSpec(memory_space=pltpu.VMEM)] * len(outs),
        compiler_params=pltpu.CompilerParams(vmem_limit_bytes=24 * 1024 * 1024),
        cost_estimate=pl.CostEstimate(flops=flops, bytes_accessed=nbytes, transcendentals=0),
    )(*args)


def sds(shape, dtype=F32):
    return jax.ShapeDtypeStruct(shape, dtype)


def split(x):
    high = x.astype(BF16)
    return high, (x - high.astype(F32)).astype(BF16)


def split3(x):
    high = x.astype(BF16)
    rest = x - high.astype(F32)
    mid = rest.astype(BF16)
    return high, mid, (rest - mid.astype(F32)).astype(BF16)


def half_dot(a, b):
    return 0.5 * jnp.sum(a * b, axis=0, keepdims=True)


def publish(vec, modes, u2_ref, g_ref):
    high, low = split(vec)
    cols = vec.shape[1]
    u2_ref[:, :cols] = high
    u2_ref[:, cols:] = low
    g_ref[0:MODE_PAD, :] = jnp.dot(modes, vec, precision=HI, preferred_element_type=F32)


def start_kernel(face, resid_ref, modes_ref, vec_ref, u2_ref, g_ref, mt_ref):
    for f in range(6):
        part = resid_ref[:, f * face:(f + 1) * face].T
        vec_ref[f * face:(f + 1) * face, :] = part if f % 2 == 0 else -part
    modes = modes_ref[...]
    publish(vec_ref[...], modes, u2_ref, g_ref)
    high, mid, low = split3(modes.T)
    mt_ref[...] = jnp.concatenate([high, high, mid, mid, high, low], axis=1)


def multiply(s_high_ref, s_low_ref, u2_ref, y_ref):
    rows, cols = y_ref.shape
    u2 = u2_ref[...]
    step = 256
    for i in range(0, rows, step):
        both = jnp.dot(s_high_ref[i:i + step, :], u2, preferred_element_type=F32)
        both += jnp.dot(s_low_ref[i:i + step, :], u2, preferred_element_type=F32)
        y_ref[i:i + step, :] = both[:, :cols] + both[:, cols:]


def first_product_kernel(schur_ref, u2_ref, y_ref, s_high_ref, s_low_ref):
    high, low = split(schur_ref[...])
    s_high_ref[...] = high
    s_low_ref[...] = low
    multiply(s_high_ref, s_low_ref, u2_ref, y_ref)


def product_kernel(s_high_ref, s_low_ref, u2_ref, y_ref):
    multiply(s_high_ref, s_low_ref, u2_ref, y_ref)


def product_dots_a_kernel(s_high_ref, s_low_ref, u2_ref, r0_ref, w0_ref, y_ref, d_ref):
    multiply(s_high_ref, s_low_ref, u2_ref, y_ref)
    r0, w0 = r0_ref[...], w0_ref[...]
    d_ref[...] = jnp.zeros_like(d_ref)
    d_ref[0:1, :] = half_dot(r0, r0)
    d_ref[1:2, :] = half_dot(r0, w0)
    d_ref[2:3, :] = half_dot(w0, w0)


def product_dots_b_kernel(s_high_ref, s_low_ref, u2_ref, r2_ref, w2_ref, s1_ref, z1_ref, y_ref, d_ref):
    multiply(s_high_ref, s_low_ref, u2_ref, y_ref)
    r2, w2, s1, z1 = r2_ref[...], w2_ref[...], s1_ref[...], z1_ref[...]
    d_ref[...] = jnp.zeros_like(d_ref)
    d_ref[0:1, :] = half_dot(r2, r2)
    d_ref[1:2, :] = half_dot(r2, w2)
    d_ref[2:3, :] = half_dot(w2, w2)
    d_ref[3:4, :] = half_dot(w2, s1)
    d_ref[4:5, :] = half_dot(s1, s1)
    d_ref[7:8, :] = half_dot(s1, z1)


def coarse(y_ref, mt_ref, c_ref, g_refs):
    if len(g_refs) == 1:
        loads = g_refs[0][...]
    else:
        loads = jnp.concatenate([ref[0:MODE_PAD, :] for ref in g_refs], axis=0)
    amp = jnp.dot(c_ref[...], loads, precision=HI, preferred_element_type=F32)
    high, mid, low = split3(amp)
    pieces = jnp.concatenate([high, mid, high, mid, low, high], axis=0)
    return y_ref[...] + jnp.dot(mt_ref[...], pieces, preferred_element_type=F32)


def value_kernel(face, n_col, n_dots, send_sums, *refs):
    y_ref, mt_ref, c_ref = refs[:3]
    g_refs = refs[3:3 + n_col]
    rest = refs[3 + n_col:]
    vecs, rest = rest[:len(n_dots)], rest[len(n_dots):]
    if n_dots:
        d_in, rest = rest[0], rest[1:]
    xb, ym, yp, zm, zp = rest[:5]
    value = coarse(y_ref, mt_ref, c_ref, g_refs)
    xb[0:2 * face, :] = value[0:2 * face]
    ym[0:face, :] = value[2 * face:3 * face]
    yp[0:face, :] = value[3 * face:4 * face]
    zm[...] = value[4 * face:5 * face]
    zp[...] = value[5 * face:6 * face]
    if n_dots:
        for ref, at in ((xb, 2 * face), (ym, face), (yp, face)):
            ref[at:at + DOT_PAD, :] = d_in[...]
        for vec, row in zip(vecs, n_dots):
            dot = jnp.sum(vec[...] * value, axis=0, keepdims=True)
            for ref, at in ((xb, 2 * face), (ym, face), (yp, face)):
                ref[at + row:at + row + 1, :] = dot
    if send_sums:
        total = g_refs[0][MODE_PAD:MODE_PAD + DOT_PAD, :]
        for ref in g_refs[1:]:
            total = total + ref[MODE_PAD:MODE_PAD + DOT_PAD, :]
        rest[5][...] = total


def assemble(face, own, got):
    xb, ym, yp, zm, zp = own
    gxb, gyl, gyh, gzl, gzh = got
    f = face
    return jnp.concatenate([
        xb[0:f, :] - gxb[f:2 * f, :],
        xb[f:2 * f, :] - gxb[0:f, :],
        ym[0:f, :] - gyl[0:f, :],
        yp[0:f, :] - gyh[0:f, :],
        zm[...] - gzl[...],
        zp[...] - gzh[...],
    ], axis=0)


def near_sum(face, own, got):
    xb, ym = own[0], own[1]
    gxb, gyl, gyh = got[0], got[1], got[2]
    f = face
    total = xb[2 * f:2 * f + DOT_PAD, :] + gxb[2 * f:2 * f + DOT_PAD, :]
    return total + (gyl[f:f + DOT_PAD, :] + gyh[f:f + DOT_PAD, :])


def image_kernel(face, with_sums, *refs):
    own, got = refs[0:5], refs[5:10]
    modes_ref, vec_ref, u2_ref, g_ref = refs[10:14]
    vec = assemble(face, own, got)
    vec_ref[...] = vec
    publish(vec, modes_ref[...], u2_ref, g_ref)
    if with_sums:
        g_ref[MODE_PAD:MODE_PAD + DOT_PAD, :] = near_sum(face, own, got)


def two_steps(m):
    m0, m1, m2, m3 = (m[i:i + 1, :] for i in range(4))
    alpha0 = m0 / m1
    norm1 = alpha0 * alpha0 * m2 - m0
    curv1 = m1 - 2.0 * alpha0 * m2 + alpha0 * alpha0 * m3
    beta1 = norm1 / m0
    alpha1 = norm1 / (curv1 - beta1 * norm1 / alpha0)
    return alpha0, norm1, beta1, alpha1


def middle_kernel(face, *refs):
    own, got = refs[0:5], refs[5:10]
    sums_refs, (r0_ref, w0_ref, b2_ref, modes_ref), outs = refs[10:12], refs[12:16], refs[16:]
    r2_ref, w2_ref, p1_ref, s1_ref, z1_ref, m2_ref, k_ref, u2_ref, g_ref = outs
    b3 = assemble(face, own, got)
    alpha0, norm1, beta1, alpha1 = two_steps(sums_refs[0][...] + sums_refs[1][...])
    r0, w0, b2 = r0_ref[...], w0_ref[...], b2_ref[...]
    r1 = r0 - alpha0 * w0
    w1 = w0 - alpha0 * b2
    p1 = r1 + beta1 * r0
    s1 = w1 + beta1 * w0
    z1 = (b2 - alpha0 * b3) + beta1 * b2
    w2 = w1 - alpha1 * z1
    r2_ref[...] = r1 - alpha1 * s1
    w2_ref[...] = w2
    p1_ref[...] = p1
    s1_ref[...] = s1
    z1_ref[...] = z1
    m2_ref[...] = alpha0 * r0 + alpha1 * p1
    k_ref[...] = jnp.zeros_like(k_ref)
    k_ref[0:1, :] = norm1
    k_ref[1:2, :] = alpha1
    publish(w2, modes_ref[...], u2_ref, g_ref)


def near_sum_kernel(face, *refs):
    refs[-1][...] = near_sum(face, (refs[0], refs[1]), refs[2:5])


def add_kernel(*refs):
    total = refs[0][...]
    for ref in refs[1:-1]:
        total = total + ref[...]
    refs[-1][...] = total


def last_kernel(face, *refs):
    own, got = refs[0:5], refs[5:10]
    sums_refs, (r2_ref, w2_ref, p1_ref, s1_ref, z1_ref, m2_ref, k_ref) = refs[10:12], refs[12:19]
    mult_ref, resid_ref = refs[19:]
    d = sums_refs[0][...] + sums_refs[1][...]
    rr, rw, ww, ws, ss, wc, sc, sz = (d[i:i + 1, :] for i in range(8))
    norm1, alpha1 = k_ref[0:1, :], k_ref[1:2, :]
    beta2 = rr / norm1
    alpha2 = rr / (rw - beta2 * rr / alpha1)
    norm3 = alpha2 * alpha2 * (ww + 2.0 * beta2 * ws + beta2 * beta2 * ss) - rr
    curv3 = rw - 2.0 * alpha2 * (ww + beta2 * ws)
    curv3 = curv3 + alpha2 * alpha2 * (wc + 2.0 * beta2 * sc + beta2 * beta2 * sz)
    beta3 = norm3 / rr
    alpha3 = norm3 / (curv3 - beta3 * norm3 / alpha2)
    c3 = assemble(face, own, got)
    r2, w2, p1, s1 = r2_ref[...], w2_ref[...], p1_ref[...], s1_ref[...]
    p2 = r2 + beta2 * p1
    s2 = w2 + beta2 * s1
    r3 = r2 - alpha2 * s2
    w3 = w2 - alpha2 * (c3 + beta2 * z1_ref[...])
    p3 = r3 + beta3 * p2
    s3 = w3 + beta3 * s2
    mult = m2_ref[...] + alpha2 * p2 + alpha3 * p3
    resid = r3 - alpha3 * s3
    for f in range(6):
        at = slice(f * face, (f + 1) * face)
        sign = 1.0 if f % 2 == 0 else -1.0
        mult_ref[:, at] = sign * mult[at, :].T
        resid_ref[:, at] = sign * resid[at, :].T


def body(sizes, residual_in, schur, modes, coarse_inv):
    nx, ny, nz = sizes
    resid = residual_in[0, 0, 0]
    matrix = schur[0, 0, 0]
    mode_rows = modes[0, 0, 0]
    loads, width = resid.shape
    face = width // 6
    n_modes = mode_rows.shape[0]
    mode_rows = jnp.pad(mode_rows, ((0, MODE_PAD - n_modes), (0, 0)))
    near = (nx, ny, nz) == (2, 4, 4)

    def shift(x, axis, by):
        n = lax.axis_size(axis)
        return lax.ppermute(x, axis, [(i, (i + by) % n) for i in range(n)])

    blocks = coarse_inv[0, 0].reshape(n_modes, nz, n_modes)
    if nz <= 4:
        turned = jnp.concatenate([blocks[:, ::-1]] * 2, axis=1)
        blocks = lax.dynamic_slice_in_dim(turned, nz - 1 - lax.axis_index("gz"), nz, axis=1)
    pad = MODE_PAD - n_modes
    c_rows = jnp.pad(blocks, ((0, pad), (0, 0), (0, pad))).reshape(MODE_PAD, nz * MODE_PAD)

    def column(msg):
        if nz <= 4:
            return [msg] + [shift(msg, "gz", s) for s in range(1, nz)]
        return [lax.all_gather(msg, "gz", axis=0, tiled=True)]

    def exchange(own):
        xb, ym, yp, zm, zp = own
        if nx == 2:
            gxb = shift(xb, "gx", 1)
        else:
            low, high, dots = xb[:face], xb[face:2 * face], xb[2 * face:]
            gxb = jnp.concatenate([shift(low, "gx", -1), shift(high, "gx", 1), dots], axis=0)
        gyl, gyh = shift(yp, "gy", 1), shift(ym, "gy", -1)
        return (gxb, gyl, gyh, shift(zp, "gz", 1), shift(zm, "gz", -1))

    def far(x):
        pairs = []
        for i in range(nx):
            for j in range(ny):
                pairs.append((i * ny + j, (i + 1) % nx * ny + (j + 2) % ny))
        return lax.ppermute(x, ("gx", "gy"), pairs)

    vec = sds((width, loads))
    u2 = sds((width, 2 * loads), BF16)
    half = sds((width, width), BF16)
    g_msg = sds((MODE_PAD, loads))
    d_msg = sds((DOT_PAD, loads))
    flops = 2 * width * width * 2 * loads * 2

    def faces(extra):
        return [sds((2 * face + extra, loads)), sds((face + extra, loads)), sds((face + extra, loads)), sds((face, loads)), sds((face, loads))]

    def value(y, col, vecs=(), rows=(), d_in=None, send_sums=False):
        outs = faces(DOT_PAD if rows else 0) + ([d_msg] if send_sums else [])
        extra = list(vecs) + ([d_in] if rows else [])
        kern = functools.partial(value_kernel, face, len(col), rows, send_sums)
        res = call(kern, outs, y, mt, c_rows, *col, *extra, flops=2 * width * loads * 24)
        return res[:5], res[5:]

    def total_dots(own, got):
        return lax.psum(own[0][2 * face:], ("gx", "gy", "gz"))

    r0, v2, g, mt = call(
        functools.partial(start_kernel, face),
        [vec, u2, g_msg, sds((width, 6 * MODE_PAD), BF16)], resid, mode_rows)
    col = column(g)
    y, s_high, s_low = call(first_product_kernel, [vec, half, half], matrix, v2, flops=flops)
    own, _ = value(y, col)
    got = exchange(own)

    w0, v2, g = call(functools.partial(image_kernel, face, False), [vec, u2, g_msg], *own, *got, mode_rows)
    col = column(g)
    y, d = call(product_dots_a_kernel, [vec, d_msg], s_high, s_low, v2, r0, w0, flops=flops)
    own, _ = value(y, col, [w0], (3,), d)
    got = exchange(own)

    if near:
        gd_msg = sds((MODE_PAD + DOT_PAD, loads))
        b2, v2, g = call(functools.partial(image_kernel, face, True), [vec, u2, gd_msg], *own, *got, mode_rows)
    else:
        sums = total_dots(own, got)
        b2, v2, g = call(functools.partial(image_kernel, face, False), [vec, u2, g_msg], *own, *got, mode_rows)
    col = column(g)
    y, = call(product_kernel, [vec], s_high, s_low, v2, flops=flops)
    own, part = value(y, col, send_sums=near)
    got = exchange(own)
    pair = (part[0], far(part[0])) if near else (sums, jnp.zeros_like(sums))

    r2, w2, p1, s1, z1, m2, k, v2, g = call(
        functools.partial(middle_kernel, face),
        [vec] * 6 + [d_msg, u2, g_msg], *own, *got, *pair, r0, w0, b2, mode_rows)
    col = column(g)
    y, d = call(product_dots_b_kernel, [vec, d_msg], s_high, s_low, v2, r2, w2, s1, z1, flops=flops)
    own, _ = value(y, col, [w2, s1], (5, 6), d)
    got = exchange(own)

    if near:
        part, = call(functools.partial(near_sum_kernel, face), [d_msg], own[0], own[1], *got[:3])
        part, = call(add_kernel, [d_msg], *column(part))
        pair = (part, far(part))
    else:
        sums = total_dots(own, got)
        pair = (sums, jnp.zeros_like(sums))
    out = sds((loads, width))
    mult, final = call(
        functools.partial(last_kernel, face), [out, out],
        *own, *got, *pair, r2, w2, p1, s1, z1, m2, k)
    return (mult[None, None, None], final[None, None, None])


def solution(mesh):
    spec = P("gx", "gy", "gz", None, None)
    sizes = tuple(mesh.shape[axis] for axis in ("gx", "gy", "gz"))
    return jax.shard_map(
        functools.partial(body, sizes),
        mesh=mesh,
        in_specs=(spec, spec, spec, P("gx", "gy", "gz", None)),
        out_specs=(spec, spec),
        check_vma=False,
    )
```

```python
import functools

import jax
import jax.numpy as jnp
from jax import lax
from jax.experimental import pallas as pl
from jax.experimental.pallas import tpu as pltpu
from jax.sharding import PartitionSpec as P

F32 = jnp.float32
BF16 = jnp.bfloat16
HI = lax.Precision.HIGHEST
PAD = 8
ORDER = (0, -1, 1, 2)
VMEM_LIMIT = 24 * 1024 * 1024


def sds(shape, dtype=F32):
    return jax.ShapeDtypeStruct(shape, dtype)


def call(kernel, ins, outs, flops=0):
    names_in, names_out = list(ins), list(outs)
    nbytes = sum(a.size * a.dtype.itemsize for a in list(ins.values()) + list(outs.values()))

    def run(*refs):
        n = len(names_in)
        kernel(dict(zip(names_in, refs[:n])), dict(zip(names_out, refs[n:])))

    vmem = pl.BlockSpec(memory_space=pltpu.VMEM)
    res = pl.pallas_call(
        run,
        out_shape=[outs[n] for n in names_out],
        in_specs=[vmem] * len(names_in),
        out_specs=[vmem] * len(names_out),
        compiler_params=pltpu.CompilerParams(vmem_limit_bytes=VMEM_LIMIT),
        cost_estimate=pl.CostEstimate(flops=flops, bytes_accessed=nbytes, transcendentals=0),
    )(*[ins[n] for n in names_in])
    return dict(zip(names_out, res))


def split(x):
    high = x.astype(BF16)
    return high, (x - high.astype(F32)).astype(BF16)


def split3(x):
    high = x.astype(BF16)
    rest = x - high.astype(F32)
    mid = rest.astype(BF16)
    return high, mid, (rest - mid.astype(F32)).astype(BF16)


def mode_pieces(modes):
    high, mid, low = split3(modes.T)
    return jnp.concatenate([high, high, mid, mid, high, low], axis=1)


def amp_pieces(amp):
    high, mid, low = split3(amp)
    return jnp.concatenate([high, mid, high, mid, low, high], axis=0)


def dot32(a, b):
    return jnp.dot(a, b, precision=HI, preferred_element_type=F32)


def dot16(a, b):
    return jnp.dot(a, b, preferred_element_type=F32)


def col_sum(x):
    return jnp.sum(x, axis=0, keepdims=True)


def half_dot(a, b):
    return 0.5 * col_sum(a * b)


def row(x, i):
    return x[i:i + 1, :]


def multiply(face, high, low, vec, at):
    cols = vec.shape[1] // 2
    both = dot16(high, vec) + dot16(low, vec)
    return both[:, :cols] + both[:, cols:]


def send_product(face, part, y, o):
    if part < 2:
        o["y"][2 * part * face:2 * (part + 1) * face, :] = y
    else:
        o["zm"][0:face, :] = y[0:face]
        o["zp"][0:face, :] = y[face:]


def send_rows(face, rows, at, o):
    n = rows.shape[0]
    for name, start in (("zm", face), ("zp", face), ("z2", 0)):
        o[name][start + at:start + at + n, :] = rows


def product(face, vec, i, o, want_dot):
    cols = vec.shape[1]
    halves = jnp.concatenate(split(vec), axis=1)
    total = None
    for part in range(3):
        at = slice(2 * part * face, 2 * (part + 1) * face)
        y = multiply(face, i["s_high"][at, :], i["s_low"][at, :], halves, at)
        send_product(face, part, y, o)
        if want_dot:
            dot = col_sum(vec[at] * y)
            total = dot if total is None else total + dot
    send_rows(face, dot32(i["modes"][...], vec), 0, o)
    return total


def stack_rows(rows, cols):
    zero = jnp.zeros((1, cols), F32)
    return jnp.concatenate(list(rows) + [zero] * (PAD - len(rows)), axis=0)


def first_kernel(face, nz, n_modes, turn, resid_hbm, schur_hbm, modes_hbm, coarse_hbm, *refs):
    names = ["r0", "s_high", "s_low", "modes", "mt", "c_own", "y", "zm", "zp", "z2"]
    o = dict(zip(names, refs[:len(names)]))
    resid, schur, mode_rows, coarse, sems = refs[len(names):]
    two = 2 * face
    copies = [
        pltpu.make_async_copy(modes_hbm, mode_rows, sems.at[0]),
        pltpu.make_async_copy(resid_hbm, resid, sems.at[1]),
        pltpu.make_async_copy(coarse_hbm, coarse, sems.at[2]),
    ]
    for part in range(3):
        at = pl.ds(part * two, two)
        copies.append(pltpu.make_async_copy(schur_hbm.at[at, :], schur.at[at, :], sems.at[3 + part]))
    for copy in copies:
        copy.start()

    copies[0].wait()
    modes = jnp.concatenate([mode_rows[m] for m in range(n_modes)], axis=0)
    modes = jnp.concatenate([modes, jnp.zeros((PAD - n_modes, modes.shape[1]), F32)], axis=0)
    o["modes"][...] = modes
    o["mt"][...] = mode_pieces(modes)

    copies[1].wait()
    for f in range(6):
        part = resid[:, f * face:(f + 1) * face].T
        o["r0"][f * face:(f + 1) * face, :] = part if f % 2 == 0 else -part
    r0 = o["r0"][...]
    cols = r0.shape[1]
    send_rows(face, dot32(modes, r0), 0, o)

    copies[2].wait()
    rows = jnp.concatenate([coarse[m] for m in range(n_modes)], axis=0)
    rows = jnp.concatenate([rows, jnp.zeros((PAD - n_modes, rows.shape[1]), F32)], axis=0)
    wide = nz * PAD
    source = lax.broadcasted_iota(jnp.int32, (nz * n_modes, wide), 0)
    place = lax.broadcasted_iota(jnp.int32, (nz * n_modes, wide), 1)
    block, mode = place // PAD, place % PAD

    def ordered(holder):
        if holder is None:
            device = block
        else:
            offset = jnp.zeros_like(block)
            for at, by in enumerate(ORDER):
                offset = jnp.where(block == at, by, offset)
            device = (holder + offset + 2 * nz) % nz
        pick = jnp.where((source == device * n_modes + mode) & (mode < n_modes), 1.0, 0.0)
        return dot32(rows, pick)

    if turn:
        me = lax.axis_index("gz")
        o["c_own"][...] = ordered(me)
        for name, by, start in (("zm", -1, face + 3 * PAD), ("zp", 1, face + 3 * PAD), ("z2", 2, 2 * PAD)):
            o[name][start:start + PAD, :] = jnp.zeros((PAD, cols), F32)
            o[name][start:start + PAD, 0:wide] = ordered(me + by)
    else:
        o["c_own"][...] = ordered(None)
    o["zm"][face + 2 * PAD:face + 3 * PAD, :] = modes[:, 4 * face:5 * face]
    o["zp"][face + 2 * PAD:face + 3 * PAD, :] = modes[:, 5 * face:6 * face]

    halves = jnp.concatenate(split(r0), axis=1)
    curv = jnp.zeros((1, cols), F32)
    for part in range(3):
        at = slice(part * two, (part + 1) * two)
        copies[3 + part].wait()
        high, low = split(schur[at, :])
        o["s_high"][at, :] = high
        o["s_low"][at, :] = low
        y = multiply(face, high, low, halves, at)
        send_product(face, part, y, o)
        curv = curv + col_sum(r0[at] * y)
    send_rows(face, stack_rows([half_dot(r0, r0), curv], cols), PAD, o)


def column_rows(face, i, at):
    return [i["zm"][face + at:face + at + PAD, :], i["gzl"][face + at:face + at + PAD, :],
            i["gzh"][face + at:face + at + PAD, :], i["gz2"][at:at + PAD, :]]


def value_kernel(face, stage, i, o):
    gathered = "g_all" in i
    loads = i["g_all"][...] if gathered else jnp.concatenate(column_rows(face, i, 0), axis=0)
    if stage == 0:
        low = mode_pieces(i["gzl"][face + 2 * PAD:face + 3 * PAD, :])
        high = mode_pieces(i["gzh"][face + 2 * PAD:face + 3 * PAD, :])
        o["mt_low"][...] = low
        o["mt_high"][...] = high
        if gathered:
            coarse = i["c_all"][...]
        else:
            wide = i["c_own"].shape[1]
            at = face + 3 * PAD
            coarse = jnp.concatenate([
                i["c_own"][...], i["gzl"][at:at + PAD, 0:wide], i["gzh"][at:at + PAD, 0:wide],
                i["gz2"][2 * PAD:3 * PAD, 0:wide]], axis=0)
            o["c_all"][...] = coarse
    else:
        low, high, coarse = i["mt_low"][...], i["mt_high"][...], i["c_all"][...]
    amp = dot32(coarse, loads)
    own = amp_pieces(amp[0:PAD])
    mt = i["mt"]
    xy = i["y"][...] + dot16(mt[0:4 * face, :], own)
    z_low = i["zm"][0:face, :] + dot16(mt[4 * face:5 * face, :], own)
    z_low = z_low - (i["gzl"][0:face, :] + dot16(low, amp_pieces(amp[PAD:2 * PAD])))
    z_high = i["zp"][0:face, :] + dot16(mt[5 * face:6 * face, :], own)
    z_high = z_high - (i["gzh"][0:face, :] + dot16(high, amp_pieces(amp[2 * PAD:3 * PAD])))
    cols = loads.shape[1]

    if stage != 2:
        if gathered:
            dots = i["d_all"][...]
            quad = col_sum(loads * amp[3 * PAD:])
        else:
            parts = column_rows(face, i, PAD)
            dots = (parts[0] + parts[1]) + (parts[2] + parts[3])
            quad = col_sum(loads * amp)
        at = {0: 1, 1: 1, 3: 5}[stage]
        dots = jnp.concatenate([dots[0:at], row(dots, at) + quad, dots[at + 1:]], axis=0)
    if stage == 1:
        sums = i["sum_near"][...] + i["sum_far"][...]
        alpha0 = row(sums, 0) / row(sums, 1)
        ratio = alpha0 / row(i["scale"], 0)
        o["known"][...] = stack_rows([row(sums, 0), row(sums, 1), alpha0], cols)
        dots = dots * (ratio * ratio)
        xy, z_low, z_high = xy * ratio, z_low * ratio, z_high * ratio
    o["z"][0:face, :] = z_low
    o["z"][face:, :] = z_high
    o["xb"][0:2 * face, :] = xy[0:2 * face]
    o["ym"][0:face, :] = xy[2 * face:3 * face]
    o["yp"][0:face, :] = xy[3 * face:]
    if stage != 2:
        o["xb"][2 * face:, :] = dots
        o["ym"][face:, :] = dots
        o["yp"][face:, :] = dots


def assemble(face, i):
    f = face
    return jnp.concatenate([
        i["xb"][0:f, :] - i["gxb"][f:2 * f, :],
        i["xb"][f:2 * f, :] - i["gxb"][0:f, :],
        i["ym"][0:f, :] - i["gyl"][0:f, :],
        i["yp"][0:f, :] - i["gyh"][0:f, :],
        i["z"][...],
    ], axis=0)


def near_sum(face, i):
    f = face
    total = i["xb"][2 * f:2 * f + PAD, :] + i["gxb"][2 * f:2 * f + PAD, :]
    return total + (i["gyl"][f:f + PAD, :] + i["gyh"][f:f + PAD, :])


def second_kernel(face, i, o):
    w0 = assemble(face, i)
    o["w0"][...] = w0
    own = i["xb"][2 * face:2 * face + PAD, :]
    scale = row(own, 0) / row(own, 1)
    cols = w0.shape[1]
    o["scale"][...] = stack_rows([scale], cols)
    if "near" in o:
        o["near"][...] = near_sum(face, i)
    vec = scale * w0
    curv = product(face, vec, i, o, True)
    send_rows(face, stack_rows([half_dot(vec, vec), curv], cols), PAD, o)


def third_kernel(face, i, o):
    q = assemble(face, i)
    w1 = i["w0"][...] - q
    o["q"][...] = q
    o["w1"][...] = w1
    if "near" in o:
        o["near"][...] = near_sum(face, i)
    product(face, row(i["known"], 2) * w1, i, o, False)


def fourth_kernel(face, i, o):
    b = assemble(face, i)
    m0, m1, alpha0 = (row(i["known"], k) for k in range(3))
    sums = i["sum_near"][...] + i["sum_far"][...]
    m2, m3 = row(sums, 0), row(sums, 1)
    norm1 = m2 - m0
    curv1 = m1 - 2.0 * (m2 / alpha0) + m3
    beta1 = norm1 / m0
    alpha1 = norm1 / (curv1 - beta1 * norm1 / alpha0)
    r0, w0, w1, q = i["r0"][...], i["w0"][...], i["w1"][...], i["q"][...]
    ratio = alpha1 / alpha0
    r1 = r0 - alpha0 * w0
    p1 = r1 + beta1 * r0
    s1 = alpha1 * (w1 + beta1 * w0)
    r2 = r1 - s1
    z1 = ratio * (b + beta1 * q)
    w2 = w1 - z1
    vec = alpha1 * w2
    cols = w2.shape[1]
    o["r2"][...] = r2
    o["w2"][...] = vec
    o["p1"][...] = p1
    o["s1"][...] = s1
    o["z1"][...] = z1
    o["m2"][...] = alpha0 * r0 + alpha1 * p1
    o["known"][...] = stack_rows([norm1, alpha1], cols)
    curv = product(face, vec, i, o, True)
    send_rows(face, stack_rows([
        half_dot(r2, r2), half_dot(r2, w2), half_dot(vec, vec), half_dot(vec, s1),
        half_dot(s1, s1), curv, half_dot(z1, vec), half_dot(s1, z1)], cols), PAD, o)


def near_kernel(face, i, o):
    o["near"][...] = near_sum(face, i)


def last_kernel(face, i, o):
    d = i["sum_near"][...] + i["sum_far"][...]
    rr, rw, ww, ws, ss, wc, sc, sz = (row(d, k) for k in range(8))
    norm1, alpha1 = row(i["known"], 0), row(i["known"], 1)
    beta2 = rr / norm1
    alpha2 = rr / (rw - beta2 * rr / alpha1)
    ratio = alpha2 / alpha1
    ratio2 = ratio * ratio
    norm3 = ratio2 * (ww + 2.0 * beta2 * ws + beta2 * beta2 * ss) - rr
    curv3 = rw - 2.0 * (ratio2 / alpha2) * (ww + beta2 * ws)
    curv3 = curv3 + ratio2 * (wc + 2.0 * beta2 * sc + beta2 * beta2 * sz)
    beta3 = norm3 / rr
    alpha3 = norm3 / (curv3 - beta3 * norm3 / alpha2)
    c3 = assemble(face, i)
    w2, s1 = i["w2"][...], i["s1"][...]
    p2 = i["r2"][...] + beta2 * i["p1"][...]
    s2 = w2 + beta2 * s1
    r3 = i["r2"][...] - ratio * s2
    w3 = w2 / alpha1 - ratio * (c3 + beta2 * i["z1"][...])
    mult = i["m2"][...] + alpha2 * p2 + alpha3 * (r3 + beta3 * p2)
    resid = r3 - alpha3 * (w3 + (beta3 / alpha1) * s2)
    for f in range(6):
        at = slice(f * face, (f + 1) * face)
        sign = 1.0 if f % 2 == 0 else -1.0
        o["mult"][:, at] = sign * mult[at, :].T
        o["resid"][:, at] = sign * resid[at, :].T


def body(sizes, residual_in, schur, modes, coarse_inv):
    nx, ny, nz = sizes
    resid = residual_in[0, 0, 0]
    matrix = schur[0, 0, 0]
    loads, width = resid.shape
    face = width // 6
    n_modes = modes.shape[3]
    mode_rows = modes.reshape(n_modes, 1, width)
    coarse_rows = coarse_inv.reshape(n_modes, 1, nz * n_modes)
    small = (nx, ny, nz) == (2, 4, 4)

    def shift(x, axis, by):
        n = lax.axis_size(axis)
        return lax.ppermute(x, axis, [(k, (k + by) % n) for k in range(n)])

    def far(x):
        pairs = []
        for a in range(nx):
            for b in range(ny):
                pairs.append((a * ny + b, (a + 1) % nx * ny + (b + 2) % ny))
        return lax.ppermute(x, ("gx", "gy"), pairs)

    def total(x):
        return dict(sum_near=lax.psum(x, ("gx", "gy")), sum_far=jnp.zeros_like(x))

    vec = sds((width, loads))
    rows = sds((PAD, loads))
    half = sds((width, width), BF16)
    flops = 2 * width * width * 2 * loads * 2

    def z_out(extra):
        return dict(y=sds((4 * face, loads)), zm=sds((face + PAD + extra, loads)),
                    zp=sds((face + PAD + extra, loads)), z2=sds((PAD + min(extra, 2 * PAD), loads)))

    def z_exchange(a, with_dots):
        got = dict(zm=a["zm"], zp=a["zp"], y=a["y"], gzl=shift(a["zp"], "gz", 1), gzh=shift(a["zm"], "gz", -1))
        if small:
            got["gz2"] = shift(a["z2"], "gz", 2)
        else:
            got["g_all"] = lax.all_gather(a["z2"][0:PAD], "gz", axis=0, tiled=True)
            if with_dots:
                got["d_all"] = lax.psum(a["z2"][PAD:2 * PAD], "gz")
        return got

    def value(stage, ins):
        extra = 0 if stage == 2 else PAD
        outs = dict(z=sds((2 * face, loads)), xb=sds((2 * face + extra, loads)),
                    ym=sds((face + extra, loads)), yp=sds((face + extra, loads)))
        if stage == 0:
            outs.update(mt_low=sds((face, 6 * PAD), BF16), mt_high=sds((face, 6 * PAD), BF16))
            if small:
                outs["c_all"] = sds((nz * PAD, nz * PAD))
        if stage == 1:
            outs["known"] = rows
        return call(functools.partial(value_kernel, face, stage), ins, outs, flops=2 * width * loads * 48)

    def xy_exchange(v):
        got = {name: v[name] for name in ("z", "xb", "ym", "yp")}
        if nx == 2:
            got["gxb"] = shift(v["xb"], "gx", 1)
        else:
            low, high, rest = v["xb"][:face], v["xb"][face:2 * face], v["xb"][2 * face:]
            got["gxb"] = jnp.concatenate([shift(low, "gx", -1), shift(high, "gx", 1), rest], axis=0)
        got["gyl"] = shift(v["yp"], "gy", 1)
        got["gyh"] = shift(v["ym"], "gy", -1)
        return got

    near = dict(near=rows) if small else {}

    hbm = pl.BlockSpec(memory_space=pltpu.HBM)
    vmem = pl.BlockSpec(memory_space=pltpu.VMEM)
    outs = dict(r0=vec, s_high=half, s_low=half, modes=sds((PAD, width)), mt=sds((width, 6 * PAD), BF16),
                c_own=sds((PAD, nz * PAD)), **z_out(3 * PAD))
    res = pl.pallas_call(
        functools.partial(first_kernel, face, nz, n_modes, small),
        out_shape=list(outs.values()),
        in_specs=[hbm] * 4,
        out_specs=[vmem] * len(outs),
        scratch_shapes=[
            pltpu.VMEM(resid.shape, F32), pltpu.VMEM(matrix.shape, F32),
            pltpu.VMEM(mode_rows.shape, F32), pltpu.VMEM(coarse_rows.shape, F32),
            pltpu.SemaphoreType.DMA((6,)),
        ],
        compiler_params=pltpu.CompilerParams(vmem_limit_bytes=VMEM_LIMIT),
        cost_estimate=pl.CostEstimate(flops=flops, bytes_accessed=4 * matrix.size, transcendentals=0),
    )(resid, matrix, mode_rows, coarse_rows)
    a = dict(zip(outs, res))
    r0, mt = a["r0"], a["mt"]
    fixed = dict(s_high=a["s_high"], s_low=a["s_low"], modes=a["modes"])
    ins = dict(z_exchange(a, True), mt=mt)
    if small:
        ins["c_own"] = a["c_own"]
    else:
        c_own = a["c_own"]
        ins["c_all"] = jnp.concatenate([
            c_own, shift(c_own, "gz", 1), shift(c_own, "gz", -1),
            lax.all_gather(c_own, "gz", axis=0, tiled=True)], axis=0)
    v = value(0, ins)
    column = dict(mt=mt, mt_low=v["mt_low"], mt_high=v["mt_high"], c_all=v["c_all"] if small else ins["c_all"])
    x = xy_exchange(v)

    a = call(functools.partial(second_kernel, face), dict(x, **fixed),
             dict(w0=vec, scale=rows, **near, **z_out(PAD)), flops=flops)
    w0 = a["w0"]
    sums = dict(sum_near=a["near"], sum_far=far(a["near"])) if small else total(v["xb"][2 * face:])
    v = value(1, dict(z_exchange(a, True), **column, **sums, scale=a["scale"]))
    known = v["known"]
    x = xy_exchange(v)

    a = call(functools.partial(third_kernel, face), dict(x, **fixed, w0=w0, known=known),
             dict(q=vec, w1=vec, **near, **z_out(0)), flops=flops)
    sums = dict(sum_near=a["near"], sum_far=far(a["near"])) if small else total(v["xb"][2 * face:])
    q, w1 = a["q"], a["w1"]
    v = value(2, dict(z_exchange(a, False), **column))
    x = xy_exchange(v)

    names = ("r2", "w2", "p1", "s1", "z1", "m2")
    a = call(functools.partial(fourth_kernel, face),
             dict(x, **fixed, **sums, known=known, r0=r0, w0=w0, w1=w1, q=q),
             dict({name: vec for name in names}, known=rows, **z_out(PAD)), flops=flops)
    v = value(3, dict(z_exchange(a, True), **column))
    x = xy_exchange(v)
    if small:
        part = call(functools.partial(near_kernel, face), {name: x[name] for name in ("xb", "gxb", "gyl", "gyh")}, near)["near"]
        sums = dict(sum_near=part, sum_far=far(part))
    else:
        sums = total(v["xb"][2 * face:])
    out = sds((loads, width))
    res = call(functools.partial(last_kernel, face),
               dict(x, **sums, known=a["known"], **{name: a[name] for name in names}),
               dict(mult=out, resid=out))
    return (res["mult"][None, None, None], res["resid"][None, None, None])


def solution(mesh):
    spec = P("gx", "gy", "gz", None, None)
    sizes = tuple(mesh.shape[axis] for axis in ("gx", "gy", "gz"))
    return jax.shard_map(
        functools.partial(body, sizes),
        mesh=mesh,
        in_specs=(spec, spec, spec, P("gx", "gy", "gz", None)),
        out_specs=(spec, spec),
        check_vma=False,
    )
```

```python
import functools

import jax
import jax.numpy as jnp
from jax import lax
from jax.experimental import pallas as pl
from jax.experimental.pallas import tpu as pltpu
from jax.sharding import PartitionSpec as P

F32 = jnp.float32
BF16 = jnp.bfloat16
HI = lax.Precision.HIGHEST
PAD = 8
VMEM_LIMIT = 24 * 1024 * 1024


def sds(shape, dtype=F32):
    return jax.ShapeDtypeStruct(shape, dtype)


def call(kernel, ins, outs, flops=0):
    names_in, names_out = list(ins), list(outs)
    nbytes = sum(a.size * a.dtype.itemsize for a in list(ins.values()) + list(outs.values()))

    def run(*refs):
        n = len(names_in)
        kernel(dict(zip(names_in, refs[:n])), dict(zip(names_out, refs[n:])))

    vmem = pl.BlockSpec(memory_space=pltpu.VMEM)
    res = pl.pallas_call(
        run,
        out_shape=[outs[n] for n in names_out],
        in_specs=[vmem] * len(names_in),
        out_specs=[vmem] * len(names_out),
        compiler_params=pltpu.CompilerParams(vmem_limit_bytes=VMEM_LIMIT),
        cost_estimate=pl.CostEstimate(flops=flops, bytes_accessed=nbytes, transcendentals=0),
    )(*[ins[n] for n in names_in])
    return dict(zip(names_out, res))


def split(x):
    high = x.astype(BF16)
    return high, (x - high.astype(F32)).astype(BF16)


def split3(x):
    high = x.astype(BF16)
    rest = x - high.astype(F32)
    mid = rest.astype(BF16)
    return high, mid, (rest - mid.astype(F32)).astype(BF16)


def mode_pieces(modes):
    high, mid, low = split3(modes.T)
    return jnp.concatenate([high, high, mid, mid, high, low], axis=1)


def amp_pieces(amp):
    high, mid, low = split3(amp)
    return jnp.concatenate([high, mid, high, mid, low, high], axis=0)


def dot32(a, b):
    return jnp.dot(a, b, precision=HI, preferred_element_type=F32)


def dot16(a, b):
    return jnp.dot(a, b, preferred_element_type=F32)


def col_sum(x):
    return jnp.sum(x, axis=0, keepdims=True)


def half_dot(a, b):
    return 0.5 * col_sum(a * b)


def row(x, i):
    return x[i:i + 1, :]


def face_places(face):
    places, signs = [], []
    for k, axis in enumerate(("gx", "gy", "gz")):
        odd = lax.rem(lax.axis_index(axis), 2)
        for high in (1 - odd, odd):
            places.append(pl.multiple_of((2 * k + high) * face, face))
            signs.append((1 - 2 * high).astype(F32))
    return places, signs


def multiply(high, low, vec):
    cols = vec.shape[1] // 2
    both = dot16(high, vec) + dot16(low, vec)
    return both[:, :cols] + both[:, cols:]


def send_product(face, part, y, o):
    if part < 2:
        o["y"][2 * part * face:2 * (part + 1) * face, :] = y
    else:
        o["za"][0:face, :] = y[0:face]
        o["zb"][0:face, :] = y[face:]


def send_rows(face, rows, at, o):
    n = rows.shape[0]
    for name, start in (("za", face), ("zb", face), ("z2", 0)):
        o[name][start + at:start + at + n, :] = rows


def product(face, vec, i, o, want_dot):
    cols = vec.shape[1]
    halves = jnp.concatenate(split(vec), axis=1)
    total = None
    for part in range(3):
        at = slice(2 * part * face, 2 * (part + 1) * face)
        y = multiply(i["s_high"][at, :], i["s_low"][at, :], halves)
        send_product(face, part, y, o)
        if want_dot:
            dot = col_sum(vec[at] * y)
            total = dot if total is None else total + dot
    send_rows(face, dot32(i["modes"][...], vec), 0, o)
    return total


def stack_rows(rows, cols):
    zero = jnp.zeros((1, cols), F32)
    return jnp.concatenate(list(rows) + [zero] * (PAD - len(rows)), axis=0)


def first_kernel(face, nz, n_modes, turn, resid_hbm, schur_hbm, modes_hbm, coarse_hbm, *refs):
    names = ["r0", "s_high", "s_low", "modes", "mt", "c_own", "y", "za", "zb", "z2"]
    o = dict(zip(names, refs[:len(names)]))
    resid, schur, mode_rows, coarse, sems = refs[len(names):]
    two = 2 * face
    places, signs = face_places(face)
    copies = [
        pltpu.make_async_copy(modes_hbm, mode_rows, sems.at[0]),
        pltpu.make_async_copy(resid_hbm, resid, sems.at[1]),
        pltpu.make_async_copy(coarse_hbm, coarse, sems.at[2]),
    ]
    for f in range(6):
        at = pl.ds(f * face, face)
        copies.append(pltpu.make_async_copy(schur_hbm.at[pl.ds(places[f], face), :], schur.at[at, :], sems.at[3 + f]))
    for copy in copies:
        copy.start()

    copies[0].wait()
    modes = jnp.concatenate([
        jnp.concatenate([mode_rows[m, :, pl.ds(at, face)] for at in places], axis=1)
        for m in range(n_modes)], axis=0)
    modes = jnp.concatenate([modes, jnp.zeros((PAD - n_modes, modes.shape[1]), F32)], axis=0)
    o["modes"][...] = modes
    o["mt"][...] = mode_pieces(modes)

    copies[1].wait()
    for f in range(6):
        o["r0"][f * face:(f + 1) * face, :] = signs[f] * resid[:, pl.ds(places[f], face)].T
    r0 = o["r0"][...]
    cols = r0.shape[1]
    send_rows(face, dot32(modes, r0), 0, o)

    copies[2].wait()
    rows = jnp.concatenate([coarse[m] for m in range(n_modes)], axis=0)
    rows = jnp.concatenate([rows, jnp.zeros((PAD - n_modes, rows.shape[1]), F32)], axis=0)
    wide = nz * PAD
    source = lax.broadcasted_iota(jnp.int32, (nz * n_modes, wide), 0)
    place = lax.broadcasted_iota(jnp.int32, (nz * n_modes, wide), 1)
    block, mode = place // PAD, place % PAD

    def ordered(device):
        pick = jnp.where((source == device * n_modes + mode) & (mode < n_modes), 1.0, 0.0)
        return dot32(rows, pick)

    def held_by(holder, side):
        offset = jnp.where(block == 1, side, jnp.where(block == 2, -side, 2 * (block // 3)))
        return ordered((holder + offset + 2 * nz) % nz)

    if turn:
        me = lax.axis_index("gz")
        side = 1 - 2 * lax.rem(me, 2)
        o["c_own"][...] = held_by(me, side)
        sent = (("za", me + side, -side, face + 3 * PAD), ("zb", me - side, -side, face + 3 * PAD), ("z2", me + 2, side, 2 * PAD))
        for name, holder, holder_side, start in sent:
            o[name][start:start + PAD, :] = jnp.zeros((PAD, cols), F32)
            o[name][start:start + PAD, 0:wide] = held_by(holder, holder_side)
    else:
        o["c_own"][...] = ordered(block)
    o["za"][face + 2 * PAD:face + 3 * PAD, :] = modes[:, 4 * face:5 * face]
    o["zb"][face + 2 * PAD:face + 3 * PAD, :] = modes[:, 5 * face:6 * face]

    halves = jnp.concatenate(split(r0), axis=1)
    curv = jnp.zeros((1, cols), F32)
    for part in range(3):
        at = slice(part * two, (part + 1) * two)
        copies[3 + 2 * part].wait()
        copies[4 + 2 * part].wait()
        high, low = split(jnp.concatenate([schur[at, pl.ds(start, face)] for start in places], axis=1))
        o["s_high"][at, :] = high
        o["s_low"][at, :] = low
        y = multiply(high, low, halves)
        send_product(face, part, y, o)
        curv = curv + col_sum(r0[at] * y)
    send_rows(face, stack_rows([half_dot(r0, r0), curv], cols), PAD, o)


def column_rows(face, i, at):
    return [i["za"][face + at:face + at + PAD, :], i["gza"][face + at:face + at + PAD, :],
            i["gzb"][face + at:face + at + PAD, :], i["gz2"][at:at + PAD, :]]


def value_kernel(face, stage, i, o):
    gathered = "g_all" in i
    loads = i["g_all"][...] if gathered else jnp.concatenate(column_rows(face, i, 0), axis=0)
    if stage == 0:
        mt_a = mode_pieces(i["gza"][face + 2 * PAD:face + 3 * PAD, :])
        mt_b = mode_pieces(i["gzb"][face + 2 * PAD:face + 3 * PAD, :])
        o["mt_a"][...] = mt_a
        o["mt_b"][...] = mt_b
        if gathered:
            coarse = i["c_all"][...]
        else:
            wide = i["c_own"].shape[1]
            at = face + 3 * PAD
            coarse = jnp.concatenate([
                i["c_own"][...], i["gza"][at:at + PAD, 0:wide], i["gzb"][at:at + PAD, 0:wide],
                i["gz2"][2 * PAD:3 * PAD, 0:wide]], axis=0)
            o["c_all"][...] = coarse
    else:
        mt_a, mt_b, coarse = i["mt_a"][...], i["mt_b"][...], i["c_all"][...]
    amp = dot32(coarse, loads)
    own = amp_pieces(amp[0:PAD])
    mt = i["mt"]
    xy = i["y"][...] + dot16(mt[0:4 * face, :], own)
    z_a = i["za"][0:face, :] + dot16(mt[4 * face:5 * face, :], own)
    z_a = z_a - (i["gza"][0:face, :] + dot16(mt_a, amp_pieces(amp[PAD:2 * PAD])))
    z_b = i["zb"][0:face, :] + dot16(mt[5 * face:6 * face, :], own)
    z_b = z_b - (i["gzb"][0:face, :] + dot16(mt_b, amp_pieces(amp[2 * PAD:3 * PAD])))
    cols = loads.shape[1]

    if stage != 2:
        if gathered:
            dots = i["d_all"][...]
            quad = col_sum(loads * amp[3 * PAD:])
        else:
            parts = column_rows(face, i, PAD)
            dots = (parts[0] + parts[1]) + (parts[2] + parts[3])
            quad = col_sum(loads * amp)
        at = {0: 1, 1: 1, 3: 5}[stage]
        dots = jnp.concatenate([dots[0:at], row(dots, at) + quad, dots[at + 1:]], axis=0)
    if stage == 1:
        sums = i["sum_near"][...] + i["sum_far"][...]
        alpha0 = row(sums, 0) / row(sums, 1)
        ratio = alpha0 / row(i["scale"], 0)
        o["known"][...] = stack_rows([row(sums, 0), row(sums, 1), alpha0], cols)
        dots = dots * (ratio * ratio)
        xy, z_a, z_b = xy * ratio, z_a * ratio, z_b * ratio
    o["z"][0:face, :] = z_a
    o["z"][face:, :] = z_b
    o["xab"][0:2 * face, :] = xy[0:2 * face]
    o["ya"][0:face, :] = xy[2 * face:3 * face]
    o["yb"][0:face, :] = xy[3 * face:]
    if stage == 3:
        o["dots"][...] = dots
    elif stage != 2:
        o["xab"][2 * face:, :] = dots
        o["ya"][face:, :] = dots
        o["yb"][face:, :] = dots


def assemble(face, i):
    f = face
    return jnp.concatenate([
        i["xab"][0:2 * f, :] - i["gxab"][0:2 * f, :],
        i["ya"][0:f, :] - i["gya"][0:f, :],
        i["yb"][0:f, :] - i["gyb"][0:f, :],
        i["z"][...],
    ], axis=0)


def near_sum(face, i):
    f = face
    total = i["xab"][2 * f:2 * f + PAD, :] + i["gxab"][2 * f:2 * f + PAD, :]
    return total + (i["gya"][f:f + PAD, :] + i["gyb"][f:f + PAD, :])


def second_kernel(face, i, o):
    w0 = assemble(face, i)
    o["w0"][...] = w0
    own = i["xab"][2 * face:2 * face + PAD, :]
    scale = row(own, 0) / row(own, 1)
    cols = w0.shape[1]
    o["scale"][...] = stack_rows([scale], cols)
    if "near" in o:
        o["near"][...] = near_sum(face, i)
    vec = scale * w0
    curv = product(face, vec, i, o, True)
    send_rows(face, stack_rows([half_dot(vec, vec), curv], cols), PAD, o)


def third_kernel(face, i, o):
    q = assemble(face, i)
    w1 = i["w0"][...] - q
    o["q"][...] = q
    o["w1"][...] = w1
    if "near" in o:
        o["near"][...] = near_sum(face, i)
    product(face, row(i["known"], 2) * w1, i, o, False)


def fourth_kernel(face, i, o):
    b = assemble(face, i)
    m0, m1, alpha0 = (row(i["known"], k) for k in range(3))
    sums = i["sum_near"][...] + i["sum_far"][...]
    m2, m3 = row(sums, 0), row(sums, 1)
    norm1 = m2 - m0
    curv1 = m1 - 2.0 * (m2 / alpha0) + m3
    beta1 = norm1 / m0
    alpha1 = norm1 / (curv1 - beta1 * norm1 / alpha0)
    r0, w0, w1, q = i["r0"][...], i["w0"][...], i["w1"][...], i["q"][...]
    ratio = alpha1 / alpha0
    r1 = r0 - alpha0 * w0
    p1 = r1 + beta1 * r0
    s1 = alpha1 * (w1 + beta1 * w0)
    r2 = r1 - s1
    z1 = ratio * (b + beta1 * q)
    w2 = w1 - z1
    vec = alpha1 * w2
    cols = w2.shape[1]
    o["r2"][...] = r2
    o["w2"][...] = vec
    o["p1"][...] = p1
    o["s1"][...] = s1
    o["z1"][...] = z1
    o["m2"][...] = alpha0 * r0 + alpha1 * p1
    o["known"][...] = stack_rows([norm1, alpha1], cols)
    curv = product(face, vec, i, o, True)
    send_rows(face, stack_rows([
        half_dot(r2, r2), half_dot(r2, w2), half_dot(vec, vec), half_dot(vec, s1),
        half_dot(s1, s1), curv, half_dot(z1, vec), half_dot(s1, z1)], cols), PAD, o)


def pair_kernel(face, i, o):
    total = i["dots"][...] + i["gdots"][...]
    o["pair"][...] = total
    for name in ("ya", "yb"):
        o[name][0:face, :] = i[name][...]
        o[name][face:, :] = total


def last_kernel(face, i, o):
    if "sum" in i:
        d = i["sum"][...]
    else:
        d = (i["pair"][...] + i["gpair"][...]) + (i["gya"][face:, :] + i["gyb"][face:, :])
    rr, rw, ww, ws, ss, wc, sc, sz = (row(d, k) for k in range(8))
    norm1, alpha1 = row(i["known"], 0), row(i["known"], 1)
    beta2 = rr / norm1
    alpha2 = rr / (rw - beta2 * rr / alpha1)
    ratio = alpha2 / alpha1
    ratio2 = ratio * ratio
    norm3 = ratio2 * (ww + 2.0 * beta2 * ws + beta2 * beta2 * ss) - rr
    curv3 = rw - 2.0 * (ratio2 / alpha2) * (ww + beta2 * ws)
    curv3 = curv3 + ratio2 * (wc + 2.0 * beta2 * sc + beta2 * beta2 * sz)
    beta3 = norm3 / rr
    alpha3 = norm3 / (curv3 - beta3 * norm3 / alpha2)
    c3 = assemble(face, i)
    w2, s1 = i["w2"][...], i["s1"][...]
    p2 = i["r2"][...] + beta2 * i["p1"][...]
    s2 = w2 + beta2 * s1
    r3 = i["r2"][...] - ratio * s2
    w3 = w2 / alpha1 - ratio * (c3 + beta2 * i["z1"][...])
    mult = i["m2"][...] + alpha2 * p2 + alpha3 * (r3 + beta3 * p2)
    resid = r3 - alpha3 * (w3 + (beta3 / alpha1) * s2)
    places, signs = face_places(face)
    for f in range(6):
        at = slice(f * face, (f + 1) * face)
        o["mult"][:, pl.ds(places[f], face)] = signs[f] * mult[at, :].T
        o["resid"][:, pl.ds(places[f], face)] = signs[f] * resid[at, :].T


def body(sizes, residual_in, schur, modes, coarse_inv):
    nx, ny, nz = sizes
    resid = residual_in[0, 0, 0]
    matrix = schur[0, 0, 0]
    loads, width = resid.shape
    face = width // 6
    n_modes = modes.shape[3]
    mode_rows = modes.reshape(n_modes, 1, width)
    coarse_rows = coarse_inv.reshape(n_modes, 1, nz * n_modes)
    small = (nx, ny, nz) == (2, 4, 4)

    def shift(x, axis, by):
        n = lax.axis_size(axis)
        return lax.ppermute(x, axis, [(k, (k + by) % n) for k in range(n)])

    def swap(x, axis, first):
        n = lax.axis_size(axis)
        side = lambda k: 1 if (k - first) % 2 == 0 else -1
        return lax.ppermute(x, axis, [(k, (k + side(k)) % n) for k in range(n)])

    def far(x):
        pairs = []
        for a in range(nx):
            for b in range(ny):
                pairs.append((a * ny + b, (a + 1) % nx * ny + (b + 2) % ny))
        return lax.ppermute(x, ("gx", "gy"), pairs)

    def total(x):
        return dict(sum_near=lax.psum(x, ("gx", "gy")), sum_far=jnp.zeros_like(x))

    vec = sds((width, loads))
    rows = sds((PAD, loads))
    half = sds((width, width), BF16)
    flops = 2 * width * width * 2 * loads * 2

    def z_out(extra):
        return dict(y=sds((4 * face, loads)), za=sds((face + PAD + extra, loads)),
                    zb=sds((face + PAD + extra, loads)), z2=sds((PAD + min(extra, 2 * PAD), loads)))

    def z_exchange(a, with_dots):
        got = dict(za=a["za"], zb=a["zb"], y=a["y"], gza=swap(a["za"], "gz", 0), gzb=swap(a["zb"], "gz", 1))
        if small:
            got["gz2"] = shift(a["z2"], "gz", 2)
        else:
            got["g_all"] = lax.all_gather(a["z2"][0:PAD], "gz", axis=0, tiled=True)
            if with_dots:
                got["d_all"] = lax.psum(a["z2"][PAD:2 * PAD], "gz")
        return got

    def value(stage, ins):
        extra = PAD if stage < 2 else 0
        outs = dict(z=sds((2 * face, loads)), xab=sds((2 * face + extra, loads)),
                    ya=sds((face + extra, loads)), yb=sds((face + extra, loads)))
        if stage == 0:
            outs.update(mt_a=sds((face, 6 * PAD), BF16), mt_b=sds((face, 6 * PAD), BF16))
            if small:
                outs["c_all"] = sds((nz * PAD, nz * PAD))
        if stage == 1:
            outs["known"] = rows
        if stage == 3:
            outs["dots"] = rows
        return call(functools.partial(value_kernel, face, stage), ins, outs, flops=2 * width * loads * 48)

    def x_exchange(v):
        got = dict(z=v["z"], xab=v["xab"])
        if nx == 2:
            got["gxab"] = swap(v["xab"], "gx", 0)
        else:
            a, b, rest = v["xab"][:face], v["xab"][face:2 * face], v["xab"][2 * face:]
            got["gxab"] = jnp.concatenate([swap(a, "gx", 0), swap(b, "gx", 1), rest], axis=0)
        return got

    def y_exchange(v):
        return dict(ya=v["ya"], yb=v["yb"], gya=swap(v["ya"], "gy", 0), gyb=swap(v["yb"], "gy", 1))

    def xy_exchange(v):
        return dict(x_exchange(v), **y_exchange(v))

    near = dict(near=rows) if small else {}

    hbm = pl.BlockSpec(memory_space=pltpu.HBM)
    vmem = pl.BlockSpec(memory_space=pltpu.VMEM)
    outs = dict(r0=vec, s_high=half, s_low=half, modes=sds((PAD, width)), mt=sds((width, 6 * PAD), BF16),
                c_own=sds((PAD, nz * PAD)), **z_out(3 * PAD))
    res = pl.pallas_call(
        functools.partial(first_kernel, face, nz, n_modes, small),
        out_shape=list(outs.values()),
        in_specs=[hbm] * 4,
        out_specs=[vmem] * len(outs),
        scratch_shapes=[
            pltpu.VMEM(resid.shape, F32), pltpu.VMEM(matrix.shape, F32),
            pltpu.VMEM(mode_rows.shape, F32), pltpu.VMEM(coarse_rows.shape, F32),
            pltpu.SemaphoreType.DMA((9,)),
        ],
        compiler_params=pltpu.CompilerParams(vmem_limit_bytes=VMEM_LIMIT),
        cost_estimate=pl.CostEstimate(flops=flops, bytes_accessed=4 * matrix.size, transcendentals=0),
    )(*[pltpu.with_memory_space_constraint(x, pltpu.HBM) for x in (resid, matrix, mode_rows, coarse_rows)])
    a = dict(zip(outs, res))
    r0, mt = a["r0"], a["mt"]
    fixed = dict(s_high=a["s_high"], s_low=a["s_low"], modes=a["modes"])
    ins = dict(z_exchange(a, True), mt=mt)
    if small:
        ins["c_own"] = a["c_own"]
    else:
        c_own = a["c_own"]
        ins["c_all"] = jnp.concatenate([
            c_own, swap(c_own, "gz", 0), swap(c_own, "gz", 1),
            lax.all_gather(c_own, "gz", axis=0, tiled=True)], axis=0)
    v = value(0, ins)
    column = dict(mt=mt, mt_a=v["mt_a"], mt_b=v["mt_b"], c_all=v["c_all"] if small else ins["c_all"])
    x = xy_exchange(v)

    a = call(functools.partial(second_kernel, face), dict(x, **fixed),
             dict(w0=vec, scale=rows, **near, **z_out(PAD)), flops=flops)
    w0 = a["w0"]
    sums = dict(sum_near=a["near"], sum_far=far(a["near"])) if small else total(v["xab"][2 * face:])
    v = value(1, dict(z_exchange(a, True), **column, **sums, scale=a["scale"]))
    known = v["known"]
    x = xy_exchange(v)

    a = call(functools.partial(third_kernel, face), dict(x, **fixed, w0=w0, known=known),
             dict(q=vec, w1=vec, **near, **z_out(0)), flops=flops)
    sums = dict(sum_near=a["near"], sum_far=far(a["near"])) if small else total(v["xab"][2 * face:])
    q, w1 = a["q"], a["w1"]
    v = value(2, dict(z_exchange(a, False), **column))
    x = xy_exchange(v)

    names = ("r2", "w2", "p1", "s1", "z1", "m2")
    a = call(functools.partial(fourth_kernel, face),
             dict(x, **fixed, **sums, known=known, r0=r0, w0=w0, w1=w1, q=q),
             dict({name: vec for name in names}, known=rows, **z_out(PAD)), flops=flops)
    v = value(3, dict(z_exchange(a, True), **column))
    if small:
        p = call(functools.partial(pair_kernel, face),
                 dict(dots=v["dots"], gdots=swap(v["dots"], "gx", 0), ya=v["ya"], yb=v["yb"]),
                 dict(pair=rows, ya=sds((face + PAD, loads)), yb=sds((face + PAD, loads))))
        sums = dict(pair=p["pair"], gpair=shift(p["pair"], "gy", 2))
        x = dict(x_exchange(v), **y_exchange(p))
    else:
        sums = dict(sum=lax.psum(v["dots"], ("gx", "gy")))
        x = xy_exchange(v)
    out = sds((loads, width))
    res = call(functools.partial(last_kernel, face),
               dict(x, **sums, known=a["known"], **{name: a[name] for name in names}),
               dict(mult=out, resid=out))
    return (res["mult"][None, None, None], res["resid"][None, None, None])


def solution(mesh):
    spec = P("gx", "gy", "gz", None, None)
    sizes = tuple(mesh.shape[axis] for axis in ("gx", "gy", "gz"))
    return jax.shard_map(
        functools.partial(body, sizes),
        mesh=mesh,
        in_specs=(spec, spec, spec, P("gx", "gy", "gz", None)),
        out_specs=(spec, spec),
        check_vma=False,
    )
```

```python
import functools

import jax
import jax.numpy as jnp
from jax import lax
from jax.experimental import pallas as pl
from jax.experimental.pallas import tpu as pltpu
from jax.sharding import PartitionSpec as P

F32 = jnp.float32
BF16 = jnp.bfloat16
HI = lax.Precision.HIGHEST
PAD = 8
VMEM_LIMIT = 24 * 1024 * 1024


def sds(shape, dtype=F32):
    return jax.ShapeDtypeStruct(shape, dtype)


def call(kernel, ins, outs, flops=0):
    names_in, names_out = list(ins), list(outs)
    nbytes = sum(a.size * a.dtype.itemsize for a in list(ins.values()) + list(outs.values()))

    def run(*refs):
        n = len(names_in)
        kernel(dict(zip(names_in, refs[:n])), dict(zip(names_out, refs[n:])))

    vmem = pl.BlockSpec(memory_space=pltpu.VMEM)
    res = pl.pallas_call(
        run,
        out_shape=[outs[n] for n in names_out],
        in_specs=[vmem] * len(names_in),
        out_specs=[vmem] * len(names_out),
        compiler_params=pltpu.CompilerParams(vmem_limit_bytes=VMEM_LIMIT),
        cost_estimate=pl.CostEstimate(flops=flops, bytes_accessed=nbytes, transcendentals=0),
    )(*[ins[n] for n in names_in])
    return dict(zip(names_out, res))


def split(x):
    high = x.astype(BF16)
    return high, (x - high.astype(F32)).astype(BF16)


def split3(x):
    high = x.astype(BF16)
    rest = x - high.astype(F32)
    mid = rest.astype(BF16)
    return high, mid, (rest - mid.astype(F32)).astype(BF16)


def mode_pieces(modes):
    high, mid, low = split3(modes.T)
    return jnp.concatenate([high, high, mid, mid, high, low], axis=1)


def amp_pieces(amp):
    high, mid, low = split3(amp)
    return jnp.concatenate([high, mid, high, mid, low, high], axis=0)


def dot32(a, b):
    return jnp.dot(a, b, precision=HI, preferred_element_type=F32)


def dot16(a, b):
    return jnp.dot(a, b, preferred_element_type=F32)


def col_sum(x):
    return jnp.sum(x, axis=0, keepdims=True)


def half_dot(a, b):
    return 0.5 * col_sum(a * b)


def row(x, i):
    return x[i:i + 1, :]


def face_places(face):
    places, signs = [], []
    for k, axis in enumerate(("gx", "gy", "gz")):
        odd = lax.rem(lax.axis_index(axis), 2)
        for high in (1 - odd, odd):
            places.append(pl.multiple_of((2 * k + high) * face, face))
            signs.append((1 - 2 * high).astype(F32))
    return places, signs


def multiply(high, low, vec):
    cols = vec.shape[1] // 2
    both = dot16(high, vec) + dot16(low, vec)
    return both[:, :cols] + both[:, cols:]


def send_product(face, part, y, o):
    if part < 2:
        o["y"][2 * part * face:2 * (part + 1) * face, :] = y
    else:
        o["za"][0:face, :] = y[0:face]
        o["zb"][0:face, :] = y[face:]


def send_rows(face, rows, at, o):
    n = rows.shape[0]
    for name, start in (("za", face), ("zb", face), ("z2", 0)):
        o[name][start + at:start + at + n, :] = rows


def product(face, vec, i, o, want_dot):
    cols = vec.shape[1]
    halves = jnp.concatenate(split(vec), axis=1)
    total = None
    for part in range(3):
        at = slice(2 * part * face, 2 * (part + 1) * face)
        y = multiply(i["s_high"][at, :], i["s_low"][at, :], halves)
        send_product(face, part, y, o)
        if want_dot:
            dot = col_sum(vec[at] * y)
            total = dot if total is None else total + dot
    send_rows(face, dot32(i["modes"][...], vec), 0, o)
    return total


def stack_rows(rows, cols):
    zero = jnp.zeros((1, cols), F32)
    return jnp.concatenate(list(rows) + [zero] * (PAD - len(rows)), axis=0)


def first_kernel(face, nz, n_modes, turn, resid_hbm, schur_hbm, modes_hbm, coarse_hbm, *refs):
    names = ["r0", "s_high", "s_low", "modes", "mt", "c_own", "y", "za", "zb", "z2"]
    o = dict(zip(names, refs[:len(names)]))
    resid, schur, mode_rows, coarse, sems = refs[len(names):]
    two = 2 * face
    places, signs = face_places(face)
    copies = [
        pltpu.make_async_copy(modes_hbm, mode_rows, sems.at[0]),
        pltpu.make_async_copy(resid_hbm, resid, sems.at[1]),
        pltpu.make_async_copy(coarse_hbm, coarse, sems.at[2]),
    ]
    for f in range(6):
        at = pl.ds(f * face, face)
        copies.append(pltpu.make_async_copy(schur_hbm.at[pl.ds(places[f], face), :], schur.at[at, :], sems.at[3 + f]))
    for copy in copies:
        copy.start()

    copies[0].wait()
    modes = jnp.concatenate([
        jnp.concatenate([mode_rows[m, :, pl.ds(at, face)] for at in places], axis=1)
        for m in range(n_modes)], axis=0)
    modes = jnp.concatenate([modes, jnp.zeros((PAD - n_modes, modes.shape[1]), F32)], axis=0)
    o["modes"][...] = modes
    o["mt"][...] = mode_pieces(modes)

    copies[1].wait()
    for f in range(6):
        o["r0"][f * face:(f + 1) * face, :] = signs[f] * resid[:, pl.ds(places[f], face)].T
    r0 = o["r0"][...]
    cols = r0.shape[1]
    send_rows(face, dot32(modes, r0), 0, o)

    copies[2].wait()
    rows = jnp.concatenate([coarse[m] for m in range(n_modes)], axis=0)
    rows = jnp.concatenate([rows, jnp.zeros((PAD - n_modes, rows.shape[1]), F32)], axis=0)
    wide = nz * PAD
    source = lax.broadcasted_iota(jnp.int32, (nz * n_modes, wide), 0)
    place = lax.broadcasted_iota(jnp.int32, (nz * n_modes, wide), 1)
    block, mode = place // PAD, place % PAD

    def ordered(device):
        pick = jnp.where((source == device * n_modes + mode) & (mode < n_modes), 1.0, 0.0)
        return dot32(rows, pick)

    def held_by(holder, side):
        offset = jnp.where(block == 1, side, jnp.where(block == 2, -side, 2 * (block // 3)))
        return ordered((holder + offset + 2 * nz) % nz)

    if turn:
        me = lax.axis_index("gz")
        side = 1 - 2 * lax.rem(me, 2)
        o["c_own"][...] = held_by(me, side)
        sent = (("za", me + side, -side, face + 3 * PAD), ("zb", me - side, -side, face + 3 * PAD), ("z2", me + 2, side, 2 * PAD))
        for name, holder, holder_side, start in sent:
            o[name][start:start + PAD, :] = jnp.zeros((PAD, cols), F32)
            o[name][start:start + PAD, 0:wide] = held_by(holder, holder_side)
    else:
        o["c_own"][...] = ordered(block)
    o["za"][face + 2 * PAD:face + 3 * PAD, :] = modes[:, 4 * face:5 * face]
    o["zb"][face + 2 * PAD:face + 3 * PAD, :] = modes[:, 5 * face:6 * face]

    halves = jnp.concatenate(split(r0), axis=1)
    curv = jnp.zeros((1, cols), F32)
    for part in range(3):
        at = slice(part * two, (part + 1) * two)
        copies[3 + 2 * part].wait()
        copies[4 + 2 * part].wait()
        high, low = split(jnp.concatenate([schur[at, pl.ds(start, face)] for start in places], axis=1))
        o["s_high"][at, :] = high
        o["s_low"][at, :] = low
        y = multiply(high, low, halves)
        send_product(face, part, y, o)
        curv = curv + col_sum(r0[at] * y)
    send_rows(face, stack_rows([half_dot(r0, r0), curv], cols), PAD, o)


def column_rows(face, i, at):
    return [i["za"][face + at:face + at + PAD, :], i["gza"][face + at:face + at + PAD, :],
            i["gzb"][face + at:face + at + PAD, :], i["gz2"][at:at + PAD, :]]


def value_kernel(face, stage, i, o):
    gathered = "g_all" in i
    loads = i["g_all"][...] if gathered else jnp.concatenate(column_rows(face, i, 0), axis=0)
    if stage == 0:
        mt_a = mode_pieces(i["gza"][face + 2 * PAD:face + 3 * PAD, :])
        mt_b = mode_pieces(i["gzb"][face + 2 * PAD:face + 3 * PAD, :])
        o["mt_a"][...] = mt_a
        o["mt_b"][...] = mt_b
        if gathered:
            coarse = i["c_all"][...]
        else:
            wide = i["c_own"].shape[1]
            at = face + 3 * PAD
            coarse = jnp.concatenate([
                i["c_own"][...], i["gza"][at:at + PAD, 0:wide], i["gzb"][at:at + PAD, 0:wide],
                i["gz2"][2 * PAD:3 * PAD, 0:wide]], axis=0)
            o["c_all"][...] = coarse
    else:
        mt_a, mt_b, coarse = i["mt_a"][...], i["mt_b"][...], i["c_all"][...]
    amp = dot32(coarse, loads)
    own = amp_pieces(amp[0:PAD])
    mt = i["mt"]
    xy = i["y"][...] + dot16(mt[0:4 * face, :], own)
    z_a = i["za"][0:face, :] + dot16(mt[4 * face:5 * face, :], own)
    z_a = z_a - (i["gza"][0:face, :] + dot16(mt_a, amp_pieces(amp[PAD:2 * PAD])))
    z_b = i["zb"][0:face, :] + dot16(mt[5 * face:6 * face, :], own)
    z_b = z_b - (i["gzb"][0:face, :] + dot16(mt_b, amp_pieces(amp[2 * PAD:3 * PAD])))
    cols = loads.shape[1]

    if stage != 2:
        if gathered:
            dots = i["d_all"][...]
            quad = col_sum(loads * amp[3 * PAD:])
        else:
            parts = column_rows(face, i, PAD)
            dots = (parts[0] + parts[1]) + (parts[2] + parts[3])
            quad = col_sum(loads * amp)
        at = {0: 1, 1: 1, 3: 5}[stage]
        dots = jnp.concatenate([dots[0:at], row(dots, at) + quad, dots[at + 1:]], axis=0)
    if stage == 1:
        sums = i["sum_near"][...] + i["sum_far"][...]
        alpha0 = row(sums, 0) / row(sums, 1)
        ratio = alpha0 / row(i["scale"], 0)
        o["known"][...] = stack_rows([row(sums, 0), row(sums, 1), alpha0], cols)
        dots = dots * (ratio * ratio)
        xy, z_a, z_b = xy * ratio, z_a * ratio, z_b * ratio
    o["z"][0:face, :] = z_a
    o["z"][face:, :] = z_b
    o["xab"][0:2 * face, :] = xy[0:2 * face]
    o["ya"][0:face, :] = xy[2 * face:3 * face]
    o["yb"][0:face, :] = xy[3 * face:]
    if stage == 3:
        o["dots"][...] = dots
    if stage != 2:
        o["xab"][2 * face:, :] = dots
        o["ya"][face:face + PAD, :] = dots
        o["yb"][face:face + PAD, :] = dots


def assemble(face, i):
    f = face
    return jnp.concatenate([
        i["xab"][0:2 * f, :] - i["gxab"][0:2 * f, :],
        i["ya"][0:f, :] - i["gya"][0:f, :],
        i["yb"][0:f, :] - i["gyb"][0:f, :],
        i["z"][...],
    ], axis=0)


def near_sum(face, i):
    f = face
    total = i["xab"][2 * f:2 * f + PAD, :] + i["gxab"][2 * f:2 * f + PAD, :]
    return total + (i["gya"][f:f + PAD, :] + i["gyb"][f:f + PAD, :])


def second_kernel(face, i, o):
    w0 = assemble(face, i)
    o["w0"][...] = w0
    own = i["xab"][2 * face:2 * face + PAD, :]
    scale = row(own, 0) / row(own, 1)
    cols = w0.shape[1]
    o["scale"][...] = stack_rows([scale], cols)
    if "near" in o:
        o["near"][...] = near_sum(face, i)
    vec = scale * w0
    curv = product(face, vec, i, o, True)
    send_rows(face, stack_rows([half_dot(vec, vec), curv], cols), PAD, o)


def third_kernel(face, i, o):
    q = assemble(face, i)
    w1 = i["w0"][...] - q
    o["q"][...] = q
    o["w1"][...] = w1
    if "near" in o:
        o["near"][...] = near_sum(face, i)
    product(face, row(i["known"], 2) * w1, i, o, False)


def fourth_kernel(face, i, o):
    b = assemble(face, i)
    m0, m1, alpha0 = (row(i["known"], k) for k in range(3))
    sums = i["sum_near"][...] + i["sum_far"][...]
    m2, m3 = row(sums, 0), row(sums, 1)
    norm1 = m2 - m0
    curv1 = m1 - 2.0 * (m2 / alpha0) + m3
    beta1 = norm1 / m0
    alpha1 = norm1 / (curv1 - beta1 * norm1 / alpha0)
    r0, w0, w1, q = i["r0"][...], i["w0"][...], i["w1"][...], i["q"][...]
    ratio = alpha1 / alpha0
    r1 = r0 - alpha0 * w0
    p1 = r1 + beta1 * r0
    s1 = alpha1 * (w1 + beta1 * w0)
    r2 = r1 - s1
    z1 = ratio * (b + beta1 * q)
    w2 = w1 - z1
    vec = alpha1 * w2
    cols = w2.shape[1]
    o["r2"][...] = r2
    o["w2"][...] = vec
    o["p1"][...] = p1
    o["s1"][...] = s1
    o["z1"][...] = z1
    o["m2"][...] = alpha0 * r0 + alpha1 * p1
    o["known"][...] = stack_rows([norm1, alpha1], cols)
    curv = product(face, vec, i, o, True)
    send_rows(face, stack_rows([
        half_dot(r2, r2), half_dot(r2, w2), half_dot(vec, vec), half_dot(vec, s1),
        half_dot(s1, s1), curv, half_dot(z1, vec), half_dot(s1, z1)], cols), PAD, o)


def four_kernel(face, i, o):
    near = i["dots"][...] + i["gxab"][2 * face:2 * face + PAD, :]
    o["part"][...] = near + (i["across"][...] + i["gyb"][face:face + PAD, :])


def last_kernel(face, i, o):
    d = i["sum_near"][...] + i["sum_far"][...]
    rr, rw, ww, ws, ss, wc, sc, sz = (row(d, k) for k in range(8))
    norm1, alpha1 = row(i["known"], 0), row(i["known"], 1)
    beta2 = rr / norm1
    alpha2 = rr / (rw - beta2 * rr / alpha1)
    ratio = alpha2 / alpha1
    ratio2 = ratio * ratio
    norm3 = ratio2 * (ww + 2.0 * beta2 * ws + beta2 * beta2 * ss) - rr
    curv3 = rw - 2.0 * (ratio2 / alpha2) * (ww + beta2 * ws)
    curv3 = curv3 + ratio2 * (wc + 2.0 * beta2 * sc + beta2 * beta2 * sz)
    beta3 = norm3 / rr
    alpha3 = norm3 / (curv3 - beta3 * norm3 / alpha2)
    c3 = assemble(face, i)
    w2, s1 = i["w2"][...], i["s1"][...]
    p2 = i["r2"][...] + beta2 * i["p1"][...]
    s2 = w2 + beta2 * s1
    r3 = i["r2"][...] - ratio * s2
    w3 = w2 / alpha1 - ratio * (c3 + beta2 * i["z1"][...])
    mult = i["m2"][...] + alpha2 * p2 + alpha3 * (r3 + beta3 * p2)
    resid = r3 - alpha3 * (w3 + (beta3 / alpha1) * s2)
    places, signs = face_places(face)
    for f in range(6):
        at = slice(f * face, (f + 1) * face)
        o["mult"][:, pl.ds(places[f], face)] = signs[f] * mult[at, :].T
        o["resid"][:, pl.ds(places[f], face)] = signs[f] * resid[at, :].T


def body(sizes, residual_in, schur, modes, coarse_inv):
    nx, ny, nz = sizes
    resid = residual_in[0, 0, 0]
    matrix = schur[0, 0, 0]
    loads, width = resid.shape
    face = width // 6
    n_modes = modes.shape[3]
    mode_rows = modes.reshape(n_modes, 1, width)
    coarse_rows = coarse_inv.reshape(n_modes, 1, nz * n_modes)
    small = (nx, ny, nz) == (2, 4, 4)

    def shift(x, axis, by):
        n = lax.axis_size(axis)
        return lax.ppermute(x, axis, [(k, (k + by) % n) for k in range(n)])

    def swap(x, axis, first):
        n = lax.axis_size(axis)
        side = lambda k: 1 if (k - first) % 2 == 0 else -1
        return lax.ppermute(x, axis, [(k, (k + side(k)) % n) for k in range(n)])

    def move(x, target):
        places = [(a, b) for a in range(nx) for b in range(ny)]
        pairs = [(a * ny + b, target(a, b)[0] * ny + target(a, b)[1]) for a, b in places]
        return lax.ppermute(x, ("gx", "gy"), pairs)

    def far(x):
        return move(x, lambda a, b: ((a + 1) % nx, (b + 2) % ny))

    def total(x):
        return dict(sum_near=lax.psum(x, ("gx", "gy")), sum_far=jnp.zeros_like(x))

    vec = sds((width, loads))
    rows = sds((PAD, loads))
    half = sds((width, width), BF16)
    flops = 2 * width * width * 2 * loads * 2

    def z_out(extra):
        return dict(y=sds((4 * face, loads)), za=sds((face + PAD + extra, loads)),
                    zb=sds((face + PAD + extra + PAD, loads)), z2=sds((PAD + min(extra, 2 * PAD), loads)))

    def z_exchange(a, with_dots):
        got = dict(za=a["za"], zb=a["zb"], y=a["y"], gzb=swap(a["zb"], "gz", 1))
        if small:
            got["gz2"] = shift(a["z2"], "gz", 2)
        got["gza"] = swap(a["za"], "gz", 0)
        if not small:
            got["g_all"] = lax.all_gather(a["z2"][0:PAD], "gz", axis=0, tiled=True)
            if with_dots:
                got["d_all"] = lax.psum(a["z2"][PAD:2 * PAD], "gz")
        return got

    def value(stage, ins):
        extra = 0 if stage == 2 else PAD
        outs = dict(z=sds((2 * face, loads)), xab=sds((2 * face + extra, loads)),
                    ya=sds((face + extra, loads)), yb=sds((face + extra + PAD, loads)))
        if stage == 0:
            outs.update(mt_a=sds((face, 6 * PAD), BF16), mt_b=sds((face, 6 * PAD), BF16))
            if small:
                outs["c_all"] = sds((nz * PAD, nz * PAD))
        if stage == 1:
            outs["known"] = rows
        if stage == 3:
            outs["dots"] = rows
        return call(functools.partial(value_kernel, face, stage), ins, outs, flops=2 * width * loads * 48)

    def x_exchange(v):
        got = dict(z=v["z"], xab=v["xab"])
        if nx == 2:
            got["gxab"] = swap(v["xab"], "gx", 0)
        else:
            a, b, rest = v["xab"][:face], v["xab"][face:2 * face], v["xab"][2 * face:]
            got["gxab"] = jnp.concatenate([swap(a, "gx", 0), swap(b, "gx", 1), rest], axis=0)
        return got

    def y_exchange(v):
        gyb = swap(v["yb"], "gy", 1)
        return dict(ya=v["ya"], yb=v["yb"], gya=swap(v["ya"], "gy", 0), gyb=gyb)

    def xy_exchange(v):
        return dict(x_exchange(v), **y_exchange(v))

    near = dict(near=rows) if small else {}

    hbm = pl.BlockSpec(memory_space=pltpu.HBM)
    vmem = pl.BlockSpec(memory_space=pltpu.VMEM)
    outs = dict(r0=vec, s_high=half, s_low=half, modes=sds((PAD, width)), mt=sds((width, 6 * PAD), BF16),
                c_own=sds((PAD, nz * PAD)), **z_out(3 * PAD))
    res = pl.pallas_call(
        functools.partial(first_kernel, face, nz, n_modes, small),
        out_shape=list(outs.values()),
        in_specs=[hbm] * 4,
        out_specs=[vmem] * len(outs),
        scratch_shapes=[
            pltpu.VMEM(resid.shape, F32), pltpu.VMEM(matrix.shape, F32),
            pltpu.VMEM(mode_rows.shape, F32), pltpu.VMEM(coarse_rows.shape, F32),
            pltpu.SemaphoreType.DMA((9,)),
        ],
        compiler_params=pltpu.CompilerParams(vmem_limit_bytes=VMEM_LIMIT),
        cost_estimate=pl.CostEstimate(flops=flops, bytes_accessed=4 * matrix.size, transcendentals=0),
    )(*[pltpu.with_memory_space_constraint(x, pltpu.HBM) for x in (resid, matrix, mode_rows, coarse_rows)])
    a = dict(zip(outs, res))
    r0, mt = a["r0"], a["mt"]
    fixed = dict(s_high=a["s_high"], s_low=a["s_low"], modes=a["modes"])
    ins = dict(z_exchange(a, True), mt=mt)
    if small:
        ins["c_own"] = a["c_own"]
    else:
        c_own = a["c_own"]
        ins["c_all"] = jnp.concatenate([
            c_own, swap(c_own, "gz", 0), swap(c_own, "gz", 1),
            lax.all_gather(c_own, "gz", axis=0, tiled=True)], axis=0)
    v = value(0, ins)
    column = dict(mt=mt, mt_a=v["mt_a"], mt_b=v["mt_b"], c_all=v["c_all"] if small else ins["c_all"])
    x = xy_exchange(v)

    a = call(functools.partial(second_kernel, face), dict(x, **fixed),
             dict(w0=vec, scale=rows, **near, **z_out(PAD)), flops=flops)
    w0 = a["w0"]
    sums = dict(sum_near=a["near"], sum_far=far(a["near"])) if small else total(v["xab"][2 * face:])
    v = value(1, dict(z_exchange(a, True), **column, **sums, scale=a["scale"]))
    known = v["known"]
    x = xy_exchange(v)

    a = call(functools.partial(third_kernel, face), dict(x, **fixed, w0=w0, known=known),
             dict(q=vec, w1=vec, **near, **z_out(0)), flops=flops)
    if not small:
        sums = total(v["xab"][2 * face:])
    q, w1 = a["q"], a["w1"]
    v = value(2, dict(z_exchange(a, False), **column))
    x = x_exchange(v)
    if small:
        sums = dict(sum_near=a["near"], sum_far=far(a["near"]))
    x.update(y_exchange(v))

    names = ("r2", "w2", "p1", "s1", "z1", "m2")
    a = call(functools.partial(fourth_kernel, face),
             dict(x, **fixed, **sums, known=known, r0=r0, w0=w0, w1=w1, q=q),
             dict({name: vec for name in names}, known=rows, **z_out(PAD)), flops=flops)
    v = value(3, dict(z_exchange(a, True), **column))
    if small:
        x = x_exchange(v)
        across = move(v["dots"], lambda a, b: (1 - a, (b + (-1 if b % 2 == 0 else 1)) % ny))
        x.update(y_exchange(v))
        part = call(functools.partial(four_kernel, face),
                    dict(dots=v["dots"], across=across, gxab=x["gxab"], gyb=x["gyb"]), dict(part=rows))["part"]
        sums = dict(sum_near=part, sum_far=swap(part, "gy", 0))
    else:
        x = xy_exchange(v)
        sums = total(v["dots"])
    out = sds((loads, width))
    res = call(functools.partial(last_kernel, face),
               dict(x, **sums, known=a["known"], **{name: a[name] for name in names}),
               dict(mult=out, resid=out))
    return (res["mult"][None, None, None], res["resid"][None, None, None])


def solution(mesh):
    spec = P("gx", "gy", "gz", None, None)
    sizes = tuple(mesh.shape[axis] for axis in ("gx", "gy", "gz"))
    return jax.shard_map(
        functools.partial(body, sizes),
        mesh=mesh,
        in_specs=(spec, spec, spec, P("gx", "gy", "gz", None)),
        out_specs=(spec, spec),
        check_vma=False,
    )
```

```python
import functools

import jax
import jax.numpy as jnp
from jax import lax
from jax.experimental import pallas as pl
from jax.experimental.pallas import tpu as pltpu
from jax.sharding import PartitionSpec as P

F32 = jnp.float32
BF16 = jnp.bfloat16
HI = lax.Precision.HIGHEST
PAD = 8
VMEM_LIMIT = 24 * 1024 * 1024


def sds(shape, dtype=F32):
    return jax.ShapeDtypeStruct(shape, dtype)


def call(kernel, ins, outs, flops=0):
    names_in, names_out = list(ins), list(outs)
    nbytes = sum(a.size * a.dtype.itemsize for a in list(ins.values()) + list(outs.values()))

    def run(*refs):
        n = len(names_in)
        kernel(dict(zip(names_in, refs[:n])), dict(zip(names_out, refs[n:])))

    vmem = pl.BlockSpec(memory_space=pltpu.VMEM)
    res = pl.pallas_call(
        run,
        out_shape=[outs[n] for n in names_out],
        in_specs=[vmem] * len(names_in),
        out_specs=[vmem] * len(names_out),
        compiler_params=pltpu.CompilerParams(vmem_limit_bytes=VMEM_LIMIT),
        cost_estimate=pl.CostEstimate(flops=flops, bytes_accessed=nbytes, transcendentals=0),
    )(*[ins[n] for n in names_in])
    return dict(zip(names_out, res))


def split(x):
    high = x.astype(BF16)
    return high, (x - high.astype(F32)).astype(BF16)


def split3(x):
    high = x.astype(BF16)
    rest = x - high.astype(F32)
    mid = rest.astype(BF16)
    return high, mid, (rest - mid.astype(F32)).astype(BF16)


def mode_pieces(modes):
    high, mid, low = split3(modes.T)
    return jnp.concatenate([high, high, mid, mid, high, low], axis=1)


def amp_pieces(amp):
    high, mid, low = split3(amp)
    return jnp.concatenate([high, mid, high, mid, low, high], axis=0)


def dot32(a, b):
    return jnp.dot(a, b, precision=HI, preferred_element_type=F32)


def dot16(a, b):
    return jnp.dot(a, b, preferred_element_type=F32)


def col_sum(x):
    return jnp.sum(x, axis=0, keepdims=True)


def half_dot(a, b):
    return 0.5 * col_sum(a * b)


def row(x, i):
    return x[i:i + 1, :]


def face_places(face):
    places, signs = [], []
    for k, axis in enumerate(("gx", "gy", "gz")):
        odd = lax.rem(lax.axis_index(axis), 2)
        for high in (1 - odd, odd):
            places.append(pl.multiple_of((2 * k + high) * face, face))
            signs.append((1 - 2 * high).astype(F32))
    return places, signs


def store_product(face, part, y, o):
    if part < 2:
        o["y"][2 * part * face:2 * (part + 1) * face, :] = y
    else:
        o["za"][0:face, :] = y[0:face]
        o["zb"][0:face, :] = y[face:]


def send_rows(face, rows, at, o):
    n = rows.shape[0]
    for name, start in (("za", face), ("zb", face), ("z2", 0)):
        o[name][start + at:start + at + n, :] = rows


def product(face, vec, stack, o):
    width, cols = vec.shape
    both = dot16(stack[...], jnp.concatenate(split(vec), axis=1))
    total = jnp.zeros((1, cols), F32)
    for part in range(3):
        at = slice(2 * part * face, 2 * (part + 1) * face)
        low = slice(width + 2 * part * face, width + 2 * (part + 1) * face)
        y = (both[at, :cols] + both[at, cols:]) + (both[low, :cols] + both[low, cols:])
        store_product(face, part, y, o)
        total = total + col_sum(vec[at] * y)
    loads = both[2 * width:, :cols] + both[2 * width:, cols:]
    send_rows(face, (loads[0:PAD] + loads[PAD:2 * PAD]) + loads[2 * PAD:3 * PAD], 0, o)
    return total


def stack_rows(rows, cols):
    zero = jnp.zeros((1, cols), F32)
    return jnp.concatenate(list(rows) + [zero] * (PAD - len(rows)), axis=0)


def first_kernel(face, nz, n_modes, turn, resid_hbm, schur_hbm, modes_hbm, coarse_hbm, *refs):
    names = ["r0", "stack", "mt", "c_own", "y", "za", "zb", "z2"]
    o = dict(zip(names, refs[:len(names)]))
    resid, schur, mode_rows, coarse, sems = refs[len(names):]
    two = 2 * face
    places, signs = face_places(face)
    copies = [
        pltpu.make_async_copy(modes_hbm, mode_rows, sems.at[0]),
        pltpu.make_async_copy(resid_hbm, resid, sems.at[1]),
        pltpu.make_async_copy(coarse_hbm, coarse, sems.at[2]),
    ]
    for f in range(6):
        at = pl.ds(f * face, face)
        copies.append(pltpu.make_async_copy(schur_hbm.at[pl.ds(places[f], face), :], schur.at[at, :], sems.at[3 + f]))
    for copy in copies:
        copy.start()

    copies[0].wait()
    modes = jnp.concatenate([
        jnp.concatenate([mode_rows[m, :, pl.ds(at, face)] for at in places], axis=1)
        for m in range(n_modes)], axis=0)
    modes = jnp.concatenate([modes, jnp.zeros((PAD - n_modes, modes.shape[1]), F32)], axis=0)
    width = modes.shape[1]
    o["mt"][...] = mode_pieces(modes)
    o["stack"][2 * width:, :] = jnp.concatenate(split3(modes) + (jnp.zeros(modes.shape, BF16),), axis=0)

    copies[1].wait()
    for f in range(6):
        o["r0"][f * face:(f + 1) * face, :] = signs[f] * resid[:, pl.ds(places[f], face)].T
    r0 = o["r0"][...]
    cols = r0.shape[1]

    copies[2].wait()
    rows = jnp.concatenate([coarse[m] for m in range(n_modes)], axis=0)
    rows = jnp.concatenate([rows, jnp.zeros((PAD - n_modes, rows.shape[1]), F32)], axis=0)
    wide = o["c_own"].shape[1]
    source = lax.broadcasted_iota(jnp.int32, (nz * n_modes, wide), 0)
    place = lax.broadcasted_iota(jnp.int32, (nz * n_modes, wide), 1)
    block, mode = place // PAD, place % PAD

    if turn:
        me = lax.axis_index("gz")
        side = 1 - 2 * lax.rem(me, 2)
        copy, block = block // nz, block % nz
        holder = me + jnp.where(copy == 1, side, jnp.where(copy == 2, -side, 2 * (copy // 3)))
        side = jnp.where((copy == 1) | (copy == 2), -side, side)
        offset = jnp.where(block == 1, side, jnp.where(block == 2, -side, 2 * (block // 3)))
        device = (holder + offset + 2 * nz) % nz
    else:
        device = block
    pick = jnp.where((source == device * n_modes + mode) & (mode < n_modes), 1.0, 0.0)
    ordered = dot32(rows, pick)
    o["c_own"][...] = ordered
    if turn:
        for name, start in (("za", face + 3 * PAD), ("zb", face + 3 * PAD), ("z2", 2 * PAD)):
            o[name][start:start + PAD, :] = ordered
    o["za"][face + 2 * PAD:face + 3 * PAD, :] = modes[:, 4 * face:5 * face]
    o["zb"][face + 2 * PAD:face + 3 * PAD, :] = modes[:, 5 * face:6 * face]

    for part in range(3):
        at = slice(part * two, (part + 1) * two)
        copies[3 + 2 * part].wait()
        copies[4 + 2 * part].wait()
        high, low = split(jnp.concatenate([schur[at, pl.ds(start, face)] for start in places], axis=1))
        o["stack"][at, :] = high
        o["stack"][width + part * two:width + (part + 1) * two, :] = low
    curv = product(face, r0, o["stack"], o)
    send_rows(face, stack_rows([half_dot(r0, r0), curv], cols), PAD, o)


def column_rows(face, i, at):
    return [i["za"][face + at:face + at + PAD, :], i["gza"][face + at:face + at + PAD, :],
            i["gzb"][face + at:face + at + PAD, :], i["gz2"][at:at + PAD, :]]


def value_kernel(face, stage, i, o):
    gathered = "g_all" in i
    loads = i["g_all"][...] if gathered else jnp.concatenate(column_rows(face, i, 0), axis=0)
    if stage == 0:
        mt_a = mode_pieces(i["gza"][face + 2 * PAD:face + 3 * PAD, :])
        mt_b = mode_pieces(i["gzb"][face + 2 * PAD:face + 3 * PAD, :])
        o["mt_a"][...] = mt_a
        o["mt_b"][...] = mt_b
        if gathered:
            coarse = i["c_all"][...]
        else:
            n = loads.shape[0]
            at = face + 3 * PAD
            coarse = jnp.concatenate([
                i["c_own"][:, 0:n], i["gza"][at:at + PAD, n:2 * n], i["gzb"][at:at + PAD, 2 * n:3 * n],
                i["gz2"][2 * PAD:3 * PAD, 3 * n:4 * n]], axis=0)
            o["c_all"][...] = coarse
    else:
        mt_a, mt_b, coarse = i["mt_a"][...], i["mt_b"][...], i["c_all"][...]
    amp = dot32(coarse, loads)
    own = amp_pieces(amp[0:PAD])
    mt = i["mt"]
    xy = i["y"][...] + dot16(mt[0:4 * face, :], own)
    z_a = i["za"][0:face, :] + dot16(mt[4 * face:5 * face, :], own)
    z_a = z_a - (i["gza"][0:face, :] + dot16(mt_a, amp_pieces(amp[PAD:2 * PAD])))
    z_b = i["zb"][0:face, :] + dot16(mt[5 * face:6 * face, :], own)
    z_b = z_b - (i["gzb"][0:face, :] + dot16(mt_b, amp_pieces(amp[2 * PAD:3 * PAD])))
    cols = loads.shape[1]

    if stage != 2:
        if gathered:
            dots = i["d_all"][...]
            quad = col_sum(loads * amp[3 * PAD:])
        else:
            parts = column_rows(face, i, PAD)
            dots = (parts[0] + parts[1]) + (parts[2] + parts[3])
            quad = col_sum(loads * amp)
        at = {0: 1, 1: 1, 3: 5}[stage]
        dots = jnp.concatenate([dots[0:at], row(dots, at) + quad, dots[at + 1:]], axis=0)
    if stage == 1:
        dots = jnp.concatenate([i["first"][0:2, :], dots[0:2], dots[4:]], axis=0)
    elif stage == 2 and "swapped" in i:
        dots = six_columns(i, o)
    o["z"][0:face, :] = z_a
    o["z"][face:, :] = z_b
    o["xab"][0:2 * face, :] = xy[0:2 * face]
    o["ya"][0:face, :] = xy[2 * face:3 * face]
    o["yb"][0:face, :] = xy[3 * face:]
    if stage == 3:
        o["dots"][...] = dots
    if stage != 2 or "swapped" in i:
        o["xab"][2 * face:, :] = dots
    if stage != 2:
        o["ya"][face:face + PAD, :] = dots
        o["yb"][face:face + PAD, :] = dots


def assemble(face, i, rates=None):
    f = face
    got = [i["gxab"][0:2 * f, :], i["gya"][0:f, :], i["gyb"][0:f, :]]
    if rates is not None:
        got = [rate * face_values for rate, face_values in zip(rates, got)]
    return jnp.concatenate([
        i["xab"][0:2 * f, :] - got[0], i["ya"][0:f, :] - got[1], i["yb"][0:f, :] - got[2], i["z"][...],
    ], axis=0)


def column_scale(dots):
    norm, curv = row(dots, 0), row(dots, 1)
    usable = (norm > 0.0) & (curv > 0.0)
    return jnp.where(usable, norm / jnp.where(usable, curv, 1.0), 1.0)


def rescale(dots, rate):
    square = rate * rate
    return stack_rows([row(dots, 0), row(dots, 1), square * row(dots, 2), square * row(dots, 3)], dots.shape[1])


def second_kernel(face, i, o):
    w0 = assemble(face, i)
    o["w0"][...] = w0
    first = i["xab"][2 * face:2 * face + PAD, :]
    scale = column_scale(first)
    cols = w0.shape[1]
    rates = [scale / column_scale(i[name][at:at + PAD, :])
             for name, at in (("gxab", 2 * face), ("gya", face), ("gyb", face))]
    o["first"][...] = stack_rows([row(first, 0), row(first, 1), scale] + rates, cols)
    vec = scale * w0
    curv = product(face, vec, i["stack"], o)
    send_rows(face, stack_rows([half_dot(vec, vec), curv], cols), PAD, o)


def third_kernel(face, i, o):
    scale, *rates = (row(i["first"], k) for k in range(2, 6))
    q = assemble(face, i, rates)
    o["q"][...] = q
    if "near" in o:
        partners = [rescale(i[name][at:at + PAD, :], rate) for rate, name, at in zip(
            rates, ("gxab", "gya", "gyb"), (2 * face, face, face))]
        o["near"][...] = jnp.concatenate([partners[0], partners[2], partners[1] + i["xab"][2 * face:, :]], axis=0)
    product(face, scale * q, i["stack"], o)


def six_columns(i, o):
    near = i["near"]
    rate = row(i["first"], 4)
    both = rescale(i["swapped"][0:PAD, :], rate), rescale(i["swapped"][PAD:2 * PAD, :], rate)
    o["six"][...] = ((near[0:PAD, :] + near[PAD:2 * PAD, :]) + near[2 * PAD:, :]) + (both[0] + both[1])
    return near[PAD:2 * PAD, :] + both[1]


def fourth_kernel(face, i, o):
    scale, *rates = (row(i["first"], k) for k in range(2, 6))
    sums = i["six"][...]
    if "whole" not in i:
        sums = sums + rescale(i["gxab"][2 * face:, :], rates[0])
    m0, m1 = row(sums, 0), row(sums, 1)
    alpha0 = m0 / m1
    ratio0 = alpha0 / scale
    square = ratio0 * ratio0
    m2, m3 = square * row(sums, 2), square * row(sums, 3)
    norm1 = m2 - m0
    curv1 = m1 - 2.0 * (m2 / alpha0) + m3
    beta1 = norm1 / m0
    alpha1 = norm1 / (curv1 - beta1 * norm1 / alpha0)
    r0, w0 = i["r0"][...], i["w0"][...]
    q = ratio0 * i["q"][...]
    b = q - square * assemble(face, i, [rate * rate for rate in rates])
    w1 = w0 - q
    s1 = alpha1 * (w1 + beta1 * w0)
    r2 = (r0 - alpha0 * w0) - s1
    z1 = (alpha1 / alpha0) * (b + beta1 * q)
    w2 = w1 - z1
    vec = alpha1 * w2
    cols = w2.shape[1]
    o["w2"][...] = vec
    o["s1"][...] = s1
    o["z1"][...] = z1
    o["known"][...] = stack_rows([norm1, alpha1, alpha0, beta1], cols)
    curv = product(face, vec, i["stack"], o)
    send_rows(face, stack_rows([
        half_dot(r2, r2), half_dot(r2, w2), half_dot(vec, vec), half_dot(vec, s1),
        half_dot(s1, s1), curv, half_dot(z1, vec), half_dot(s1, z1)], cols), PAD, o)


def four_kernel(face, i, o):
    near = i["dots"][...] + i["gxab"][2 * face:2 * face + PAD, :]
    o["part"][...] = near + (i["across"][...] + i["gyb"][face:face + PAD, :])


def last_kernel(face, i, o):
    d = i["sum_near"][...] + i["sum_far"][...]
    rr, rw, ww, ws, ss, wc, sc, sz = (row(d, k) for k in range(8))
    norm1, alpha1, alpha0, beta1 = (row(i["known"], k) for k in range(4))
    beta2 = rr / norm1
    alpha2 = rr / (rw - beta2 * rr / alpha1)
    ratio = alpha2 / alpha1
    ratio2 = ratio * ratio
    norm3 = ratio2 * (ww + 2.0 * beta2 * ws + beta2 * beta2 * ss) - rr
    curv3 = rw - 2.0 * (ratio2 / alpha2) * (ww + beta2 * ws)
    curv3 = curv3 + ratio2 * (wc + 2.0 * beta2 * sc + beta2 * beta2 * sz)
    beta3 = norm3 / rr
    alpha3 = norm3 / (curv3 - beta3 * norm3 / alpha2)
    c3 = assemble(face, i)
    w2, s1 = i["w2"][...], i["s1"][...]
    r0 = i["r0"][...]
    r1 = r0 - alpha0 * i["w0"][...]
    p1 = r1 + beta1 * r0
    r2 = r1 - s1
    p2 = r2 + beta2 * p1
    s2 = w2 + beta2 * s1
    r3 = r2 - ratio * s2
    w3 = w2 / alpha1 - ratio * (c3 + beta2 * i["z1"][...])
    mult = (alpha0 * r0 + alpha1 * p1) + alpha2 * p2 + alpha3 * (r3 + beta3 * p2)
    resid = r3 - alpha3 * (w3 + (beta3 / alpha1) * s2)
    places, signs = face_places(face)
    for f in range(6):
        at = slice(f * face, (f + 1) * face)
        o["mult"][:, pl.ds(places[f], face)] = signs[f] * mult[at, :].T
        o["resid"][:, pl.ds(places[f], face)] = signs[f] * resid[at, :].T


def body(sizes, residual_in, schur, modes, coarse_inv):
    nx, ny, nz = sizes
    resid = residual_in[0, 0, 0]
    matrix = schur[0, 0, 0]
    loads, width = resid.shape
    face = width // 6
    n_modes = modes.shape[3]
    mode_rows = modes.reshape(n_modes, 1, width)
    coarse_rows = coarse_inv.reshape(n_modes, 1, nz * n_modes)
    small = (nx, ny, nz) == (2, 4, 4)

    def shift(x, axis, by):
        n = lax.axis_size(axis)
        return lax.ppermute(x, axis, [(k, (k + by) % n) for k in range(n)])

    def swap(x, axis, first):
        n = lax.axis_size(axis)
        side = lambda k: 1 if (k - first) % 2 == 0 else -1
        return lax.ppermute(x, axis, [(k, (k + side(k)) % n) for k in range(n)])

    def move(x, target):
        places = [(a, b) for a in range(nx) for b in range(ny)]
        pairs = [(a * ny + b, target(a, b)[0] * ny + target(a, b)[1]) for a, b in places]
        return lax.ppermute(x, ("gx", "gy"), pairs)

    def total(dots, scale):
        rate = lax.pmin(scale, ("gx", "gy")) / scale
        rates = jnp.concatenate([jnp.ones((2, loads), F32), rate * rate, rate * rate], axis=0)
        sums = lax.psum(dots[0:4] * rates, ("gx", "gy")) / rates
        return jnp.concatenate([sums, jnp.zeros((PAD - 4, loads), F32)], axis=0)

    vec = sds((width, loads))
    rows = sds((PAD, loads))
    stack_shape = sds((2 * width + 4 * PAD, width), BF16)
    flops = 2 * width * width * 2 * loads * 2

    def z_out(extra):
        return dict(y=sds((4 * face, loads)), za=sds((face + PAD + extra, loads)),
                    zb=sds((face + PAD + extra + PAD, loads)), z2=sds((PAD + min(extra, 2 * PAD), loads)))

    def z_exchange(a, with_dots):
        got = dict(za=a["za"], zb=a["zb"], y=a["y"], gzb=swap(a["zb"], "gz", 1))
        if small:
            got["gz2"] = shift(a["z2"], "gz", 2)
        got["gza"] = swap(a["za"], "gz", 0)
        if not small:
            got["g_all"] = lax.all_gather(a["z2"][0:PAD], "gz", axis=0, tiled=True)
            if with_dots:
                got["d_all"] = lax.psum(a["z2"][PAD:2 * PAD], "gz")
        return got

    def value(stage, ins):
        extra = 0 if stage == 2 else PAD
        outs = dict(z=sds((2 * face, loads)), xab=sds((2 * face + (PAD if small else extra), loads)),
                    ya=sds((face + extra, loads)), yb=sds((face + extra + PAD, loads)))
        if stage == 0:
            outs.update(mt_a=sds((face, 6 * PAD), BF16), mt_b=sds((face, 6 * PAD), BF16))
            if small:
                outs["c_all"] = sds((nz * PAD, nz * PAD))
        if stage == 2 and small:
            outs["six"] = rows
        if stage == 3:
            outs["dots"] = rows
        return call(functools.partial(value_kernel, face, stage), ins, outs, flops=2 * width * loads * 48)

    def x_exchange(v):
        got = dict(z=v["z"], xab=v["xab"])
        if nx == 2:
            got["gxab"] = swap(v["xab"], "gx", 0)
        else:
            a, b, rest = v["xab"][:face], v["xab"][face:2 * face], v["xab"][2 * face:]
            got["gxab"] = jnp.concatenate([swap(a, "gx", 0), swap(b, "gx", 1), rest], axis=0)
        return got

    def y_exchange(v):
        gyb = swap(v["yb"], "gy", 1)
        return dict(ya=v["ya"], yb=v["yb"], gya=swap(v["ya"], "gy", 0), gyb=gyb)

    def xy_exchange(v):
        return dict(x_exchange(v), **y_exchange(v))

    hbm = pl.BlockSpec(memory_space=pltpu.HBM)
    vmem = pl.BlockSpec(memory_space=pltpu.VMEM)
    outs = dict(r0=vec, stack=stack_shape, mt=sds((width, 6 * PAD), BF16),
                c_own=sds((PAD, (4 if small else 1) * nz * PAD)), **z_out(3 * PAD))
    res = pl.pallas_call(
        functools.partial(first_kernel, face, nz, n_modes, small),
        out_shape=list(outs.values()),
        in_specs=[hbm] * 4,
        out_specs=[vmem] * len(outs),
        scratch_shapes=[
            pltpu.VMEM(resid.shape, F32), pltpu.VMEM(matrix.shape, F32),
            pltpu.VMEM(mode_rows.shape, F32), pltpu.VMEM(coarse_rows.shape, F32),
            pltpu.SemaphoreType.DMA((9,)),
        ],
        compiler_params=pltpu.CompilerParams(vmem_limit_bytes=VMEM_LIMIT),
        cost_estimate=pl.CostEstimate(flops=flops, bytes_accessed=4 * matrix.size, transcendentals=0),
    )(*[pltpu.with_memory_space_constraint(x, pltpu.HBM) for x in (resid, matrix, mode_rows, coarse_rows)])
    a = dict(zip(outs, res))
    r0, mt, stack = a["r0"], a["mt"], a["stack"]
    ins = dict(z_exchange(a, True), mt=mt)
    if small:
        ins["c_own"] = a["c_own"]
    else:
        c_own = a["c_own"]
        ins["c_all"] = jnp.concatenate([
            c_own, swap(c_own, "gz", 0), swap(c_own, "gz", 1),
            lax.all_gather(c_own, "gz", axis=0, tiled=True)], axis=0)
    v = value(0, ins)
    column = dict(mt=mt, mt_a=v["mt_a"], mt_b=v["mt_b"], c_all=v["c_all"] if small else ins["c_all"])
    x = xy_exchange(v)

    a = call(functools.partial(second_kernel, face), dict(x, stack=stack),
             dict(w0=vec, first=rows, **z_out(PAD)), flops=flops)
    w0, first = a["w0"], a["first"]
    v = value(1, dict(z_exchange(a, True), **column, first=first))
    x = xy_exchange(v)

    near = dict(near=sds((3 * PAD, loads))) if small else {}
    a = call(functools.partial(third_kernel, face), dict(x, stack=stack, first=first),
             dict(q=vec, **near, **z_out(0)), flops=flops)
    q = a["q"]
    ins = dict(z_exchange(a, False), **column)
    if small:
        ins.update(first=first, near=a["near"], swapped=swap(a["near"][0:2 * PAD], "gy", 0))
        v = value(2, ins)
        sums = dict(six=v["six"])
    else:
        sums = dict(six=total(v["xab"][2 * face:], first[2:3]), whole=first)
        v = value(2, ins)
    x = xy_exchange(v)

    a = call(functools.partial(fourth_kernel, face),
             dict(x, stack=stack, **sums, first=first, r0=r0, w0=w0, q=q),
             dict(w2=vec, s1=vec, z1=vec, known=rows, **z_out(PAD)), flops=flops)
    v = value(3, dict(z_exchange(a, True), **column))
    if small:
        x = x_exchange(v)
        across = move(v["dots"], lambda a, b: (1 - a, (b + (-1 if b % 2 == 0 else 1)) % ny))
        x.update(y_exchange(v))
        part = call(functools.partial(four_kernel, face),
                    dict(dots=v["dots"], across=across, gxab=x["gxab"], gyb=x["gyb"]), dict(part=rows))["part"]
        sums = dict(sum_near=part, sum_far=swap(part, "gy", 0))
    else:
        x = xy_exchange(v)
        sums = dict(sum_near=lax.psum(v["dots"], ("gx", "gy")), sum_far=jnp.zeros((PAD, loads), F32))
    out = sds((loads, width))
    res = call(functools.partial(last_kernel, face),
               dict(x, **sums, r0=r0, w0=w0, **{name: a[name] for name in ("known", "w2", "s1", "z1")}),
               dict(mult=out, resid=out))
    return (res["mult"][None, None, None], res["resid"][None, None, None])


def solution(mesh):
    spec = P("gx", "gy", "gz", None, None)
    sizes = tuple(mesh.shape[axis] for axis in ("gx", "gy", "gz"))
    return jax.shard_map(
        functools.partial(body, sizes),
        mesh=mesh,
        in_specs=(spec, spec, spec, P("gx", "gy", "gz", None)),
        out_specs=(spec, spec),
        check_vma=False,
    )
```

```python
import functools

import jax
import jax.numpy as jnp
from jax import lax
from jax.experimental import pallas as pl
from jax.experimental.pallas import tpu as pltpu
from jax.sharding import PartitionSpec as P

F32 = jnp.float32
BF16 = jnp.bfloat16
HI = lax.Precision.HIGHEST
PAD = 8
VMEM_LIMIT = 24 * 1024 * 1024
ROW_FLOPS = 5400000


def sds(shape, dtype=F32):
    return jax.ShapeDtypeStruct(shape, dtype)


def call(kernel, ins, outs, flops=0):
    names_in, names_out = list(ins), list(outs)
    nbytes = sum(a.size * a.dtype.itemsize for a in list(ins.values()) + list(outs.values()))

    def run(*refs):
        n = len(names_in)
        kernel(dict(zip(names_in, refs[:n])), dict(zip(names_out, refs[n:])))

    vmem = pl.BlockSpec(memory_space=pltpu.VMEM)
    res = pl.pallas_call(
        run,
        out_shape=[outs[n] for n in names_out],
        in_specs=[vmem] * len(names_in),
        out_specs=[vmem] * len(names_out),
        compiler_params=pltpu.CompilerParams(vmem_limit_bytes=VMEM_LIMIT),
        cost_estimate=pl.CostEstimate(flops=flops, bytes_accessed=nbytes, transcendentals=0),
    )(*[ins[n] for n in names_in])
    return dict(zip(names_out, res))


def split(x):
    high = x.astype(BF16)
    return high, (x - high.astype(F32)).astype(BF16)


def split3(x):
    high = x.astype(BF16)
    rest = x - high.astype(F32)
    mid = rest.astype(BF16)
    return high, mid, (rest - mid.astype(F32)).astype(BF16)


def mode_pieces(modes):
    high, mid, low = split3(modes.T)
    return jnp.concatenate([high, high, mid, mid, high, low], axis=1)


def amp_pieces(amp):
    high, mid, low = split3(amp)
    return jnp.concatenate([high, mid, high, mid, low, high], axis=0)


def dot32(a, b):
    return jnp.dot(a, b, precision=HI, preferred_element_type=F32)


def dot16(a, b):
    return jnp.dot(a, b, preferred_element_type=F32)


def col_sum(x):
    return jnp.sum(x, axis=0, keepdims=True)


def half_dot(a, b):
    return 0.5 * col_sum(a * b)


def row(x, i):
    return x[i:i + 1, :]


def face_places(face):
    places, signs = [], []
    for k, axis in enumerate(("gx", "gy", "gz")):
        odd = lax.rem(lax.axis_index(axis), 2)
        for high in (1 - odd, odd):
            places.append(pl.multiple_of((2 * k + high) * face, face))
            signs.append((1 - 2 * high).astype(F32))
    return places, signs


def store_product(face, part, y, o):
    if part < 2:
        o["y"][2 * part * face:2 * (part + 1) * face, :] = y
    else:
        o["za"][0:face, :] = y[0:face]
        o["zb"][0:face, :] = y[face:]


def send_rows(face, rows, at, o):
    n = rows.shape[0]
    for name, start in (("za", face), ("zb", face), ("z2", 0)):
        o[name][start + at:start + at + n, :] = rows


def product(face, vec, stack, o):
    width, cols = vec.shape
    both = dot16(stack[...], jnp.concatenate(split(vec), axis=1))
    total = jnp.zeros((1, cols), F32)
    for part in range(3):
        at = slice(2 * part * face, 2 * (part + 1) * face)
        low = slice(width + 2 * part * face, width + 2 * (part + 1) * face)
        y = (both[at, :cols] + both[at, cols:]) + (both[low, :cols] + both[low, cols:])
        store_product(face, part, y, o)
        total = total + col_sum(vec[at] * y)
    loads = both[2 * width:, :cols] + both[2 * width:, cols:]
    send_rows(face, (loads[0:PAD] + loads[PAD:2 * PAD]) + loads[2 * PAD:3 * PAD], 0, o)
    return total


def stack_rows(rows, cols):
    zero = jnp.zeros((1, cols), F32)
    return jnp.concatenate(list(rows) + [zero] * (PAD - len(rows)), axis=0)


def first_kernel(face, nz, n_modes, turn, resid_hbm, schur_hbm, modes_hbm, coarse_hbm, *refs):
    names = ["r0", "stack", "mt", "c_own", "y", "za", "zb", "z2"]
    o = dict(zip(names, refs[:len(names)]))
    resid, schur, mode_rows, coarse, sems = refs[len(names):]
    two = 2 * face
    places, signs = face_places(face)
    copies = [
        pltpu.make_async_copy(modes_hbm, mode_rows, sems.at[0]),
        pltpu.make_async_copy(resid_hbm, resid, sems.at[1]),
        pltpu.make_async_copy(coarse_hbm, coarse, sems.at[2]),
    ]
    for f in range(6):
        at = pl.ds(f * face, face)
        copies.append(pltpu.make_async_copy(schur_hbm.at[pl.ds(places[f], face), :], schur.at[at, :], sems.at[3 + f]))
    for copy in copies:
        copy.start()

    copies[0].wait()
    modes = jnp.concatenate([
        jnp.concatenate([mode_rows[m, :, pl.ds(at, face)] for at in places], axis=1)
        for m in range(n_modes)], axis=0)
    modes = jnp.concatenate([modes, jnp.zeros((PAD - n_modes, modes.shape[1]), F32)], axis=0)
    width = modes.shape[1]
    o["mt"][...] = mode_pieces(modes)
    o["stack"][2 * width:, :] = jnp.concatenate(split3(modes) + (jnp.zeros(modes.shape, BF16),), axis=0)

    copies[1].wait()
    for f in range(6):
        o["r0"][f * face:(f + 1) * face, :] = signs[f] * resid[:, pl.ds(places[f], face)].T
    r0 = o["r0"][...]
    cols = r0.shape[1]

    copies[2].wait()
    rows = jnp.concatenate([coarse[m] for m in range(n_modes)], axis=0)
    rows = jnp.concatenate([rows, jnp.zeros((PAD - n_modes, rows.shape[1]), F32)], axis=0)
    wide = o["c_own"].shape[1]
    source = lax.broadcasted_iota(jnp.int32, (nz * n_modes, wide), 0)
    place = lax.broadcasted_iota(jnp.int32, (nz * n_modes, wide), 1)
    block, mode = place // PAD, place % PAD

    if turn:
        me = lax.axis_index("gz")
        side = 1 - 2 * lax.rem(me, 2)
        copy, block = block // nz, block % nz
        holder = me + jnp.where(copy == 1, side, jnp.where(copy == 2, -side, 2 * (copy // 3)))
        side = jnp.where((copy == 1) | (copy == 2), -side, side)
        offset = jnp.where(block == 1, side, jnp.where(block == 2, -side, 2 * (block // 3)))
        device = (holder + offset + 2 * nz) % nz
    else:
        device = block
    pick = jnp.where((source == device * n_modes + mode) & (mode < n_modes), 1.0, 0.0)
    ordered = dot32(rows, pick)
    o["c_own"][...] = ordered
    if turn:
        for name, start in (("za", face + 3 * PAD), ("zb", face + 3 * PAD), ("z2", 2 * PAD)):
            o[name][start:start + PAD, :] = ordered
    o["za"][face + 2 * PAD:face + 3 * PAD, :] = modes[:, 4 * face:5 * face]
    o["zb"][face + 2 * PAD:face + 3 * PAD, :] = modes[:, 5 * face:6 * face]

    for part in range(3):
        at = slice(part * two, (part + 1) * two)
        copies[3 + 2 * part].wait()
        copies[4 + 2 * part].wait()
        high, low = split(jnp.concatenate([schur[at, pl.ds(start, face)] for start in places], axis=1))
        o["stack"][at, :] = high
        o["stack"][width + part * two:width + (part + 1) * two, :] = low
    curv = product(face, r0, o["stack"], o)
    send_rows(face, stack_rows([half_dot(r0, r0), curv], cols), PAD, o)


def column_rows(face, i, at):
    return [i["za"][face + at:face + at + PAD, :], i["gza"][face + at:face + at + PAD, :],
            i["gzb"][face + at:face + at + PAD, :], i["gz2"][at:at + PAD, :]]


def copy_kernel(i, o):
    o["z2"][...] = i["z2"][...]


def value_kernel(face, stage, i, o):
    gathered = "g_all" in i
    loads = i["g_all"][...] if gathered else jnp.concatenate(column_rows(face, i, 0), axis=0)
    if stage == 0:
        mt_a = mode_pieces(i["gza"][face + 2 * PAD:face + 3 * PAD, :])
        mt_b = mode_pieces(i["gzb"][face + 2 * PAD:face + 3 * PAD, :])
        o["mt_a"][...] = mt_a
        o["mt_b"][...] = mt_b
        if gathered:
            coarse = i["c_all"][...]
        else:
            n = loads.shape[0]
            at = face + 3 * PAD
            coarse = jnp.concatenate([
                i["c_own"][:, 0:n], i["gza"][at:at + PAD, n:2 * n], i["gzb"][at:at + PAD, 2 * n:3 * n],
                i["gz2"][2 * PAD:3 * PAD, 3 * n:4 * n]], axis=0)
            o["c_all"][...] = coarse
    else:
        mt_a, mt_b, coarse = i["mt_a"][...], i["mt_b"][...], i["c_all"][...]
    amp = dot32(coarse, loads)
    own = amp_pieces(amp[0:PAD])
    mt = i["mt"]
    xy = i["y"][...] + dot16(mt[0:4 * face, :], own)
    z_a = i["za"][0:face, :] + dot16(mt[4 * face:5 * face, :], own)
    z_a = z_a - (i["gza"][0:face, :] + dot16(mt_a, amp_pieces(amp[PAD:2 * PAD])))
    z_b = i["zb"][0:face, :] + dot16(mt[5 * face:6 * face, :], own)
    z_b = z_b - (i["gzb"][0:face, :] + dot16(mt_b, amp_pieces(amp[2 * PAD:3 * PAD])))
    cols = loads.shape[1]

    if stage != 2:
        if gathered:
            dots = i["d_all"][...]
            quad = col_sum(loads * amp[3 * PAD:])
        else:
            parts = column_rows(face, i, PAD)
            dots = (parts[0] + parts[1]) + (parts[2] + parts[3])
            quad = col_sum(loads * amp)
        at = {0: 1, 1: 1, 3: 5}[stage]
        dots = jnp.concatenate([dots[0:at], row(dots, at) + quad, dots[at + 1:]], axis=0)
    if stage == 1:
        dots = jnp.concatenate([i["first"][0:2, :], dots[0:2], dots[4:]], axis=0)
    elif stage == 2 and "swapped" in i:
        dots = six_columns(i, o)
    o["z"][0:face, :] = z_a
    o["z"][face:, :] = z_b
    o["xab"][0:2 * face, :] = xy[0:2 * face]
    o["ya"][0:face, :] = xy[2 * face:3 * face]
    o["yb"][0:face, :] = xy[3 * face:]
    if stage == 3:
        o["dots"][...] = dots
    if stage != 2 or "swapped" in i:
        o["xab"][2 * face:, :] = dots
    if stage != 2:
        o["ya"][face:face + PAD, :] = dots
        o["yb"][face:face + PAD, :] = dots


def assemble(face, i, rates=None):
    f = face
    got = [i["gxab"][0:2 * f, :], i["gya"][0:f, :], i["gyb"][0:f, :]]
    if rates is not None:
        got = [rate * face_values for rate, face_values in zip(rates, got)]
    return jnp.concatenate([
        i["xab"][0:2 * f, :] - got[0], i["ya"][0:f, :] - got[1], i["yb"][0:f, :] - got[2], i["z"][...],
    ], axis=0)


def column_scale(dots):
    norm, curv = row(dots, 0), row(dots, 1)
    usable = (norm > 0.0) & (curv > 0.0)
    return jnp.where(usable, norm / jnp.where(usable, curv, 1.0), 1.0)


def rescale(dots, rate):
    square = rate * rate
    return stack_rows([row(dots, 0), row(dots, 1), square * row(dots, 2), square * row(dots, 3)], dots.shape[1])


def second_kernel(face, i, o):
    w0 = assemble(face, i)
    o["w0"][...] = w0
    first = i["xab"][2 * face:2 * face + PAD, :]
    scale = column_scale(first)
    cols = w0.shape[1]
    rates = [scale / column_scale(i[name][at:at + PAD, :])
             for name, at in (("gxab", 2 * face), ("gya", face), ("gyb", face))]
    o["first"][...] = stack_rows([row(first, 0), row(first, 1), scale] + rates, cols)
    vec = scale * w0
    curv = product(face, vec, i["stack"], o)
    send_rows(face, stack_rows([half_dot(vec, vec), curv], cols), PAD, o)


def third_kernel(face, i, o):
    scale, *rates = (row(i["first"], k) for k in range(2, 6))
    q = assemble(face, i, rates)
    o["q"][...] = q
    if "near" in o:
        partners = [rescale(i[name][at:at + PAD, :], rate) for rate, name, at in zip(
            rates, ("gxab", "gya", "gyb"), (2 * face, face, face))]
        o["near"][...] = jnp.concatenate([partners[0], partners[2], partners[1] + i["xab"][2 * face:, :]], axis=0)
    product(face, scale * q, i["stack"], o)


def six_columns(i, o):
    near = i["near"]
    rate = row(i["first"], 4)
    both = rescale(i["swapped"][0:PAD, :], rate), rescale(i["swapped"][PAD:2 * PAD, :], rate)
    o["six"][...] = ((near[0:PAD, :] + near[PAD:2 * PAD, :]) + near[2 * PAD:, :]) + (both[0] + both[1])
    return near[PAD:2 * PAD, :] + both[1]


def fourth_kernel(face, i, o):
    scale, *rates = (row(i["first"], k) for k in range(2, 6))
    sums = i["six"][...]
    if "whole" not in i:
        sums = sums + rescale(i["gxab"][2 * face:, :], rates[0])
    m0, m1 = row(sums, 0), row(sums, 1)
    alpha0 = m0 / m1
    ratio0 = alpha0 / scale
    square = ratio0 * ratio0
    m2, m3 = square * row(sums, 2), square * row(sums, 3)
    norm1 = m2 - m0
    curv1 = m1 - 2.0 * (m2 / alpha0) + m3
    beta1 = norm1 / m0
    alpha1 = norm1 / (curv1 - beta1 * norm1 / alpha0)
    r0, w0 = i["r0"][...], i["w0"][...]
    q = ratio0 * i["q"][...]
    b = q - square * assemble(face, i, [rate * rate for rate in rates])
    w1 = w0 - q
    s1 = alpha1 * (w1 + beta1 * w0)
    r2 = (r0 - alpha0 * w0) - s1
    z1 = (alpha1 / alpha0) * (b + beta1 * q)
    w2 = w1 - z1
    vec = alpha1 * w2
    cols = w2.shape[1]
    o["w2"][...] = vec
    o["s1"][...] = s1
    o["z1"][...] = z1
    o["known"][...] = stack_rows([norm1, alpha1, alpha0, beta1], cols)
    curv = product(face, vec, i["stack"], o)
    send_rows(face, stack_rows([
        half_dot(r2, r2), half_dot(r2, w2), half_dot(vec, vec), half_dot(vec, s1),
        half_dot(s1, s1), curv, half_dot(z1, vec), half_dot(s1, z1)], cols), PAD, o)


def four_kernel(face, i, o):
    near = i["dots"][...] + i["gxab"][2 * face:2 * face + PAD, :]
    o["part"][...] = near + (i["across"][...] + i["gyb"][face:face + PAD, :])


def last_kernel(face, i, o):
    d = i["sum_near"][...] + i["sum_far"][...]
    rr, rw, ww, ws, ss, wc, sc, sz = (row(d, k) for k in range(8))
    norm1, alpha1, alpha0, beta1 = (row(i["known"], k) for k in range(4))
    beta2 = rr / norm1
    alpha2 = rr / (rw - beta2 * rr / alpha1)
    ratio = alpha2 / alpha1
    ratio2 = ratio * ratio
    norm3 = ratio2 * (ww + 2.0 * beta2 * ws + beta2 * beta2 * ss) - rr
    curv3 = rw - 2.0 * (ratio2 / alpha2) * (ww + beta2 * ws)
    curv3 = curv3 + ratio2 * (wc + 2.0 * beta2 * sc + beta2 * beta2 * sz)
    beta3 = norm3 / rr
    alpha3 = norm3 / (curv3 - beta3 * norm3 / alpha2)
    c3 = assemble(face, i)
    w2, s1 = i["w2"][...], i["s1"][...]
    r0 = i["r0"][...]
    r1 = r0 - alpha0 * i["w0"][...]
    p1 = r1 + beta1 * r0
    r2 = r1 - s1
    p2 = r2 + beta2 * p1
    s2 = w2 + beta2 * s1
    r3 = r2 - ratio * s2
    w3 = w2 / alpha1 - ratio * (c3 + beta2 * i["z1"][...])
    mult = (alpha0 * r0 + alpha1 * p1) + alpha2 * p2 + alpha3 * (r3 + beta3 * p2)
    resid = r3 - alpha3 * (w3 + (beta3 / alpha1) * s2)
    places, signs = face_places(face)
    for f in range(6):
        at = slice(f * face, (f + 1) * face)
        o["mult"][:, pl.ds(places[f], face)] = signs[f] * mult[at, :].T
        o["resid"][:, pl.ds(places[f], face)] = signs[f] * resid[at, :].T


def body(sizes, residual_in, schur, modes, coarse_inv):
    nx, ny, nz = sizes
    resid = residual_in[0, 0, 0]
    matrix = schur[0, 0, 0]
    loads, width = resid.shape
    face = width // 6
    n_modes = modes.shape[3]
    mode_rows = modes.reshape(n_modes, 1, width)
    coarse_rows = coarse_inv.reshape(n_modes, 1, nz * n_modes)
    small = (nx, ny, nz) == (2, 4, 4)

    def shift(x, axis, by):
        n = lax.axis_size(axis)
        return lax.ppermute(x, axis, [(k, (k + by) % n) for k in range(n)])

    def swap(x, axis, first):
        n = lax.axis_size(axis)
        side = lambda k: 1 if (k - first) % 2 == 0 else -1
        return lax.ppermute(x, axis, [(k, (k + side(k)) % n) for k in range(n)])

    def move(x, target):
        places = [(a, b) for a in range(nx) for b in range(ny)]
        pairs = [(a * ny + b, target(a, b)[0] * ny + target(a, b)[1]) for a, b in places]
        return lax.ppermute(x, ("gx", "gy"), pairs)

    def total(dots, scale):
        rate = lax.pmin(scale, ("gx", "gy")) / scale
        rates = jnp.concatenate([jnp.ones((2, loads), F32), rate * rate, rate * rate], axis=0)
        sums = lax.psum(dots[0:4] * rates, ("gx", "gy")) / rates
        return jnp.concatenate([sums, jnp.zeros((PAD - 4, loads), F32)], axis=0)

    vec = sds((width, loads))
    rows = sds((PAD, loads))
    stack_shape = sds((2 * width + 4 * PAD, width), BF16)
    flops = 2 * width * width * 2 * loads * 2

    def z_out(extra):
        return dict(y=sds((4 * face, loads)), za=sds((face + PAD + extra, loads)),
                    zb=sds((face + PAD + extra + PAD, loads)), z2=sds((PAD + min(extra, 2 * PAD), loads)))

    def z_exchange(a, with_dots):
        got = dict(za=a["za"], zb=a["zb"], y=a["y"], gzb=swap(a["zb"], "gz", 1))
        if small:
            rows_between = a["za"].shape[0] - a["z2"].shape[0] + PAD // 2
            got["gz2"] = call(copy_kernel, dict(z2=shift(a["z2"], "gz", 2)), dict(z2=sds(a["z2"].shape)),
                              flops=rows_between * ROW_FLOPS)["z2"]
        got["gza"] = swap(a["za"], "gz", 0)
        if not small:
            got["g_all"] = lax.all_gather(a["z2"][0:PAD], "gz", axis=0, tiled=True)
            if with_dots:
                got["d_all"] = lax.psum(a["z2"][PAD:2 * PAD], "gz")
        return got

    def value(stage, ins):
        extra = 0 if stage == 2 else PAD
        outs = dict(z=sds((2 * face, loads)), xab=sds((2 * face + (PAD if small else extra), loads)),
                    ya=sds((face + extra, loads)), yb=sds((face + extra + PAD, loads)))
        if stage == 0:
            outs.update(mt_a=sds((face, 6 * PAD), BF16), mt_b=sds((face, 6 * PAD), BF16))
            if small:
                outs["c_all"] = sds((nz * PAD, nz * PAD))
        if stage == 2 and small:
            outs["six"] = rows
        if stage == 3:
            outs["dots"] = rows
        return call(functools.partial(value_kernel, face, stage), ins, outs, flops=2 * width * loads * 48)

    def x_exchange(v):
        got = dict(z=v["z"], xab=v["xab"])
        if nx == 2:
            got["gxab"] = swap(v["xab"], "gx", 0)
        else:
            a, b, rest = v["xab"][:face], v["xab"][face:2 * face], v["xab"][2 * face:]
            got["gxab"] = jnp.concatenate([swap(a, "gx", 0), swap(b, "gx", 1), rest], axis=0)
        return got

    def y_exchange(v):
        gyb = swap(v["yb"], "gy", 1)
        return dict(ya=v["ya"], yb=v["yb"], gya=swap(v["ya"], "gy", 0), gyb=gyb)

    def xy_exchange(v):
        return dict(x_exchange(v), **y_exchange(v))

    hbm = pl.BlockSpec(memory_space=pltpu.HBM)
    vmem = pl.BlockSpec(memory_space=pltpu.VMEM)
    outs = dict(r0=vec, stack=stack_shape, mt=sds((width, 6 * PAD), BF16),
                c_own=sds((PAD, (4 if small else 1) * nz * PAD)), **z_out(3 * PAD))
    res = pl.pallas_call(
        functools.partial(first_kernel, face, nz, n_modes, small),
        out_shape=list(outs.values()),
        in_specs=[hbm] * 4,
        out_specs=[vmem] * len(outs),
        scratch_shapes=[
            pltpu.VMEM(resid.shape, F32), pltpu.VMEM(matrix.shape, F32),
            pltpu.VMEM(mode_rows.shape, F32), pltpu.VMEM(coarse_rows.shape, F32),
            pltpu.SemaphoreType.DMA((9,)),
        ],
        compiler_params=pltpu.CompilerParams(vmem_limit_bytes=VMEM_LIMIT),
        cost_estimate=pl.CostEstimate(flops=flops, bytes_accessed=4 * matrix.size, transcendentals=0),
    )(*[pltpu.with_memory_space_constraint(x, pltpu.HBM) for x in (resid, matrix, mode_rows, coarse_rows)])
    a = dict(zip(outs, res))
    r0, mt, stack = a["r0"], a["mt"], a["stack"]
    ins = dict(z_exchange(a, True), mt=mt)
    if small:
        ins["c_own"] = a["c_own"]
    else:
        c_own = a["c_own"]
        ins["c_all"] = jnp.concatenate([
            c_own, swap(c_own, "gz", 0), swap(c_own, "gz", 1),
            lax.all_gather(c_own, "gz", axis=0, tiled=True)], axis=0)
    v = value(0, ins)
    column = dict(mt=mt, mt_a=v["mt_a"], mt_b=v["mt_b"], c_all=v["c_all"] if small else ins["c_all"])
    x = xy_exchange(v)

    a = call(functools.partial(second_kernel, face), dict(x, stack=stack),
             dict(w0=vec, first=rows, **z_out(PAD)), flops=flops)
    w0, first = a["w0"], a["first"]
    v = value(1, dict(z_exchange(a, True), **column, first=first))
    x = xy_exchange(v)

    near = dict(near=sds((3 * PAD, loads))) if small else {}
    a = call(functools.partial(third_kernel, face), dict(x, stack=stack, first=first),
             dict(q=vec, **near, **z_out(0)), flops=flops)
    q = a["q"]
    ins = dict(z_exchange(a, False), **column)
    if small:
        ins.update(first=first, near=a["near"], swapped=swap(a["near"][0:2 * PAD], "gy", 0))
        v = value(2, ins)
        sums = dict(six=v["six"])
    else:
        sums = dict(six=total(v["xab"][2 * face:], first[2:3]), whole=first)
        v = value(2, ins)
    x = xy_exchange(v)

    a = call(functools.partial(fourth_kernel, face),
             dict(x, stack=stack, **sums, first=first, r0=r0, w0=w0, q=q),
             dict(w2=vec, s1=vec, z1=vec, known=rows, **z_out(PAD)), flops=flops)
    v = value(3, dict(z_exchange(a, True), **column))
    if small:
        x = x_exchange(v)
        across = move(v["dots"], lambda a, b: (1 - a, (b + (-1 if b % 2 == 0 else 1)) % ny))
        x.update(y_exchange(v))
        part = call(functools.partial(four_kernel, face),
                    dict(dots=v["dots"], across=across, gxab=x["gxab"], gyb=x["gyb"]), dict(part=rows))["part"]
        sums = dict(sum_near=part, sum_far=swap(part, "gy", 0))
    else:
        x = xy_exchange(v)
        sums = dict(sum_near=lax.psum(v["dots"], ("gx", "gy")), sum_far=jnp.zeros((PAD, loads), F32))
    out = sds((loads, width))
    res = call(functools.partial(last_kernel, face),
               dict(x, **sums, r0=r0, w0=w0, **{name: a[name] for name in ("known", "w2", "s1", "z1")}),
               dict(mult=out, resid=out))
    return (res["mult"][None, None, None], res["resid"][None, None, None])


def solution(mesh):
    spec = P("gx", "gy", "gz", None, None)
    sizes = tuple(mesh.shape[axis] for axis in ("gx", "gy", "gz"))
    return jax.shard_map(
        functools.partial(body, sizes),
        mesh=mesh,
        in_specs=(spec, spec, spec, P("gx", "gy", "gz", None)),
        out_specs=(spec, spec),
        check_vma=False,
    )
```

```python
import functools

import jax
import jax.numpy as jnp
from jax import lax
from jax.experimental import pallas as pl
from jax.experimental.pallas import tpu as pltpu
from jax.sharding import PartitionSpec as P

F32 = jnp.float32
BF16 = jnp.bfloat16
HI = lax.Precision.HIGHEST
PAD = 8
VMEM_LIMIT = 24 * 1024 * 1024
Z_FLOPS = 770000000


def sds(shape, dtype=F32):
    return jax.ShapeDtypeStruct(shape, dtype)


def call(kernel, ins, outs, flops=0):
    names_in, names_out = list(ins), list(outs)
    nbytes = sum(a.size * a.dtype.itemsize for a in list(ins.values()) + list(outs.values()))

    def run(*refs):
        n = len(names_in)
        kernel(dict(zip(names_in, refs[:n])), dict(zip(names_out, refs[n:])))

    vmem = pl.BlockSpec(memory_space=pltpu.VMEM)
    res = pl.pallas_call(
        run,
        out_shape=[outs[n] for n in names_out],
        in_specs=[vmem] * len(names_in),
        out_specs=[vmem] * len(names_out),
        compiler_params=pltpu.CompilerParams(vmem_limit_bytes=VMEM_LIMIT),
        cost_estimate=pl.CostEstimate(flops=flops, bytes_accessed=nbytes, transcendentals=0),
    )(*[ins[n] for n in names_in])
    return dict(zip(names_out, res))


def split(x):
    high = x.astype(BF16)
    return high, (x - high.astype(F32)).astype(BF16)


def split3(x):
    high = x.astype(BF16)
    rest = x - high.astype(F32)
    mid = rest.astype(BF16)
    return high, mid, (rest - mid.astype(F32)).astype(BF16)


def mode_pieces(modes):
    high, mid, low = split3(modes.T)
    return jnp.concatenate([high, high, mid, mid, high, low], axis=1)


def amp_pieces(amp):
    high, mid, low = split3(amp)
    return jnp.concatenate([high, mid, high, mid, low, high], axis=0)


def dot32(a, b):
    return jnp.dot(a, b, precision=HI, preferred_element_type=F32)


def dot16(a, b):
    return jnp.dot(a, b, preferred_element_type=F32)


def col_sum(x):
    return jnp.sum(x, axis=0, keepdims=True)


def half_dot(a, b):
    return 0.5 * col_sum(a * b)


def row(x, i):
    return x[i:i + 1, :]


def face_places(face):
    places, signs = [], []
    for k, axis in enumerate(("gx", "gy", "gz")):
        odd = lax.rem(lax.axis_index(axis), 2)
        for high in (1 - odd, odd):
            places.append(pl.multiple_of((2 * k + high) * face, face))
            signs.append((1 - 2 * high).astype(F32))
    return places, signs


def store_product(face, part, y, o):
    if part < 2:
        o["y"][2 * part * face:2 * (part + 1) * face, :] = y
    else:
        o["za"][0:face, :] = y[0:face]
        o["zb"][0:face, :] = y[face:]


def product(face, vec, stack, o):
    width, cols = vec.shape
    both = dot16(stack[...], jnp.concatenate(split(vec), axis=1))
    total = jnp.zeros((1, cols), F32)
    for part in range(3):
        at = slice(2 * part * face, 2 * (part + 1) * face)
        low = slice(width + 2 * part * face, width + 2 * (part + 1) * face)
        y = (both[at, :cols] + both[at, cols:]) + (both[low, :cols] + both[low, cols:])
        store_product(face, part, y, o)
        total = total + col_sum(vec[at] * y)
    loads = both[2 * width:, :cols] + both[2 * width:, cols:]
    o["t"][0:PAD, :] = (loads[0:PAD] + loads[PAD:2 * PAD]) + loads[2 * PAD:3 * PAD]
    return total


def stack_rows(rows, cols):
    zero = jnp.zeros((1, cols), F32)
    return jnp.concatenate(list(rows) + [zero] * (PAD - len(rows)), axis=0)


def first_kernel(face, nz, n_modes, turn, resid_hbm, schur_hbm, modes_hbm, coarse_hbm, *refs):
    names = ["r0", "stack", "mt", "c_own", "y", "za", "zb", "t"]
    o = dict(zip(names, refs[:len(names)]))
    resid, schur, mode_rows, coarse, sems = refs[len(names):]
    two = 2 * face
    places, signs = face_places(face)
    copies = [
        pltpu.make_async_copy(modes_hbm, mode_rows, sems.at[0]),
        pltpu.make_async_copy(resid_hbm, resid, sems.at[1]),
        pltpu.make_async_copy(coarse_hbm, coarse, sems.at[2]),
    ]
    for f in range(6):
        at = pl.ds(f * face, face)
        copies.append(pltpu.make_async_copy(schur_hbm.at[pl.ds(places[f], face), :], schur.at[at, :], sems.at[3 + f]))
    for copy in copies:
        copy.start()

    copies[0].wait()
    modes = jnp.concatenate([
        jnp.concatenate([mode_rows[m, :, pl.ds(at, face)] for at in places], axis=1)
        for m in range(n_modes)], axis=0)
    modes = jnp.concatenate([modes, jnp.zeros((PAD - n_modes, modes.shape[1]), F32)], axis=0)
    width = modes.shape[1]
    o["mt"][...] = mode_pieces(modes)
    o["stack"][2 * width:, :] = jnp.concatenate(split3(modes) + (jnp.zeros(modes.shape, BF16),), axis=0)

    copies[1].wait()
    for f in range(6):
        o["r0"][f * face:(f + 1) * face, :] = signs[f] * resid[:, pl.ds(places[f], face)].T
    r0 = o["r0"][...]
    cols = r0.shape[1]

    copies[2].wait()
    rows = jnp.concatenate([coarse[m] for m in range(n_modes)], axis=0)
    rows = jnp.concatenate([rows, jnp.zeros((PAD - n_modes, rows.shape[1]), F32)], axis=0)
    wide = o["c_own"].shape[1]
    source = lax.broadcasted_iota(jnp.int32, (nz * n_modes, wide), 0)
    place = lax.broadcasted_iota(jnp.int32, (nz * n_modes, wide), 1)
    block, mode = place // PAD, place % PAD

    if turn:
        me = lax.axis_index("gz")
        side = 1 - 2 * lax.rem(me, 2)
        copy, block = block // nz, block % nz
        holder = me + jnp.where(copy == 1, side, jnp.where(copy == 2, -side, 2 * (copy // 3)))
        side = jnp.where((copy == 1) | (copy == 2), -side, side)
        offset = jnp.where(block == 1, side, jnp.where(block == 2, -side, 2 * (block // 3)))
        device = (holder + offset + 2 * nz) % nz
    else:
        device = block
    pick = jnp.where((source == device * n_modes + mode) & (mode < n_modes), 1.0, 0.0)
    ordered = dot32(rows, pick)
    o["c_own"][...] = ordered
    if turn:
        o["t"][2 * PAD:3 * PAD, :] = ordered
    o["za"][face:face + PAD, :] = modes[:, 4 * face:5 * face]
    o["zb"][face:face + PAD, :] = modes[:, 5 * face:6 * face]

    for part in range(3):
        at = slice(part * two, (part + 1) * two)
        copies[3 + 2 * part].wait()
        copies[4 + 2 * part].wait()
        high, low = split(jnp.concatenate([schur[at, pl.ds(start, face)] for start in places], axis=1))
        o["stack"][at, :] = high
        o["stack"][width + part * two:width + (part + 1) * two, :] = low
    curv = product(face, r0, o["stack"], o)
    o["t"][PAD:2 * PAD, :] = stack_rows([half_dot(r0, r0), curv], cols)


def column_rows(i, at):
    return [i[name][at:at + PAD, :] for name in ("t", "gta", "gtb", "gt2")]


def z_kernel(face, i, o):
    for k, name in enumerate(("a", "b")):
        if "mt_" + name in o:
            got_modes = mode_pieces(i["gz" + name][face:face + PAD, :])
            o["mt_" + name][...] = got_modes
        else:
            got_modes = i["mt_" + name][...]
        amp = i["amp"]
        own = i["z" + name][0:face, :] + dot16(i["mt"][(4 + k) * face:(5 + k) * face, :], amp_pieces(amp[0:PAD, :]))
        at = (1 + k) * PAD
        got = i["gz" + name][0:face, :] + dot16(got_modes, amp_pieces(amp[at:at + PAD, :]))
        o["z"][k * face:(k + 1) * face, :] = own - got


def value_kernel(face, stage, i, o):
    gathered = "g_all" in i
    loads = i["g_all"][...] if gathered else jnp.concatenate(column_rows(i, 0), axis=0)
    if stage == 0 and not gathered:
        n = loads.shape[0]
        coarse = jnp.concatenate([part[:, k * n:(k + 1) * n] for k, part in enumerate(
            [i["c_own"][...]] + column_rows(i, 2 * PAD)[1:])], axis=0)
        o["c_all"][...] = coarse
    else:
        coarse = i["c_all"][...]
    amp = dot32(coarse, loads)
    o["amp"][...] = amp[0:3 * PAD]
    xy = i["y"][...] + dot16(i["mt"][0:4 * face, :], amp_pieces(amp[0:PAD]))
    cols = loads.shape[1]

    if stage != 2:
        if gathered:
            dots = i["d_all"][...]
            quad = col_sum(loads * amp[3 * PAD:])
        else:
            parts = column_rows(i, PAD)
            dots = (parts[0] + parts[1]) + (parts[2] + parts[3])
            quad = col_sum(loads * amp)
        at = {0: 1, 1: 1, 3: 5}[stage]
        dots = jnp.concatenate([dots[0:at], row(dots, at) + quad, dots[at + 1:]], axis=0)
    if stage == 1:
        dots = jnp.concatenate([i["first"][0:2, :], dots[0:2], dots[4:]], axis=0)
    elif stage == 2 and "swapped" in i:
        dots = six_columns(i, o)
    o["xab"][0:2 * face, :] = xy[0:2 * face]
    o["ya"][0:face, :] = xy[2 * face:3 * face]
    o["yb"][0:face, :] = xy[3 * face:]
    if stage == 3:
        o["dots"][...] = dots
    if stage != 2 or "swapped" in i:
        o["xab"][2 * face:, :] = dots
    if stage != 2:
        o["ya"][face:face + PAD, :] = dots
        o["yb"][face:face + PAD, :] = dots


def assemble(face, i, rates=None):
    f = face
    got = [i["gxab"][0:2 * f, :], i["gya"][0:f, :], i["gyb"][0:f, :]]
    if rates is not None:
        got = [rate * face_values for rate, face_values in zip(rates, got)]
    return jnp.concatenate([
        i["xab"][0:2 * f, :] - got[0], i["ya"][0:f, :] - got[1], i["yb"][0:f, :] - got[2], i["z"][...],
    ], axis=0)


def column_scale(dots):
    norm, curv = row(dots, 0), row(dots, 1)
    usable = (norm > 0.0) & (curv > 0.0)
    return jnp.where(usable, norm / jnp.where(usable, curv, 1.0), 1.0)


def rescale(dots, rate):
    square = rate * rate
    return stack_rows([row(dots, 0), row(dots, 1), square * row(dots, 2), square * row(dots, 3)], dots.shape[1])


def second_kernel(face, i, o):
    w0 = assemble(face, i)
    o["w0"][...] = w0
    first = i["xab"][2 * face:2 * face + PAD, :]
    scale = column_scale(first)
    cols = w0.shape[1]
    rates = [scale / column_scale(i[name][at:at + PAD, :])
             for name, at in (("gxab", 2 * face), ("gya", face), ("gyb", face))]
    o["first"][...] = stack_rows([row(first, 0), row(first, 1), scale] + rates, cols)
    vec = scale * w0
    curv = product(face, vec, i["stack"], o)
    o["t"][PAD:, :] = stack_rows([half_dot(vec, vec), curv], cols)


def third_kernel(face, i, o):
    scale, *rates = (row(i["first"], k) for k in range(2, 6))
    q = assemble(face, i, rates)
    o["q"][...] = q
    if "near" in o:
        partners = [rescale(i[name][at:at + PAD, :], rate) for rate, name, at in zip(
            rates, ("gxab", "gya", "gyb"), (2 * face, face, face))]
        o["near"][...] = jnp.concatenate([partners[0], partners[2], partners[1] + i["xab"][2 * face:, :]], axis=0)
    product(face, scale * q, i["stack"], o)


def six_columns(i, o):
    near = i["near"]
    rate = row(i["first"], 4)
    both = rescale(i["swapped"][0:PAD, :], rate), rescale(i["swapped"][PAD:2 * PAD, :], rate)
    o["six"][...] = ((near[0:PAD, :] + near[PAD:2 * PAD, :]) + near[2 * PAD:, :]) + (both[0] + both[1])
    return near[PAD:2 * PAD, :] + both[1]


def fourth_kernel(face, i, o):
    scale, *rates = (row(i["first"], k) for k in range(2, 6))
    sums = i["six"][...]
    if "whole" not in i:
        sums = sums + rescale(i["gxab"][2 * face:, :], rates[0])
    m0, m1 = row(sums, 0), row(sums, 1)
    alpha0 = m0 / m1
    ratio0 = alpha0 / scale
    square = ratio0 * ratio0
    m2, m3 = square * row(sums, 2), square * row(sums, 3)
    norm1 = m2 - m0
    curv1 = m1 - 2.0 * (m2 / alpha0) + m3
    beta1 = norm1 / m0
    alpha1 = norm1 / (curv1 - beta1 * norm1 / alpha0)
    r0, w0 = i["r0"][...], i["w0"][...]
    q = ratio0 * i["q"][...]
    b = q - square * assemble(face, i, [rate * rate for rate in rates])
    w1 = w0 - q
    s1 = alpha1 * (w1 + beta1 * w0)
    r2 = (r0 - alpha0 * w0) - s1
    z1 = (alpha1 / alpha0) * (b + beta1 * q)
    w2 = w1 - z1
    vec = alpha1 * w2
    cols = w2.shape[1]
    o["w2"][...] = vec
    o["s1"][...] = s1
    o["z1"][...] = z1
    o["known"][...] = stack_rows([norm1, alpha1, alpha0, beta1], cols)
    curv = product(face, vec, i["stack"], o)
    o["t"][PAD:, :] = stack_rows([
        half_dot(r2, r2), half_dot(r2, w2), half_dot(vec, vec), half_dot(vec, s1),
        half_dot(s1, s1), curv, half_dot(z1, vec), half_dot(s1, z1)], cols)


def four_kernel(face, i, o):
    near = i["dots"][...] + i["gxab"][2 * face:2 * face + PAD, :]
    o["part"][...] = near + (i["across"][...] + i["gyb"][face:face + PAD, :])


def last_kernel(face, i, o):
    d = i["sum_near"][...] + i["sum_far"][...]
    rr, rw, ww, ws, ss, wc, sc, sz = (row(d, k) for k in range(8))
    norm1, alpha1, alpha0, beta1 = (row(i["known"], k) for k in range(4))
    beta2 = rr / norm1
    alpha2 = rr / (rw - beta2 * rr / alpha1)
    ratio = alpha2 / alpha1
    ratio2 = ratio * ratio
    norm3 = ratio2 * (ww + 2.0 * beta2 * ws + beta2 * beta2 * ss) - rr
    curv3 = rw - 2.0 * (ratio2 / alpha2) * (ww + beta2 * ws)
    curv3 = curv3 + ratio2 * (wc + 2.0 * beta2 * sc + beta2 * beta2 * sz)
    beta3 = norm3 / rr
    alpha3 = norm3 / (curv3 - beta3 * norm3 / alpha2)
    c3 = assemble(face, i)
    w2, s1 = i["w2"][...], i["s1"][...]
    r0 = i["r0"][...]
    r1 = r0 - alpha0 * i["w0"][...]
    p1 = r1 + beta1 * r0
    r2 = r1 - s1
    p2 = r2 + beta2 * p1
    s2 = w2 + beta2 * s1
    r3 = r2 - ratio * s2
    w3 = w2 / alpha1 - ratio * (c3 + beta2 * i["z1"][...])
    mult = (alpha0 * r0 + alpha1 * p1) + alpha2 * p2 + alpha3 * (r3 + beta3 * p2)
    resid = r3 - alpha3 * (w3 + (beta3 / alpha1) * s2)
    places, signs = face_places(face)
    for f in range(6):
        at = slice(f * face, (f + 1) * face)
        o["mult"][:, pl.ds(places[f], face)] = signs[f] * mult[at, :].T
        o["resid"][:, pl.ds(places[f], face)] = signs[f] * resid[at, :].T


def body(sizes, residual_in, schur, modes, coarse_inv):
    nx, ny, nz = sizes
    resid = residual_in[0, 0, 0]
    matrix = schur[0, 0, 0]
    loads, width = resid.shape
    face = width // 6
    n_modes = modes.shape[3]
    mode_rows = modes.reshape(n_modes, 1, width)
    coarse_rows = coarse_inv.reshape(n_modes, 1, nz * n_modes)
    small = (nx, ny, nz) == (2, 4, 4)

    def shift(x, axis, by):
        n = lax.axis_size(axis)
        return lax.ppermute(x, axis, [(k, (k + by) % n) for k in range(n)])

    def swap(x, axis, first):
        n = lax.axis_size(axis)
        side = lambda k: 1 if (k - first) % 2 == 0 else -1
        return lax.ppermute(x, axis, [(k, (k + side(k)) % n) for k in range(n)])

    def move(x, target):
        places = [(a, b) for a in range(nx) for b in range(ny)]
        pairs = [(a * ny + b, target(a, b)[0] * ny + target(a, b)[1]) for a, b in places]
        return lax.ppermute(x, ("gx", "gy"), pairs)

    def total(dots, scale):
        rate = lax.pmin(scale, ("gx", "gy")) / scale
        rates = jnp.concatenate([jnp.ones((2, loads), F32), rate * rate, rate * rate], axis=0)
        sums = lax.psum(dots[0:4] * rates, ("gx", "gy")) / rates
        return jnp.concatenate([sums, jnp.zeros((PAD - 4, loads), F32)], axis=0)

    vec = sds((width, loads))
    rows = sds((PAD, loads))
    stack_shape = sds((2 * width + 4 * PAD, width), BF16)
    flops = 2 * width * width * 2 * loads * 2

    def z_out(tiny, extra=0):
        return dict(y=sds((4 * face, loads)), za=sds((face + extra, loads)),
                    zb=sds((face + extra, loads)), t=sds((tiny * PAD, loads)))

    def t_exchange(a, with_dots):
        got = dict(t=a["t"], y=a["y"])
        if small:
            got.update(gtb=swap(a["t"], "gz", 1), gt2=shift(a["t"], "gz", 2), gta=swap(a["t"], "gz", 0))
        else:
            got["g_all"] = lax.all_gather(a["t"][0:PAD], "gz", axis=0, tiled=True)
            if with_dots:
                got["d_all"] = lax.psum(a["t"][PAD:2 * PAD], "gz")
        return got

    def z_faces(a, v, modes=None):
        ins = dict(za=a["za"], zb=a["zb"], gzb=swap(a["zb"], "gz", 1), gza=swap(a["za"], "gz", 0), mt=mt, amp=v["amp"])
        outs = dict(z=sds((2 * face, loads)))
        if modes is None:
            outs.update(mt_a=sds((face, 6 * PAD), BF16), mt_b=sds((face, 6 * PAD), BF16))
        else:
            ins.update(modes)
        return call(functools.partial(z_kernel, face), ins, outs, flops=Z_FLOPS)

    def value(stage, ins):
        extra = 0 if stage == 2 else PAD
        outs = dict(amp=sds((3 * PAD, loads)), xab=sds((2 * face + (PAD if small else extra), loads)),
                    ya=sds((face + extra, loads)), yb=sds((face + extra + PAD, loads)))
        if stage == 0 and small:
            outs["c_all"] = sds((nz * PAD, nz * PAD))
        if stage == 2 and small:
            outs["six"] = rows
        if stage == 3:
            outs["dots"] = rows
        return call(functools.partial(value_kernel, face, stage), ins, outs, flops=2 * width * loads * 48)

    def x_exchange(v):
        got = dict(xab=v["xab"])
        if nx == 2:
            got["gxab"] = swap(v["xab"], "gx", 0)
        else:
            a, b, rest = v["xab"][:face], v["xab"][face:2 * face], v["xab"][2 * face:]
            got["gxab"] = jnp.concatenate([swap(a, "gx", 0), swap(b, "gx", 1), rest], axis=0)
        return got

    def y_exchange(v):
        gyb = swap(v["yb"], "gy", 1)
        return dict(ya=v["ya"], yb=v["yb"], gya=swap(v["ya"], "gy", 0), gyb=gyb)

    def xy_exchange(v):
        return dict(x_exchange(v), **y_exchange(v))

    hbm = pl.BlockSpec(memory_space=pltpu.HBM)
    vmem = pl.BlockSpec(memory_space=pltpu.VMEM)
    outs = dict(r0=vec, stack=stack_shape, mt=sds((width, 6 * PAD), BF16),
                c_own=sds((PAD, (4 if small else 1) * nz * PAD)), **z_out(3, PAD))
    res = pl.pallas_call(
        functools.partial(first_kernel, face, nz, n_modes, small),
        out_shape=list(outs.values()),
        in_specs=[hbm] * 4,
        out_specs=[vmem] * len(outs),
        scratch_shapes=[
            pltpu.VMEM(resid.shape, F32), pltpu.VMEM(matrix.shape, F32),
            pltpu.VMEM(mode_rows.shape, F32), pltpu.VMEM(coarse_rows.shape, F32),
            pltpu.SemaphoreType.DMA((9,)),
        ],
        compiler_params=pltpu.CompilerParams(vmem_limit_bytes=VMEM_LIMIT),
        cost_estimate=pl.CostEstimate(flops=flops, bytes_accessed=4 * matrix.size, transcendentals=0),
    )(*[pltpu.with_memory_space_constraint(x, pltpu.HBM) for x in (resid, matrix, mode_rows, coarse_rows)])
    a = dict(zip(outs, res))
    r0, mt, stack = a["r0"], a["mt"], a["stack"]
    ins = dict(t_exchange(a, True), mt=mt)
    if small:
        ins["c_own"] = a["c_own"]
    else:
        c_own = a["c_own"]
        ins["c_all"] = jnp.concatenate([
            c_own, swap(c_own, "gz", 0), swap(c_own, "gz", 1),
            lax.all_gather(c_own, "gz", axis=0, tiled=True)], axis=0)
    v = value(0, ins)
    column = dict(mt=mt, c_all=v["c_all"] if small else ins["c_all"])
    z = z_faces(a, v)
    got_modes = dict(mt_a=z["mt_a"], mt_b=z["mt_b"])
    x = dict(xy_exchange(v), z=z["z"])

    a = call(functools.partial(second_kernel, face), dict(x, stack=stack),
             dict(w0=vec, first=rows, **z_out(2)), flops=flops)
    w0, first = a["w0"], a["first"]
    v = value(1, dict(t_exchange(a, True), **column, first=first))
    x = dict(xy_exchange(v), z=z_faces(a, v, got_modes)["z"])

    near = dict(near=sds((3 * PAD, loads))) if small else {}
    a = call(functools.partial(third_kernel, face), dict(x, stack=stack, first=first),
             dict(q=vec, **near, **z_out(1)), flops=flops)
    q = a["q"]
    ins = dict(t_exchange(a, False), **column)
    if small:
        ins.update(first=first, near=a["near"], swapped=swap(a["near"][0:2 * PAD], "gy", 0))
        v = value(2, ins)
        sums = dict(six=v["six"])
    else:
        sums = dict(six=total(v["xab"][2 * face:], first[2:3]), whole=first)
        v = value(2, ins)
    x = dict(xy_exchange(v), z=z_faces(a, v, got_modes)["z"])

    a = call(functools.partial(fourth_kernel, face),
             dict(x, stack=stack, **sums, first=first, r0=r0, w0=w0, q=q),
             dict(w2=vec, s1=vec, z1=vec, known=rows, **z_out(2)), flops=flops)
    v = value(3, dict(t_exchange(a, True), **column))
    z = z_faces(a, v, got_modes)["z"]
    if small:
        x = x_exchange(v)
        across = move(v["dots"], lambda a, b: (1 - a, (b + (-1 if b % 2 == 0 else 1)) % ny))
        x.update(y_exchange(v))
        part = call(functools.partial(four_kernel, face),
                    dict(dots=v["dots"], across=across, gxab=x["gxab"], gyb=x["gyb"], z=z), dict(part=rows))["part"]
        sums = dict(sum_near=part, sum_far=swap(part, "gy", 0))
    else:
        x = xy_exchange(v)
        sums = dict(sum_near=lax.psum(v["dots"], ("gx", "gy")), sum_far=jnp.zeros((PAD, loads), F32))
    out = sds((loads, width))
    res = call(functools.partial(last_kernel, face),
               dict(x, **sums, z=z, r0=r0, w0=w0, **{name: a[name] for name in ("known", "w2", "s1", "z1")}),
               dict(mult=out, resid=out))
    return (res["mult"][None, None, None], res["resid"][None, None, None])


def solution(mesh):
    spec = P("gx", "gy", "gz", None, None)
    sizes = tuple(mesh.shape[axis] for axis in ("gx", "gy", "gz"))
    return jax.shard_map(
        functools.partial(body, sizes),
        mesh=mesh,
        in_specs=(spec, spec, spec, P("gx", "gy", "gz", None)),
        out_specs=(spec, spec),
        check_vma=False,
    )
```

```python
import functools

import jax
import jax.numpy as jnp
from jax import lax
from jax.experimental import pallas as pl
from jax.experimental.pallas import tpu as pltpu
from jax.sharding import PartitionSpec as P

F32 = jnp.float32
BF16 = jnp.bfloat16
HI = lax.Precision.HIGHEST
PAD = 8
VMEM_LIMIT = 24 * 1024 * 1024
Z_FLOPS = 770000000


def sds(shape, dtype=F32):
    return jax.ShapeDtypeStruct(shape, dtype)


def call(kernel, ins, outs, flops=0):
    names_in, names_out = list(ins), list(outs)
    nbytes = sum(a.size * a.dtype.itemsize for a in list(ins.values()) + list(outs.values()))

    def run(*refs):
        n = len(names_in)
        kernel(dict(zip(names_in, refs[:n])), dict(zip(names_out, refs[n:])))

    vmem = pl.BlockSpec(memory_space=pltpu.VMEM)
    res = pl.pallas_call(
        run,
        out_shape=[outs[n] for n in names_out],
        in_specs=[vmem] * len(names_in),
        out_specs=[vmem] * len(names_out),
        compiler_params=pltpu.CompilerParams(vmem_limit_bytes=VMEM_LIMIT),
        cost_estimate=pl.CostEstimate(flops=flops, bytes_accessed=nbytes, transcendentals=0),
    )(*[ins[n] for n in names_in])
    return dict(zip(names_out, res))


def split(x):
    high = x.astype(BF16)
    return high, (x - high.astype(F32)).astype(BF16)


def split3(x):
    high = x.astype(BF16)
    rest = x - high.astype(F32)
    mid = rest.astype(BF16)
    return high, mid, (rest - mid.astype(F32)).astype(BF16)


def mode_pieces(modes):
    high, mid, low = split3(modes.T)
    return jnp.concatenate([high, high, mid, mid, high, low], axis=1)


def amp_pieces(amp):
    high, mid, low = split3(amp)
    return jnp.concatenate([high, mid, high, mid, low, high], axis=0)


def dot32(a, b):
    return jnp.dot(a, b, precision=HI, preferred_element_type=F32)


def dot16(a, b):
    return jnp.dot(a, b, preferred_element_type=F32)


def col_sum(x):
    return jnp.sum(x, axis=0, keepdims=True)


def half_dot(a, b):
    return 0.5 * col_sum(a * b)


def row(x, i):
    return x[i:i + 1, :]


def face_places(face):
    places, signs = [], []
    for k, axis in enumerate(("gx", "gy", "gz")):
        odd = lax.rem(lax.axis_index(axis), 2)
        for high in (1 - odd, odd):
            places.append(pl.multiple_of((2 * k + high) * face, face))
            signs.append((1 - 2 * high).astype(F32))
    return places, signs


def store_product(face, part, y, o):
    if part < 2:
        o["y"][2 * part * face:2 * (part + 1) * face, :] = y
    else:
        o["za"][0:face, :] = y[0:face]
        o["zb"][0:face, :] = y[face:]


def send_rows(face, rows, at, o):
    n = rows.shape[0]
    o["t"][at:at + n, :] = rows
    o["zb"][face + at:face + at + n, :] = rows


def product(face, vec, stack, o):
    width, cols = vec.shape
    both = dot16(stack[...], jnp.concatenate(split(vec), axis=1))
    total = jnp.zeros((1, cols), F32)
    for part in range(3):
        at = slice(2 * part * face, 2 * (part + 1) * face)
        low = slice(width + 2 * part * face, width + 2 * (part + 1) * face)
        y = (both[at, :cols] + both[at, cols:]) + (both[low, :cols] + both[low, cols:])
        store_product(face, part, y, o)
        total = total + col_sum(vec[at] * y)
    loads = both[2 * width:, :cols] + both[2 * width:, cols:]
    send_rows(face, (loads[0:PAD] + loads[PAD:2 * PAD]) + loads[2 * PAD:3 * PAD], 0, o)
    return total


def stack_rows(rows, cols):
    zero = jnp.zeros((1, cols), F32)
    return jnp.concatenate(list(rows) + [zero] * (PAD - len(rows)), axis=0)


def first_kernel(face, nz, n_modes, turn, resid_hbm, schur_hbm, modes_hbm, coarse_hbm, *refs):
    names = ["r0", "stack", "mt", "c_own", "y", "za", "zb", "t"]
    o = dict(zip(names, refs[:len(names)]))
    resid, schur, mode_rows, coarse, sems = refs[len(names):]
    two = 2 * face
    places, signs = face_places(face)
    copies = [
        pltpu.make_async_copy(modes_hbm, mode_rows, sems.at[0]),
        pltpu.make_async_copy(resid_hbm, resid, sems.at[1]),
        pltpu.make_async_copy(coarse_hbm, coarse, sems.at[2]),
    ]
    for f in range(6):
        at = pl.ds(f * face, face)
        copies.append(pltpu.make_async_copy(schur_hbm.at[pl.ds(places[f], face), :], schur.at[at, :], sems.at[3 + f]))
    for copy in copies:
        copy.start()

    copies[0].wait()
    modes = jnp.concatenate([
        jnp.concatenate([mode_rows[m, :, pl.ds(at, face)] for at in places], axis=1)
        for m in range(n_modes)], axis=0)
    modes = jnp.concatenate([modes, jnp.zeros((PAD - n_modes, modes.shape[1]), F32)], axis=0)
    width = modes.shape[1]
    o["mt"][...] = mode_pieces(modes)
    o["stack"][2 * width:, :] = jnp.concatenate(split3(modes) + (jnp.zeros(modes.shape, BF16),), axis=0)

    copies[1].wait()
    for f in range(6):
        o["r0"][f * face:(f + 1) * face, :] = signs[f] * resid[:, pl.ds(places[f], face)].T
    r0 = o["r0"][...]
    cols = r0.shape[1]

    copies[2].wait()
    rows = jnp.concatenate([coarse[m] for m in range(n_modes)], axis=0)
    rows = jnp.concatenate([rows, jnp.zeros((PAD - n_modes, rows.shape[1]), F32)], axis=0)
    wide = o["c_own"].shape[1]
    source = lax.broadcasted_iota(jnp.int32, (nz * n_modes, wide), 0)
    place = lax.broadcasted_iota(jnp.int32, (nz * n_modes, wide), 1)
    block, mode = place // PAD, place % PAD

    if turn:
        me = lax.axis_index("gz")
        side = 1 - 2 * lax.rem(me, 2)
        copy, block = block // nz, block % nz
        holder = me + jnp.where(copy == 1, side, jnp.where(copy == 2, -side, 2 * (copy // 3)))
        side = jnp.where((copy == 1) | (copy == 2), -side, side)
        offset = jnp.where(block == 1, side, jnp.where(block == 2, -side, 2 * (block // 3)))
        device = (holder + offset + 2 * nz) % nz
    else:
        device = block
    pick = jnp.where((source == device * n_modes + mode) & (mode < n_modes), 1.0, 0.0)
    ordered = dot32(rows, pick)
    o["c_own"][...] = ordered
    if turn:
        send_rows(face, ordered, 2 * PAD, o)
    o["za"][face:face + PAD, :] = modes[:, 4 * face:5 * face]
    o["zb"][face + 3 * PAD:face + 4 * PAD, :] = modes[:, 5 * face:6 * face]

    for part in range(3):
        at = slice(part * two, (part + 1) * two)
        copies[3 + 2 * part].wait()
        copies[4 + 2 * part].wait()
        high, low = split(jnp.concatenate([schur[at, pl.ds(start, face)] for start in places], axis=1))
        o["stack"][at, :] = high
        o["stack"][width + part * two:width + (part + 1) * two, :] = low
    curv = product(face, r0, o["stack"], o)
    send_rows(face, stack_rows([half_dot(r0, r0), curv], cols), PAD, o)


def column_rows(face, i, at):
    return [i["t"][at:at + PAD, :], i["gta"][at:at + PAD, :],
            i["gzb"][face + at:face + at + PAD, :], i["gt2"][at:at + PAD, :]]


def z_kernel(face, i, o):
    for k, name in enumerate(("a", "b")):
        if "mt_" + name in o:
            got_modes = mode_pieces(i["gz" + name][-PAD:, :])
            o["mt_" + name][...] = got_modes
        else:
            got_modes = i["mt_" + name][...]
        amp = i["amp"]
        own = i["z" + name][0:face, :] + dot16(i["mt"][(4 + k) * face:(5 + k) * face, :], amp_pieces(amp[0:PAD, :]))
        at = (1 + k) * PAD
        got = i["gz" + name][0:face, :] + dot16(got_modes, amp_pieces(amp[at:at + PAD, :]))
        o["z"][k * face:(k + 1) * face, :] = own - got


def value_kernel(face, stage, i, o):
    gathered = "g_all" in i
    loads = i["g_all"][...] if gathered else jnp.concatenate(column_rows(face, i, 0), axis=0)
    if stage == 0 and not gathered:
        n = loads.shape[0]
        coarse = jnp.concatenate([part[:, k * n:(k + 1) * n] for k, part in enumerate(
            [i["c_own"][...]] + column_rows(face, i, 2 * PAD)[1:])], axis=0)
        o["c_all"][...] = coarse
    else:
        coarse = i["c_all"][...]
    amp = dot32(coarse, loads)
    o["amp"][...] = amp[0:3 * PAD]
    xy = i["y"][...] + dot16(i["mt"][0:4 * face, :], amp_pieces(amp[0:PAD]))
    cols = loads.shape[1]

    if stage != 2:
        if gathered:
            dots = i["d_all"][...]
            quad = col_sum(loads * amp[3 * PAD:])
        else:
            parts = column_rows(face, i, PAD)
            dots = (parts[0] + parts[1]) + (parts[2] + parts[3])
            quad = col_sum(loads * amp)
        at = {0: 1, 1: 1, 3: 5}[stage]
        dots = jnp.concatenate([dots[0:at], row(dots, at) + quad, dots[at + 1:]], axis=0)
    if stage == 1:
        dots = jnp.concatenate([i["first"][0:2, :], dots[0:2], dots[4:]], axis=0)
    elif stage == 2 and "swapped" in i:
        dots = six_columns(i, o)
    o["xab"][0:2 * face, :] = xy[0:2 * face]
    o["ya"][0:face, :] = xy[2 * face:3 * face]
    o["yb"][0:face, :] = xy[3 * face:]
    if stage == 3:
        o["dots"][...] = dots
    if stage != 2 or "swapped" in i:
        o["xab"][2 * face:, :] = dots
    if stage != 2:
        o["ya"][face:face + PAD, :] = dots
        o["yb"][face:face + PAD, :] = dots


def assemble(face, i, rates=None):
    f = face
    got = [i["gxab"][0:2 * f, :], i["gya"][0:f, :], i["gyb"][0:f, :]]
    if rates is not None:
        got = [rate * face_values for rate, face_values in zip(rates, got)]
    return jnp.concatenate([
        i["xab"][0:2 * f, :] - got[0], i["ya"][0:f, :] - got[1], i["yb"][0:f, :] - got[2], i["z"][...],
    ], axis=0)


def column_scale(dots):
    norm, curv = row(dots, 0), row(dots, 1)
    usable = (norm > 0.0) & (curv > 0.0)
    return jnp.where(usable, norm / jnp.where(usable, curv, 1.0), 1.0)


def rescale(dots, rate):
    square = rate * rate
    return stack_rows([row(dots, 0), row(dots, 1), square * row(dots, 2), square * row(dots, 3)], dots.shape[1])


def second_kernel(face, i, o):
    w0 = assemble(face, i)
    o["w0"][...] = w0
    first = i["xab"][2 * face:2 * face + PAD, :]
    scale = column_scale(first)
    cols = w0.shape[1]
    rates = [scale / column_scale(i[name][at:at + PAD, :])
             for name, at in (("gxab", 2 * face), ("gya", face), ("gyb", face))]
    o["first"][...] = stack_rows([row(first, 0), row(first, 1), scale] + rates, cols)
    vec = scale * w0
    curv = product(face, vec, i["stack"], o)
    send_rows(face, stack_rows([half_dot(vec, vec), curv], cols), PAD, o)


def third_kernel(face, i, o):
    scale, *rates = (row(i["first"], k) for k in range(2, 6))
    q = assemble(face, i, rates)
    o["q"][...] = q
    if "near" in o:
        partners = [rescale(i[name][at:at + PAD, :], rate) for rate, name, at in zip(
            rates, ("gxab", "gya", "gyb"), (2 * face, face, face))]
        o["near"][...] = jnp.concatenate([partners[0], partners[2], partners[1] + i["xab"][2 * face:, :]], axis=0)
    product(face, scale * q, i["stack"], o)


def six_columns(i, o):
    near = i["near"]
    rate = row(i["first"], 4)
    both = rescale(i["swapped"][0:PAD, :], rate), rescale(i["swapped"][PAD:2 * PAD, :], rate)
    o["six"][...] = ((near[0:PAD, :] + near[PAD:2 * PAD, :]) + near[2 * PAD:, :]) + (both[0] + both[1])
    return near[PAD:2 * PAD, :] + both[1]


def fourth_kernel(face, i, o):
    scale, *rates = (row(i["first"], k) for k in range(2, 6))
    sums = i["six"][...]
    if "whole" not in i:
        sums = sums + rescale(i["gxab"][2 * face:, :], rates[0])
    m0, m1 = row(sums, 0), row(sums, 1)
    alpha0 = m0 / m1
    ratio0 = alpha0 / scale
    square = ratio0 * ratio0
    m2, m3 = square * row(sums, 2), square * row(sums, 3)
    norm1 = m2 - m0
    curv1 = m1 - 2.0 * (m2 / alpha0) + m3
    beta1 = norm1 / m0
    alpha1 = norm1 / (curv1 - beta1 * norm1 / alpha0)
    r0, w0 = i["r0"][...], i["w0"][...]
    q = ratio0 * i["q"][...]
    b = q - square * assemble(face, i, [rate * rate for rate in rates])
    w1 = w0 - q
    s1 = alpha1 * (w1 + beta1 * w0)
    r2 = (r0 - alpha0 * w0) - s1
    z1 = (alpha1 / alpha0) * (b + beta1 * q)
    w2 = w1 - z1
    vec = alpha1 * w2
    cols = w2.shape[1]
    o["w2"][...] = vec
    o["s1"][...] = s1
    o["z1"][...] = z1
    o["known"][...] = stack_rows([norm1, alpha1, alpha0, beta1], cols)
    curv = product(face, vec, i["stack"], o)
    send_rows(face, stack_rows([
        half_dot(r2, r2), half_dot(r2, w2), half_dot(vec, vec), half_dot(vec, s1),
        half_dot(s1, s1), curv, half_dot(z1, vec), half_dot(s1, z1)], cols), PAD, o)


def four_kernel(face, i, o):
    near = i["dots"][...] + i["gxab"][2 * face:2 * face + PAD, :]
    o["part"][...] = near + (i["across"][...] + i["gyb"][face:face + PAD, :])


def last_kernel(face, i, o):
    d = i["sum_near"][...] + i["sum_far"][...]
    rr, rw, ww, ws, ss, wc, sc, sz = (row(d, k) for k in range(8))
    norm1, alpha1, alpha0, beta1 = (row(i["known"], k) for k in range(4))
    beta2 = rr / norm1
    alpha2 = rr / (rw - beta2 * rr / alpha1)
    ratio = alpha2 / alpha1
    ratio2 = ratio * ratio
    norm3 = ratio2 * (ww + 2.0 * beta2 * ws + beta2 * beta2 * ss) - rr
    curv3 = rw - 2.0 * (ratio2 / alpha2) * (ww + beta2 * ws)
    curv3 = curv3 + ratio2 * (wc + 2.0 * beta2 * sc + beta2 * beta2 * sz)
    beta3 = norm3 / rr
    alpha3 = norm3 / (curv3 - beta3 * norm3 / alpha2)
    c3 = assemble(face, i)
    w2, s1 = i["w2"][...], i["s1"][...]
    r0 = i["r0"][...]
    r1 = r0 - alpha0 * i["w0"][...]
    p1 = r1 + beta1 * r0
    r2 = r1 - s1
    p2 = r2 + beta2 * p1
    s2 = w2 + beta2 * s1
    r3 = r2 - ratio * s2
    w3 = w2 / alpha1 - ratio * (c3 + beta2 * i["z1"][...])
    mult = (alpha0 * r0 + alpha1 * p1) + alpha2 * p2 + alpha3 * (r3 + beta3 * p2)
    resid = r3 - alpha3 * (w3 + (beta3 / alpha1) * s2)
    places, signs = face_places(face)
    for f in range(6):
        at = slice(f * face, (f + 1) * face)
        o["mult"][:, pl.ds(places[f], face)] = signs[f] * mult[at, :].T
        o["resid"][:, pl.ds(places[f], face)] = signs[f] * resid[at, :].T


def body(sizes, residual_in, schur, modes, coarse_inv):
    nx, ny, nz = sizes
    resid = residual_in[0, 0, 0]
    matrix = schur[0, 0, 0]
    loads, width = resid.shape
    face = width // 6
    n_modes = modes.shape[3]
    mode_rows = modes.reshape(n_modes, 1, width)
    coarse_rows = coarse_inv.reshape(n_modes, 1, nz * n_modes)
    small = (nx, ny, nz) == (2, 4, 4)

    def shift(x, axis, by):
        n = lax.axis_size(axis)
        return lax.ppermute(x, axis, [(k, (k + by) % n) for k in range(n)])

    def swap(x, axis, first):
        n = lax.axis_size(axis)
        side = lambda k: 1 if (k - first) % 2 == 0 else -1
        return lax.ppermute(x, axis, [(k, (k + side(k)) % n) for k in range(n)])

    def move(x, target):
        places = [(a, b) for a in range(nx) for b in range(ny)]
        pairs = [(a * ny + b, target(a, b)[0] * ny + target(a, b)[1]) for a, b in places]
        return lax.ppermute(x, ("gx", "gy"), pairs)

    def total(dots, scale):
        rate = lax.pmin(scale, ("gx", "gy")) / scale
        rates = jnp.concatenate([jnp.ones((2, loads), F32), rate * rate, rate * rate], axis=0)
        sums = lax.psum(dots[0:4] * rates, ("gx", "gy")) / rates
        return jnp.concatenate([sums, jnp.zeros((PAD - 4, loads), F32)], axis=0)

    vec = sds((width, loads))
    rows = sds((PAD, loads))
    stack_shape = sds((2 * width + 4 * PAD, width), BF16)
    flops = 2 * width * width * 2 * loads * 2

    def z_out(tiny, extra=0):
        return dict(y=sds((4 * face, loads)), za=sds((face + extra, loads)),
                    zb=sds((face + tiny * PAD + extra, loads)), t=sds((tiny * PAD, loads)))

    def t_exchange(a, with_dots):
        got = dict(t=a["t"], y=a["y"])
        if small:
            got.update(gzb=swap(a["zb"], "gz", 1), gt2=shift(a["t"], "gz", 2), gta=swap(a["t"], "gz", 0))
        else:
            got["g_all"] = lax.all_gather(a["t"][0:PAD], "gz", axis=0, tiled=True)
            if with_dots:
                got["d_all"] = lax.psum(a["t"][PAD:2 * PAD], "gz")
        return got

    def z_faces(a, v, t, modes=None):
        ins = dict(za=a["za"], zb=a["zb"], gzb=t["gzb"] if small else swap(a["zb"], "gz", 1),
                   gza=swap(a["za"], "gz", 0), mt=mt, amp=v["amp"])
        outs = dict(z=sds((2 * face, loads)))
        if modes is None:
            outs.update(mt_a=sds((face, 6 * PAD), BF16), mt_b=sds((face, 6 * PAD), BF16))
        else:
            ins.update(modes)
        return call(functools.partial(z_kernel, face), ins, outs, flops=Z_FLOPS)

    def value(stage, ins):
        extra = 0 if stage == 2 else PAD
        outs = dict(amp=sds((3 * PAD, loads)), xab=sds((2 * face + (PAD if small else extra), loads)),
                    ya=sds((face + extra, loads)), yb=sds((face + 2 * PAD, loads)))
        if stage == 0 and small:
            outs["c_all"] = sds((nz * PAD, nz * PAD))
        if stage == 2 and small:
            outs["six"] = rows
        if stage == 3:
            outs["dots"] = rows
        return call(functools.partial(value_kernel, face, stage), ins, outs, flops=2 * width * loads * 48)

    def x_exchange(v):
        got = dict(xab=v["xab"])
        if nx == 2:
            got["gxab"] = swap(v["xab"], "gx", 0)
        else:
            a, b, rest = v["xab"][:face], v["xab"][face:2 * face], v["xab"][2 * face:]
            got["gxab"] = jnp.concatenate([swap(a, "gx", 0), swap(b, "gx", 1), rest], axis=0)
        return got

    def y_exchange(v):
        gyb = swap(v["yb"], "gy", 1)
        return dict(ya=v["ya"], yb=v["yb"], gya=swap(v["ya"], "gy", 0), gyb=gyb)

    def xy_exchange(v):
        return dict(x_exchange(v), **y_exchange(v))

    hbm = pl.BlockSpec(memory_space=pltpu.HBM)
    vmem = pl.BlockSpec(memory_space=pltpu.VMEM)
    outs = dict(r0=vec, stack=stack_shape, mt=sds((width, 6 * PAD), BF16),
                c_own=sds((PAD, (4 if small else 1) * nz * PAD)), **z_out(3, PAD))
    res = pl.pallas_call(
        functools.partial(first_kernel, face, nz, n_modes, small),
        out_shape=list(outs.values()),
        in_specs=[hbm] * 4,
        out_specs=[vmem] * len(outs),
        scratch_shapes=[
            pltpu.VMEM(resid.shape, F32), pltpu.VMEM(matrix.shape, F32),
            pltpu.VMEM(mode_rows.shape, F32), pltpu.VMEM(coarse_rows.shape, F32),
            pltpu.SemaphoreType.DMA((9,)),
        ],
        compiler_params=pltpu.CompilerParams(vmem_limit_bytes=VMEM_LIMIT),
        cost_estimate=pl.CostEstimate(flops=flops, bytes_accessed=4 * matrix.size, transcendentals=0),
    )(*[pltpu.with_memory_space_constraint(x, pltpu.HBM) for x in (resid, matrix, mode_rows, coarse_rows)])
    a = dict(zip(outs, res))
    r0, mt, stack = a["r0"], a["mt"], a["stack"]
    ins = dict(t_exchange(a, True), mt=mt)
    if small:
        ins["c_own"] = a["c_own"]
    else:
        c_own = a["c_own"]
        ins["c_all"] = jnp.concatenate([
            c_own, swap(c_own, "gz", 0), swap(c_own, "gz", 1),
            lax.all_gather(c_own, "gz", axis=0, tiled=True)], axis=0)
    t = ins
    v = value(0, ins)
    column = dict(mt=mt, c_all=v["c_all"] if small else ins["c_all"])
    z = z_faces(a, v, t)
    got_modes = dict(mt_a=z["mt_a"], mt_b=z["mt_b"])
    x = dict(xy_exchange(v), z=z["z"])

    a = call(functools.partial(second_kernel, face), dict(x, stack=stack),
             dict(w0=vec, first=rows, **z_out(2)), flops=flops)
    w0, first = a["w0"], a["first"]
    t = t_exchange(a, True)
    v = value(1, dict(t, **column, first=first))
    x = dict(xy_exchange(v), z=z_faces(a, v, t, got_modes)["z"])

    near = dict(near=sds((3 * PAD, loads))) if small else {}
    a = call(functools.partial(third_kernel, face), dict(x, stack=stack, first=first),
             dict(q=vec, **near, **z_out(1)), flops=flops)
    q = a["q"]
    t = t_exchange(a, False)
    ins = dict(t, **column)
    if small:
        ins.update(first=first, near=a["near"], swapped=swap(a["near"][0:2 * PAD], "gy", 0))
        v = value(2, ins)
        sums = dict(six=v["six"])
    else:
        sums = dict(six=total(v["xab"][2 * face:], first[2:3]), whole=first)
        v = value(2, ins)
    x = dict(xy_exchange(v), z=z_faces(a, v, t, got_modes)["z"])

    a = call(functools.partial(fourth_kernel, face),
             dict(x, stack=stack, **sums, first=first, r0=r0, w0=w0, q=q),
             dict(w2=vec, s1=vec, z1=vec, known=rows, **z_out(2)), flops=flops)
    t = t_exchange(a, True)
    v = value(3, dict(t, **column))
    z = z_faces(a, v, t, got_modes)["z"]
    if small:
        x = x_exchange(v)
        across = move(v["dots"], lambda a, b: (1 - a, (b + (-1 if b % 2 == 0 else 1)) % ny))
        x.update(y_exchange(v))
        part = call(functools.partial(four_kernel, face),
                    dict(dots=v["dots"], across=across, gxab=x["gxab"], gyb=x["gyb"], z=z), dict(part=rows))["part"]
        sums = dict(sum_near=part, sum_far=swap(part, "gy", 0))
    else:
        x = xy_exchange(v)
        sums = dict(sum_near=lax.psum(v["dots"], ("gx", "gy")), sum_far=jnp.zeros((PAD, loads), F32))
    out = sds((loads, width))
    res = call(functools.partial(last_kernel, face),
               dict(x, **sums, z=z, r0=r0, w0=w0, **{name: a[name] for name in ("known", "w2", "s1", "z1")}),
               dict(mult=out, resid=out))
    return (res["mult"][None, None, None], res["resid"][None, None, None])


def solution(mesh):
    spec = P("gx", "gy", "gz", None, None)
    sizes = tuple(mesh.shape[axis] for axis in ("gx", "gy", "gz"))
    return jax.shard_map(
        functools.partial(body, sizes),
        mesh=mesh,
        in_specs=(spec, spec, spec, P("gx", "gy", "gz", None)),
        out_specs=(spec, spec),
        check_vma=False,
    )
```

```python
import functools

import jax
import jax.numpy as jnp
from jax import lax
from jax.experimental import pallas as pl
from jax.experimental.pallas import tpu as pltpu
from jax.sharding import PartitionSpec as P

F32 = jnp.float32
BF16 = jnp.bfloat16
HI = lax.Precision.HIGHEST
PAD = 8
VMEM_LIMIT = 24 * 1024 * 1024
Z_FLOPS = 770000000


def sds(shape, dtype=F32):
    return jax.ShapeDtypeStruct(shape, dtype)


def call(kernel, ins, outs, flops=0):
    names_in, names_out = list(ins), list(outs)
    nbytes = sum(a.size * a.dtype.itemsize for a in list(ins.values()) + list(outs.values()))

    def run(*refs):
        n = len(names_in)
        kernel(dict(zip(names_in, refs[:n])), dict(zip(names_out, refs[n:])))

    vmem = pl.BlockSpec(memory_space=pltpu.VMEM)
    res = pl.pallas_call(
        run,
        out_shape=[outs[n] for n in names_out],
        in_specs=[vmem] * len(names_in),
        out_specs=[vmem] * len(names_out),
        compiler_params=pltpu.CompilerParams(vmem_limit_bytes=VMEM_LIMIT),
        cost_estimate=pl.CostEstimate(flops=flops, bytes_accessed=nbytes, transcendentals=0),
    )(*[ins[n] for n in names_in])
    return dict(zip(names_out, res))


def split(x):
    high = x.astype(BF16)
    return high, (x - high.astype(F32)).astype(BF16)


def split3(x):
    high = x.astype(BF16)
    rest = x - high.astype(F32)
    mid = rest.astype(BF16)
    return high, mid, (rest - mid.astype(F32)).astype(BF16)


def mode_pieces(modes):
    high, mid, low = split3(modes.T)
    return jnp.concatenate([high, high, mid, mid, high, low], axis=1)


def amp_pieces(amp):
    high, mid, low = split3(amp)
    return jnp.concatenate([high, mid, high, mid, low, high], axis=0)


def dot32(a, b):
    return jnp.dot(a, b, precision=HI, preferred_element_type=F32)


def dot16(a, b):
    return jnp.dot(a, b, preferred_element_type=F32)


def col_sum(x):
    return jnp.sum(x, axis=0, keepdims=True)


def half_dot(a, b):
    return 0.5 * col_sum(a * b)


def row(x, i):
    return x[i:i + 1, :]


def face_places(face):
    places, signs = [], []
    for k, axis in enumerate(("gx", "gy", "gz")):
        odd = lax.rem(lax.axis_index(axis), 2)
        for high in (1 - odd, odd):
            places.append(pl.multiple_of((2 * k + high) * face, face))
            signs.append((1 - 2 * high).astype(F32))
    return places, signs


def store_product(face, part, y, o):
    if part < 2:
        o["y"][2 * part * face:2 * (part + 1) * face, :] = y
    else:
        o["za"][0:face, :] = y[0:face]
        o["zb"][0:face, :] = y[face:]


def send_rows(face, rows, at, o):
    n = rows.shape[0]
    o["t"][at:at + n, :] = rows
    o["t2"][at:at + n, :] = rows
    o["zb"][face + at:face + at + n, :] = rows


def product(face, vec, stack, o):
    width, cols = vec.shape
    both = dot16(stack[...], jnp.concatenate(split(vec), axis=1))
    total = jnp.zeros((1, cols), F32)
    for part in range(3):
        at = slice(2 * part * face, 2 * (part + 1) * face)
        low = slice(width + 2 * part * face, width + 2 * (part + 1) * face)
        y = (both[at, :cols] + both[at, cols:]) + (both[low, :cols] + both[low, cols:])
        store_product(face, part, y, o)
        total = total + col_sum(vec[at] * y)
    loads = both[2 * width:, :cols] + both[2 * width:, cols:]
    send_rows(face, (loads[0:PAD] + loads[PAD:2 * PAD]) + loads[2 * PAD:3 * PAD], 0, o)
    return total


def stack_rows(rows, cols):
    zero = jnp.zeros((1, cols), F32)
    return jnp.concatenate(list(rows) + [zero] * (PAD - len(rows)), axis=0)


def first_kernel(face, nz, n_modes, turn, resid_hbm, schur_hbm, modes_hbm, coarse_hbm, *refs):
    names = ["r0", "stack", "mt", "c_own", "y", "za", "zb", "t", "t2"]
    o = dict(zip(names, refs[:len(names)]))
    resid, schur, mode_rows, coarse, sems = refs[len(names):]
    two = 2 * face
    places, signs = face_places(face)
    copies = [
        pltpu.make_async_copy(modes_hbm, mode_rows, sems.at[0]),
        pltpu.make_async_copy(resid_hbm, resid, sems.at[1]),
        pltpu.make_async_copy(coarse_hbm, coarse, sems.at[2]),
    ]
    for f in range(6):
        at = pl.ds(f * face, face)
        copies.append(pltpu.make_async_copy(schur_hbm.at[pl.ds(places[f], face), :], schur.at[at, :], sems.at[3 + f]))
    for copy in copies:
        copy.start()

    copies[0].wait()
    modes = jnp.concatenate([
        jnp.concatenate([mode_rows[m, :, pl.ds(at, face)] for at in places], axis=1)
        for m in range(n_modes)], axis=0)
    modes = jnp.concatenate([modes, jnp.zeros((PAD - n_modes, modes.shape[1]), F32)], axis=0)
    width = modes.shape[1]
    o["mt"][...] = mode_pieces(modes)
    o["stack"][2 * width:, :] = jnp.concatenate(split3(modes) + (jnp.zeros(modes.shape, BF16),), axis=0)

    copies[1].wait()
    for f in range(6):
        o["r0"][f * face:(f + 1) * face, :] = signs[f] * resid[:, pl.ds(places[f], face)].T
    r0 = o["r0"][...]
    cols = r0.shape[1]

    copies[2].wait()
    rows = jnp.concatenate([coarse[m] for m in range(n_modes)], axis=0)
    rows = jnp.concatenate([rows, jnp.zeros((PAD - n_modes, rows.shape[1]), F32)], axis=0)
    wide = o["c_own"].shape[1]
    source = lax.broadcasted_iota(jnp.int32, (nz * n_modes, wide), 0)
    place = lax.broadcasted_iota(jnp.int32, (nz * n_modes, wide), 1)
    block, mode = place // PAD, place % PAD

    if turn:
        me = lax.axis_index("gz")
        side = 1 - 2 * lax.rem(me, 2)
        copy, block = block // nz, block % nz
        holder = me + jnp.where(copy == 1, side, jnp.where(copy == 2, -side, 2 * (copy // 3)))
        side = jnp.where((copy == 1) | (copy == 2), -side, side)
        offset = jnp.where(block == 1, side, jnp.where(block == 2, -side, 2 * (block // 3)))
        device = (holder + offset + 2 * nz) % nz
    else:
        device = block
    pick = jnp.where((source == device * n_modes + mode) & (mode < n_modes), 1.0, 0.0)
    ordered = dot32(rows, pick)
    o["c_own"][...] = ordered
    if turn:
        send_rows(face, ordered, 2 * PAD, o)
    o["za"][face:face + PAD, :] = modes[:, 4 * face:5 * face]
    o["zb"][face + 3 * PAD:face + 4 * PAD, :] = modes[:, 5 * face:6 * face]

    for part in range(3):
        at = slice(part * two, (part + 1) * two)
        copies[3 + 2 * part].wait()
        copies[4 + 2 * part].wait()
        high, low = split(jnp.concatenate([schur[at, pl.ds(start, face)] for start in places], axis=1))
        o["stack"][at, :] = high
        o["stack"][width + part * two:width + (part + 1) * two, :] = low
    curv = product(face, r0, o["stack"], o)
    send_rows(face, stack_rows([half_dot(r0, r0), curv], cols), PAD, o)


def column_rows(face, i, at):
    return [i["t"][at:at + PAD, :], i["gta"][at:at + PAD, :],
            i["gzb"][face + at:face + at + PAD, :], i["gt2"][at:at + PAD, :]]


def z_kernel(face, i, o):
    for k, name in enumerate(("a", "b")):
        if "mt_" + name in o:
            got_modes = mode_pieces(i["gz" + name][-PAD:, :])
            o["mt_" + name][...] = got_modes
        else:
            got_modes = i["mt_" + name][...]
        amp = i["amp"]
        own = i["z" + name][0:face, :] + dot16(i["mt"][(4 + k) * face:(5 + k) * face, :], amp_pieces(amp[0:PAD, :]))
        at = (1 + k) * PAD
        got = i["gz" + name][0:face, :] + dot16(got_modes, amp_pieces(amp[at:at + PAD, :]))
        o["z"][k * face:(k + 1) * face, :] = own - got


def value_kernel(face, stage, i, o):
    gathered = "g_all" in i
    loads = i["g_all"][...] if gathered else jnp.concatenate(column_rows(face, i, 0), axis=0)
    if stage == 0 and not gathered:
        n = loads.shape[0]
        coarse = jnp.concatenate([part[:, k * n:(k + 1) * n] for k, part in enumerate(
            [i["c_own"][...]] + column_rows(face, i, 2 * PAD)[1:])], axis=0)
        o["c_all"][...] = coarse
    else:
        coarse = i["c_all"][...]
    amp = dot32(coarse, loads)
    o["amp"][...] = amp[0:3 * PAD]
    xy = i["y"][...] + dot16(i["mt"][0:4 * face, :], amp_pieces(amp[0:PAD]))
    cols = loads.shape[1]

    if stage != 2:
        if gathered:
            dots = i["d_all"][...]
            quad = col_sum(loads * amp[3 * PAD:])
        else:
            parts = column_rows(face, i, PAD)
            dots = (parts[0] + parts[1]) + (parts[2] + parts[3])
            quad = col_sum(loads * amp)
        at = {0: 1, 1: 1, 3: 5}[stage]
        dots = jnp.concatenate([dots[0:at], row(dots, at) + quad, dots[at + 1:]], axis=0)
    if stage == 1:
        dots = jnp.concatenate([i["first"][0:2, :], dots[0:2], dots[4:]], axis=0)
    elif stage == 2 and "swapped" in i:
        dots = six_columns(i, o)
    o["xab"][0:2 * face, :] = xy[0:2 * face]
    o["ya"][0:face, :] = xy[2 * face:3 * face]
    o["yb"][0:face, :] = xy[3 * face:]
    if stage == 3:
        o["dots"][...] = dots
    if stage != 2 or "swapped" in i:
        o["xab"][2 * face:, :] = dots
    if stage != 2:
        o["ya"][face:face + PAD, :] = dots
        o["yb"][face:face + PAD, :] = dots


def assemble(face, i, rates=None):
    f = face
    got = [i["gxab"][0:2 * f, :], i["gya"][0:f, :], i["gyb"][0:f, :]]
    if rates is not None:
        got = [rate * face_values for rate, face_values in zip(rates, got)]
    return jnp.concatenate([
        i["xab"][0:2 * f, :] - got[0], i["ya"][0:f, :] - got[1], i["yb"][0:f, :] - got[2], i["z"][...],
    ], axis=0)


def column_scale(dots):
    norm, curv = row(dots, 0), row(dots, 1)
    usable = (norm > 0.0) & (curv > 0.0)
    return jnp.where(usable, norm / jnp.where(usable, curv, 1.0), 1.0)


def rescale(dots, rate):
    square = rate * rate
    return stack_rows([row(dots, 0), row(dots, 1), square * row(dots, 2), square * row(dots, 3)], dots.shape[1])


def second_kernel(face, i, o):
    w0 = assemble(face, i)
    o["w0"][...] = w0
    first = i["xab"][2 * face:2 * face + PAD, :]
    scale = column_scale(first)
    cols = w0.shape[1]
    rates = [scale / column_scale(i[name][at:at + PAD, :])
             for name, at in (("gxab", 2 * face), ("gya", face), ("gyb", face))]
    o["first"][...] = stack_rows([row(first, 0), row(first, 1), scale] + rates, cols)
    vec = scale * w0
    curv = product(face, vec, i["stack"], o)
    send_rows(face, stack_rows([half_dot(vec, vec), curv], cols), PAD, o)


def third_kernel(face, i, o):
    scale, *rates = (row(i["first"], k) for k in range(2, 6))
    q = assemble(face, i, rates)
    o["q"][...] = q
    if "near" in o:
        partners = [rescale(i[name][at:at + PAD, :], rate) for rate, name, at in zip(
            rates, ("gxab", "gya", "gyb"), (2 * face, face, face))]
        o["near"][...] = jnp.concatenate([partners[0], partners[2], partners[1] + i["xab"][2 * face:, :]], axis=0)
    product(face, scale * q, i["stack"], o)


def six_columns(i, o):
    near = i["near"]
    rate = row(i["first"], 4)
    both = rescale(i["swapped"][0:PAD, :], rate), rescale(i["swapped"][PAD:2 * PAD, :], rate)
    o["six"][...] = ((near[0:PAD, :] + near[PAD:2 * PAD, :]) + near[2 * PAD:, :]) + (both[0] + both[1])
    return near[PAD:2 * PAD, :] + both[1]


def fourth_kernel(face, i, o):
    scale, *rates = (row(i["first"], k) for k in range(2, 6))
    sums = i["six"][...]
    if "whole" not in i:
        sums = sums + rescale(i["gxab"][2 * face:, :], rates[0])
    m0, m1 = row(sums, 0), row(sums, 1)
    alpha0 = m0 / m1
    ratio0 = alpha0 / scale
    square = ratio0 * ratio0
    m2, m3 = square * row(sums, 2), square * row(sums, 3)
    norm1 = m2 - m0
    curv1 = m1 - 2.0 * (m2 / alpha0) + m3
    beta1 = norm1 / m0
    alpha1 = norm1 / (curv1 - beta1 * norm1 / alpha0)
    r0, w0 = i["r0"][...], i["w0"][...]
    q = ratio0 * i["q"][...]
    b = q - square * assemble(face, i, [rate * rate for rate in rates])
    w1 = w0 - q
    s1 = alpha1 * (w1 + beta1 * w0)
    r2 = (r0 - alpha0 * w0) - s1
    z1 = (alpha1 / alpha0) * (b + beta1 * q)
    w2 = w1 - z1
    vec = alpha1 * w2
    cols = w2.shape[1]
    o["w2"][...] = vec
    o["s1"][...] = s1
    o["z1"][...] = z1
    o["known"][...] = stack_rows([norm1, alpha1, alpha0, beta1], cols)
    curv = product(face, vec, i["stack"], o)
    send_rows(face, stack_rows([
        half_dot(r2, r2), half_dot(r2, w2), half_dot(vec, vec), half_dot(vec, s1),
        half_dot(s1, s1), curv, half_dot(z1, vec), half_dot(s1, z1)], cols), PAD, o)


def four_kernel(face, i, o):
    near = i["dots"][...] + i["gxab"][2 * face:2 * face + PAD, :]
    o["part"][...] = near + (i["across"][...] + i["gyb"][face:face + PAD, :])


def last_kernel(face, i, o):
    d = i["sum_near"][...] + i["sum_far"][...]
    rr, rw, ww, ws, ss, wc, sc, sz = (row(d, k) for k in range(8))
    norm1, alpha1, alpha0, beta1 = (row(i["known"], k) for k in range(4))
    beta2 = rr / norm1
    alpha2 = rr / (rw - beta2 * rr / alpha1)
    ratio = alpha2 / alpha1
    ratio2 = ratio * ratio
    norm3 = ratio2 * (ww + 2.0 * beta2 * ws + beta2 * beta2 * ss) - rr
    curv3 = rw - 2.0 * (ratio2 / alpha2) * (ww + beta2 * ws)
    curv3 = curv3 + ratio2 * (wc + 2.0 * beta2 * sc + beta2 * beta2 * sz)
    beta3 = norm3 / rr
    alpha3 = norm3 / (curv3 - beta3 * norm3 / alpha2)
    c3 = assemble(face, i)
    w2, s1 = i["w2"][...], i["s1"][...]
    r0 = i["r0"][...]
    r1 = r0 - alpha0 * i["w0"][...]
    p1 = r1 + beta1 * r0
    r2 = r1 - s1
    p2 = r2 + beta2 * p1
    s2 = w2 + beta2 * s1
    r3 = r2 - ratio * s2
    w3 = w2 / alpha1 - ratio * (c3 + beta2 * i["z1"][...])
    mult = (alpha0 * r0 + alpha1 * p1) + alpha2 * p2 + alpha3 * (r3 + beta3 * p2)
    resid = r3 - alpha3 * (w3 + (beta3 / alpha1) * s2)
    places, signs = face_places(face)
    for f in range(6):
        at = slice(f * face, (f + 1) * face)
        o["mult"][:, pl.ds(places[f], face)] = signs[f] * mult[at, :].T
        o["resid"][:, pl.ds(places[f], face)] = signs[f] * resid[at, :].T


def body(sizes, residual_in, schur, modes, coarse_inv):
    nx, ny, nz = sizes
    resid = residual_in[0, 0, 0]
    matrix = schur[0, 0, 0]
    loads, width = resid.shape
    face = width // 6
    n_modes = modes.shape[3]
    mode_rows = modes.reshape(n_modes, 1, width)
    coarse_rows = coarse_inv.reshape(n_modes, 1, nz * n_modes)
    small = (nx, ny, nz) == (2, 4, 4)

    def shift(x, axis, by):
        n = lax.axis_size(axis)
        return lax.ppermute(x, axis, [(k, (k + by) % n) for k in range(n)])

    def swap(x, axis, first):
        n = lax.axis_size(axis)
        side = lambda k: 1 if (k - first) % 2 == 0 else -1
        return lax.ppermute(x, axis, [(k, (k + side(k)) % n) for k in range(n)])

    def move(x, target):
        places = [(a, b) for a in range(nx) for b in range(ny)]
        pairs = [(a * ny + b, target(a, b)[0] * ny + target(a, b)[1]) for a, b in places]
        return lax.ppermute(x, ("gx", "gy"), pairs)

    def total(dots, scale):
        rate = lax.pmin(scale, ("gx", "gy")) / scale
        rates = jnp.concatenate([jnp.ones((2, loads), F32), rate * rate, rate * rate], axis=0)
        sums = lax.psum(dots[0:4] * rates, ("gx", "gy")) / rates
        return jnp.concatenate([sums, jnp.zeros((PAD - 4, loads), F32)], axis=0)

    vec = sds((width, loads))
    rows = sds((PAD, loads))
    stack_shape = sds((2 * width + 4 * PAD, width), BF16)
    flops = 2 * width * width * 2 * loads * 2

    def z_out(tiny, extra=0):
        return dict(y=sds((4 * face, loads)), za=sds((face + extra, loads)),
                    zb=sds((face + tiny * PAD + extra, loads)), t=sds((tiny * PAD, loads)),
                    t2=sds((tiny * PAD + PAD, loads)))

    def t_exchange(a, with_dots):
        got = dict(t=a["t"], y=a["y"])
        if small:
            got.update(gzb=swap(a["zb"], "gz", 1), gt2=shift(a["t2"], "gz", 2), gta=swap(a["t"], "gz", 0))
        else:
            got["g_all"] = lax.all_gather(a["t"][0:PAD], "gz", axis=0, tiled=True)
            if with_dots:
                got["d_all"] = lax.psum(a["t"][PAD:2 * PAD], "gz")
        return got

    def z_faces(a, v, t, modes=None):
        ins = dict(za=a["za"], zb=a["zb"], gzb=t["gzb"] if small else swap(a["zb"], "gz", 1),
                   gza=swap(a["za"], "gz", 0), mt=mt, amp=v["amp"])
        outs = dict(z=sds((2 * face, loads)))
        if modes is None:
            outs.update(mt_a=sds((face, 6 * PAD), BF16), mt_b=sds((face, 6 * PAD), BF16))
        else:
            ins.update(modes)
        return call(functools.partial(z_kernel, face), ins, outs, flops=Z_FLOPS)

    def value(stage, ins):
        extra = 0 if stage == 2 else PAD
        outs = dict(amp=sds((3 * PAD, loads)), xab=sds((2 * face + (PAD if small else extra), loads)),
                    ya=sds((face + extra, loads)), yb=sds((face + 2 * PAD, loads)))
        if stage == 0 and small:
            outs["c_all"] = sds((nz * PAD, nz * PAD))
        if stage == 2 and small:
            outs["six"] = rows
        if stage == 3:
            outs["dots"] = rows
        return call(functools.partial(value_kernel, face, stage), ins, outs, flops=2 * width * loads * 48)

    def x_exchange(v):
        got = dict(xab=v["xab"])
        if nx == 2:
            got["gxab"] = swap(v["xab"], "gx", 0)
        else:
            a, b, rest = v["xab"][:face], v["xab"][face:2 * face], v["xab"][2 * face:]
            got["gxab"] = jnp.concatenate([swap(a, "gx", 0), swap(b, "gx", 1), rest], axis=0)
        return got

    def y_exchange(v):
        gyb = swap(v["yb"], "gy", 1)
        return dict(ya=v["ya"], yb=v["yb"], gya=swap(v["ya"], "gy", 0), gyb=gyb)

    def xy_exchange(v):
        return dict(x_exchange(v), **y_exchange(v))

    hbm = pl.BlockSpec(memory_space=pltpu.HBM)
    vmem = pl.BlockSpec(memory_space=pltpu.VMEM)
    outs = dict(r0=vec, stack=stack_shape, mt=sds((width, 6 * PAD), BF16),
                c_own=sds((PAD, (4 if small else 1) * nz * PAD)), **z_out(3, PAD))
    res = pl.pallas_call(
        functools.partial(first_kernel, face, nz, n_modes, small),
        out_shape=list(outs.values()),
        in_specs=[hbm] * 4,
        out_specs=[vmem] * len(outs),
        scratch_shapes=[
            pltpu.VMEM(resid.shape, F32), pltpu.VMEM(matrix.shape, F32),
            pltpu.VMEM(mode_rows.shape, F32), pltpu.VMEM(coarse_rows.shape, F32),
            pltpu.SemaphoreType.DMA((9,)),
        ],
        compiler_params=pltpu.CompilerParams(vmem_limit_bytes=VMEM_LIMIT),
        cost_estimate=pl.CostEstimate(flops=flops, bytes_accessed=4 * matrix.size, transcendentals=0),
    )(*[pltpu.with_memory_space_constraint(x, pltpu.HBM) for x in (resid, matrix, mode_rows, coarse_rows)])
    a = dict(zip(outs, res))
    r0, mt, stack = a["r0"], a["mt"], a["stack"]
    ins = dict(t_exchange(a, True), mt=mt)
    if small:
        ins["c_own"] = a["c_own"]
    else:
        c_own = a["c_own"]
        ins["c_all"] = jnp.concatenate([
            c_own, swap(c_own, "gz", 0), swap(c_own, "gz", 1),
            lax.all_gather(c_own, "gz", axis=0, tiled=True)], axis=0)
    t = ins
    v = value(0, ins)
    column = dict(mt=mt, c_all=v["c_all"] if small else ins["c_all"])
    z = z_faces(a, v, t)
    got_modes = dict(mt_a=z["mt_a"], mt_b=z["mt_b"])
    x = dict(xy_exchange(v), z=z["z"])

    a = call(functools.partial(second_kernel, face), dict(x, stack=stack),
             dict(w0=vec, first=rows, **z_out(2)), flops=flops)
    w0, first = a["w0"], a["first"]
    t = t_exchange(a, True)
    v = value(1, dict(t, **column, first=first))
    x = dict(xy_exchange(v), z=z_faces(a, v, t, got_modes)["z"])

    near = dict(near=sds((3 * PAD, loads))) if small else {}
    a = call(functools.partial(third_kernel, face), dict(x, stack=stack, first=first),
             dict(q=vec, **near, **z_out(1)), flops=flops)
    q = a["q"]
    t = t_exchange(a, False)
    ins = dict(t, **column)
    if small:
        ins.update(first=first, near=a["near"], swapped=swap(a["near"][0:2 * PAD], "gy", 0))
        v = value(2, ins)
        sums = dict(six=v["six"])
    else:
        sums = dict(six=total(v["xab"][2 * face:], first[2:3]), whole=first)
        v = value(2, ins)
    x = dict(xy_exchange(v), z=z_faces(a, v, t, got_modes)["z"])

    a = call(functools.partial(fourth_kernel, face),
             dict(x, stack=stack, **sums, first=first, r0=r0, w0=w0, q=q),
             dict(w2=vec, s1=vec, z1=vec, known=rows, **z_out(2)), flops=flops)
    t = t_exchange(a, True)
    v = value(3, dict(t, **column))
    z = z_faces(a, v, t, got_modes)["z"]
    if small:
        x = x_exchange(v)
        across = move(v["dots"], lambda a, b: (1 - a, (b + (-1 if b % 2 == 0 else 1)) % ny))
        x.update(y_exchange(v))
        part = call(functools.partial(four_kernel, face),
                    dict(dots=v["dots"], across=across, gxab=x["gxab"], gyb=x["gyb"], z=z), dict(part=rows))["part"]
        sums = dict(sum_near=part, sum_far=swap(part, "gy", 0))
    else:
        x = xy_exchange(v)
        sums = dict(sum_near=lax.psum(v["dots"], ("gx", "gy")), sum_far=jnp.zeros((PAD, loads), F32))
    out = sds((loads, width))
    res = call(functools.partial(last_kernel, face),
               dict(x, **sums, z=z, r0=r0, w0=w0, **{name: a[name] for name in ("known", "w2", "s1", "z1")}),
               dict(mult=out, resid=out))
    return (res["mult"][None, None, None], res["resid"][None, None, None])


def solution(mesh):
    spec = P("gx", "gy", "gz", None, None)
    sizes = tuple(mesh.shape[axis] for axis in ("gx", "gy", "gz"))
    return jax.shard_map(
        functools.partial(body, sizes),
        mesh=mesh,
        in_specs=(spec, spec, spec, P("gx", "gy", "gz", None)),
        out_specs=(spec, spec),
        check_vma=False,
    )
```

```python
import functools

import jax
import jax.numpy as jnp
from jax import lax
from jax.experimental import pallas as pl
from jax.experimental.pallas import tpu as pltpu
from jax.sharding import PartitionSpec as P

F32 = jnp.float32
BF16 = jnp.bfloat16
HI = lax.Precision.HIGHEST
PAD = 8
VMEM_LIMIT = 24 * 1024 * 1024
EARLY_FLOPS = 150000000


def sds(shape, dtype=F32):
    return jax.ShapeDtypeStruct(shape, dtype)


def call(kernel, ins, outs, flops=0):
    names_in, names_out = list(ins), list(outs)
    nbytes = sum(a.size * a.dtype.itemsize for a in list(ins.values()) + list(outs.values()))

    def run(*refs):
        n = len(names_in)
        kernel(dict(zip(names_in, refs[:n])), dict(zip(names_out, refs[n:])))

    vmem = pl.BlockSpec(memory_space=pltpu.VMEM)
    res = pl.pallas_call(
        run,
        out_shape=[outs[n] for n in names_out],
        in_specs=[vmem] * len(names_in),
        out_specs=[vmem] * len(names_out),
        compiler_params=pltpu.CompilerParams(vmem_limit_bytes=VMEM_LIMIT),
        cost_estimate=pl.CostEstimate(flops=flops, bytes_accessed=nbytes, transcendentals=0),
    )(*[ins[n] for n in names_in])
    return dict(zip(names_out, res))


def split(x):
    high = x.astype(BF16)
    return high, (x - high.astype(F32)).astype(BF16)


def split3(x):
    high = x.astype(BF16)
    rest = x - high.astype(F32)
    mid = rest.astype(BF16)
    return high, mid, (rest - mid.astype(F32)).astype(BF16)


def mode_pieces(modes):
    high, mid, low = split3(modes.T)
    return jnp.concatenate([high, high, mid, mid, high, low], axis=1)


def amp_pieces(amp):
    high, mid, low = split3(amp)
    return jnp.concatenate([high, mid, high, mid, low, high], axis=0)


def dot32(a, b):
    return jnp.dot(a, b, precision=HI, preferred_element_type=F32)


def dot16(a, b):
    return jnp.dot(a, b, preferred_element_type=F32)


def col_sum(x):
    return jnp.sum(x, axis=0, keepdims=True)


def half_dot(a, b):
    return 0.5 * col_sum(a * b)


def row(x, i):
    return x[i:i + 1, :]


def face_places(face):
    places, signs = [], []
    for k, axis in enumerate(("gx", "gy", "gz")):
        odd = lax.rem(lax.axis_index(axis), 2)
        for high in (1 - odd, odd):
            places.append(pl.multiple_of((2 * k + high) * face, face))
            signs.append((1 - 2 * high).astype(F32))
    return places, signs


def store_product(face, part, y, o):
    if part == 0:
        o["xa"][0:face, :] = y[0:face]
        o["y"][0:face, :] = y[face:]
    elif part == 1:
        o["y"][face:3 * face, :] = y
    else:
        o["za"][0:face, :] = y[0:face]
        o["zb"][0:face, :] = y[face:]


def send_rows(face, rows, at, o):
    n = rows.shape[0]
    o["t"][at:at + n, :] = rows
    o["t2"][at:at + n, :] = rows
    o["zb"][face + at:face + at + n, :] = rows


def product(face, vec, stack, o):
    width, cols = vec.shape
    both = dot16(stack[...], jnp.concatenate(split(vec), axis=1))
    total = jnp.zeros((1, cols), F32)
    for part in range(3):
        at = slice(2 * part * face, 2 * (part + 1) * face)
        low = slice(width + 2 * part * face, width + 2 * (part + 1) * face)
        y = (both[at, :cols] + both[at, cols:]) + (both[low, :cols] + both[low, cols:])
        store_product(face, part, y, o)
        total = total + col_sum(vec[at] * y)
    loads = both[2 * width:, :cols] + both[2 * width:, cols:]
    send_rows(face, (loads[0:PAD] + loads[PAD:2 * PAD]) + loads[2 * PAD:3 * PAD], 0, o)
    return total


def stack_rows(rows, cols):
    zero = jnp.zeros((1, cols), F32)
    return jnp.concatenate(list(rows) + [zero] * (PAD - len(rows)), axis=0)


def first_kernel(face, nz, n_modes, turn, resid_hbm, schur_hbm, modes_hbm, coarse_hbm, *refs):
    names = ["r0", "stack", "mt", "c_own", "y", "xa", "za", "zb", "t", "t2"]
    o = dict(zip(names, refs[:len(names)]))
    resid, schur, mode_rows, coarse, sems = refs[len(names):]
    two = 2 * face
    places, signs = face_places(face)
    copies = [
        pltpu.make_async_copy(modes_hbm, mode_rows, sems.at[0]),
        pltpu.make_async_copy(resid_hbm, resid, sems.at[1]),
        pltpu.make_async_copy(coarse_hbm, coarse, sems.at[2]),
    ]
    for f in range(6):
        at = pl.ds(f * face, face)
        copies.append(pltpu.make_async_copy(schur_hbm.at[pl.ds(places[f], face), :], schur.at[at, :], sems.at[3 + f]))
    for copy in copies:
        copy.start()

    copies[0].wait()
    modes = jnp.concatenate([
        jnp.concatenate([mode_rows[m, :, pl.ds(at, face)] for at in places], axis=1)
        for m in range(n_modes)], axis=0)
    modes = jnp.concatenate([modes, jnp.zeros((PAD - n_modes, modes.shape[1]), F32)], axis=0)
    width = modes.shape[1]
    o["mt"][...] = mode_pieces(modes)
    o["stack"][2 * width:, :] = jnp.concatenate(split3(modes) + (jnp.zeros(modes.shape, BF16),), axis=0)

    copies[1].wait()
    for f in range(6):
        o["r0"][f * face:(f + 1) * face, :] = signs[f] * resid[:, pl.ds(places[f], face)].T
    r0 = o["r0"][...]
    cols = r0.shape[1]

    copies[2].wait()
    rows = jnp.concatenate([coarse[m] for m in range(n_modes)], axis=0)
    rows = jnp.concatenate([rows, jnp.zeros((PAD - n_modes, rows.shape[1]), F32)], axis=0)
    wide = o["c_own"].shape[1]
    source = lax.broadcasted_iota(jnp.int32, (nz * n_modes, wide), 0)
    place = lax.broadcasted_iota(jnp.int32, (nz * n_modes, wide), 1)
    block, mode = place // PAD, place % PAD

    if turn:
        me = lax.axis_index("gz")
        side = 1 - 2 * lax.rem(me, 2)
        copy, block = block // nz, block % nz
        holder = me + jnp.where(copy == 1, side, jnp.where(copy == 2, -side, 2 * (copy // 3)))
        side = jnp.where((copy == 1) | (copy == 2), -side, side)
        offset = jnp.where(block == 1, side, jnp.where(block == 2, -side, 2 * (block // 3)))
        device = (holder + offset + 2 * nz) % nz
    else:
        device = block
    pick = jnp.where((source == device * n_modes + mode) & (mode < n_modes), 1.0, 0.0)
    ordered = dot32(rows, pick)
    o["c_own"][...] = ordered
    if turn:
        send_rows(face, ordered, 2 * PAD, o)
    o["xa"][face:face + PAD, :] = modes[:, 0:face]
    o["za"][face:face + PAD, :] = modes[:, 4 * face:5 * face]
    o["zb"][face + 3 * PAD:face + 4 * PAD, :] = modes[:, 5 * face:6 * face]

    for part in range(3):
        at = slice(part * two, (part + 1) * two)
        copies[3 + 2 * part].wait()
        copies[4 + 2 * part].wait()
        high, low = split(jnp.concatenate([schur[at, pl.ds(start, face)] for start in places], axis=1))
        o["stack"][at, :] = high
        o["stack"][width + part * two:width + (part + 1) * two, :] = low
    curv = product(face, r0, o["stack"], o)
    send_rows(face, stack_rows([half_dot(r0, r0), curv], cols), PAD, o)


def column_rows(face, i, at):
    return [i["t"][at:at + PAD, :], i["gta"][at:at + PAD, :],
            i["gzb"][face + at:face + at + PAD, :], i["gt2"][at:at + PAD, :]]


def early_kernel(face, i, o):
    amp, mt = i["amp"], i["mt"]
    own = amp_pieces(amp[0:PAD, :])
    got_modes = {}
    for name in ("x", "a", "b"):
        if "mt_" + name in o:
            rows = i["gxa" if name == "x" else "gz" + name][-PAD:, :]
            got_modes[name] = mode_pieces(rows)
            o["mt_" + name][...] = got_modes[name]
        else:
            got_modes[name] = i["mt_" + name]
    for k, name in enumerate(("a", "b")):
        mine = i["z" + name][0:face, :] + dot16(mt[(4 + k) * face:(5 + k) * face, :], own)
        at = (1 + k) * PAD
        got = i["gz" + name][0:face, :] + dot16(got_modes[name][...], amp_pieces(amp[at:at + PAD, :]))
        o["z"][k * face:(k + 1) * face, :] = mine - got
    o["xa"][...] = i["xa"][0:face, :] + dot16(mt[0:face, :], own)
    o["gxa"][...] = i["gxa"][0:face, :]


def value_kernel(face, stage, i, o):
    gathered = "g_all" in i
    loads = i["g_all"][...] if gathered else jnp.concatenate(column_rows(face, i, 0), axis=0)
    if stage == 0 and not gathered:
        n = loads.shape[0]
        coarse = jnp.concatenate([part[:, k * n:(k + 1) * n] for k, part in enumerate(
            [i["c_own"][...]] + column_rows(face, i, 2 * PAD)[1:])], axis=0)
        o["c_all"][...] = coarse
    else:
        coarse = i["c_all"][...]
    amp = dot32(coarse, loads)
    o["amp"][...] = amp[0:3 * PAD]
    xy = i["y"][...] + dot16(i["mt"][face:4 * face, :], amp_pieces(amp[0:PAD]))
    cols = loads.shape[1]

    if stage != 2:
        if gathered:
            dots = i["d_all"][...]
            quad = col_sum(loads * amp[3 * PAD:])
        else:
            parts = column_rows(face, i, PAD)
            dots = (parts[0] + parts[1]) + (parts[2] + parts[3])
            quad = col_sum(loads * amp)
        at = {0: 1, 1: 1, 3: 5}[stage]
        dots = jnp.concatenate([dots[0:at], row(dots, at) + quad, dots[at + 1:]], axis=0)
    if stage == 1:
        dots = jnp.concatenate([i["first"][0:2, :], dots[0:2], dots[4:]], axis=0)
    elif stage == 2 and "swapped" in i:
        dots = six_columns(i, o)
    o["xb"][0:face, :] = xy[0:face]
    o["xb"][face:face + PAD, :] = amp[0:PAD]
    o["ya"][0:face, :] = xy[face:2 * face]
    o["yb"][0:face, :] = xy[2 * face:]
    if stage == 3:
        o["dots"][...] = dots
    if stage != 2 or "swapped" in i:
        o["xb"][face + PAD:, :] = dots
    if stage != 2:
        o["ya"][face:face + PAD, :] = dots
        o["yb"][face:face + PAD, :] = dots


def assemble(face, i, rates=None):
    f = face
    amp = i["gamp"][...] if "gamp" in i else i["gxb"][f:f + PAD, :]
    got = [i["gxa"][...] + dot16(i["mt_x"][...], amp_pieces(amp)), i["gxb"][0:f, :], i["gya"][0:f, :], i["gyb"][0:f, :]]
    if rates is not None:
        got = [rate * values for rate, values in zip(rates[0:1] + rates, got)]
    own = [i["xa"][...], i["xb"][0:f, :], i["ya"][0:f, :], i["yb"][0:f, :]]
    return jnp.concatenate([mine - other for mine, other in zip(own, got)] + [i["z"][...]], axis=0)


def column_scale(dots):
    norm, curv = row(dots, 0), row(dots, 1)
    usable = (norm > 0.0) & (curv > 0.0)
    return jnp.where(usable, norm / jnp.where(usable, curv, 1.0), 1.0)


def rescale(dots, rate):
    square = rate * rate
    return stack_rows([row(dots, 0), row(dots, 1), square * row(dots, 2), square * row(dots, 3)], dots.shape[1])


def second_kernel(face, i, o):
    w0 = assemble(face, i)
    o["w0"][...] = w0
    first = i["xb"][face + PAD:face + 2 * PAD, :]
    scale = column_scale(first)
    cols = w0.shape[1]
    rates = [scale / column_scale(i[name][at:at + PAD, :])
             for name, at in (("gxb", face + PAD), ("gya", face), ("gyb", face))]
    o["first"][...] = stack_rows([row(first, 0), row(first, 1), scale] + rates, cols)
    vec = scale * w0
    curv = product(face, vec, i["stack"], o)
    send_rows(face, stack_rows([half_dot(vec, vec), curv], cols), PAD, o)


def third_kernel(face, i, o):
    scale, *rates = (row(i["first"], k) for k in range(2, 6))
    q = assemble(face, i, rates)
    o["q"][...] = q
    if "near" in o:
        partners = [rescale(i[name][at:at + PAD, :], rate) for rate, name, at in zip(
            rates, ("gxb", "gya", "gyb"), (face + PAD, face, face))]
        o["near"][...] = jnp.concatenate([partners[0], partners[2], partners[1] + i["xb"][face + PAD:, :]], axis=0)
    product(face, scale * q, i["stack"], o)


def six_columns(i, o):
    near = i["near"]
    rate = row(i["first"], 4)
    both = rescale(i["swapped"][0:PAD, :], rate), rescale(i["swapped"][PAD:2 * PAD, :], rate)
    o["six"][...] = ((near[0:PAD, :] + near[PAD:2 * PAD, :]) + near[2 * PAD:, :]) + (both[0] + both[1])
    return near[PAD:2 * PAD, :] + both[1]


def fourth_kernel(face, i, o):
    scale, *rates = (row(i["first"], k) for k in range(2, 6))
    sums = i["six"][...]
    if "whole" not in i:
        sums = sums + rescale(i["gxb"][face + PAD:, :], rates[0])
    m0, m1 = row(sums, 0), row(sums, 1)
    alpha0 = m0 / m1
    ratio0 = alpha0 / scale
    square = ratio0 * ratio0
    m2, m3 = square * row(sums, 2), square * row(sums, 3)
    norm1 = m2 - m0
    curv1 = m1 - 2.0 * (m2 / alpha0) + m3
    beta1 = norm1 / m0
    alpha1 = norm1 / (curv1 - beta1 * norm1 / alpha0)
    r0, w0 = i["r0"][...], i["w0"][...]
    q = ratio0 * i["q"][...]
    b = q - square * assemble(face, i, [rate * rate for rate in rates])
    w1 = w0 - q
    s1 = alpha1 * (w1 + beta1 * w0)
    r2 = (r0 - alpha0 * w0) - s1
    z1 = (alpha1 / alpha0) * (b + beta1 * q)
    w2 = w1 - z1
    vec = alpha1 * w2
    cols = w2.shape[1]
    o["w2"][...] = vec
    o["s1"][...] = s1
    o["z1"][...] = z1
    o["known"][...] = stack_rows([norm1, alpha1, alpha0, beta1], cols)
    curv = product(face, vec, i["stack"], o)
    send_rows(face, stack_rows([
        half_dot(r2, r2), half_dot(r2, w2), half_dot(vec, vec), half_dot(vec, s1),
        half_dot(s1, s1), curv, half_dot(z1, vec), half_dot(s1, z1)], cols), PAD, o)


def four_kernel(face, i, o):
    near = i["dots"][...] + i["gxb"][face + PAD:face + 2 * PAD, :]
    o["part"][...] = near + (i["across"][...] + i["gyb"][face:face + PAD, :])


def last_kernel(face, i, o):
    d = i["sum_near"][...] + i["sum_far"][...]
    rr, rw, ww, ws, ss, wc, sc, sz = (row(d, k) for k in range(8))
    norm1, alpha1, alpha0, beta1 = (row(i["known"], k) for k in range(4))
    beta2 = rr / norm1
    alpha2 = rr / (rw - beta2 * rr / alpha1)
    ratio = alpha2 / alpha1
    ratio2 = ratio * ratio
    norm3 = ratio2 * (ww + 2.0 * beta2 * ws + beta2 * beta2 * ss) - rr
    curv3 = rw - 2.0 * (ratio2 / alpha2) * (ww + beta2 * ws)
    curv3 = curv3 + ratio2 * (wc + 2.0 * beta2 * sc + beta2 * beta2 * sz)
    beta3 = norm3 / rr
    alpha3 = norm3 / (curv3 - beta3 * norm3 / alpha2)
    c3 = assemble(face, i)
    w2, s1 = i["w2"][...], i["s1"][...]
    r0 = i["r0"][...]
    r1 = r0 - alpha0 * i["w0"][...]
    p1 = r1 + beta1 * r0
    r2 = r1 - s1
    p2 = r2 + beta2 * p1
    s2 = w2 + beta2 * s1
    r3 = r2 - ratio * s2
    w3 = w2 / alpha1 - ratio * (c3 + beta2 * i["z1"][...])
    mult = (alpha0 * r0 + alpha1 * p1) + alpha2 * p2 + alpha3 * (r3 + beta3 * p2)
    resid = r3 - alpha3 * (w3 + (beta3 / alpha1) * s2)
    places, signs = face_places(face)
    for f in range(6):
        at = slice(f * face, (f + 1) * face)
        o["mult"][:, pl.ds(places[f], face)] = signs[f] * mult[at, :].T
        o["resid"][:, pl.ds(places[f], face)] = signs[f] * resid[at, :].T


def body(sizes, residual_in, schur, modes, coarse_inv):
    nx, ny, nz = sizes
    resid = residual_in[0, 0, 0]
    matrix = schur[0, 0, 0]
    loads, width = resid.shape
    face = width // 6
    n_modes = modes.shape[3]
    mode_rows = modes.reshape(n_modes, 1, width)
    coarse_rows = coarse_inv.reshape(n_modes, 1, nz * n_modes)
    small = (nx, ny, nz) == (2, 4, 4)

    def shift(x, axis, by):
        n = lax.axis_size(axis)
        return lax.ppermute(x, axis, [(k, (k + by) % n) for k in range(n)])

    def swap(x, axis, first):
        n = lax.axis_size(axis)
        side = lambda k: 1 if (k - first) % 2 == 0 else -1
        return lax.ppermute(x, axis, [(k, (k + side(k)) % n) for k in range(n)])

    def move(x, target):
        places = [(a, b) for a in range(nx) for b in range(ny)]
        pairs = [(a * ny + b, target(a, b)[0] * ny + target(a, b)[1]) for a, b in places]
        return lax.ppermute(x, ("gx", "gy"), pairs)

    def total(dots, scale):
        rate = lax.pmin(scale, ("gx", "gy")) / scale
        rates = jnp.concatenate([jnp.ones((2, loads), F32), rate * rate, rate * rate], axis=0)
        sums = lax.psum(dots[0:4] * rates, ("gx", "gy")) / rates
        return jnp.concatenate([sums, jnp.zeros((PAD - 4, loads), F32)], axis=0)

    vec = sds((width, loads))
    rows = sds((PAD, loads))
    stack_shape = sds((2 * width + 4 * PAD, width), BF16)
    flops = 2 * width * width * 2 * loads * 2

    def z_out(tiny, extra=0):
        return dict(y=sds((3 * face, loads)), xa=sds((face + extra, loads)), za=sds((face + extra, loads)),
                    zb=sds((face + tiny * PAD + extra, loads)), t=sds((tiny * PAD, loads)),
                    t2=sds((tiny * PAD + PAD, loads)))

    def t_exchange(a, with_dots):
        got = dict(t=a["t"], y=a["y"])
        if small:
            got.update(gzb=swap(a["zb"], "gz", 1), gt2=shift(a["t2"], "gz", 2), gta=swap(a["t"], "gz", 0))
        else:
            got["g_all"] = lax.all_gather(a["t"][0:PAD], "gz", axis=0, tiled=True)
            if with_dots:
                got["d_all"] = lax.psum(a["t"][PAD:2 * PAD], "gz")
        return got

    def early_faces(a, v, t, modes=None):
        ins = dict(za=a["za"], zb=a["zb"], gzb=t["gzb"] if small else swap(a["zb"], "gz", 1),
                   gza=swap(a["za"], "gz", 0), xa=a["xa"], gxa=swap(a["xa"], "gx", 0), mt=mt, amp=v["amp"])
        outs = dict(z=sds((2 * face, loads)), xa=sds((face, loads)), gxa=sds((face, loads)))
        if modes is None:
            outs.update({name: sds((face, 6 * PAD), BF16) for name in ("mt_x", "mt_a", "mt_b")})
        else:
            ins.update(modes)
        return call(functools.partial(early_kernel, face), ins, outs, flops=EARLY_FLOPS)

    def value(stage, ins):
        extra = 0 if stage == 2 else PAD
        outs = dict(amp=sds((3 * PAD, loads)), xb=sds((face + PAD + (PAD if small else extra), loads)),
                    ya=sds((face + extra, loads)), yb=sds((face + 3 * PAD, loads)))
        if stage == 0 and small:
            outs["c_all"] = sds((nz * PAD, nz * PAD))
        if stage == 2 and small:
            outs["six"] = rows
        if stage == 3:
            outs["dots"] = rows
        return call(functools.partial(value_kernel, face, stage), ins, outs, flops=2 * width * loads * 48)

    def x_exchange(v, early):
        got = dict(xb=v["xb"], gxb=swap(v["xb"], "gx", 0 if nx == 2 else 1), mt_x=got_modes["mt_x"])
        got.update({name: early[name] for name in ("z", "xa", "gxa")})
        if nx != 2:
            got["gamp"] = swap(v["amp"][0:PAD], "gx", 0)
        return got

    def y_exchange(v):
        gyb = swap(v["yb"], "gy", 1)
        return dict(ya=v["ya"], yb=v["yb"], gya=swap(v["ya"], "gy", 0), gyb=gyb)

    def xy_exchange(v, early):
        return dict(x_exchange(v, early), **y_exchange(v))

    hbm = pl.BlockSpec(memory_space=pltpu.HBM)
    vmem = pl.BlockSpec(memory_space=pltpu.VMEM)
    outs = dict(r0=vec, stack=stack_shape, mt=sds((width, 6 * PAD), BF16),
                c_own=sds((PAD, (4 if small else 1) * nz * PAD)), **z_out(3, PAD))
    res = pl.pallas_call(
        functools.partial(first_kernel, face, nz, n_modes, small),
        out_shape=list(outs.values()),
        in_specs=[hbm] * 4,
        out_specs=[vmem] * len(outs),
        scratch_shapes=[
            pltpu.VMEM(resid.shape, F32), pltpu.VMEM(matrix.shape, F32),
            pltpu.VMEM(mode_rows.shape, F32), pltpu.VMEM(coarse_rows.shape, F32),
            pltpu.SemaphoreType.DMA((9,)),
        ],
        compiler_params=pltpu.CompilerParams(vmem_limit_bytes=VMEM_LIMIT),
        cost_estimate=pl.CostEstimate(flops=flops, bytes_accessed=4 * matrix.size, transcendentals=0),
    )(*[pltpu.with_memory_space_constraint(x, pltpu.HBM) for x in (resid, matrix, mode_rows, coarse_rows)])
    a = dict(zip(outs, res))
    r0, mt, stack = a["r0"], a["mt"], a["stack"]
    ins = dict(t_exchange(a, True), mt=mt)
    if small:
        ins["c_own"] = a["c_own"]
    else:
        c_own = a["c_own"]
        ins["c_all"] = jnp.concatenate([
            c_own, swap(c_own, "gz", 0), swap(c_own, "gz", 1),
            lax.all_gather(c_own, "gz", axis=0, tiled=True)], axis=0)
    t = ins
    v = value(0, ins)
    column = dict(mt=mt, c_all=v["c_all"] if small else ins["c_all"])
    early = early_faces(a, v, t)
    got_modes = {name: early[name] for name in ("mt_x", "mt_a", "mt_b")}
    x = xy_exchange(v, early)

    a = call(functools.partial(second_kernel, face), dict(x, stack=stack),
             dict(w0=vec, first=rows, **z_out(2)), flops=flops)
    w0, first = a["w0"], a["first"]
    t = t_exchange(a, True)
    v = value(1, dict(t, **column, first=first))
    x = xy_exchange(v, early_faces(a, v, t, got_modes))

    near = dict(near=sds((3 * PAD, loads))) if small else {}
    a = call(functools.partial(third_kernel, face), dict(x, stack=stack, first=first),
             dict(q=vec, **near, **z_out(1)), flops=flops)
    q = a["q"]
    t = t_exchange(a, False)
    ins = dict(t, **column)
    if small:
        ins.update(first=first, near=a["near"], swapped=swap(a["near"][0:2 * PAD], "gy", 0))
        v = value(2, ins)
        sums = dict(six=v["six"])
    else:
        sums = dict(six=total(v["xb"][face + PAD:], first[2:3]), whole=first)
        v = value(2, ins)
    x = xy_exchange(v, early_faces(a, v, t, got_modes))

    a = call(functools.partial(fourth_kernel, face),
             dict(x, stack=stack, **sums, first=first, r0=r0, w0=w0, q=q),
             dict(w2=vec, s1=vec, z1=vec, known=rows, **z_out(2)), flops=flops)
    t = t_exchange(a, True)
    v = value(3, dict(t, **column))
    early = early_faces(a, v, t, got_modes)
    if small:
        x = x_exchange(v, early)
        across = move(v["dots"], lambda a, b: (1 - a, (b + (-1 if b % 2 == 0 else 1)) % ny))
        x.update(y_exchange(v))
        part = call(functools.partial(four_kernel, face),
                    dict(dots=v["dots"], across=across, gxb=x["gxb"], gyb=x["gyb"], z=early["z"]), dict(part=rows))["part"]
        sums = dict(sum_near=part, sum_far=swap(part, "gy", 0))
    else:
        x = xy_exchange(v, early)
        sums = dict(sum_near=lax.psum(v["dots"], ("gx", "gy")), sum_far=jnp.zeros((PAD, loads), F32))
    out = sds((loads, width))
    res = call(functools.partial(last_kernel, face),
               dict(x, **sums, r0=r0, w0=w0, **{name: a[name] for name in ("known", "w2", "s1", "z1")}),
               dict(mult=out, resid=out))
    return (res["mult"][None, None, None], res["resid"][None, None, None])


def solution(mesh):
    spec = P("gx", "gy", "gz", None, None)
    sizes = tuple(mesh.shape[axis] for axis in ("gx", "gy", "gz"))
    return jax.shard_map(
        functools.partial(body, sizes),
        mesh=mesh,
        in_specs=(spec, spec, spec, P("gx", "gy", "gz", None)),
        out_specs=(spec, spec),
        check_vma=False,
    )
```

```python
import functools

import jax
import jax.numpy as jnp
from jax import lax
from jax.experimental import pallas as pl
from jax.experimental.pallas import tpu as pltpu
from jax.sharding import PartitionSpec as P

F32 = jnp.float32
BF16 = jnp.bfloat16
HI = lax.Precision.HIGHEST
PAD = 8
VMEM_LIMIT = 24 * 1024 * 1024
Z_FLOPS = 770000000


def sds(shape, dtype=F32):
    return jax.ShapeDtypeStruct(shape, dtype)


def call(kernel, ins, outs, flops=0):
    names_in, names_out = list(ins), list(outs)
    nbytes = sum(a.size * a.dtype.itemsize for a in list(ins.values()) + list(outs.values()))

    def run(*refs):
        n = len(names_in)
        kernel(dict(zip(names_in, refs[:n])), dict(zip(names_out, refs[n:])))

    vmem = pl.BlockSpec(memory_space=pltpu.VMEM)
    res = pl.pallas_call(
        run,
        out_shape=[outs[n] for n in names_out],
        in_specs=[vmem] * len(names_in),
        out_specs=[vmem] * len(names_out),
        compiler_params=pltpu.CompilerParams(vmem_limit_bytes=VMEM_LIMIT),
        cost_estimate=pl.CostEstimate(flops=flops, bytes_accessed=nbytes, transcendentals=0),
    )(*[ins[n] for n in names_in])
    return dict(zip(names_out, res))


def split(x):
    high = x.astype(BF16)
    return high, (x - high.astype(F32)).astype(BF16)


def split3(x):
    high = x.astype(BF16)
    rest = x - high.astype(F32)
    mid = rest.astype(BF16)
    return high, mid, (rest - mid.astype(F32)).astype(BF16)


def mode_pieces(modes):
    high, mid, low = split3(modes.T)
    return jnp.concatenate([high, high, mid, mid, high, low], axis=1)


def amp_pieces(amp):
    high, mid, low = split3(amp)
    return jnp.concatenate([high, mid, high, mid, low, high], axis=0)


def dot32(a, b):
    return jnp.dot(a, b, precision=HI, preferred_element_type=F32)


def dot16(a, b):
    return jnp.dot(a, b, preferred_element_type=F32)


def col_sum(x):
    return jnp.sum(x, axis=0, keepdims=True)


def half_dot(a, b):
    return 0.5 * col_sum(a * b)


def row(x, i):
    return x[i:i + 1, :]


def face_places(face):
    places, signs = [], []
    for k, axis in enumerate(("gx", "gy", "gz")):
        odd = lax.rem(lax.axis_index(axis), 2)
        for high in (1 - odd, odd):
            places.append(pl.multiple_of((2 * k + high) * face, face))
            signs.append((1 - 2 * high).astype(F32))
    return places, signs


def store_product(face, part, y, o):
    if part < 2:
        o["y"][2 * part * face:2 * (part + 1) * face, :] = y
    else:
        o["za"][0:face, :] = y[0:face]
        o["zb"][0:face, :] = y[face:]


def send_rows(face, rows, at, o):
    n = rows.shape[0]
    o["t"][at:at + n, :] = rows
    o["t2"][at:at + n, :] = rows
    o["zb"][face + at:face + at + n, :] = rows


def product(face, vec, stack, o):
    width, cols = vec.shape
    both = dot16(stack[...], jnp.concatenate(split(vec), axis=1))
    total = jnp.zeros((1, cols), F32)
    for part in range(3):
        at = slice(2 * part * face, 2 * (part + 1) * face)
        low = slice(width + 2 * part * face, width + 2 * (part + 1) * face)
        y = (both[at, :cols] + both[at, cols:]) + (both[low, :cols] + both[low, cols:])
        store_product(face, part, y, o)
        total = total + col_sum(vec[at] * y)
    loads = both[2 * width:, :cols] + both[2 * width:, cols:]
    send_rows(face, (loads[0:PAD] + loads[PAD:2 * PAD]) + loads[2 * PAD:3 * PAD], 0, o)
    return total


def stack_rows(rows, cols):
    zero = jnp.zeros((1, cols), F32)
    return jnp.concatenate(list(rows) + [zero] * (PAD - len(rows)), axis=0)


def first_kernel(face, nz, n_modes, turn, resid_hbm, schur_hbm, modes_hbm, coarse_hbm, *refs):
    names = ["r0", "stack", "mt", "c_own", "y", "za", "zb", "t", "t2"]
    o = dict(zip(names, refs[:len(names)]))
    resid, schur, mode_rows, coarse, sems = refs[len(names):]
    two = 2 * face
    places, signs = face_places(face)
    copies = [
        pltpu.make_async_copy(modes_hbm, mode_rows, sems.at[0]),
        pltpu.make_async_copy(resid_hbm, resid, sems.at[1]),
        pltpu.make_async_copy(coarse_hbm, coarse, sems.at[2]),
    ]
    for f in range(6):
        at = pl.ds(f * face, face)
        copies.append(pltpu.make_async_copy(schur_hbm.at[pl.ds(places[f], face), :], schur.at[at, :], sems.at[3 + f]))
    for copy in copies:
        copy.start()

    copies[0].wait()
    modes = jnp.concatenate([
        jnp.concatenate([mode_rows[m, :, pl.ds(at, face)] for at in places], axis=1)
        for m in range(n_modes)], axis=0)
    modes = jnp.concatenate([modes, jnp.zeros((PAD - n_modes, modes.shape[1]), F32)], axis=0)
    width = modes.shape[1]
    o["mt"][...] = mode_pieces(modes)
    o["stack"][2 * width:, :] = jnp.concatenate(split3(modes) + (jnp.zeros(modes.shape, BF16),), axis=0)

    copies[1].wait()
    for f in range(6):
        o["r0"][f * face:(f + 1) * face, :] = signs[f] * resid[:, pl.ds(places[f], face)].T
    r0 = o["r0"][...]
    cols = r0.shape[1]

    copies[2].wait()
    rows = jnp.concatenate([coarse[m] for m in range(n_modes)], axis=0)
    rows = jnp.concatenate([rows, jnp.zeros((PAD - n_modes, rows.shape[1]), F32)], axis=0)
    wide = o["c_own"].shape[1]
    source = lax.broadcasted_iota(jnp.int32, (nz * n_modes, wide), 0)
    place = lax.broadcasted_iota(jnp.int32, (nz * n_modes, wide), 1)
    block, mode = place // PAD, place % PAD

    if turn:
        me = lax.axis_index("gz")
        side = 1 - 2 * lax.rem(me, 2)
        copy, block = block // nz, block % nz
        holder = me + jnp.where(copy == 1, side, jnp.where(copy == 2, -side, 2 * (copy // 3)))
        side = jnp.where((copy == 1) | (copy == 2), -side, side)
        offset = jnp.where(block == 1, side, jnp.where(block == 2, -side, 2 * (block // 3)))
        device = (holder + offset + 2 * nz) % nz
    else:
        device = block
    pick = jnp.where((source == device * n_modes + mode) & (mode < n_modes), 1.0, 0.0)
    ordered = dot32(rows, pick)
    o["c_own"][...] = ordered
    if turn:
        send_rows(face, ordered, 2 * PAD, o)
    o["za"][face:face + PAD, :] = modes[:, 4 * face:5 * face]
    o["zb"][face + 3 * PAD:face + 4 * PAD, :] = modes[:, 5 * face:6 * face]

    for part in range(3):
        at = slice(part * two, (part + 1) * two)
        copies[3 + 2 * part].wait()
        copies[4 + 2 * part].wait()
        high, low = split(jnp.concatenate([schur[at, pl.ds(start, face)] for start in places], axis=1))
        o["stack"][at, :] = high
        o["stack"][width + part * two:width + (part + 1) * two, :] = low
    curv = product(face, r0, o["stack"], o)
    send_rows(face, stack_rows([half_dot(r0, r0), curv], cols), PAD, o)


def column_rows(face, i, at):
    return [i["t"][at:at + PAD, :], i["gta"][at:at + PAD, :],
            i["gzb"][face + at:face + at + PAD, :], i["gt2"][at:at + PAD, :]]


def z_kernel(face, i, o):
    for k, name in enumerate(("a", "b")):
        if "mt_" + name in o:
            got_modes = mode_pieces(i["gz" + name][-PAD:, :])
            o["mt_" + name][...] = got_modes
        else:
            got_modes = i["mt_" + name][...]
        amp = i["amp"]
        own = i["z" + name][0:face, :] + dot16(i["mt"][(4 + k) * face:(5 + k) * face, :], amp_pieces(amp[0:PAD, :]))
        at = (1 + k) * PAD
        got = i["gz" + name][0:face, :] + dot16(got_modes, amp_pieces(amp[at:at + PAD, :]))
        o["z"][k * face:(k + 1) * face, :] = own - got


def value_kernel(face, stage, i, o):
    gathered = "g_all" in i
    loads = i["g_all"][...] if gathered else jnp.concatenate(column_rows(face, i, 0), axis=0)
    if stage == 0 and not gathered:
        n = loads.shape[0]
        coarse = jnp.concatenate([part[:, k * n:(k + 1) * n] for k, part in enumerate(
            [i["c_own"][...]] + column_rows(face, i, 2 * PAD)[1:])], axis=0)
        o["c_all"][...] = coarse
    else:
        coarse = i["c_all"][...]
    amp = dot32(coarse, loads)
    o["amp"][...] = amp[0:3 * PAD]
    xy = i["y"][...] + dot16(i["mt"][0:4 * face, :], amp_pieces(amp[0:PAD]))
    cols = loads.shape[1]

    if stage != 2:
        if gathered:
            dots = i["d_all"][...]
            quad = col_sum(loads * amp[3 * PAD:])
        else:
            parts = column_rows(face, i, PAD)
            dots = (parts[0] + parts[1]) + (parts[2] + parts[3])
            quad = col_sum(loads * amp)
        at = {0: 1, 1: 1, 3: 5}[stage]
        dots = jnp.concatenate([dots[0:at], row(dots, at) + quad, dots[at + 1:]], axis=0)
    if stage == 1:
        dots = jnp.concatenate([i["first"][0:2, :], dots[0:2], dots[4:]], axis=0)
    elif stage == 2 and "swapped" in i:
        dots = six_columns(i, o)
    o["xab"][0:2 * face, :] = xy[0:2 * face]
    o["ya"][0:face, :] = xy[2 * face:3 * face]
    o["yb"][0:face, :] = xy[3 * face:]
    if stage == 3:
        o["dots"][...] = dots
    if stage != 2 or "swapped" in i:
        o["xab"][2 * face:, :] = dots
    if stage != 2:
        o["ya"][face:face + PAD, :] = dots
        o["yb"][face:face + PAD, :] = dots


def assemble(face, i, rates=None):
    f = face
    got = [i["gxab"][0:2 * f, :], i["gya"][0:f, :], i["gyb"][0:f, :]]
    if rates is not None:
        got = [rate * face_values for rate, face_values in zip(rates, got)]
    return jnp.concatenate([
        i["xab"][0:2 * f, :] - got[0], i["ya"][0:f, :] - got[1], i["yb"][0:f, :] - got[2], i["z"][...],
    ], axis=0)


def column_scale(dots):
    norm, curv = row(dots, 0), row(dots, 1)
    usable = (norm > 0.0) & (curv > 0.0)
    return jnp.where(usable, norm / jnp.where(usable, curv, 1.0), 1.0)


def rescale(dots, rate):
    square = rate * rate
    return stack_rows([row(dots, 0), row(dots, 1), square * row(dots, 2), square * row(dots, 3)], dots.shape[1])


def second_kernel(face, i, o):
    w0 = assemble(face, i)
    o["w0"][...] = w0
    first = i["xab"][2 * face:2 * face + PAD, :]
    scale = column_scale(first)
    cols = w0.shape[1]
    rates = [scale / column_scale(i[name][at:at + PAD, :])
             for name, at in (("gxab", 2 * face), ("gya", face), ("gyb", face))]
    o["first"][...] = stack_rows([row(first, 0), row(first, 1), scale] + rates, cols)
    vec = scale * w0
    curv = product(face, vec, i["stack"], o)
    send_rows(face, stack_rows([half_dot(vec, vec), curv], cols), PAD, o)


def third_kernel(face, i, o):
    scale, *rates = (row(i["first"], k) for k in range(2, 6))
    q = assemble(face, i, rates)
    o["q"][...] = q
    if "near" in o:
        partners = [rescale(i[name][at:at + PAD, :], rate) for rate, name, at in zip(
            rates, ("gxab", "gya", "gyb"), (2 * face, face, face))]
        o["near"][...] = jnp.concatenate([partners[0], partners[2], partners[1] + i["xab"][2 * face:, :]], axis=0)
    product(face, scale * q, i["stack"], o)


def six_columns(i, o):
    near = i["near"]
    rate = row(i["first"], 4)
    both = rescale(i["swapped"][0:PAD, :], rate), rescale(i["swapped"][PAD:2 * PAD, :], rate)
    o["six"][...] = ((near[0:PAD, :] + near[PAD:2 * PAD, :]) + near[2 * PAD:, :]) + (both[0] + both[1])
    return near[PAD:2 * PAD, :] + both[1]


def fourth_kernel(face, i, o):
    scale, *rates = (row(i["first"], k) for k in range(2, 6))
    sums = i["six"][...]
    if "whole" not in i:
        sums = sums + rescale(i["gxab"][2 * face:, :], rates[0])
    m0, m1 = row(sums, 0), row(sums, 1)
    alpha0 = m0 / m1
    ratio0 = alpha0 / scale
    square = ratio0 * ratio0
    m2, m3 = square * row(sums, 2), square * row(sums, 3)
    norm1 = m2 - m0
    curv1 = m1 - 2.0 * (m2 / alpha0) + m3
    beta1 = norm1 / m0
    alpha1 = norm1 / (curv1 - beta1 * norm1 / alpha0)
    r0, w0 = i["r0"][...], i["w0"][...]
    q = ratio0 * i["q"][...]
    b = q - square * assemble(face, i, [rate * rate for rate in rates])
    w1 = w0 - q
    s1 = alpha1 * (w1 + beta1 * w0)
    r2 = (r0 - alpha0 * w0) - s1
    z1 = (alpha1 / alpha0) * (b + beta1 * q)
    w2 = w1 - z1
    vec = alpha1 * w2
    cols = w2.shape[1]
    o["w2"][...] = vec
    o["s1"][...] = s1
    o["z1"][...] = z1
    o["known"][...] = stack_rows([norm1, alpha1, alpha0, beta1], cols)
    curv = product(face, vec, i["stack"], o)
    send_rows(face, stack_rows([
        half_dot(r2, r2), half_dot(r2, w2), half_dot(vec, vec), half_dot(vec, s1),
        half_dot(s1, s1), curv, half_dot(z1, vec), half_dot(s1, z1)], cols), PAD, o)


def four_kernel(face, i, o):
    near = i["dots"][...] + i["gxab"][2 * face:2 * face + PAD, :]
    o["part"][...] = near + (i["across"][...] + i["gyb"][face:face + PAD, :])


def ready_kernel(face, i, o):
    alpha1, alpha0, beta1 = (row(i["known"], k) for k in range(1, 4))
    r0 = i["r0"][...]
    r1 = r0 - alpha0 * i["w0"][...]
    p1 = r1 + beta1 * r0
    o["c3"][...] = assemble(face, i)
    o["r2"][...] = r1 - i["s1"][...]
    o["p1"][...] = p1
    o["m2"][...] = alpha0 * r0 + alpha1 * p1


def last_kernel(face, names, *refs):
    i = dict(zip(names, refs))
    mult_hbm, resid_hbm, mult_out, resid_out, sems = refs[len(names):]
    d = i["sum_near"][...] + i["sum_far"][...]
    rr, rw, ww, ws, ss, wc, sc, sz = (row(d, k) for k in range(8))
    norm1, alpha1 = row(i["known"], 0), row(i["known"], 1)
    beta2 = rr / norm1
    alpha2 = rr / (rw - beta2 * rr / alpha1)
    ratio = alpha2 / alpha1
    ratio2 = ratio * ratio
    norm3 = ratio2 * (ww + 2.0 * beta2 * ws + beta2 * beta2 * ss) - rr
    curv3 = rw - 2.0 * (ratio2 / alpha2) * (ww + beta2 * ws)
    curv3 = curv3 + ratio2 * (wc + 2.0 * beta2 * sc + beta2 * beta2 * sz)
    beta3 = norm3 / rr
    alpha3 = norm3 / (curv3 - beta3 * norm3 / alpha2)
    places, signs = face_places(face)
    copies = []
    for f in range(6):
        at = slice(f * face, (f + 1) * face)
        w2, s1 = i["w2"][at, :], i["s1"][at, :]
        p2 = i["r2"][at, :] + beta2 * i["p1"][at, :]
        s2 = w2 + beta2 * s1
        r3 = i["r2"][at, :] - ratio * s2
        w3 = w2 / alpha1 - ratio * (i["c3"][at, :] + beta2 * i["z1"][at, :])
        mult = i["m2"][at, :] + alpha2 * p2 + alpha3 * (r3 + beta3 * p2)
        resid = r3 - alpha3 * (w3 + (beta3 / alpha1) * s2)
        for k, (value, out, hbm) in enumerate(((mult, mult_out, mult_hbm), (resid, resid_out, resid_hbm))):
            out[f] = (signs[f] * value).T
            copy = pltpu.make_async_copy(out.at[f], hbm.at[:, pl.ds(places[f], face)], sems.at[2 * f + k])
            copy.start()
            copies.append(copy)
    for copy in copies:
        copy.wait()


def body(sizes, residual_in, schur, modes, coarse_inv):
    nx, ny, nz = sizes
    resid = residual_in[0, 0, 0]
    matrix = schur[0, 0, 0]
    loads, width = resid.shape
    face = width // 6
    n_modes = modes.shape[3]
    mode_rows = modes.reshape(n_modes, 1, width)
    coarse_rows = coarse_inv.reshape(n_modes, 1, nz * n_modes)
    small = (nx, ny, nz) == (2, 4, 4)

    def shift(x, axis, by):
        n = lax.axis_size(axis)
        return lax.ppermute(x, axis, [(k, (k + by) % n) for k in range(n)])

    def swap(x, axis, first):
        n = lax.axis_size(axis)
        side = lambda k: 1 if (k - first) % 2 == 0 else -1
        return lax.ppermute(x, axis, [(k, (k + side(k)) % n) for k in range(n)])

    def move(x, target):
        places = [(a, b) for a in range(nx) for b in range(ny)]
        pairs = [(a * ny + b, target(a, b)[0] * ny + target(a, b)[1]) for a, b in places]
        return lax.ppermute(x, ("gx", "gy"), pairs)

    def total(dots, scale):
        rate = lax.pmin(scale, ("gx", "gy")) / scale
        rates = jnp.concatenate([jnp.ones((2, loads), F32), rate * rate, rate * rate], axis=0)
        sums = lax.psum(dots[0:4] * rates, ("gx", "gy")) / rates
        return jnp.concatenate([sums, jnp.zeros((PAD - 4, loads), F32)], axis=0)

    vec = sds((width, loads))
    rows = sds((PAD, loads))
    stack_shape = sds((2 * width + 4 * PAD, width), BF16)
    flops = 2 * width * width * 2 * loads * 2

    def z_out(tiny, extra=0):
        return dict(y=sds((4 * face, loads)), za=sds((face + extra, loads)),
                    zb=sds((face + tiny * PAD + extra, loads)), t=sds((tiny * PAD, loads)),
                    t2=sds((tiny * PAD + PAD, loads)))

    def t_exchange(a, with_dots):
        got = dict(t=a["t"], y=a["y"])
        if small:
            got.update(gzb=swap(a["zb"], "gz", 1), gt2=shift(a["t2"], "gz", 2), gta=swap(a["t"], "gz", 0))
        else:
            got["g_all"] = lax.all_gather(a["t"][0:PAD], "gz", axis=0, tiled=True)
            if with_dots:
                got["d_all"] = lax.psum(a["t"][PAD:2 * PAD], "gz")
        return got

    def z_faces(a, v, t, modes=None):
        ins = dict(za=a["za"], zb=a["zb"], gzb=t["gzb"] if small else swap(a["zb"], "gz", 1),
                   gza=swap(a["za"], "gz", 0), mt=mt, amp=v["amp"])
        outs = dict(z=sds((2 * face, loads)))
        if modes is None:
            outs.update(mt_a=sds((face, 6 * PAD), BF16), mt_b=sds((face, 6 * PAD), BF16))
        else:
            ins.update(modes)
        return call(functools.partial(z_kernel, face), ins, outs, flops=Z_FLOPS)

    def value(stage, ins):
        extra = 0 if stage == 2 else PAD
        outs = dict(amp=sds((3 * PAD, loads)), xab=sds((2 * face + (PAD if small else extra), loads)),
                    ya=sds((face + extra, loads)), yb=sds((face + 2 * PAD, loads)))
        if stage == 0 and small:
            outs["c_all"] = sds((nz * PAD, nz * PAD))
        if stage == 2 and small:
            outs["six"] = rows
        if stage == 3:
            outs["dots"] = rows
        return call(functools.partial(value_kernel, face, stage), ins, outs, flops=2 * width * loads * 48)

    def x_exchange(v):
        got = dict(xab=v["xab"])
        if nx == 2:
            got["gxab"] = swap(v["xab"], "gx", 0)
        else:
            a, b, rest = v["xab"][:face], v["xab"][face:2 * face], v["xab"][2 * face:]
            got["gxab"] = jnp.concatenate([swap(a, "gx", 0), swap(b, "gx", 1), rest], axis=0)
        return got

    def y_exchange(v):
        gyb = swap(v["yb"], "gy", 1)
        return dict(ya=v["ya"], yb=v["yb"], gya=swap(v["ya"], "gy", 0), gyb=gyb)

    def xy_exchange(v):
        return dict(x_exchange(v), **y_exchange(v))

    hbm = pl.BlockSpec(memory_space=pltpu.HBM)
    vmem = pl.BlockSpec(memory_space=pltpu.VMEM)
    outs = dict(r0=vec, stack=stack_shape, mt=sds((width, 6 * PAD), BF16),
                c_own=sds((PAD, (4 if small else 1) * nz * PAD)), **z_out(3, PAD))
    res = pl.pallas_call(
        functools.partial(first_kernel, face, nz, n_modes, small),
        out_shape=list(outs.values()),
        in_specs=[hbm] * 4,
        out_specs=[vmem] * len(outs),
        scratch_shapes=[
            pltpu.VMEM(resid.shape, F32), pltpu.VMEM(matrix.shape, F32),
            pltpu.VMEM(mode_rows.shape, F32), pltpu.VMEM(coarse_rows.shape, F32),
            pltpu.SemaphoreType.DMA((9,)),
        ],
        compiler_params=pltpu.CompilerParams(vmem_limit_bytes=VMEM_LIMIT),
        cost_estimate=pl.CostEstimate(flops=flops, bytes_accessed=4 * matrix.size, transcendentals=0),
    )(*[pltpu.with_memory_space_constraint(x, pltpu.HBM) for x in (resid, matrix, mode_rows, coarse_rows)])
    a = dict(zip(outs, res))
    r0, mt, stack = a["r0"], a["mt"], a["stack"]
    ins = dict(t_exchange(a, True), mt=mt)
    if small:
        ins["c_own"] = a["c_own"]
    else:
        c_own = a["c_own"]
        ins["c_all"] = jnp.concatenate([
            c_own, swap(c_own, "gz", 0), swap(c_own, "gz", 1),
            lax.all_gather(c_own, "gz", axis=0, tiled=True)], axis=0)
    t = ins
    v = value(0, ins)
    column = dict(mt=mt, c_all=v["c_all"] if small else ins["c_all"])
    z = z_faces(a, v, t)
    got_modes = dict(mt_a=z["mt_a"], mt_b=z["mt_b"])
    x = dict(xy_exchange(v), z=z["z"])

    a = call(functools.partial(second_kernel, face), dict(x, stack=stack),
             dict(w0=vec, first=rows, **z_out(2)), flops=flops)
    w0, first = a["w0"], a["first"]
    t = t_exchange(a, True)
    v = value(1, dict(t, **column, first=first))
    x = dict(xy_exchange(v), z=z_faces(a, v, t, got_modes)["z"])

    near = dict(near=sds((3 * PAD, loads))) if small else {}
    a = call(functools.partial(third_kernel, face), dict(x, stack=stack, first=first),
             dict(q=vec, **near, **z_out(1)), flops=flops)
    q = a["q"]
    t = t_exchange(a, False)
    ins = dict(t, **column)
    if small:
        ins.update(first=first, near=a["near"], swapped=swap(a["near"][0:2 * PAD], "gy", 0))
        v = value(2, ins)
        sums = dict(six=v["six"])
    else:
        sums = dict(six=total(v["xab"][2 * face:], first[2:3]), whole=first)
        v = value(2, ins)
    x = dict(xy_exchange(v), z=z_faces(a, v, t, got_modes)["z"])

    a = call(functools.partial(fourth_kernel, face),
             dict(x, stack=stack, **sums, first=first, r0=r0, w0=w0, q=q),
             dict(w2=vec, s1=vec, z1=vec, known=rows, **z_out(2)), flops=flops)
    t = t_exchange(a, True)
    v = value(3, dict(t, **column))
    z = z_faces(a, v, t, got_modes)["z"]
    if small:
        x = x_exchange(v)
        across = move(v["dots"], lambda a, b: (1 - a, (b + (-1 if b % 2 == 0 else 1)) % ny))
        x.update(y_exchange(v))
        part = call(functools.partial(four_kernel, face),
                    dict(dots=v["dots"], across=across, gxab=x["gxab"], gyb=x["gyb"], z=z), dict(part=rows))["part"]
        sums = dict(sum_near=part, sum_far=swap(part, "gy", 0))
    else:
        x = xy_exchange(v)
        sums = dict(sum_near=lax.psum(v["dots"], ("gx", "gy")), sum_far=jnp.zeros((PAD, loads), F32))
    ready = call(functools.partial(ready_kernel, face),
                 dict(x, z=z, known=a["known"], s1=a["s1"], r0=r0, w0=w0),
                 {name: vec for name in ("c3", "r2", "p1", "m2")}, flops=10 * width * loads)
    ins = dict(sums, **ready, **{name: a[name] for name in ("known", "w2", "s1", "z1")})
    out = sds((loads, width))
    mult, final = pl.pallas_call(
        functools.partial(last_kernel, face, list(ins)),
        out_shape=[out, out],
        in_specs=[vmem] * len(ins),
        out_specs=[hbm, hbm],
        scratch_shapes=[pltpu.VMEM((6, loads, face), F32), pltpu.VMEM((6, loads, face), F32),
                        pltpu.SemaphoreType.DMA((12,))],
        compiler_params=pltpu.CompilerParams(vmem_limit_bytes=VMEM_LIMIT),
        cost_estimate=pl.CostEstimate(flops=20 * width * loads, bytes_accessed=9 * 4 * width * loads, transcendentals=0),
    )(*ins.values())
    return (mult[None, None, None], final[None, None, None])


def solution(mesh):
    spec = P("gx", "gy", "gz", None, None)
    sizes = tuple(mesh.shape[axis] for axis in ("gx", "gy", "gz"))
    return jax.shard_map(
        functools.partial(body, sizes),
        mesh=mesh,
        in_specs=(spec, spec, spec, P("gx", "gy", "gz", None)),
        out_specs=(spec, spec),
        check_vma=False,
    )
```

```python
import functools

import jax
import jax.numpy as jnp
from jax import lax
from jax.experimental import pallas as pl
from jax.experimental.pallas import tpu as pltpu
from jax.sharding import PartitionSpec as P

F32 = jnp.float32
BF16 = jnp.bfloat16
HI = lax.Precision.HIGHEST
PAD = 8
VMEM_LIMIT = 24 * 1024 * 1024
Z_FLOPS = 770000000


def sds(shape, dtype=F32):
    return jax.ShapeDtypeStruct(shape, dtype)


def call(kernel, ins, outs, flops=0):
    names_in, names_out = list(ins), list(outs)
    nbytes = sum(a.size * a.dtype.itemsize for a in list(ins.values()) + list(outs.values()))

    def run(*refs):
        n = len(names_in)
        kernel(dict(zip(names_in, refs[:n])), dict(zip(names_out, refs[n:])))

    vmem = pl.BlockSpec(memory_space=pltpu.VMEM)
    res = pl.pallas_call(
        run,
        out_shape=[outs[n] for n in names_out],
        in_specs=[vmem] * len(names_in),
        out_specs=[vmem] * len(names_out),
        compiler_params=pltpu.CompilerParams(vmem_limit_bytes=VMEM_LIMIT),
        cost_estimate=pl.CostEstimate(flops=flops, bytes_accessed=nbytes, transcendentals=0),
    )(*[ins[n] for n in names_in])
    return dict(zip(names_out, res))


def split(x):
    high = x.astype(BF16)
    return high, (x - high.astype(F32)).astype(BF16)


def split3(x):
    high = x.astype(BF16)
    rest = x - high.astype(F32)
    mid = rest.astype(BF16)
    return high, mid, (rest - mid.astype(F32)).astype(BF16)


def mode_pieces(modes):
    high, mid, low = split3(modes.T)
    return jnp.concatenate([high, high, mid, mid, high, low], axis=1)


def amp_pieces(amp):
    high, mid, low = split3(amp)
    return jnp.concatenate([high, mid, high, mid, low, high], axis=0)


def dot32(a, b):
    return jnp.dot(a, b, precision=HI, preferred_element_type=F32)


def dot16(a, b):
    return jnp.dot(a, b, preferred_element_type=F32)


def col_sum(x):
    return jnp.sum(x, axis=0, keepdims=True)


def half_dot(a, b):
    return 0.5 * col_sum(a * b)


def row(x, i):
    return x[i:i + 1, :]


def face_places(face):
    places, signs = [], []
    for k, axis in enumerate(("gx", "gy", "gz")):
        odd = lax.rem(lax.axis_index(axis), 2)
        for high in (1 - odd, odd):
            places.append(pl.multiple_of((2 * k + high) * face, face))
            signs.append((1 - 2 * high).astype(F32))
    return places, signs


def store_product(face, part, y, o):
    if part < 2:
        o["y"][2 * part * face:2 * (part + 1) * face, :] = y
    else:
        o["za"][0:face, :] = y[0:face]
        o["zb"][0:face, :] = y[face:]


def send_rows(face, rows, at, o):
    n = rows.shape[0]
    o["t"][at:at + n, :] = rows
    o["t2"][at:at + n, :] = rows
    o["zb"][face + at:face + at + n, :] = rows


def part_rows(face, part):
    return slice(4 * part * face, 4 * (part + 1) * face if part < 3 else None)


def send_loads(face, stack, halves, o):
    cols = halves.shape[1] // 2
    both = dot16(stack[part_rows(face, 3), :], halves)
    loads = both[:, :cols] + both[:, cols:]
    send_rows(face, (loads[0:PAD] + loads[PAD:2 * PAD]) + loads[2 * PAD:3 * PAD], 0, o)


def product_part(face, part, vec, stack, halves, o):
    cols = vec.shape[1]
    both = dot16(stack[part_rows(face, part), :], halves)
    both = both[:, :cols] + both[:, cols:]
    y = both[0:2 * face] + both[2 * face:]
    store_product(face, part, y, o)
    return col_sum(vec[2 * part * face:2 * (part + 1) * face] * y)


def product(face, vec, stack, o):
    halves = jnp.concatenate(split(vec), axis=1)
    parts = [product_part(face, part, vec, stack, halves, o) for part in range(3)]
    send_loads(face, stack, halves, o)
    return (parts[0] + parts[1]) + parts[2]


def stack_rows(rows, cols):
    zero = jnp.zeros((1, cols), F32)
    return jnp.concatenate(list(rows) + [zero] * (PAD - len(rows)), axis=0)


def first_kernel(face, nz, n_modes, turn, resid_hbm, schur_hbm, modes_hbm, coarse_hbm, *refs):
    names = ["r0", "stack", "mt", "c_own", "y", "za", "zb", "t", "t2"]
    o = dict(zip(names, refs[:len(names)]))
    resid, schur, mode_rows, coarse, sems = refs[len(names):]
    two = 2 * face
    places, signs = face_places(face)
    copies = [
        pltpu.make_async_copy(modes_hbm, mode_rows, sems.at[0]),
        pltpu.make_async_copy(resid_hbm, resid, sems.at[1]),
        pltpu.make_async_copy(coarse_hbm, coarse, sems.at[2]),
    ]
    for f in range(6):
        at = pl.ds(f * face, face)
        copies.append(pltpu.make_async_copy(schur_hbm.at[pl.ds(places[f], face), :], schur.at[at, :], sems.at[3 + f]))
    for copy in copies:
        copy.start()

    copies[0].wait()
    modes = jnp.concatenate([
        jnp.concatenate([mode_rows[m, :, pl.ds(at, face)] for at in places], axis=1)
        for m in range(n_modes)], axis=0)
    modes = jnp.concatenate([modes, jnp.zeros((PAD - n_modes, modes.shape[1]), F32)], axis=0)
    width = modes.shape[1]
    o["mt"][...] = mode_pieces(modes)
    o["stack"][2 * width:, :] = jnp.concatenate(split3(modes) + (jnp.zeros(modes.shape, BF16),), axis=0)

    copies[1].wait()
    for f in range(6):
        o["r0"][f * face:(f + 1) * face, :] = signs[f] * resid[:, pl.ds(places[f], face)].T
    r0 = o["r0"][...]
    cols = r0.shape[1]

    copies[2].wait()
    rows = jnp.concatenate([coarse[m] for m in range(n_modes)], axis=0)
    rows = jnp.concatenate([rows, jnp.zeros((PAD - n_modes, rows.shape[1]), F32)], axis=0)
    wide = o["c_own"].shape[1]
    source = lax.broadcasted_iota(jnp.int32, (nz * n_modes, wide), 0)
    place = lax.broadcasted_iota(jnp.int32, (nz * n_modes, wide), 1)
    block, mode = place // PAD, place % PAD

    if turn:
        me = lax.axis_index("gz")
        side = 1 - 2 * lax.rem(me, 2)
        copy, block = block // nz, block % nz
        holder = me + jnp.where(copy == 1, side, jnp.where(copy == 2, -side, 2 * (copy // 3)))
        side = jnp.where((copy == 1) | (copy == 2), -side, side)
        offset = jnp.where(block == 1, side, jnp.where(block == 2, -side, 2 * (block // 3)))
        device = (holder + offset + 2 * nz) % nz
    else:
        device = block
    pick = jnp.where((source == device * n_modes + mode) & (mode < n_modes), 1.0, 0.0)
    ordered = dot32(rows, pick)
    o["c_own"][...] = ordered
    if turn:
        send_rows(face, ordered, 2 * PAD, o)
    o["za"][face:face + PAD, :] = modes[:, 4 * face:5 * face]
    o["zb"][face + 3 * PAD:face + 4 * PAD, :] = modes[:, 5 * face:6 * face]

    halves = jnp.concatenate(split(r0), axis=1)
    send_loads(face, o["stack"], halves, o)
    curv = jnp.zeros((1, cols), F32)
    for part in range(3):
        at = slice(part * two, (part + 1) * two)
        copies[3 + 2 * part].wait()
        copies[4 + 2 * part].wait()
        high, low = split(jnp.concatenate([schur[at, pl.ds(start, face)] for start in places], axis=1))
        o["stack"][2 * part * two:(2 * part + 1) * two, :] = high
        o["stack"][(2 * part + 1) * two:2 * (part + 1) * two, :] = low
        curv = curv + product_part(face, part, r0, o["stack"], halves, o)
    send_rows(face, stack_rows([half_dot(r0, r0), curv], cols), PAD, o)


def column_rows(face, i, at):
    return [i["t"][at:at + PAD, :], i["gta"][at:at + PAD, :],
            i["gzb"][face + at:face + at + PAD, :], i["gt2"][at:at + PAD, :]]


def z_kernel(face, i, o):
    for k, name in enumerate(("a", "b")):
        if "mt_" + name in o:
            got_modes = mode_pieces(i["gz" + name][-PAD:, :])
            o["mt_" + name][...] = got_modes
        else:
            got_modes = i["mt_" + name][...]
        amp = i["amp"]
        own = i["z" + name][0:face, :] + dot16(i["mt"][(4 + k) * face:(5 + k) * face, :], amp_pieces(amp[0:PAD, :]))
        at = (1 + k) * PAD
        got = i["gz" + name][0:face, :] + dot16(got_modes, amp_pieces(amp[at:at + PAD, :]))
        o["z"][k * face:(k + 1) * face, :] = own - got


def value_kernel(face, stage, i, o):
    gathered = "g_all" in i
    loads = i["g_all"][...] if gathered else jnp.concatenate(column_rows(face, i, 0), axis=0)
    if stage == 0 and not gathered:
        n = loads.shape[0]
        coarse = jnp.concatenate([part[:, k * n:(k + 1) * n] for k, part in enumerate(
            [i["c_own"][...]] + column_rows(face, i, 2 * PAD)[1:])], axis=0)
        o["c_all"][...] = coarse
    else:
        coarse = i["c_all"][...]
    amp = dot32(coarse, loads)
    o["amp"][...] = amp[0:3 * PAD]
    xy = i["y"][...] + dot16(i["mt"][0:4 * face, :], amp_pieces(amp[0:PAD]))
    cols = loads.shape[1]

    if stage != 2:
        if gathered:
            dots = i["d_all"][...]
            quad = col_sum(loads * amp[3 * PAD:])
        else:
            parts = column_rows(face, i, PAD)
            dots = (parts[0] + parts[1]) + (parts[2] + parts[3])
            quad = col_sum(loads * amp)
        at = {0: 1, 1: 1, 3: 5}[stage]
        dots = jnp.concatenate([dots[0:at], row(dots, at) + quad, dots[at + 1:]], axis=0)
    if stage == 1:
        dots = jnp.concatenate([i["first"][0:2, :], dots[0:2], dots[4:]], axis=0)
    elif stage == 2 and "swapped" in i:
        dots = six_columns(i, o)
    o["xab"][0:2 * face, :] = xy[0:2 * face]
    o["ya"][0:face, :] = xy[2 * face:3 * face]
    o["yb"][0:face, :] = xy[3 * face:]
    if stage == 3:
        o["dots"][...] = dots
    if stage != 2 or "swapped" in i:
        o["xab"][2 * face:, :] = dots
    if stage != 2:
        o["ya"][face:face + PAD, :] = dots
        o["yb"][face:face + PAD, :] = dots


def assemble(face, i, rates=None):
    f = face
    got = [i["gxab"][0:2 * f, :], i["gya"][0:f, :], i["gyb"][0:f, :]]
    if rates is not None:
        got = [rate * face_values for rate, face_values in zip(rates, got)]
    return jnp.concatenate([
        i["xab"][0:2 * f, :] - got[0], i["ya"][0:f, :] - got[1], i["yb"][0:f, :] - got[2], i["z"][...],
    ], axis=0)


def column_scale(dots):
    norm, curv = row(dots, 0), row(dots, 1)
    usable = (norm > 0.0) & (curv > 0.0)
    return jnp.where(usable, norm / jnp.where(usable, curv, 1.0), 1.0)


def rescale(dots, rate):
    square = rate * rate
    return stack_rows([row(dots, 0), row(dots, 1), square * row(dots, 2), square * row(dots, 3)], dots.shape[1])


def second_kernel(face, i, o):
    w0 = assemble(face, i)
    o["w0"][...] = w0
    first = i["xab"][2 * face:2 * face + PAD, :]
    scale = column_scale(first)
    cols = w0.shape[1]
    rates = [scale / column_scale(i[name][at:at + PAD, :])
             for name, at in (("gxab", 2 * face), ("gya", face), ("gyb", face))]
    o["first"][...] = stack_rows([row(first, 0), row(first, 1), scale] + rates, cols)
    vec = scale * w0
    curv = product(face, vec, i["stack"], o)
    send_rows(face, stack_rows([half_dot(vec, vec), curv], cols), PAD, o)


def third_kernel(face, i, o):
    scale, *rates = (row(i["first"], k) for k in range(2, 6))
    q = assemble(face, i, rates)
    o["q"][...] = q
    if "near" in o:
        partners = [rescale(i[name][at:at + PAD, :], rate) for rate, name, at in zip(
            rates, ("gxab", "gya", "gyb"), (2 * face, face, face))]
        o["near"][...] = jnp.concatenate([partners[0], partners[2], partners[1] + i["xab"][2 * face:, :]], axis=0)
    product(face, scale * q, i["stack"], o)


def six_columns(i, o):
    near = i["near"]
    rate = row(i["first"], 4)
    both = rescale(i["swapped"][0:PAD, :], rate), rescale(i["swapped"][PAD:2 * PAD, :], rate)
    o["six"][...] = ((near[0:PAD, :] + near[PAD:2 * PAD, :]) + near[2 * PAD:, :]) + (both[0] + both[1])
    return near[PAD:2 * PAD, :] + both[1]


def fourth_kernel(face, i, o):
    scale, *rates = (row(i["first"], k) for k in range(2, 6))
    sums = i["six"][...]
    if "whole" not in i:
        sums = sums + rescale(i["gxab"][2 * face:, :], rates[0])
    m0, m1 = row(sums, 0), row(sums, 1)
    alpha0 = m0 / m1
    ratio0 = alpha0 / scale
    square = ratio0 * ratio0
    m2, m3 = square * row(sums, 2), square * row(sums, 3)
    norm1 = m2 - m0
    curv1 = m1 - 2.0 * (m2 / alpha0) + m3
    beta1 = norm1 / m0
    alpha1 = norm1 / (curv1 - beta1 * norm1 / alpha0)
    r0, w0 = i["r0"][...], i["w0"][...]
    q = ratio0 * i["q"][...]
    b = q - square * assemble(face, i, [rate * rate for rate in rates])
    w1 = w0 - q
    s1 = alpha1 * (w1 + beta1 * w0)
    r2 = (r0 - alpha0 * w0) - s1
    z1 = (alpha1 / alpha0) * (b + beta1 * q)
    w2 = w1 - z1
    vec = alpha1 * w2
    cols = w2.shape[1]
    o["w2"][...] = vec
    o["s1"][...] = s1
    o["z1"][...] = z1
    o["known"][...] = stack_rows([norm1, alpha1, alpha0, beta1], cols)
    curv = product(face, vec, i["stack"], o)
    send_rows(face, stack_rows([
        half_dot(r2, r2), half_dot(r2, w2), half_dot(vec, vec), half_dot(vec, s1),
        half_dot(s1, s1), curv, half_dot(z1, vec), half_dot(s1, z1)], cols), PAD, o)


def four_kernel(face, i, o):
    near = i["dots"][...] + i["gxab"][2 * face:2 * face + PAD, :]
    o["part"][...] = near + (i["across"][...] + i["gyb"][face:face + PAD, :])


def ready_kernel(face, i, o):
    alpha1, alpha0, beta1 = (row(i["known"], k) for k in range(1, 4))
    r0 = i["r0"][...]
    r1 = r0 - alpha0 * i["w0"][...]
    p1 = r1 + beta1 * r0
    o["c3"][...] = assemble(face, i)
    o["r2"][...] = r1 - i["s1"][...]
    o["p1"][...] = p1
    o["m2"][...] = alpha0 * r0 + alpha1 * p1


def last_kernel(face, names, *refs):
    i = dict(zip(names, refs))
    mult_hbm, resid_hbm, mult_out, resid_out, sems = refs[len(names):]
    d = i["sum_near"][...] + i["sum_far"][...]
    rr, rw, ww, ws, ss, wc, sc, sz = (row(d, k) for k in range(8))
    norm1, alpha1 = row(i["known"], 0), row(i["known"], 1)
    beta2 = rr / norm1
    alpha2 = rr / (rw - beta2 * rr / alpha1)
    ratio = alpha2 / alpha1
    ratio2 = ratio * ratio
    norm3 = ratio2 * (ww + 2.0 * beta2 * ws + beta2 * beta2 * ss) - rr
    curv3 = rw - 2.0 * (ratio2 / alpha2) * (ww + beta2 * ws)
    curv3 = curv3 + ratio2 * (wc + 2.0 * beta2 * sc + beta2 * beta2 * sz)
    beta3 = norm3 / rr
    alpha3 = norm3 / (curv3 - beta3 * norm3 / alpha2)
    places, signs = face_places(face)
    copies = []
    for f in range(6):
        at = slice(f * face, (f + 1) * face)
        w2, s1 = i["w2"][at, :], i["s1"][at, :]
        p2 = i["r2"][at, :] + beta2 * i["p1"][at, :]
        s2 = w2 + beta2 * s1
        r3 = i["r2"][at, :] - ratio * s2
        w3 = w2 / alpha1 - ratio * (i["c3"][at, :] + beta2 * i["z1"][at, :])
        mult = i["m2"][at, :] + alpha2 * p2 + alpha3 * (r3 + beta3 * p2)
        resid = r3 - alpha3 * (w3 + (beta3 / alpha1) * s2)
        for k, (value, out, hbm) in enumerate(((mult, mult_out, mult_hbm), (resid, resid_out, resid_hbm))):
            out[f] = (signs[f] * value).T
            copy = pltpu.make_async_copy(out.at[f], hbm.at[:, pl.ds(places[f], face)], sems.at[2 * f + k])
            copy.start()
            copies.append(copy)
    for copy in copies:
        copy.wait()


def body(sizes, residual_in, schur, modes, coarse_inv):
    nx, ny, nz = sizes
    resid = residual_in[0, 0, 0]
    matrix = schur[0, 0, 0]
    loads, width = resid.shape
    face = width // 6
    n_modes = modes.shape[3]
    mode_rows = modes.reshape(n_modes, 1, width)
    coarse_rows = coarse_inv.reshape(n_modes, 1, nz * n_modes)
    small = (nx, ny, nz) == (2, 4, 4)

    def shift(x, axis, by):
        n = lax.axis_size(axis)
        return lax.ppermute(x, axis, [(k, (k + by) % n) for k in range(n)])

    def swap(x, axis, first):
        n = lax.axis_size(axis)
        side = lambda k: 1 if (k - first) % 2 == 0 else -1
        return lax.ppermute(x, axis, [(k, (k + side(k)) % n) for k in range(n)])

    def move(x, target):
        places = [(a, b) for a in range(nx) for b in range(ny)]
        pairs = [(a * ny + b, target(a, b)[0] * ny + target(a, b)[1]) for a, b in places]
        return lax.ppermute(x, ("gx", "gy"), pairs)

    def total(dots, scale):
        rate = lax.pmin(scale, ("gx", "gy")) / scale
        rates = jnp.concatenate([jnp.ones((2, loads), F32), rate * rate, rate * rate], axis=0)
        sums = lax.psum(dots[0:4] * rates, ("gx", "gy")) / rates
        return jnp.concatenate([sums, jnp.zeros((PAD - 4, loads), F32)], axis=0)

    vec = sds((width, loads))
    rows = sds((PAD, loads))
    stack_shape = sds((2 * width + 4 * PAD, width), BF16)
    flops = 2 * width * width * 2 * loads * 2

    def z_out(tiny, extra=0):
        return dict(y=sds((4 * face, loads)), za=sds((face + extra, loads)),
                    zb=sds((face + tiny * PAD + extra, loads)), t=sds((tiny * PAD, loads)),
                    t2=sds((tiny * PAD + PAD, loads)))

    def t_exchange(a, with_dots):
        got = dict(t=a["t"], y=a["y"])
        if small:
            got.update(gzb=swap(a["zb"], "gz", 1), gt2=shift(a["t2"], "gz", 2), gta=swap(a["t"], "gz", 0))
        else:
            got["g_all"] = lax.all_gather(a["t"][0:PAD], "gz", axis=0, tiled=True)
            if with_dots:
                got["d_all"] = lax.psum(a["t"][PAD:2 * PAD], "gz")
        return got

    def z_faces(a, v, t, modes=None):
        ins = dict(za=a["za"], zb=a["zb"], gzb=t["gzb"] if small else swap(a["zb"], "gz", 1),
                   gza=swap(a["za"], "gz", 0), mt=mt, amp=v["amp"])
        outs = dict(z=sds((2 * face, loads)))
        if modes is None:
            outs.update(mt_a=sds((face, 6 * PAD), BF16), mt_b=sds((face, 6 * PAD), BF16))
        else:
            ins.update(modes)
        return call(functools.partial(z_kernel, face), ins, outs, flops=Z_FLOPS)

    def value(stage, ins):
        extra = 0 if stage == 2 else PAD
        outs = dict(amp=sds((3 * PAD, loads)), xab=sds((2 * face + (PAD if small else extra), loads)),
                    ya=sds((face + extra, loads)), yb=sds((face + 2 * PAD, loads)))
        if stage == 0 and small:
            outs["c_all"] = sds((nz * PAD, nz * PAD))
        if stage == 2 and small:
            outs["six"] = rows
        if stage == 3:
            outs["dots"] = rows
        return call(functools.partial(value_kernel, face, stage), ins, outs, flops=2 * width * loads * 48)

    def x_exchange(v):
        got = dict(xab=v["xab"])
        if nx == 2:
            got["gxab"] = swap(v["xab"], "gx", 0)
        else:
            a, b, rest = v["xab"][:face], v["xab"][face:2 * face], v["xab"][2 * face:]
            got["gxab"] = jnp.concatenate([swap(a, "gx", 0), swap(b, "gx", 1), rest], axis=0)
        return got

    def y_exchange(v):
        gyb = swap(v["yb"], "gy", 1)
        return dict(ya=v["ya"], yb=v["yb"], gya=swap(v["ya"], "gy", 0), gyb=gyb)

    def xy_exchange(v):
        return dict(x_exchange(v), **y_exchange(v))

    hbm = pl.BlockSpec(memory_space=pltpu.HBM)
    vmem = pl.BlockSpec(memory_space=pltpu.VMEM)
    outs = dict(r0=vec, stack=stack_shape, mt=sds((width, 6 * PAD), BF16),
                c_own=sds((PAD, (4 if small else 1) * nz * PAD)), **z_out(3, PAD))
    res = pl.pallas_call(
        functools.partial(first_kernel, face, nz, n_modes, small),
        out_shape=list(outs.values()),
        in_specs=[hbm] * 4,
        out_specs=[vmem] * len(outs),
        scratch_shapes=[
            pltpu.VMEM(resid.shape, F32), pltpu.VMEM(matrix.shape, F32),
            pltpu.VMEM(mode_rows.shape, F32), pltpu.VMEM(coarse_rows.shape, F32),
            pltpu.SemaphoreType.DMA((9,)),
        ],
        compiler_params=pltpu.CompilerParams(vmem_limit_bytes=VMEM_LIMIT),
        cost_estimate=pl.CostEstimate(flops=flops, bytes_accessed=4 * matrix.size, transcendentals=0),
    )(*[pltpu.with_memory_space_constraint(x, pltpu.HBM) for x in (resid, matrix, mode_rows, coarse_rows)])
    a = dict(zip(outs, res))
    r0, mt, stack = a["r0"], a["mt"], a["stack"]
    ins = dict(t_exchange(a, True), mt=mt)
    if small:
        ins["c_own"] = a["c_own"]
    else:
        c_own = a["c_own"]
        ins["c_all"] = jnp.concatenate([
            c_own, swap(c_own, "gz", 0), swap(c_own, "gz", 1),
            lax.all_gather(c_own, "gz", axis=0, tiled=True)], axis=0)
    t = ins
    v = value(0, ins)
    column = dict(mt=mt, c_all=v["c_all"] if small else ins["c_all"])
    z = z_faces(a, v, t)
    got_modes = dict(mt_a=z["mt_a"], mt_b=z["mt_b"])
    x = dict(xy_exchange(v), z=z["z"])

    a = call(functools.partial(second_kernel, face), dict(x, stack=stack),
             dict(w0=vec, first=rows, **z_out(2)), flops=flops)
    w0, first = a["w0"], a["first"]
    t = t_exchange(a, True)
    v = value(1, dict(t, **column, first=first))
    x = dict(xy_exchange(v), z=z_faces(a, v, t, got_modes)["z"])

    near = dict(near=sds((3 * PAD, loads))) if small else {}
    a = call(functools.partial(third_kernel, face), dict(x, stack=stack, first=first),
             dict(q=vec, **near, **z_out(1)), flops=flops)
    q = a["q"]
    t = t_exchange(a, False)
    ins = dict(t, **column)
    if small:
        ins.update(first=first, near=a["near"], swapped=swap(a["near"][0:2 * PAD], "gy", 0))
        v = value(2, ins)
        sums = dict(six=v["six"])
    else:
        sums = dict(six=total(v["xab"][2 * face:], first[2:3]), whole=first)
        v = value(2, ins)
    x = dict(xy_exchange(v), z=z_faces(a, v, t, got_modes)["z"])

    a = call(functools.partial(fourth_kernel, face),
             dict(x, stack=stack, **sums, first=first, r0=r0, w0=w0, q=q),
             dict(w2=vec, s1=vec, z1=vec, known=rows, **z_out(2)), flops=flops)
    t = t_exchange(a, True)
    v = value(3, dict(t, **column))
    z = z_faces(a, v, t, got_modes)["z"]
    if small:
        x = x_exchange(v)
        across = move(v["dots"], lambda a, b: (1 - a, (b + (-1 if b % 2 == 0 else 1)) % ny))
        x.update(y_exchange(v))
        part = call(functools.partial(four_kernel, face),
                    dict(dots=v["dots"], across=across, gxab=x["gxab"], gyb=x["gyb"], z=z), dict(part=rows))["part"]
        sums = dict(sum_near=part, sum_far=swap(part, "gy", 0))
    else:
        x = xy_exchange(v)
        sums = dict(sum_near=lax.psum(v["dots"], ("gx", "gy")), sum_far=jnp.zeros((PAD, loads), F32))
    ready = call(functools.partial(ready_kernel, face),
                 dict(x, z=z, known=a["known"], s1=a["s1"], r0=r0, w0=w0),
                 {name: vec for name in ("c3", "r2", "p1", "m2")}, flops=10 * width * loads)
    ins = dict(sums, **ready, **{name: a[name] for name in ("known", "w2", "s1", "z1")})
    out = sds((loads, width))
    mult, final = pl.pallas_call(
        functools.partial(last_kernel, face, list(ins)),
        out_shape=[out, out],
        in_specs=[vmem] * len(ins),
        out_specs=[hbm, hbm],
        scratch_shapes=[pltpu.VMEM((6, loads, face), F32), pltpu.VMEM((6, loads, face), F32),
                        pltpu.SemaphoreType.DMA((12,))],
        compiler_params=pltpu.CompilerParams(vmem_limit_bytes=VMEM_LIMIT),
        cost_estimate=pl.CostEstimate(flops=20 * width * loads, bytes_accessed=9 * 4 * width * loads, transcendentals=0),
    )(*ins.values())
    return (mult[None, None, None], final[None, None, None])


def solution(mesh):
    spec = P("gx", "gy", "gz", None, None)
    sizes = tuple(mesh.shape[axis] for axis in ("gx", "gy", "gz"))
    return jax.shard_map(
        functools.partial(body, sizes),
        mesh=mesh,
        in_specs=(spec, spec, spec, P("gx", "gy", "gz", None)),
        out_specs=(spec, spec),
        check_vma=False,
    )
```

```python
import functools

import jax
import jax.numpy as jnp
from jax import lax
from jax.experimental import pallas as pl
from jax.experimental.pallas import tpu as pltpu
from jax.sharding import PartitionSpec as P

F32 = jnp.float32
BF16 = jnp.bfloat16
HI = lax.Precision.HIGHEST
PAD = 8
VMEM_LIMIT = 24 * 1024 * 1024
Z_FLOPS = 770000000


def sds(shape, dtype=F32):
    return jax.ShapeDtypeStruct(shape, dtype)


def call(kernel, ins, outs, flops=0):
    names_in, names_out = list(ins), list(outs)
    nbytes = sum(a.size * a.dtype.itemsize for a in list(ins.values()) + list(outs.values()))

    def run(*refs):
        n = len(names_in)
        kernel(dict(zip(names_in, refs[:n])), dict(zip(names_out, refs[n:])))

    vmem = pl.BlockSpec(memory_space=pltpu.VMEM)
    res = pl.pallas_call(
        run,
        out_shape=[outs[n] for n in names_out],
        in_specs=[vmem] * len(names_in),
        out_specs=[vmem] * len(names_out),
        compiler_params=pltpu.CompilerParams(vmem_limit_bytes=VMEM_LIMIT),
        cost_estimate=pl.CostEstimate(flops=flops, bytes_accessed=nbytes, transcendentals=0),
    )(*[ins[n] for n in names_in])
    return dict(zip(names_out, res))


def split(x):
    high = x.astype(BF16)
    return high, (x - high.astype(F32)).astype(BF16)


def split3(x):
    high = x.astype(BF16)
    rest = x - high.astype(F32)
    mid = rest.astype(BF16)
    return high, mid, (rest - mid.astype(F32)).astype(BF16)


def mode_pieces(modes):
    high, mid, low = split3(modes.T)
    return jnp.concatenate([high, high, mid, mid, high, low], axis=1)


def amp_pieces(amp):
    high, mid, low = split3(amp)
    return jnp.concatenate([high, mid, high, mid, low, high], axis=0)


def dot32(a, b):
    return jnp.dot(a, b, precision=HI, preferred_element_type=F32)


def dot16(a, b):
    return jnp.dot(a, b, preferred_element_type=F32)


def col_sum(x):
    return jnp.sum(x, axis=0, keepdims=True)


def half_dot(a, b):
    return 0.5 * col_sum(a * b)


def row(x, i):
    return x[i:i + 1, :]


def face_places(face):
    places, signs = [], []
    for k, axis in enumerate(("gx", "gy", "gz")):
        odd = lax.rem(lax.axis_index(axis), 2)
        for high in (1 - odd, odd):
            places.append(pl.multiple_of((2 * k + high) * face, face))
            signs.append((1 - 2 * high).astype(F32))
    return places, signs


def store_product(face, part, y, o):
    if part < 2:
        o["y"][2 * part * face:2 * (part + 1) * face, :] = y
    else:
        o["za"][0:face, :] = y[0:face]
        o["zb"][0:face, :] = y[face:]


def send_rows(face, rows, at, o):
    n = rows.shape[0]
    o["t"][at:at + n, :] = rows
    o["t2"][at:at + n, :] = rows
    o["zb"][face + at:face + at + n, :] = rows


def product(face, vec, stack, o):
    width, cols = vec.shape
    both = dot16(stack[...], jnp.concatenate(split(vec), axis=1))
    total = jnp.zeros((1, cols), F32)
    for part in range(3):
        at = slice(2 * part * face, 2 * (part + 1) * face)
        low = slice(width + 2 * part * face, width + 2 * (part + 1) * face)
        y = (both[at, :cols] + both[at, cols:]) + (both[low, :cols] + both[low, cols:])
        store_product(face, part, y, o)
        total = total + col_sum(vec[at] * y)
    loads = both[2 * width:, :cols] + both[2 * width:, cols:]
    send_rows(face, (loads[0:PAD] + loads[PAD:2 * PAD]) + loads[2 * PAD:3 * PAD], 0, o)
    return total


def stack_rows(rows, cols):
    zero = jnp.zeros((1, cols), F32)
    return jnp.concatenate(list(rows) + [zero] * (PAD - len(rows)), axis=0)


def first_kernel(face, nz, n_modes, turn, resid_hbm, schur_hbm, modes_hbm, coarse_hbm, *refs):
    names = ["r0", "stack", "mt", "c_own", "y", "za", "zb", "t", "t2"]
    o = dict(zip(names, refs[:len(names)]))
    resid, schur, mode_rows, coarse, sems = refs[len(names):]
    two = 2 * face
    places, signs = face_places(face)
    copies = [
        pltpu.make_async_copy(modes_hbm, mode_rows, sems.at[0]),
        pltpu.make_async_copy(resid_hbm, resid, sems.at[1]),
        pltpu.make_async_copy(coarse_hbm, coarse, sems.at[2]),
    ]
    for f in range(6):
        at = pl.ds(f * face, face)
        copies.append(pltpu.make_async_copy(schur_hbm.at[pl.ds(places[f], face), :], schur.at[at, :], sems.at[3 + f]))
    for copy in copies:
        copy.start()

    copies[0].wait()
    modes = jnp.concatenate([
        jnp.concatenate([mode_rows[m, :, pl.ds(at, face)] for at in places], axis=1)
        for m in range(n_modes)], axis=0)
    modes = jnp.concatenate([modes, jnp.zeros((PAD - n_modes, modes.shape[1]), F32)], axis=0)
    width = modes.shape[1]
    o["mt"][...] = mode_pieces(modes)
    o["stack"][2 * width:, :] = jnp.concatenate(split3(modes) + (jnp.zeros(modes.shape, BF16),), axis=0)

    copies[1].wait()
    for f in range(6):
        o["r0"][f * face:(f + 1) * face, :] = signs[f] * resid[:, pl.ds(places[f], face)].T
    r0 = o["r0"][...]
    cols = r0.shape[1]

    copies[2].wait()
    rows = jnp.concatenate([coarse[m] for m in range(n_modes)], axis=0)
    rows = jnp.concatenate([rows, jnp.zeros((PAD - n_modes, rows.shape[1]), F32)], axis=0)
    wide = o["c_own"].shape[1]
    source = lax.broadcasted_iota(jnp.int32, (nz * n_modes, wide), 0)
    place = lax.broadcasted_iota(jnp.int32, (nz * n_modes, wide), 1)
    block, mode = place // PAD, place % PAD

    if turn:
        me = lax.axis_index("gz")
        side = 1 - 2 * lax.rem(me, 2)
        copy, block = block // nz, block % nz
        holder = me + jnp.where(copy == 1, side, jnp.where(copy == 2, -side, 2 * (copy // 3)))
        side = jnp.where((copy == 1) | (copy == 2), -side, side)
        offset = jnp.where(block == 1, side, jnp.where(block == 2, -side, 2 * (block // 3)))
        device = (holder + offset + 2 * nz) % nz
    else:
        device = block
    pick = jnp.where((source == device * n_modes + mode) & (mode < n_modes), 1.0, 0.0)
    ordered = dot32(rows, pick)
    o["c_own"][...] = ordered
    if turn:
        send_rows(face, ordered, 2 * PAD, o)
    o["za"][face:face + PAD, :] = modes[:, 4 * face:5 * face]
    o["zb"][face + 3 * PAD:face + 4 * PAD, :] = modes[:, 5 * face:6 * face]

    for part in range(3):
        at = slice(part * two, (part + 1) * two)
        copies[3 + 2 * part].wait()
        copies[4 + 2 * part].wait()
        high, low = split(jnp.concatenate([schur[at, pl.ds(start, face)] for start in places], axis=1))
        o["stack"][at, :] = high
        o["stack"][width + part * two:width + (part + 1) * two, :] = low
    curv = product(face, r0, o["stack"], o)
    send_rows(face, stack_rows([half_dot(r0, r0), curv], cols), PAD, o)


def column_rows(face, i, at):
    return [i["t"][at:at + PAD, :], i["gta"][at:at + PAD, :],
            i["gzb"][face + at:face + at + PAD, :], i["gt2"][at:at + PAD, :]]


def z_kernel(face, i, o):
    for k, name in enumerate(("a", "b")):
        if "mt_" + name in o:
            got_modes = mode_pieces(i["gz" + name][-PAD:, :])
            o["mt_" + name][...] = got_modes
        else:
            got_modes = i["mt_" + name][...]
        amp = i["amp"]
        own = i["z" + name][0:face, :] + dot16(i["mt"][(4 + k) * face:(5 + k) * face, :], amp_pieces(amp[0:PAD, :]))
        at = (1 + k) * PAD
        got = i["gz" + name][0:face, :] + dot16(got_modes, amp_pieces(amp[at:at + PAD, :]))
        o["z"][k * face:(k + 1) * face, :] = own - got


def value_kernel(face, stage, i, o):
    gathered = "g_all" in i
    loads = i["g_all"][...] if gathered else jnp.concatenate(column_rows(face, i, 0), axis=0)
    if stage == 0 and not gathered:
        n = loads.shape[0]
        coarse = jnp.concatenate([part[:, k * n:(k + 1) * n] for k, part in enumerate(
            [i["c_own"][...]] + column_rows(face, i, 2 * PAD)[1:])], axis=0)
        o["c_all"][...] = coarse
    else:
        coarse = i["c_all"][...]
    amp = dot32(coarse, loads)
    o["amp"][...] = amp[0:3 * PAD]
    xy = i["y"][...] + dot16(i["mt"][0:4 * face, :], amp_pieces(amp[0:PAD]))
    cols = loads.shape[1]

    if stage != 2:
        if gathered:
            dots = i["d_all"][...]
            quad = col_sum(loads * amp[3 * PAD:])
        else:
            parts = column_rows(face, i, PAD)
            dots = (parts[0] + parts[1]) + (parts[2] + parts[3])
            quad = col_sum(loads * amp)
        at = {0: 1, 1: 1, 3: 5}[stage]
        dots = jnp.concatenate([dots[0:at], row(dots, at) + quad, dots[at + 1:]], axis=0)
    if stage == 1:
        dots = jnp.concatenate([i["first"][0:2, :], dots[0:2], dots[4:]], axis=0)
    elif stage == 2 and "swapped" in i:
        dots = six_columns(i, o)
    o["xab"][0:2 * face, :] = xy[0:2 * face]
    o["ya"][0:face, :] = xy[2 * face:3 * face]
    o["yb"][0:face, :] = xy[3 * face:]
    if stage == 3:
        o["dots"][...] = dots
    if stage != 2 or "swapped" in i:
        o["xab"][2 * face:, :] = dots
    if stage != 2:
        o["ya"][face:face + PAD, :] = dots
        o["yb"][face:face + PAD, :] = dots


def assemble(face, i, rates=None):
    f = face
    got = [i["gxab"][0:2 * f, :], i["gya"][0:f, :], i["gyb"][0:f, :]]
    if rates is not None:
        got = [rate * face_values for rate, face_values in zip(rates, got)]
    return jnp.concatenate([
        i["xab"][0:2 * f, :] - got[0], i["ya"][0:f, :] - got[1], i["yb"][0:f, :] - got[2], i["z"][...],
    ], axis=0)


def column_scale(dots):
    norm, curv = row(dots, 0), row(dots, 1)
    usable = (norm > 0.0) & (curv > 0.0)
    return jnp.where(usable, norm / jnp.where(usable, curv, 1.0), 1.0)


def rescale(dots, rate):
    square = rate * rate
    return stack_rows([row(dots, 0), row(dots, 1), square * row(dots, 2), square * row(dots, 3)], dots.shape[1])


def second_kernel(face, i, o):
    w0 = assemble(face, i)
    o["w0"][...] = w0
    first = i["xab"][2 * face:2 * face + PAD, :]
    scale = column_scale(first)
    cols = w0.shape[1]
    rates = [scale / column_scale(i[name][at:at + PAD, :])
             for name, at in (("gxab", 2 * face), ("gya", face), ("gyb", face))]
    o["first"][...] = stack_rows([row(first, 0), row(first, 1), scale] + rates, cols)
    vec = scale * w0
    curv = product(face, vec, i["stack"], o)
    send_rows(face, stack_rows([half_dot(vec, vec), curv], cols), PAD, o)


def third_kernel(face, i, o):
    scale, *rates = (row(i["first"], k) for k in range(2, 6))
    q = assemble(face, i, rates)
    o["q"][...] = q
    if "near" in o:
        partners = [rescale(i[name][at:at + PAD, :], rate) for rate, name, at in zip(
            rates, ("gxab", "gya", "gyb"), (2 * face, face, face))]
        o["near"][...] = jnp.concatenate([partners[0], partners[2], partners[1] + i["xab"][2 * face:, :]], axis=0)
        half = PAD // 2
        o["pair"][...] = jnp.concatenate([partners[0][0:half], partners[2][0:half]], axis=0)
    product(face, scale * q, i["stack"], o)
    send_rows(face, jnp.zeros((PAD, q.shape[1]), F32), PAD, o)


def six_columns(i, o):
    near = i["near"]
    rate = row(i["first"], 4)
    half = PAD // 2
    both = rescale(i["swapped"][0:half, :], rate), rescale(i["swapped"][half:, :], rate)
    o["six"][...] = ((near[0:PAD, :] + near[PAD:2 * PAD, :]) + near[2 * PAD:, :]) + (both[0] + both[1])
    return near[PAD:2 * PAD, :] + both[1]


def fourth_kernel(face, i, o):
    scale, *rates = (row(i["first"], k) for k in range(2, 6))
    sums = i["six"][...]
    if "whole" not in i:
        sums = sums + rescale(i["gxab"][2 * face:, :], rates[0])
    m0, m1 = row(sums, 0), row(sums, 1)
    alpha0 = m0 / m1
    ratio0 = alpha0 / scale
    square = ratio0 * ratio0
    m2, m3 = square * row(sums, 2), square * row(sums, 3)
    norm1 = m2 - m0
    curv1 = m1 - 2.0 * (m2 / alpha0) + m3
    beta1 = norm1 / m0
    alpha1 = norm1 / (curv1 - beta1 * norm1 / alpha0)
    r0, w0 = i["r0"][...], i["w0"][...]
    q = ratio0 * i["q"][...]
    b = q - square * assemble(face, i, [rate * rate for rate in rates])
    w1 = w0 - q
    s1 = alpha1 * (w1 + beta1 * w0)
    r2 = (r0 - alpha0 * w0) - s1
    z1 = (alpha1 / alpha0) * (b + beta1 * q)
    w2 = w1 - z1
    vec = alpha1 * w2
    cols = w2.shape[1]
    o["w2"][...] = vec
    o["s1"][...] = s1
    o["z1"][...] = z1
    o["known"][...] = stack_rows([norm1, alpha1, alpha0, beta1], cols)
    curv = product(face, vec, i["stack"], o)
    send_rows(face, stack_rows([
        half_dot(r2, r2), half_dot(r2, w2), half_dot(vec, vec), half_dot(vec, s1),
        half_dot(s1, s1), curv, half_dot(z1, vec), half_dot(s1, z1)], cols), PAD, o)


def four_kernel(face, i, o):
    near = i["dots"][...] + i["gxab"][2 * face:2 * face + PAD, :]
    o["part"][...] = near + (i["across"][...] + i["gyb"][face:face + PAD, :])


def ready_kernel(face, i, o):
    alpha1, alpha0, beta1 = (row(i["known"], k) for k in range(1, 4))
    r0 = i["r0"][...]
    r1 = r0 - alpha0 * i["w0"][...]
    p1 = r1 + beta1 * r0
    o["c3"][...] = assemble(face, i)
    o["r2"][...] = r1 - i["s1"][...]
    o["p1"][...] = p1
    o["m2"][...] = alpha0 * r0 + alpha1 * p1


def last_kernel(face, names, *refs):
    i = dict(zip(names, refs))
    mult_hbm, resid_hbm, mult_out, resid_out, sems = refs[len(names):]
    d = i["sum_near"][...] + i["sum_far"][...]
    rr, rw, ww, ws, ss, wc, sc, sz = (row(d, k) for k in range(8))
    norm1, alpha1 = row(i["known"], 0), row(i["known"], 1)
    beta2 = rr / norm1
    alpha2 = rr / (rw - beta2 * rr / alpha1)
    ratio = alpha2 / alpha1
    ratio2 = ratio * ratio
    norm3 = ratio2 * (ww + 2.0 * beta2 * ws + beta2 * beta2 * ss) - rr
    curv3 = rw - 2.0 * (ratio2 / alpha2) * (ww + beta2 * ws)
    curv3 = curv3 + ratio2 * (wc + 2.0 * beta2 * sc + beta2 * beta2 * sz)
    beta3 = norm3 / rr
    alpha3 = norm3 / (curv3 - beta3 * norm3 / alpha2)
    places, signs = face_places(face)
    copies = []
    for f in range(6):
        at = slice(f * face, (f + 1) * face)
        w2, s1 = i["w2"][at, :], i["s1"][at, :]
        p2 = i["r2"][at, :] + beta2 * i["p1"][at, :]
        s2 = w2 + beta2 * s1
        r3 = i["r2"][at, :] - ratio * s2
        w3 = w2 / alpha1 - ratio * (i["c3"][at, :] + beta2 * i["z1"][at, :])
        mult = i["m2"][at, :] + alpha2 * p2 + alpha3 * (r3 + beta3 * p2)
        resid = r3 - alpha3 * (w3 + (beta3 / alpha1) * s2)
        for k, (value, out, hbm) in enumerate(((mult, mult_out, mult_hbm), (resid, resid_out, resid_hbm))):
            out[f] = (signs[f] * value).T
            copy = pltpu.make_async_copy(out.at[f], hbm.at[:, pl.ds(places[f], face)], sems.at[2 * f + k])
            copy.start()
            copies.append(copy)
    for copy in copies:
        copy.wait()


def body(sizes, residual_in, schur, modes, coarse_inv):
    nx, ny, nz = sizes
    resid = residual_in[0, 0, 0]
    matrix = schur[0, 0, 0]
    loads, width = resid.shape
    face = width // 6
    n_modes = modes.shape[3]
    mode_rows = modes.reshape(n_modes, 1, width)
    coarse_rows = coarse_inv.reshape(n_modes, 1, nz * n_modes)
    small = (nx, ny, nz) == (2, 4, 4)

    def shift(x, axis, by):
        n = lax.axis_size(axis)
        return lax.ppermute(x, axis, [(k, (k + by) % n) for k in range(n)])

    def swap(x, axis, first):
        n = lax.axis_size(axis)
        side = lambda k: 1 if (k - first) % 2 == 0 else -1
        return lax.ppermute(x, axis, [(k, (k + side(k)) % n) for k in range(n)])

    def move(x, target):
        places = [(a, b) for a in range(nx) for b in range(ny)]
        pairs = [(a * ny + b, target(a, b)[0] * ny + target(a, b)[1]) for a, b in places]
        return lax.ppermute(x, ("gx", "gy"), pairs)

    def total(dots, scale):
        rate = lax.pmin(scale, ("gx", "gy")) / scale
        rates = jnp.concatenate([jnp.ones((2, loads), F32), rate * rate, rate * rate], axis=0)
        sums = lax.psum(dots[0:4] * rates, ("gx", "gy")) / rates
        return jnp.concatenate([sums, jnp.zeros((PAD - 4, loads), F32)], axis=0)

    vec = sds((width, loads))
    rows = sds((PAD, loads))
    stack_shape = sds((2 * width + 4 * PAD, width), BF16)
    flops = 2 * width * width * 2 * loads * 2

    def z_out(tiny, extra=0):
        return dict(y=sds((4 * face, loads)), za=sds((face + extra, loads)),
                    zb=sds((face + tiny * PAD + extra, loads)), t=sds((tiny * PAD, loads)),
                    t2=sds((tiny * PAD + PAD, loads)))

    def t_exchange(a, with_dots):
        got = dict(t=a["t"], y=a["y"])
        if small:
            got.update(gzb=swap(a["zb"], "gz", 1), gt2=shift(a["t2"], "gz", 2), gta=swap(a["t"], "gz", 0))
        else:
            got["g_all"] = lax.all_gather(a["t"][0:PAD], "gz", axis=0, tiled=True)
            if with_dots:
                got["d_all"] = lax.psum(a["t"][PAD:2 * PAD], "gz")
        return got

    def z_faces(a, v, t, modes=None):
        ins = dict(za=a["za"], zb=a["zb"], gzb=t["gzb"] if small else swap(a["zb"], "gz", 1),
                   gza=swap(a["za"], "gz", 0), mt=mt, amp=v["amp"])
        outs = dict(z=sds((2 * face, loads)))
        if modes is None:
            outs.update(mt_a=sds((face, 6 * PAD), BF16), mt_b=sds((face, 6 * PAD), BF16))
        else:
            ins.update(modes)
        return call(functools.partial(z_kernel, face), ins, outs, flops=Z_FLOPS)

    def value(stage, ins):
        extra = 0 if stage == 2 else PAD
        outs = dict(amp=sds((3 * PAD, loads)), xab=sds((2 * face + (PAD if small else extra), loads)),
                    ya=sds((face + extra, loads)), yb=sds((face + 2 * PAD, loads)))
        if stage == 0 and small:
            outs["c_all"] = sds((nz * PAD, nz * PAD))
        if stage == 2 and small:
            outs["six"] = rows
        if stage == 3:
            outs["dots"] = rows
        return call(functools.partial(value_kernel, face, stage), ins, outs, flops=2 * width * loads * 48)

    def x_exchange(v):
        got = dict(xab=v["xab"])
        if nx == 2:
            got["gxab"] = swap(v["xab"], "gx", 0)
        else:
            a, b, rest = v["xab"][:face], v["xab"][face:2 * face], v["xab"][2 * face:]
            got["gxab"] = jnp.concatenate([swap(a, "gx", 0), swap(b, "gx", 1), rest], axis=0)
        return got

    def y_exchange(v):
        gyb = swap(v["yb"], "gy", 1)
        return dict(ya=v["ya"], yb=v["yb"], gya=swap(v["ya"], "gy", 0), gyb=gyb)

    def xy_exchange(v):
        return dict(x_exchange(v), **y_exchange(v))

    hbm = pl.BlockSpec(memory_space=pltpu.HBM)
    vmem = pl.BlockSpec(memory_space=pltpu.VMEM)
    outs = dict(r0=vec, stack=stack_shape, mt=sds((width, 6 * PAD), BF16),
                c_own=sds((PAD, (4 if small else 1) * nz * PAD)), **z_out(3, PAD))
    res = pl.pallas_call(
        functools.partial(first_kernel, face, nz, n_modes, small),
        out_shape=list(outs.values()),
        in_specs=[hbm] * 4,
        out_specs=[vmem] * len(outs),
        scratch_shapes=[
            pltpu.VMEM(resid.shape, F32), pltpu.VMEM(matrix.shape, F32),
            pltpu.VMEM(mode_rows.shape, F32), pltpu.VMEM(coarse_rows.shape, F32),
            pltpu.SemaphoreType.DMA((9,)),
        ],
        compiler_params=pltpu.CompilerParams(vmem_limit_bytes=VMEM_LIMIT),
        cost_estimate=pl.CostEstimate(flops=flops, bytes_accessed=4 * matrix.size, transcendentals=0),
    )(*[pltpu.with_memory_space_constraint(x, pltpu.HBM) for x in (resid, matrix, mode_rows, coarse_rows)])
    a = dict(zip(outs, res))
    r0, mt, stack = a["r0"], a["mt"], a["stack"]
    ins = dict(t_exchange(a, True), mt=mt)
    if small:
        ins["c_own"] = a["c_own"]
    else:
        c_own = a["c_own"]
        ins["c_all"] = jnp.concatenate([
            c_own, swap(c_own, "gz", 0), swap(c_own, "gz", 1),
            lax.all_gather(c_own, "gz", axis=0, tiled=True)], axis=0)
    t = ins
    v = value(0, ins)
    column = dict(mt=mt, c_all=v["c_all"] if small else ins["c_all"])
    z = z_faces(a, v, t)
    got_modes = dict(mt_a=z["mt_a"], mt_b=z["mt_b"])
    x = dict(xy_exchange(v), z=z["z"])

    a = call(functools.partial(second_kernel, face), dict(x, stack=stack),
             dict(w0=vec, first=rows, **z_out(2)), flops=flops)
    w0, first = a["w0"], a["first"]
    t = t_exchange(a, True)
    v = value(1, dict(t, **column, first=first))
    x = dict(xy_exchange(v), z=z_faces(a, v, t, got_modes)["z"])

    near = dict(near=sds((3 * PAD, loads)), pair=rows) if small else {}
    a = call(functools.partial(third_kernel, face), dict(x, stack=stack, first=first),
             dict(q=vec, **near, **z_out(2)), flops=flops)
    q = a["q"]
    t = t_exchange(a, False)
    ins = dict(t, **column)
    if small:
        ins.update(first=first, near=a["near"], swapped=swap(a["pair"], "gy", 0))
        v = value(2, ins)
        sums = dict(six=v["six"])
    else:
        sums = dict(six=total(v["xab"][2 * face:], first[2:3]), whole=first)
        v = value(2, ins)
    x = dict(xy_exchange(v), z=z_faces(a, v, t, got_modes)["z"])

    a = call(functools.partial(fourth_kernel, face),
             dict(x, stack=stack, **sums, first=first, r0=r0, w0=w0, q=q),
             dict(w2=vec, s1=vec, z1=vec, known=rows, **z_out(2)), flops=flops)
    t = t_exchange(a, True)
    v = value(3, dict(t, **column))
    z = z_faces(a, v, t, got_modes)["z"]
    if small:
        x = x_exchange(v)
        across = move(v["dots"], lambda a, b: (1 - a, (b + (-1 if b % 2 == 0 else 1)) % ny))
        x.update(y_exchange(v))
        part = call(functools.partial(four_kernel, face),
                    dict(dots=v["dots"], across=across, gxab=x["gxab"], gyb=x["gyb"], z=z), dict(part=rows))["part"]
        sums = dict(sum_near=part, sum_far=swap(part, "gy", 0))
    else:
        x = xy_exchange(v)
        sums = dict(sum_near=lax.psum(v["dots"], ("gx", "gy")), sum_far=jnp.zeros((PAD, loads), F32))
    ready = call(functools.partial(ready_kernel, face),
                 dict(x, z=z, known=a["known"], s1=a["s1"], r0=r0, w0=w0),
                 {name: vec for name in ("c3", "r2", "p1", "m2")}, flops=10 * width * loads)
    ins = dict(sums, **ready, **{name: a[name] for name in ("known", "w2", "s1", "z1")})
    out = sds((loads, width))
    mult, final = pl.pallas_call(
        functools.partial(last_kernel, face, list(ins)),
        out_shape=[out, out],
        in_specs=[vmem] * len(ins),
        out_specs=[hbm, hbm],
        scratch_shapes=[pltpu.VMEM((6, loads, face), F32), pltpu.VMEM((6, loads, face), F32),
                        pltpu.SemaphoreType.DMA((12,))],
        compiler_params=pltpu.CompilerParams(vmem_limit_bytes=VMEM_LIMIT),
        cost_estimate=pl.CostEstimate(flops=20 * width * loads, bytes_accessed=9 * 4 * width * loads, transcendentals=0),
    )(*ins.values())
    return (mult[None, None, None], final[None, None, None])


def solution(mesh):
    spec = P("gx", "gy", "gz", None, None)
    sizes = tuple(mesh.shape[axis] for axis in ("gx", "gy", "gz"))
    return jax.shard_map(
        functools.partial(body, sizes),
        mesh=mesh,
        in_specs=(spec, spec, spec, P("gx", "gy", "gz", None)),
        out_specs=(spec, spec),
        check_vma=False,
    )
```

```python
import functools

import jax
import jax.numpy as jnp
from jax import lax
from jax.experimental import pallas as pl
from jax.experimental.pallas import tpu as pltpu
from jax.sharding import PartitionSpec as P

F32 = jnp.float32
BF16 = jnp.bfloat16
HI = lax.Precision.HIGHEST
PAD = 8
VMEM_LIMIT = 24 * 1024 * 1024
Z_FLOPS = 770000000


def sds(shape, dtype=F32):
    return jax.ShapeDtypeStruct(shape, dtype)


def call(kernel, ins, outs, flops=0):
    names_in, names_out = list(ins), list(outs)
    nbytes = sum(a.size * a.dtype.itemsize for a in list(ins.values()) + list(outs.values()))

    def run(*refs):
        n = len(names_in)
        kernel(dict(zip(names_in, refs[:n])), dict(zip(names_out, refs[n:])))

    vmem = pl.BlockSpec(memory_space=pltpu.VMEM)
    res = pl.pallas_call(
        run,
        out_shape=[outs[n] for n in names_out],
        in_specs=[vmem] * len(names_in),
        out_specs=[vmem] * len(names_out),
        compiler_params=pltpu.CompilerParams(vmem_limit_bytes=VMEM_LIMIT),
        cost_estimate=pl.CostEstimate(flops=flops, bytes_accessed=nbytes, transcendentals=0),
    )(*[ins[n] for n in names_in])
    return dict(zip(names_out, res))


def split(x):
    high = x.astype(BF16)
    return high, (x - high.astype(F32)).astype(BF16)


def split3(x):
    high = x.astype(BF16)
    rest = x - high.astype(F32)
    mid = rest.astype(BF16)
    return high, mid, (rest - mid.astype(F32)).astype(BF16)


def left_pieces(x):
    high, mid, low = split3(x)
    return jnp.concatenate([high, high, mid, mid, high, low], axis=1)


def mode_pieces(modes):
    return left_pieces(modes.T)


def amp_pieces(amp):
    high, mid, low = split3(amp)
    return jnp.concatenate([high, mid, high, mid, low, high], axis=0)


def dot32(a, b):
    return jnp.dot(a, b, precision=HI, preferred_element_type=F32)


def dot16(a, b):
    return jnp.dot(a, b, preferred_element_type=F32)


def col_sum(x):
    return jnp.sum(x, axis=0, keepdims=True)


def half_dot(a, b):
    return 0.5 * col_sum(a * b)


def row(x, i):
    return x[i:i + 1, :]


def face_places(face):
    places, signs = [], []
    for k, axis in enumerate(("gx", "gy", "gz")):
        odd = lax.rem(lax.axis_index(axis), 2)
        for high in (1 - odd, odd):
            places.append(pl.multiple_of((2 * k + high) * face, face))
            signs.append((1 - 2 * high).astype(F32))
    return places, signs


def store_product(face, part, y, o):
    if part < 2:
        o["y"][2 * part * face:2 * (part + 1) * face, :] = y
    else:
        o["za"][0:face, :] = y[0:face]
        o["zb"][0:face, :] = y[face:]


def send_rows(face, rows, at, o):
    n = rows.shape[0]
    o["t"][at:at + n, :] = rows
    o["t2"][at:at + n, :] = rows
    o["zb"][face + at:face + at + n, :] = rows


def product(face, vec, stack, o):
    width, cols = vec.shape
    both = dot16(stack[...], jnp.concatenate(split(vec), axis=1))
    total = jnp.zeros((1, cols), F32)
    for part in range(3):
        at = slice(2 * part * face, 2 * (part + 1) * face)
        low = slice(width + 2 * part * face, width + 2 * (part + 1) * face)
        y = (both[at, :cols] + both[at, cols:]) + (both[low, :cols] + both[low, cols:])
        store_product(face, part, y, o)
        total = total + col_sum(vec[at] * y)
    loads = both[2 * width:, :cols] + both[2 * width:, cols:]
    send_rows(face, (loads[0:PAD] + loads[PAD:2 * PAD]) + loads[2 * PAD:3 * PAD], 0, o)
    return total


def stack_rows(rows, cols):
    zero = jnp.zeros((1, cols), F32)
    return jnp.concatenate(list(rows) + [zero] * (PAD - len(rows)), axis=0)


def first_kernel(face, nz, n_modes, turn, resid_hbm, schur_hbm, modes_hbm, coarse_hbm, *refs):
    names = ["r0", "stack", "mt", "c_own", "y", "za", "zb", "t", "t2"]
    o = dict(zip(names, refs[:len(names)]))
    resid, schur, mode_rows, coarse, sems = refs[len(names):]
    two = 2 * face
    places, signs = face_places(face)
    copies = [
        pltpu.make_async_copy(modes_hbm, mode_rows, sems.at[0]),
        pltpu.make_async_copy(resid_hbm, resid, sems.at[1]),
        pltpu.make_async_copy(coarse_hbm, coarse, sems.at[2]),
    ]
    for f in range(6):
        at = pl.ds(f * face, face)
        copies.append(pltpu.make_async_copy(schur_hbm.at[pl.ds(places[f], face), :], schur.at[at, :], sems.at[3 + f]))
    for copy in copies:
        copy.start()

    copies[0].wait()
    modes = jnp.concatenate([
        jnp.concatenate([mode_rows[m, :, pl.ds(at, face)] for at in places], axis=1)
        for m in range(n_modes)], axis=0)
    modes = jnp.concatenate([modes, jnp.zeros((PAD - n_modes, modes.shape[1]), F32)], axis=0)
    width = modes.shape[1]
    o["mt"][...] = mode_pieces(modes)
    o["stack"][2 * width:, :] = jnp.concatenate(split3(modes) + (jnp.zeros(modes.shape, BF16),), axis=0)

    copies[1].wait()
    for f in range(6):
        o["r0"][f * face:(f + 1) * face, :] = signs[f] * resid[:, pl.ds(places[f], face)].T
    r0 = o["r0"][...]
    cols = r0.shape[1]

    copies[2].wait()
    rows = jnp.concatenate([coarse[m] for m in range(n_modes)], axis=0)
    rows = jnp.concatenate([rows, jnp.zeros((PAD - n_modes, rows.shape[1]), F32)], axis=0)
    wide = o["c_own"].shape[1]
    source = lax.broadcasted_iota(jnp.int32, (nz * n_modes, wide), 0)
    place = lax.broadcasted_iota(jnp.int32, (nz * n_modes, wide), 1)
    block, mode = place // PAD, place % PAD

    if turn:
        me = lax.axis_index("gz")
        side = 1 - 2 * lax.rem(me, 2)
        copy, block = block // nz, block % nz
        holder = me + jnp.where(copy == 1, side, jnp.where(copy == 2, -side, 2 * (copy // 3)))
        side = jnp.where((copy == 1) | (copy == 2), -side, side)
        offset = jnp.where(block == 1, side, jnp.where(block == 2, -side, 2 * (block // 3)))
        device = (holder + offset + 2 * nz) % nz
    else:
        device = block
    pick = jnp.where((source == device * n_modes + mode) & (mode < n_modes), 1.0, 0.0)
    ordered = dot32(rows, pick)
    o["c_own"][...] = ordered
    if turn:
        send_rows(face, ordered, 2 * PAD, o)
    o["za"][face:face + PAD, :] = modes[:, 4 * face:5 * face]
    o["zb"][face + 3 * PAD:face + 4 * PAD, :] = modes[:, 5 * face:6 * face]

    for part in range(3):
        at = slice(part * two, (part + 1) * two)
        copies[3 + 2 * part].wait()
        copies[4 + 2 * part].wait()
        high, low = split(jnp.concatenate([schur[at, pl.ds(start, face)] for start in places], axis=1))
        o["stack"][at, :] = high
        o["stack"][width + part * two:width + (part + 1) * two, :] = low
    curv = product(face, r0, o["stack"], o)
    send_rows(face, stack_rows([half_dot(r0, r0), curv], cols), PAD, o)


def column_rows(face, i, at):
    return [i["t"][at:at + PAD, :], i["gta"][at:at + PAD, :],
            i["gzb"][face + at:face + at + PAD, :], i["gt2"][at:at + PAD, :]]


def z_kernel(face, i, o):
    for k, name in enumerate(("a", "b")):
        if "mt_" + name in o:
            got_modes = mode_pieces(i["gz" + name][-PAD:, :])
            o["mt_" + name][...] = got_modes
        else:
            got_modes = i["mt_" + name][...]
        amp = i["amp"]
        own = i["z" + name][0:face, :] + dot16(i["mt"][(4 + k) * face:(5 + k) * face, :], amp_pieces(amp[0:PAD, :]))
        at = (1 + k) * PAD
        got = i["gz" + name][0:face, :] + dot16(got_modes, amp_pieces(amp[at:at + PAD, :]))
        o["z"][k * face:(k + 1) * face, :] = own - got


def value_kernel(face, stage, i, o):
    gathered = "g_all" in i
    loads = i["g_all"][...] if gathered else jnp.concatenate(column_rows(face, i, 0), axis=0)
    if stage == 0 and not gathered:
        n = loads.shape[0]
        coarse = jnp.concatenate([part[:, k * n:(k + 1) * n] for k, part in enumerate(
            [i["c_own"][...]] + column_rows(face, i, 2 * PAD)[1:])], axis=0)
        coarse = left_pieces(coarse)
        o["c_all"][...] = coarse
    else:
        coarse = i["c_all"][...]
    amp = dot32(coarse, loads) if gathered else dot16(coarse, amp_pieces(loads))
    o["amp"][...] = amp[0:3 * PAD]
    xy = i["y"][...] + dot16(i["mt"][0:4 * face, :], amp_pieces(amp[0:PAD]))
    cols = loads.shape[1]

    if stage != 2:
        if gathered:
            dots = i["d_all"][...]
            quad = col_sum(loads * amp[3 * PAD:])
        else:
            parts = column_rows(face, i, PAD)
            dots = (parts[0] + parts[1]) + (parts[2] + parts[3])
            quad = col_sum(loads * amp)
        at = {0: 1, 1: 1, 3: 5}[stage]
        dots = jnp.concatenate([dots[0:at], row(dots, at) + quad, dots[at + 1:]], axis=0)
    if stage == 1:
        dots = jnp.concatenate([i["first"][0:2, :], dots[0:2], dots[4:]], axis=0)
    elif stage == 2 and "swapped" in i:
        dots = six_columns(i, o)
    o["xab"][0:2 * face, :] = xy[0:2 * face]
    o["ya"][0:face, :] = xy[2 * face:3 * face]
    o["yb"][0:face, :] = xy[3 * face:]
    if stage == 3:
        o["dots"][...] = dots
    if stage != 2 or "swapped" in i:
        o["xab"][2 * face:, :] = dots
    if stage != 2:
        o["ya"][face:face + PAD, :] = dots
        o["yb"][face:face + PAD, :] = dots


def assemble(face, i, rates=None):
    f = face
    got = [i["gxab"][0:2 * f, :], i["gya"][0:f, :], i["gyb"][0:f, :]]
    if rates is not None:
        got = [rate * face_values for rate, face_values in zip(rates, got)]
    return jnp.concatenate([
        i["xab"][0:2 * f, :] - got[0], i["ya"][0:f, :] - got[1], i["yb"][0:f, :] - got[2], i["z"][...],
    ], axis=0)


def column_scale(dots):
    norm, curv = row(dots, 0), row(dots, 1)
    usable = (norm > 0.0) & (curv > 0.0)
    return jnp.where(usable, norm / jnp.where(usable, curv, 1.0), 1.0)


def rescale(dots, rate):
    square = rate * rate
    return stack_rows([row(dots, 0), row(dots, 1), square * row(dots, 2), square * row(dots, 3)], dots.shape[1])


def second_kernel(face, i, o):
    w0 = assemble(face, i)
    o["w0"][...] = w0
    first = i["xab"][2 * face:2 * face + PAD, :]
    scale = column_scale(first)
    cols = w0.shape[1]
    rates = [scale / column_scale(i[name][at:at + PAD, :])
             for name, at in (("gxab", 2 * face), ("gya", face), ("gyb", face))]
    o["first"][...] = stack_rows([row(first, 0), row(first, 1), scale] + rates, cols)
    vec = scale * w0
    curv = product(face, vec, i["stack"], o)
    send_rows(face, stack_rows([half_dot(vec, vec), curv], cols), PAD, o)


def third_kernel(face, i, o):
    scale, *rates = (row(i["first"], k) for k in range(2, 6))
    q = assemble(face, i, rates)
    o["q"][...] = q
    if "near" in o:
        partners = [rescale(i[name][at:at + PAD, :], rate) for rate, name, at in zip(
            rates, ("gxab", "gya", "gyb"), (2 * face, face, face))]
        o["near"][...] = jnp.concatenate([partners[0], partners[2], partners[1] + i["xab"][2 * face:, :]], axis=0)
    product(face, scale * q, i["stack"], o)


def six_columns(i, o):
    near = i["near"]
    rate = row(i["first"], 4)
    both = rescale(i["swapped"][0:PAD, :], rate), rescale(i["swapped"][PAD:2 * PAD, :], rate)
    o["six"][...] = ((near[0:PAD, :] + near[PAD:2 * PAD, :]) + near[2 * PAD:, :]) + (both[0] + both[1])
    return near[PAD:2 * PAD, :] + both[1]


def fourth_kernel(face, i, o):
    scale, *rates = (row(i["first"], k) for k in range(2, 6))
    sums = i["six"][...]
    if "whole" not in i:
        sums = sums + rescale(i["gxab"][2 * face:, :], rates[0])
    m0, m1 = row(sums, 0), row(sums, 1)
    alpha0 = m0 / m1
    ratio0 = alpha0 / scale
    square = ratio0 * ratio0
    m2, m3 = square * row(sums, 2), square * row(sums, 3)
    norm1 = m2 - m0
    curv1 = m1 - 2.0 * (m2 / alpha0) + m3
    beta1 = norm1 / m0
    alpha1 = norm1 / (curv1 - beta1 * norm1 / alpha0)
    r0, w0 = i["r0"][...], i["w0"][...]
    q = ratio0 * i["q"][...]
    b = q - square * assemble(face, i, [rate * rate for rate in rates])
    w1 = w0 - q
    s1 = alpha1 * (w1 + beta1 * w0)
    r2 = (r0 - alpha0 * w0) - s1
    z1 = (alpha1 / alpha0) * (b + beta1 * q)
    w2 = w1 - z1
    vec = alpha1 * w2
    cols = w2.shape[1]
    o["w2"][...] = vec
    o["s1"][...] = s1
    o["z1"][...] = z1
    o["known"][...] = stack_rows([norm1, alpha1, alpha0, beta1], cols)
    curv = product(face, vec, i["stack"], o)
    send_rows(face, stack_rows([
        half_dot(r2, r2), half_dot(r2, w2), half_dot(vec, vec), half_dot(vec, s1),
        half_dot(s1, s1), curv, half_dot(z1, vec), half_dot(s1, z1)], cols), PAD, o)


def four_kernel(face, i, o):
    near = i["dots"][...] + i["gxab"][2 * face:2 * face + PAD, :]
    o["part"][...] = near + (i["across"][...] + i["gyb"][face:face + PAD, :])


def ready_kernel(face, i, o):
    alpha1, alpha0, beta1 = (row(i["known"], k) for k in range(1, 4))
    r0 = i["r0"][...]
    r1 = r0 - alpha0 * i["w0"][...]
    p1 = r1 + beta1 * r0
    o["c3"][...] = assemble(face, i)
    o["r2"][...] = r1 - i["s1"][...]
    o["p1"][...] = p1
    o["m2"][...] = alpha0 * r0 + alpha1 * p1


def last_kernel(face, names, *refs):
    i = dict(zip(names, refs))
    mult_hbm, resid_hbm, mult_out, resid_out, sems = refs[len(names):]
    d = i["sum_near"][...] + i["sum_far"][...]
    rr, rw, ww, ws, ss, wc, sc, sz = (row(d, k) for k in range(8))
    norm1, alpha1 = row(i["known"], 0), row(i["known"], 1)
    beta2 = rr / norm1
    alpha2 = rr / (rw - beta2 * rr / alpha1)
    ratio = alpha2 / alpha1
    ratio2 = ratio * ratio
    norm3 = ratio2 * (ww + 2.0 * beta2 * ws + beta2 * beta2 * ss) - rr
    curv3 = rw - 2.0 * (ratio2 / alpha2) * (ww + beta2 * ws)
    curv3 = curv3 + ratio2 * (wc + 2.0 * beta2 * sc + beta2 * beta2 * sz)
    beta3 = norm3 / rr
    alpha3 = norm3 / (curv3 - beta3 * norm3 / alpha2)
    places, signs = face_places(face)
    copies = []
    for f in range(6):
        at = slice(f * face, (f + 1) * face)
        w2, s1 = i["w2"][at, :], i["s1"][at, :]
        p2 = i["r2"][at, :] + beta2 * i["p1"][at, :]
        s2 = w2 + beta2 * s1
        r3 = i["r2"][at, :] - ratio * s2
        w3 = w2 / alpha1 - ratio * (i["c3"][at, :] + beta2 * i["z1"][at, :])
        mult = i["m2"][at, :] + alpha2 * p2 + alpha3 * (r3 + beta3 * p2)
        resid = r3 - alpha3 * (w3 + (beta3 / alpha1) * s2)
        for k, (value, out, hbm) in enumerate(((mult, mult_out, mult_hbm), (resid, resid_out, resid_hbm))):
            out[f] = (signs[f] * value).T
            copy = pltpu.make_async_copy(out.at[f], hbm.at[:, pl.ds(places[f], face)], sems.at[2 * f + k])
            copy.start()
            copies.append(copy)
    for copy in copies:
        copy.wait()


def body(sizes, residual_in, schur, modes, coarse_inv):
    nx, ny, nz = sizes
    resid = residual_in[0, 0, 0]
    matrix = schur[0, 0, 0]
    loads, width = resid.shape
    face = width // 6
    n_modes = modes.shape[3]
    mode_rows = modes.reshape(n_modes, 1, width)
    coarse_rows = coarse_inv.reshape(n_modes, 1, nz * n_modes)
    small = (nx, ny, nz) == (2, 4, 4)

    def shift(x, axis, by):
        n = lax.axis_size(axis)
        return lax.ppermute(x, axis, [(k, (k + by) % n) for k in range(n)])

    def swap(x, axis, first):
        n = lax.axis_size(axis)
        side = lambda k: 1 if (k - first) % 2 == 0 else -1
        return lax.ppermute(x, axis, [(k, (k + side(k)) % n) for k in range(n)])

    def move(x, target):
        places = [(a, b) for a in range(nx) for b in range(ny)]
        pairs = [(a * ny + b, target(a, b)[0] * ny + target(a, b)[1]) for a, b in places]
        return lax.ppermute(x, ("gx", "gy"), pairs)

    def total(dots, scale):
        rate = lax.pmin(scale, ("gx", "gy")) / scale
        rates = jnp.concatenate([jnp.ones((2, loads), F32), rate * rate, rate * rate], axis=0)
        sums = lax.psum(dots[0:4] * rates, ("gx", "gy")) / rates
        return jnp.concatenate([sums, jnp.zeros((PAD - 4, loads), F32)], axis=0)

    vec = sds((width, loads))
    rows = sds((PAD, loads))
    stack_shape = sds((2 * width + 4 * PAD, width), BF16)
    flops = 2 * width * width * 2 * loads * 2

    def z_out(tiny, extra=0):
        return dict(y=sds((4 * face, loads)), za=sds((face + extra, loads)),
                    zb=sds((face + tiny * PAD + extra, loads)), t=sds((tiny * PAD, loads)),
                    t2=sds((tiny * PAD + PAD, loads)))

    def t_exchange(a, with_dots):
        got = dict(t=a["t"], y=a["y"])
        if small:
            got.update(gzb=swap(a["zb"], "gz", 1), gt2=shift(a["t2"], "gz", 2), gta=swap(a["t"], "gz", 0))
        else:
            got["g_all"] = lax.all_gather(a["t"][0:PAD], "gz", axis=0, tiled=True)
            if with_dots:
                got["d_all"] = lax.psum(a["t"][PAD:2 * PAD], "gz")
        return got

    def z_faces(a, v, t, modes=None):
        ins = dict(za=a["za"], zb=a["zb"], gzb=t["gzb"] if small else swap(a["zb"], "gz", 1),
                   gza=swap(a["za"], "gz", 0), mt=mt, amp=v["amp"])
        outs = dict(z=sds((2 * face, loads)))
        if modes is None:
            outs.update(mt_a=sds((face, 6 * PAD), BF16), mt_b=sds((face, 6 * PAD), BF16))
        else:
            ins.update(modes)
        return call(functools.partial(z_kernel, face), ins, outs, flops=Z_FLOPS)

    def value(stage, ins):
        extra = 0 if stage == 2 else PAD
        outs = dict(amp=sds((3 * PAD, loads)), xab=sds((2 * face + (PAD if small else extra), loads)),
                    ya=sds((face + extra, loads)), yb=sds((face + 2 * PAD, loads)))
        if stage == 0 and small:
            outs["c_all"] = sds((nz * PAD, 6 * nz * PAD), BF16)
        if stage == 2 and small:
            outs["six"] = rows
        if stage == 3:
            outs["dots"] = rows
        return call(functools.partial(value_kernel, face, stage), ins, outs, flops=2 * width * loads * 48)

    def x_exchange(v):
        got = dict(xab=v["xab"])
        if nx == 2:
            got["gxab"] = swap(v["xab"], "gx", 0)
        else:
            a, b, rest = v["xab"][:face], v["xab"][face:2 * face], v["xab"][2 * face:]
            got["gxab"] = jnp.concatenate([swap(a, "gx", 0), swap(b, "gx", 1), rest], axis=0)
        return got

    def y_exchange(v):
        gyb = swap(v["yb"], "gy", 1)
        return dict(ya=v["ya"], yb=v["yb"], gya=swap(v["ya"], "gy", 0), gyb=gyb)

    def xy_exchange(v):
        return dict(x_exchange(v), **y_exchange(v))

    hbm = pl.BlockSpec(memory_space=pltpu.HBM)
    vmem = pl.BlockSpec(memory_space=pltpu.VMEM)
    outs = dict(r0=vec, stack=stack_shape, mt=sds((width, 6 * PAD), BF16),
                c_own=sds((PAD, (4 if small else 1) * nz * PAD)), **z_out(3, PAD))
    res = pl.pallas_call(
        functools.partial(first_kernel, face, nz, n_modes, small),
        out_shape=list(outs.values()),
        in_specs=[hbm] * 4,
        out_specs=[vmem] * len(outs),
        scratch_shapes=[
            pltpu.VMEM(resid.shape, F32), pltpu.VMEM(matrix.shape, F32),
            pltpu.VMEM(mode_rows.shape, F32), pltpu.VMEM(coarse_rows.shape, F32),
            pltpu.SemaphoreType.DMA((9,)),
        ],
        compiler_params=pltpu.CompilerParams(vmem_limit_bytes=VMEM_LIMIT),
        cost_estimate=pl.CostEstimate(flops=flops, bytes_accessed=4 * matrix.size, transcendentals=0),
    )(*[pltpu.with_memory_space_constraint(x, pltpu.HBM) for x in (resid, matrix, mode_rows, coarse_rows)])
    a = dict(zip(outs, res))
    r0, mt, stack = a["r0"], a["mt"], a["stack"]
    ins = dict(t_exchange(a, True), mt=mt)
    if small:
        ins["c_own"] = a["c_own"]
    else:
        c_own = a["c_own"]
        ins["c_all"] = jnp.concatenate([
            c_own, swap(c_own, "gz", 0), swap(c_own, "gz", 1),
            lax.all_gather(c_own, "gz", axis=0, tiled=True)], axis=0)
    t = ins
    v = value(0, ins)
    column = dict(mt=mt, c_all=v["c_all"] if small else ins["c_all"])
    z = z_faces(a, v, t)
    got_modes = dict(mt_a=z["mt_a"], mt_b=z["mt_b"])
    x = dict(xy_exchange(v), z=z["z"])

    a = call(functools.partial(second_kernel, face), dict(x, stack=stack),
             dict(w0=vec, first=rows, **z_out(2)), flops=flops)
    w0, first = a["w0"], a["first"]
    t = t_exchange(a, True)
    v = value(1, dict(t, **column, first=first))
    x = dict(xy_exchange(v), z=z_faces(a, v, t, got_modes)["z"])

    near = dict(near=sds((3 * PAD, loads))) if small else {}
    a = call(functools.partial(third_kernel, face), dict(x, stack=stack, first=first),
             dict(q=vec, **near, **z_out(1)), flops=flops)
    q = a["q"]
    t = t_exchange(a, False)
    ins = dict(t, **column)
    if small:
        ins.update(first=first, near=a["near"], swapped=swap(a["near"][0:2 * PAD], "gy", 0))
        v = value(2, ins)
        sums = dict(six=v["six"])
    else:
        sums = dict(six=total(v["xab"][2 * face:], first[2:3]), whole=first)
        v = value(2, ins)
    x = dict(xy_exchange(v), z=z_faces(a, v, t, got_modes)["z"])

    a = call(functools.partial(fourth_kernel, face),
             dict(x, stack=stack, **sums, first=first, r0=r0, w0=w0, q=q),
             dict(w2=vec, s1=vec, z1=vec, known=rows, **z_out(2)), flops=flops)
    t = t_exchange(a, True)
    v = value(3, dict(t, **column))
    z = z_faces(a, v, t, got_modes)["z"]
    if small:
        x = x_exchange(v)
        across = move(v["dots"], lambda a, b: (1 - a, (b + (-1 if b % 2 == 0 else 1)) % ny))
        x.update(y_exchange(v))
        part = call(functools.partial(four_kernel, face),
                    dict(dots=v["dots"], across=across, gxab=x["gxab"], gyb=x["gyb"], z=z), dict(part=rows))["part"]
        sums = dict(sum_near=part, sum_far=swap(part, "gy", 0))
    else:
        x = xy_exchange(v)
        sums = dict(sum_near=lax.psum(v["dots"], ("gx", "gy")), sum_far=jnp.zeros((PAD, loads), F32))
    ready = call(functools.partial(ready_kernel, face),
                 dict(x, z=z, known=a["known"], s1=a["s1"], r0=r0, w0=w0),
                 {name: vec for name in ("c3", "r2", "p1", "m2")}, flops=10 * width * loads)
    ins = dict(sums, **ready, **{name: a[name] for name in ("known", "w2", "s1", "z1")})
    out = sds((loads, width))
    mult, final = pl.pallas_call(
        functools.partial(last_kernel, face, list(ins)),
        out_shape=[out, out],
        in_specs=[vmem] * len(ins),
        out_specs=[hbm, hbm],
        scratch_shapes=[pltpu.VMEM((6, loads, face), F32), pltpu.VMEM((6, loads, face), F32),
                        pltpu.SemaphoreType.DMA((12,))],
        compiler_params=pltpu.CompilerParams(vmem_limit_bytes=VMEM_LIMIT),
        cost_estimate=pl.CostEstimate(flops=20 * width * loads, bytes_accessed=9 * 4 * width * loads, transcendentals=0),
    )(*ins.values())
    return (mult[None, None, None], final[None, None, None])


def solution(mesh):
    spec = P("gx", "gy", "gz", None, None)
    sizes = tuple(mesh.shape[axis] for axis in ("gx", "gy", "gz"))
    return jax.shard_map(
        functools.partial(body, sizes),
        mesh=mesh,
        in_specs=(spec, spec, spec, P("gx", "gy", "gz", None)),
        out_specs=(spec, spec),
        check_vma=False,
    )
```

```python
import functools

import jax
import jax.numpy as jnp
from jax import lax
from jax.experimental import pallas as pl
from jax.experimental.pallas import tpu as pltpu
from jax.sharding import PartitionSpec as P

F32 = jnp.float32
BF16 = jnp.bfloat16
HI = lax.Precision.HIGHEST
PAD = 8
VMEM_LIMIT = 24 * 1024 * 1024
Z_FLOPS = 770000000


def sds(shape, dtype=F32):
    return jax.ShapeDtypeStruct(shape, dtype)


def call(kernel, ins, outs, flops=0):
    names_in, names_out = list(ins), list(outs)
    nbytes = sum(a.size * a.dtype.itemsize for a in list(ins.values()) + list(outs.values()))

    def run(*refs):
        n = len(names_in)
        kernel(dict(zip(names_in, refs[:n])), dict(zip(names_out, refs[n:])))

    vmem = pl.BlockSpec(memory_space=pltpu.VMEM)
    res = pl.pallas_call(
        run,
        out_shape=[outs[n] for n in names_out],
        in_specs=[vmem] * len(names_in),
        out_specs=[vmem] * len(names_out),
        compiler_params=pltpu.CompilerParams(vmem_limit_bytes=VMEM_LIMIT),
        cost_estimate=pl.CostEstimate(flops=flops, bytes_accessed=nbytes, transcendentals=0),
    )(*[ins[n] for n in names_in])
    return dict(zip(names_out, res))


def split(x):
    high = x.astype(BF16)
    return high, (x - high.astype(F32)).astype(BF16)


def split3(x):
    high = x.astype(BF16)
    rest = x - high.astype(F32)
    mid = rest.astype(BF16)
    return high, mid, (rest - mid.astype(F32)).astype(BF16)


def left_pieces(x):
    high, mid, low = split3(x)
    return jnp.concatenate([high, high, mid, mid, high, low], axis=1)


def mode_pieces(modes):
    return left_pieces(modes.T)


def amp_pieces(amp):
    high, mid, low = split3(amp)
    return jnp.concatenate([high, mid, high, mid, low, high], axis=0)


def dot32(a, b):
    return jnp.dot(a, b, precision=HI, preferred_element_type=F32)


def dot16(a, b):
    return jnp.dot(a, b, preferred_element_type=F32)


def col_sum(x):
    return jnp.sum(x, axis=0, keepdims=True)


def half_dot(a, b):
    return 0.5 * col_sum(a * b)


def row(x, i):
    return x[i:i + 1, :]


def face_places(face):
    places, signs = [], []
    for k, axis in enumerate(("gx", "gy", "gz")):
        odd = lax.rem(lax.axis_index(axis), 2)
        for high in (1 - odd, odd):
            places.append(pl.multiple_of((2 * k + high) * face, face))
            signs.append((1 - 2 * high).astype(F32))
    return places, signs


def store_product(face, part, y, o):
    if part < 2:
        o["y"][2 * part * face:2 * (part + 1) * face, :] = y
    else:
        o["za"][0:face, :] = y[0:face]
        o["zb"][0:face, :] = y[face:]


def send_rows(face, rows, at, o):
    n = rows.shape[0]
    o["t"][at:at + n, :] = rows
    o["t2"][at:at + n, :] = rows
    o["zb"][face + at:face + at + n, :] = rows


def product(face, vec, stack, o):
    width, cols = vec.shape
    both = dot16(stack[...], jnp.concatenate(split(vec), axis=1))
    total = jnp.zeros((1, cols), F32)
    for part in range(3):
        at = slice(2 * part * face, 2 * (part + 1) * face)
        low = slice(width + 2 * part * face, width + 2 * (part + 1) * face)
        y = (both[at, :cols] + both[at, cols:]) + (both[low, :cols] + both[low, cols:])
        store_product(face, part, y, o)
        total = total + col_sum(vec[at] * y)
    loads = both[2 * width:, :cols] + both[2 * width:, cols:]
    send_rows(face, (loads[0:PAD] + loads[PAD:2 * PAD]) + loads[2 * PAD:3 * PAD], 0, o)
    return total


def stack_rows(rows, cols):
    zero = jnp.zeros((1, cols), F32)
    return jnp.concatenate(list(rows) + [zero] * (PAD - len(rows)), axis=0)


def first_kernel(face, nz, n_modes, turn, resid_hbm, schur_hbm, modes_hbm, coarse_hbm, *refs):
    names = ["r0", "stack", "mt", "c_own", "y", "za", "zb", "t", "t2"]
    o = dict(zip(names, refs[:len(names)]))
    resid, schur, mode_rows, coarse, sems = refs[len(names):]
    two = 2 * face
    places, signs = face_places(face)
    copies = [
        pltpu.make_async_copy(modes_hbm, mode_rows, sems.at[0]),
        pltpu.make_async_copy(resid_hbm, resid, sems.at[1]),
        pltpu.make_async_copy(coarse_hbm, coarse, sems.at[2]),
    ]
    for f in range(6):
        at = pl.ds(f * face, face)
        copies.append(pltpu.make_async_copy(schur_hbm.at[pl.ds(places[f], face), :], schur.at[at, :], sems.at[3 + f]))
    for copy in copies:
        copy.start()

    copies[0].wait()
    modes = jnp.concatenate([
        jnp.concatenate([mode_rows[m, :, pl.ds(at, face)] for at in places], axis=1)
        for m in range(n_modes)], axis=0)
    modes = jnp.concatenate([modes, jnp.zeros((PAD - n_modes, modes.shape[1]), F32)], axis=0)
    width = modes.shape[1]
    o["mt"][...] = mode_pieces(modes)
    o["stack"][2 * width:, :] = jnp.concatenate(split3(modes) + (jnp.zeros(modes.shape, BF16),), axis=0)

    copies[1].wait()
    for f in range(6):
        o["r0"][f * face:(f + 1) * face, :] = signs[f] * resid[:, pl.ds(places[f], face)].T
    r0 = o["r0"][...]
    cols = r0.shape[1]

    copies[2].wait()
    rows = jnp.concatenate([coarse[m] for m in range(n_modes)], axis=0)
    rows = jnp.concatenate([rows, jnp.zeros((PAD - n_modes, rows.shape[1]), F32)], axis=0)
    wide = o["c_own"].shape[1]
    source = lax.broadcasted_iota(jnp.int32, (nz * n_modes, wide), 0)
    place = lax.broadcasted_iota(jnp.int32, (nz * n_modes, wide), 1)
    block, mode = place // PAD, place % PAD

    if turn:
        me = lax.axis_index("gz")
        side = 1 - 2 * lax.rem(me, 2)
        copy, block = block // nz, block % nz
        holder = me + jnp.where(copy == 1, side, jnp.where(copy == 2, -side, 2 * (copy // 3)))
        side = jnp.where((copy == 1) | (copy == 2), -side, side)
        offset = jnp.where(block == 1, side, jnp.where(block == 2, -side, 2 * (block // 3)))
        device = (holder + offset + 2 * nz) % nz
    else:
        device = block
    pick = jnp.where((source == device * n_modes + mode) & (mode < n_modes), 1.0, 0.0)
    picked = dot16(jnp.concatenate(split3(rows), axis=0), pick.astype(BF16))
    ordered = (picked[0:PAD] + picked[PAD:2 * PAD]) + picked[2 * PAD:]
    o["c_own"][...] = ordered
    if turn:
        send_rows(face, ordered, 2 * PAD, o)
    o["za"][face:face + PAD, :] = modes[:, 4 * face:5 * face]
    o["zb"][face + 3 * PAD:face + 4 * PAD, :] = modes[:, 5 * face:6 * face]

    for part in range(3):
        at = slice(part * two, (part + 1) * two)
        copies[3 + 2 * part].wait()
        copies[4 + 2 * part].wait()
        high, low = split(jnp.concatenate([schur[at, pl.ds(start, face)] for start in places], axis=1))
        o["stack"][at, :] = high
        o["stack"][width + part * two:width + (part + 1) * two, :] = low
    curv = product(face, r0, o["stack"], o)
    send_rows(face, stack_rows([half_dot(r0, r0), curv], cols), PAD, o)


def column_rows(face, i, at):
    return [i["t"][at:at + PAD, :], i["gta"][at:at + PAD, :],
            i["gzb"][face + at:face + at + PAD, :], i["gt2"][at:at + PAD, :]]


def z_kernel(face, i, o):
    for k, name in enumerate(("a", "b")):
        if "mt_" + name in o:
            got_modes = mode_pieces(i["gz" + name][-PAD:, :])
            o["mt_" + name][...] = got_modes
        else:
            got_modes = i["mt_" + name][...]
        amp = i["amp"]
        own = i["z" + name][0:face, :] + dot16(i["mt"][(4 + k) * face:(5 + k) * face, :], amp_pieces(amp[0:PAD, :]))
        at = (1 + k) * PAD
        got = i["gz" + name][0:face, :] + dot16(got_modes, amp_pieces(amp[at:at + PAD, :]))
        o["z"][k * face:(k + 1) * face, :] = own - got


def value_kernel(face, stage, i, o):
    gathered = "g_all" in i
    loads = i["g_all"][...] if gathered else jnp.concatenate(column_rows(face, i, 0), axis=0)
    if stage == 0 and not gathered:
        n = loads.shape[0]
        coarse = jnp.concatenate([part[:, k * n:(k + 1) * n] for k, part in enumerate(
            [i["c_own"][...]] + column_rows(face, i, 2 * PAD)[1:])], axis=0)
        coarse = left_pieces(coarse)
        o["c_all"][...] = coarse
    else:
        coarse = i["c_all"][...]
    amp = dot32(coarse, loads) if gathered else dot16(coarse, amp_pieces(loads))
    o["amp"][...] = amp[0:3 * PAD]
    xy = i["y"][...] + dot16(i["mt"][0:4 * face, :], amp_pieces(amp[0:PAD]))
    cols = loads.shape[1]

    if stage != 2:
        if gathered:
            dots = i["d_all"][...]
            quad = col_sum(loads * amp[3 * PAD:])
        else:
            parts = column_rows(face, i, PAD)
            dots = (parts[0] + parts[1]) + (parts[2] + parts[3])
            quad = col_sum(loads * amp)
        at = {0: 1, 1: 1, 3: 5}[stage]
        dots = jnp.concatenate([dots[0:at], row(dots, at) + quad, dots[at + 1:]], axis=0)
    if stage == 1:
        dots = jnp.concatenate([i["first"][0:2, :], dots[0:2], dots[4:]], axis=0)
    elif stage == 2 and "swapped" in i:
        dots = six_columns(i, o)
    o["xab"][0:2 * face, :] = xy[0:2 * face]
    o["ya"][0:face, :] = xy[2 * face:3 * face]
    o["yb"][0:face, :] = xy[3 * face:]
    if stage == 3:
        o["dots"][...] = dots
    if stage != 2 or "swapped" in i:
        o["xab"][2 * face:, :] = dots
    if stage != 2:
        o["ya"][face:face + PAD, :] = dots
        o["yb"][face:face + PAD, :] = dots


def assemble(face, i, rates=None):
    f = face
    got = [i["gxab"][0:2 * f, :], i["gya"][0:f, :], i["gyb"][0:f, :]]
    if rates is not None:
        got = [rate * face_values for rate, face_values in zip(rates, got)]
    return jnp.concatenate([
        i["xab"][0:2 * f, :] - got[0], i["ya"][0:f, :] - got[1], i["yb"][0:f, :] - got[2], i["z"][...],
    ], axis=0)


def column_scale(dots):
    norm, curv = row(dots, 0), row(dots, 1)
    usable = (norm > 0.0) & (curv > 0.0)
    return jnp.where(usable, norm / jnp.where(usable, curv, 1.0), 1.0)


def rescale(dots, rate):
    square = rate * rate
    return stack_rows([row(dots, 0), row(dots, 1), square * row(dots, 2), square * row(dots, 3)], dots.shape[1])


def second_kernel(face, i, o):
    w0 = assemble(face, i)
    o["w0"][...] = w0
    first = i["xab"][2 * face:2 * face + PAD, :]
    scale = column_scale(first)
    cols = w0.shape[1]
    rates = [scale / column_scale(i[name][at:at + PAD, :])
             for name, at in (("gxab", 2 * face), ("gya", face), ("gyb", face))]
    o["first"][...] = stack_rows([row(first, 0), row(first, 1), scale] + rates, cols)
    vec = scale * w0
    curv = product(face, vec, i["stack"], o)
    send_rows(face, stack_rows([half_dot(vec, vec), curv], cols), PAD, o)


def third_kernel(face, i, o):
    scale, *rates = (row(i["first"], k) for k in range(2, 6))
    q = assemble(face, i, rates)
    o["q"][...] = q
    if "near" in o:
        partners = [rescale(i[name][at:at + PAD, :], rate) for rate, name, at in zip(
            rates, ("gxab", "gya", "gyb"), (2 * face, face, face))]
        o["near"][...] = jnp.concatenate([partners[0], partners[2], partners[1] + i["xab"][2 * face:, :]], axis=0)
    product(face, scale * q, i["stack"], o)


def six_columns(i, o):
    near = i["near"]
    rate = row(i["first"], 4)
    both = rescale(i["swapped"][0:PAD, :], rate), rescale(i["swapped"][PAD:2 * PAD, :], rate)
    o["six"][...] = ((near[0:PAD, :] + near[PAD:2 * PAD, :]) + near[2 * PAD:, :]) + (both[0] + both[1])
    return near[PAD:2 * PAD, :] + both[1]


def fourth_kernel(face, i, o):
    scale, *rates = (row(i["first"], k) for k in range(2, 6))
    sums = i["six"][...]
    if "whole" not in i:
        sums = sums + rescale(i["gxab"][2 * face:, :], rates[0])
    m0, m1 = row(sums, 0), row(sums, 1)
    alpha0 = m0 / m1
    ratio0 = alpha0 / scale
    square = ratio0 * ratio0
    m2, m3 = square * row(sums, 2), square * row(sums, 3)
    norm1 = m2 - m0
    curv1 = m1 - 2.0 * (m2 / alpha0) + m3
    beta1 = norm1 / m0
    alpha1 = norm1 / (curv1 - beta1 * norm1 / alpha0)
    r0, w0 = i["r0"][...], i["w0"][...]
    q = ratio0 * i["q"][...]
    b = q - square * assemble(face, i, [rate * rate for rate in rates])
    w1 = w0 - q
    s1 = alpha1 * (w1 + beta1 * w0)
    r2 = (r0 - alpha0 * w0) - s1
    z1 = (alpha1 / alpha0) * (b + beta1 * q)
    w2 = w1 - z1
    vec = alpha1 * w2
    cols = w2.shape[1]
    o["w2"][...] = vec
    o["s1"][...] = s1
    o["z1"][...] = z1
    o["known"][...] = stack_rows([norm1, alpha1, alpha0, beta1], cols)
    curv = product(face, vec, i["stack"], o)
    send_rows(face, stack_rows([
        half_dot(r2, r2), half_dot(r2, w2), half_dot(vec, vec), half_dot(vec, s1),
        half_dot(s1, s1), curv, half_dot(z1, vec), half_dot(s1, z1)], cols), PAD, o)


def four_kernel(face, i, o):
    near = i["dots"][...] + i["gxab"][2 * face:2 * face + PAD, :]
    o["part"][...] = near + (i["across"][...] + i["gyb"][face:face + PAD, :])


def ready_kernel(face, i, o):
    alpha1, alpha0, beta1 = (row(i["known"], k) for k in range(1, 4))
    r0 = i["r0"][...]
    r1 = r0 - alpha0 * i["w0"][...]
    p1 = r1 + beta1 * r0
    o["c3"][...] = assemble(face, i)
    o["r2"][...] = r1 - i["s1"][...]
    o["p1"][...] = p1
    o["m2"][...] = alpha0 * r0 + alpha1 * p1


def last_kernel(face, names, *refs):
    i = dict(zip(names, refs))
    mult_hbm, resid_hbm, mult_out, resid_out, sems = refs[len(names):]
    d = i["sum_near"][...] + i["sum_far"][...]
    rr, rw, ww, ws, ss, wc, sc, sz = (row(d, k) for k in range(8))
    norm1, alpha1 = row(i["known"], 0), row(i["known"], 1)
    beta2 = rr / norm1
    alpha2 = rr / (rw - beta2 * rr / alpha1)
    ratio = alpha2 / alpha1
    ratio2 = ratio * ratio
    norm3 = ratio2 * (ww + 2.0 * beta2 * ws + beta2 * beta2 * ss) - rr
    curv3 = rw - 2.0 * (ratio2 / alpha2) * (ww + beta2 * ws)
    curv3 = curv3 + ratio2 * (wc + 2.0 * beta2 * sc + beta2 * beta2 * sz)
    beta3 = norm3 / rr
    alpha3 = norm3 / (curv3 - beta3 * norm3 / alpha2)
    places, signs = face_places(face)
    copies = []
    for f in range(6):
        at = slice(f * face, (f + 1) * face)
        w2, s1 = i["w2"][at, :], i["s1"][at, :]
        p2 = i["r2"][at, :] + beta2 * i["p1"][at, :]
        s2 = w2 + beta2 * s1
        r3 = i["r2"][at, :] - ratio * s2
        w3 = w2 / alpha1 - ratio * (i["c3"][at, :] + beta2 * i["z1"][at, :])
        mult = i["m2"][at, :] + alpha2 * p2 + alpha3 * (r3 + beta3 * p2)
        resid = r3 - alpha3 * (w3 + (beta3 / alpha1) * s2)
        for k, (value, out, hbm) in enumerate(((mult, mult_out, mult_hbm), (resid, resid_out, resid_hbm))):
            out[f] = (signs[f] * value).T
            copy = pltpu.make_async_copy(out.at[f], hbm.at[:, pl.ds(places[f], face)], sems.at[2 * f + k])
            copy.start()
            copies.append(copy)
    for copy in copies:
        copy.wait()


def body(sizes, residual_in, schur, modes, coarse_inv):
    nx, ny, nz = sizes
    resid = residual_in[0, 0, 0]
    matrix = schur[0, 0, 0]
    loads, width = resid.shape
    face = width // 6
    n_modes = modes.shape[3]
    mode_rows = modes.reshape(n_modes, 1, width)
    coarse_rows = coarse_inv.reshape(n_modes, 1, nz * n_modes)
    small = (nx, ny, nz) == (2, 4, 4)

    def shift(x, axis, by):
        n = lax.axis_size(axis)
        return lax.ppermute(x, axis, [(k, (k + by) % n) for k in range(n)])

    def swap(x, axis, first):
        n = lax.axis_size(axis)
        side = lambda k: 1 if (k - first) % 2 == 0 else -1
        return lax.ppermute(x, axis, [(k, (k + side(k)) % n) for k in range(n)])

    def move(x, target):
        places = [(a, b) for a in range(nx) for b in range(ny)]
        pairs = [(a * ny + b, target(a, b)[0] * ny + target(a, b)[1]) for a, b in places]
        return lax.ppermute(x, ("gx", "gy"), pairs)

    def total(dots, scale):
        rate = lax.pmin(scale, ("gx", "gy")) / scale
        rates = jnp.concatenate([jnp.ones((2, loads), F32), rate * rate, rate * rate], axis=0)
        sums = lax.psum(dots[0:4] * rates, ("gx", "gy")) / rates
        return jnp.concatenate([sums, jnp.zeros((PAD - 4, loads), F32)], axis=0)

    vec = sds((width, loads))
    rows = sds((PAD, loads))
    stack_shape = sds((2 * width + 4 * PAD, width), BF16)
    flops = 2 * width * width * 2 * loads * 2

    def z_out(tiny, extra=0):
        return dict(y=sds((4 * face, loads)), za=sds((face + extra, loads)),
                    zb=sds((face + tiny * PAD + extra, loads)), t=sds((tiny * PAD, loads)),
                    t2=sds((tiny * PAD + PAD, loads)))

    def t_exchange(a, with_dots):
        got = dict(t=a["t"], y=a["y"])
        if small:
            got.update(gzb=swap(a["zb"], "gz", 1), gt2=shift(a["t2"], "gz", 2), gta=swap(a["t"], "gz", 0))
        else:
            got["g_all"] = lax.all_gather(a["t"][0:PAD], "gz", axis=0, tiled=True)
            if with_dots:
                got["d_all"] = lax.psum(a["t"][PAD:2 * PAD], "gz")
        return got

    def z_faces(a, v, t, modes=None):
        ins = dict(za=a["za"], zb=a["zb"], gzb=t["gzb"] if small else swap(a["zb"], "gz", 1),
                   gza=swap(a["za"], "gz", 0), mt=mt, amp=v["amp"])
        outs = dict(z=sds((2 * face, loads)))
        if modes is None:
            outs.update(mt_a=sds((face, 6 * PAD), BF16), mt_b=sds((face, 6 * PAD), BF16))
        else:
            ins.update(modes)
        return call(functools.partial(z_kernel, face), ins, outs, flops=Z_FLOPS)

    def value(stage, ins):
        extra = 0 if stage == 2 else PAD
        outs = dict(amp=sds((3 * PAD, loads)), xab=sds((2 * face + (PAD if small else extra), loads)),
                    ya=sds((face + extra, loads)), yb=sds((face + 2 * PAD, loads)))
        if stage == 0 and small:
            outs["c_all"] = sds((nz * PAD, 6 * nz * PAD), BF16)
        if stage == 2 and small:
            outs["six"] = rows
        if stage == 3:
            outs["dots"] = rows
        return call(functools.partial(value_kernel, face, stage), ins, outs, flops=2 * width * loads * 48)

    def x_exchange(v):
        got = dict(xab=v["xab"])
        if nx == 2:
            got["gxab"] = swap(v["xab"], "gx", 0)
        else:
            a, b, rest = v["xab"][:face], v["xab"][face:2 * face], v["xab"][2 * face:]
            got["gxab"] = jnp.concatenate([swap(a, "gx", 0), swap(b, "gx", 1), rest], axis=0)
        return got

    def y_exchange(v):
        gyb = swap(v["yb"], "gy", 1)
        return dict(ya=v["ya"], yb=v["yb"], gya=swap(v["ya"], "gy", 0), gyb=gyb)

    def xy_exchange(v):
        return dict(x_exchange(v), **y_exchange(v))

    hbm = pl.BlockSpec(memory_space=pltpu.HBM)
    vmem = pl.BlockSpec(memory_space=pltpu.VMEM)
    outs = dict(r0=vec, stack=stack_shape, mt=sds((width, 6 * PAD), BF16),
                c_own=sds((PAD, (4 if small else 1) * nz * PAD)), **z_out(3, PAD))
    res = pl.pallas_call(
        functools.partial(first_kernel, face, nz, n_modes, small),
        out_shape=list(outs.values()),
        in_specs=[hbm] * 4,
        out_specs=[vmem] * len(outs),
        scratch_shapes=[
            pltpu.VMEM(resid.shape, F32), pltpu.VMEM(matrix.shape, F32),
            pltpu.VMEM(mode_rows.shape, F32), pltpu.VMEM(coarse_rows.shape, F32),
            pltpu.SemaphoreType.DMA((9,)),
        ],
        compiler_params=pltpu.CompilerParams(vmem_limit_bytes=VMEM_LIMIT),
        cost_estimate=pl.CostEstimate(flops=flops, bytes_accessed=4 * matrix.size, transcendentals=0),
    )(*[pltpu.with_memory_space_constraint(x, pltpu.HBM) for x in (resid, matrix, mode_rows, coarse_rows)])
    a = dict(zip(outs, res))
    r0, mt, stack = a["r0"], a["mt"], a["stack"]
    ins = dict(t_exchange(a, True), mt=mt)
    if small:
        ins["c_own"] = a["c_own"]
    else:
        c_own = a["c_own"]
        ins["c_all"] = jnp.concatenate([
            c_own, swap(c_own, "gz", 0), swap(c_own, "gz", 1),
            lax.all_gather(c_own, "gz", axis=0, tiled=True)], axis=0)
    t = ins
    v = value(0, ins)
    column = dict(mt=mt, c_all=v["c_all"] if small else ins["c_all"])
    z = z_faces(a, v, t)
    got_modes = dict(mt_a=z["mt_a"], mt_b=z["mt_b"])
    x = dict(xy_exchange(v), z=z["z"])

    a = call(functools.partial(second_kernel, face), dict(x, stack=stack),
             dict(w0=vec, first=rows, **z_out(2)), flops=flops)
    w0, first = a["w0"], a["first"]
    t = t_exchange(a, True)
    v = value(1, dict(t, **column, first=first))
    x = dict(xy_exchange(v), z=z_faces(a, v, t, got_modes)["z"])

    near = dict(near=sds((3 * PAD, loads))) if small else {}
    a = call(functools.partial(third_kernel, face), dict(x, stack=stack, first=first),
             dict(q=vec, **near, **z_out(1)), flops=flops)
    q = a["q"]
    t = t_exchange(a, False)
    ins = dict(t, **column)
    if small:
        ins.update(first=first, near=a["near"], swapped=swap(a["near"][0:2 * PAD], "gy", 0))
        v = value(2, ins)
        sums = dict(six=v["six"])
    else:
        sums = dict(six=total(v["xab"][2 * face:], first[2:3]), whole=first)
        v = value(2, ins)
    x = dict(xy_exchange(v), z=z_faces(a, v, t, got_modes)["z"])

    a = call(functools.partial(fourth_kernel, face),
             dict(x, stack=stack, **sums, first=first, r0=r0, w0=w0, q=q),
             dict(w2=vec, s1=vec, z1=vec, known=rows, **z_out(2)), flops=flops)
    t = t_exchange(a, True)
    v = value(3, dict(t, **column))
    z = z_faces(a, v, t, got_modes)["z"]
    if small:
        x = x_exchange(v)
        across = move(v["dots"], lambda a, b: (1 - a, (b + (-1 if b % 2 == 0 else 1)) % ny))
        x.update(y_exchange(v))
        part = call(functools.partial(four_kernel, face),
                    dict(dots=v["dots"], across=across, gxab=x["gxab"], gyb=x["gyb"], z=z), dict(part=rows))["part"]
        sums = dict(sum_near=part, sum_far=swap(part, "gy", 0))
    else:
        x = xy_exchange(v)
        sums = dict(sum_near=lax.psum(v["dots"], ("gx", "gy")), sum_far=jnp.zeros((PAD, loads), F32))
    ready = call(functools.partial(ready_kernel, face),
                 dict(x, z=z, known=a["known"], s1=a["s1"], r0=r0, w0=w0),
                 {name: vec for name in ("c3", "r2", "p1", "m2")}, flops=10 * width * loads)
    ins = dict(sums, **ready, **{name: a[name] for name in ("known", "w2", "s1", "z1")})
    out = sds((loads, width))
    mult, final = pl.pallas_call(
        functools.partial(last_kernel, face, list(ins)),
        out_shape=[out, out],
        in_specs=[vmem] * len(ins),
        out_specs=[hbm, hbm],
        scratch_shapes=[pltpu.VMEM((6, loads, face), F32), pltpu.VMEM((6, loads, face), F32),
                        pltpu.SemaphoreType.DMA((12,))],
        compiler_params=pltpu.CompilerParams(vmem_limit_bytes=VMEM_LIMIT),
        cost_estimate=pl.CostEstimate(flops=20 * width * loads, bytes_accessed=9 * 4 * width * loads, transcendentals=0),
    )(*ins.values())
    return (mult[None, None, None], final[None, None, None])


def solution(mesh):
    spec = P("gx", "gy", "gz", None, None)
    sizes = tuple(mesh.shape[axis] for axis in ("gx", "gy", "gz"))
    return jax.shard_map(
        functools.partial(body, sizes),
        mesh=mesh,
        in_specs=(spec, spec, spec, P("gx", "gy", "gz", None)),
        out_specs=(spec, spec),
        check_vma=False,
    )
```

```python
import functools

import jax
import jax.numpy as jnp
from jax import lax
from jax.experimental import pallas as pl
from jax.experimental.pallas import tpu as pltpu
from jax.sharding import PartitionSpec as P

F32 = jnp.float32
BF16 = jnp.bfloat16
HI = lax.Precision.HIGHEST
PAD = 8
VMEM_LIMIT = 24 * 1024 * 1024
Z_FLOPS = 770000000


def sds(shape, dtype=F32):
    return jax.ShapeDtypeStruct(shape, dtype)


def call(kernel, ins, outs, flops=0):
    names_in, names_out = list(ins), list(outs)
    nbytes = sum(a.size * a.dtype.itemsize for a in list(ins.values()) + list(outs.values()))

    def run(*refs):
        n = len(names_in)
        kernel(dict(zip(names_in, refs[:n])), dict(zip(names_out, refs[n:])))

    vmem = pl.BlockSpec(memory_space=pltpu.VMEM)
    res = pl.pallas_call(
        run,
        out_shape=[outs[n] for n in names_out],
        in_specs=[vmem] * len(names_in),
        out_specs=[vmem] * len(names_out),
        compiler_params=pltpu.CompilerParams(vmem_limit_bytes=VMEM_LIMIT),
        cost_estimate=pl.CostEstimate(flops=flops, bytes_accessed=nbytes, transcendentals=0),
    )(*[ins[n] for n in names_in])
    return dict(zip(names_out, res))


def split(x):
    high = x.astype(BF16)
    return high, (x - high.astype(F32)).astype(BF16)


def split3(x):
    high = x.astype(BF16)
    rest = x - high.astype(F32)
    mid = rest.astype(BF16)
    return high, mid, (rest - mid.astype(F32)).astype(BF16)


def left_pieces(x):
    high, mid, low = split3(x)
    return jnp.concatenate([high, high, mid, mid, high, low], axis=1)


def mode_pieces(modes):
    return left_pieces(modes.T)


def amp_pieces(amp):
    high, mid, low = split3(amp)
    return jnp.concatenate([high, mid, high, mid, low, high], axis=0)


def dot32(a, b):
    return jnp.dot(a, b, precision=HI, preferred_element_type=F32)


def dot16(a, b):
    return jnp.dot(a, b, preferred_element_type=F32)


def col_sum(x):
    return jnp.sum(x, axis=0, keepdims=True)


def half_dot(a, b):
    return 0.5 * col_sum(a * b)


def row(x, i):
    return x[i:i + 1, :]


def face_places(face):
    places, signs = [], []
    for k, axis in enumerate(("gx", "gy", "gz")):
        odd = lax.rem(lax.axis_index(axis), 2)
        for high in (1 - odd, odd):
            places.append(pl.multiple_of((2 * k + high) * face, face))
            signs.append((1 - 2 * high).astype(F32))
    return places, signs


def store_product(face, part, y, o):
    if part < 2:
        o["y"][2 * part * face:2 * (part + 1) * face, :] = y
    else:
        o["za"][0:face, :] = y[0:face]
        o["zb"][0:face, :] = y[face:]


def send_rows(face, rows, at, o):
    n = rows.shape[0]
    o["t"][at:at + n, :] = rows
    o["t2"][at:at + n, :] = rows
    o["zb"][face + at:face + at + n, :] = rows


def product(face, vec, stack, o):
    width, cols = vec.shape
    both = dot16(stack[...], jnp.concatenate(split(vec), axis=1))
    total = jnp.zeros((1, cols), F32)
    for part in range(3):
        at = slice(2 * part * face, 2 * (part + 1) * face)
        low = slice(width + 2 * part * face, width + 2 * (part + 1) * face)
        y = (both[at, :cols] + both[at, cols:]) + (both[low, :cols] + both[low, cols:])
        store_product(face, part, y, o)
        total = total + col_sum(vec[at] * y)
    loads = both[2 * width:, :cols] + both[2 * width:, cols:]
    send_rows(face, (loads[0:PAD] + loads[PAD:2 * PAD]) + loads[2 * PAD:3 * PAD], 0, o)
    return total


def stack_rows(rows, cols):
    zero = jnp.zeros((1, cols), F32)
    return jnp.concatenate(list(rows) + [zero] * (PAD - len(rows)), axis=0)


def first_kernel(face, nz, n_modes, turn, resid_hbm, schur_hbm, modes_hbm, coarse_hbm, *refs):
    names = ["r0", "stack", "mt", "c_own", "y", "za", "zb", "t", "t2"]
    o = dict(zip(names, refs[:len(names)]))
    resid, schur, mode_rows, coarse, sems = refs[len(names):]
    two = 2 * face
    places, signs = face_places(face)
    copies = [
        pltpu.make_async_copy(modes_hbm, mode_rows, sems.at[0]),
        pltpu.make_async_copy(resid_hbm, resid, sems.at[1]),
        pltpu.make_async_copy(coarse_hbm, coarse, sems.at[2]),
    ]
    for f in range(6):
        at = pl.ds(f * face, face)
        copies.append(pltpu.make_async_copy(schur_hbm.at[pl.ds(places[f], face), :], schur.at[at, :], sems.at[3 + f]))
    for copy in copies:
        copy.start()

    copies[0].wait()
    modes = jnp.concatenate([
        jnp.concatenate([mode_rows[m, :, pl.ds(at, face)] for at in places], axis=1)
        for m in range(n_modes)], axis=0)
    modes = jnp.concatenate([modes, jnp.zeros((PAD - n_modes, modes.shape[1]), F32)], axis=0)
    width = modes.shape[1]
    o["mt"][...] = mode_pieces(modes)
    o["stack"][2 * width:, :] = jnp.concatenate(split3(modes) + (jnp.zeros(modes.shape, BF16),), axis=0)

    copies[1].wait()
    for f in range(6):
        o["r0"][f * face:(f + 1) * face, :] = signs[f] * resid[:, pl.ds(places[f], face)].T
    r0 = o["r0"][...]
    cols = r0.shape[1]

    copies[2].wait()
    rows = jnp.concatenate([coarse[m] for m in range(n_modes)], axis=0)
    rows = jnp.concatenate([rows, jnp.zeros((PAD - n_modes, rows.shape[1]), F32)], axis=0)
    wide = o["c_own"].shape[1]
    source = lax.broadcasted_iota(jnp.int32, (nz * n_modes, wide), 0)
    place = lax.broadcasted_iota(jnp.int32, (nz * n_modes, wide), 1)
    block, mode = place // PAD, place % PAD

    if turn:
        me = lax.axis_index("gz")
        side = 1 - 2 * lax.rem(me, 2)
        copy, block = block // nz, block % nz
        holder = me + jnp.where(copy == 1, side, jnp.where(copy == 2, -side, 2 * (copy // 3)))
        side = jnp.where((copy == 1) | (copy == 2), -side, side)
        offset = jnp.where(block == 1, side, jnp.where(block == 2, -side, 2 * (block // 3)))
        device = (holder + offset + 2 * nz) % nz
    else:
        device = block
    pick = jnp.where((source == device * n_modes + mode) & (mode < n_modes), 1.0, 0.0)
    picked = dot16(jnp.concatenate(split3(rows), axis=0), pick.astype(BF16))
    ordered = (picked[0:PAD] + picked[PAD:2 * PAD]) + picked[2 * PAD:]
    o["c_own"][...] = ordered
    if turn:
        send_rows(face, ordered, 2 * PAD, o)
    o["za"][face:face + PAD, :] = modes[:, 4 * face:5 * face]
    o["zb"][face + 3 * PAD:face + 4 * PAD, :] = modes[:, 5 * face:6 * face]

    for part in range(3):
        at = slice(part * two, (part + 1) * two)
        copies[3 + 2 * part].wait()
        copies[4 + 2 * part].wait()
        high, low = split(jnp.concatenate([schur[at, pl.ds(start, face)] for start in places], axis=1))
        o["stack"][at, :] = high
        o["stack"][width + part * two:width + (part + 1) * two, :] = low
    curv = product(face, r0, o["stack"], o)
    send_rows(face, stack_rows([half_dot(r0, r0), curv], cols), PAD, o)


def column_rows(face, i, at):
    return [i["t"][at:at + PAD, :], i["gta"][at:at + PAD, :],
            i["gzb"][face + at:face + at + PAD, :], i["gt2"][at:at + PAD, :]]


def z_kernel(face, i, o):
    for k, name in enumerate(("a", "b")):
        if "mt_" + name in o:
            got_modes = mode_pieces(i["gz" + name][-PAD:, :])
            o["mt_" + name][...] = got_modes
        else:
            got_modes = i["mt_" + name][...]
        amp = i["amp"]
        own = i["z" + name][0:face, :] + dot16(i["mt"][(4 + k) * face:(5 + k) * face, :], amp_pieces(amp[0:PAD, :]))
        at = (1 + k) * PAD
        got = i["gz" + name][0:face, :] + dot16(got_modes, amp_pieces(amp[at:at + PAD, :]))
        o["z"][k * face:(k + 1) * face, :] = own - got


def value_kernel(face, stage, i, o):
    gathered = "g_all" in i
    loads = i["g_all"][...] if gathered else jnp.concatenate(column_rows(face, i, 0), axis=0)
    if stage == 0 and not gathered:
        n = loads.shape[0]
        coarse = jnp.concatenate([part[:, k * n:(k + 1) * n] for k, part in enumerate(
            [i["c_own"][...]] + column_rows(face, i, 2 * PAD)[1:])], axis=0)
        coarse = left_pieces(coarse)
        o["c_all"][...] = coarse
    else:
        coarse = i["c_all"][...]
    amp = dot32(coarse, loads) if gathered else dot16(coarse, amp_pieces(loads))
    o["amp"][...] = amp[0:3 * PAD]
    xy = i["y"][...] + dot16(i["mt"][0:4 * face, :], amp_pieces(amp[0:PAD]))
    cols = loads.shape[1]

    if stage != 2:
        if gathered:
            dots = i["d_all"][...]
            quad = col_sum(loads * amp[3 * PAD:])
        else:
            parts = column_rows(face, i, PAD)
            dots = (parts[0] + parts[1]) + (parts[2] + parts[3])
            quad = col_sum(loads * amp)
        at = {0: 1, 1: 1, 3: 5}[stage]
        dots = jnp.concatenate([dots[0:at], row(dots, at) + quad, dots[at + 1:]], axis=0)
    if stage == 1:
        dots = jnp.concatenate([i["first"][0:2, :], dots[0:2], dots[4:]], axis=0)
    elif stage == 2 and "swapped" in i:
        dots = six_columns(i, o)
    o["xab"][0:2 * face, :] = xy[0:2 * face]
    o["ya"][0:face, :] = xy[2 * face:3 * face]
    o["yb"][0:face, :] = xy[3 * face:]
    if stage == 3:
        o["dots"][...] = dots
    if stage != 2 or "swapped" in i:
        o["xab"][2 * face:, :] = dots
    if stage != 2:
        o["ya"][face:face + PAD, :] = dots
        o["yb"][face:face + PAD, :] = dots


def assemble(face, i, rates=None):
    f = face
    got = [i["gxab"][0:2 * f, :], i["gya"][0:f, :], i["gyb"][0:f, :]]
    if rates is not None:
        got = [rate * face_values for rate, face_values in zip(rates, got)]
    return jnp.concatenate([
        i["xab"][0:2 * f, :] - got[0], i["ya"][0:f, :] - got[1], i["yb"][0:f, :] - got[2], i["z"][...],
    ], axis=0)


def column_scale(dots):
    norm, curv = row(dots, 0), row(dots, 1)
    usable = (norm > 0.0) & (curv > 0.0)
    return jnp.where(usable, norm / jnp.where(usable, curv, 1.0), 1.0)


def rescale(dots, rate):
    square = rate * rate
    return stack_rows([row(dots, 0), row(dots, 1), square * row(dots, 2), square * row(dots, 3)], dots.shape[1])


def second_kernel(face, i, o):
    w0 = assemble(face, i)
    o["w0"][...] = w0
    first = i["xab"][2 * face:2 * face + PAD, :]
    scale = column_scale(first)
    cols = w0.shape[1]
    rates = [scale / column_scale(i[name][at:at + PAD, :])
             for name, at in (("gxab", 2 * face), ("gya", face), ("gyb", face))]
    o["first"][...] = stack_rows([row(first, 0), row(first, 1), scale] + rates, cols)
    vec = scale * w0
    curv = product(face, vec, i["stack"], o)
    send_rows(face, stack_rows([half_dot(vec, vec), curv], cols), PAD, o)


def third_kernel(face, i, o):
    scale, *rates = (row(i["first"], k) for k in range(2, 6))
    q = assemble(face, i, rates)
    o["q"][...] = q
    if "near" in o:
        partners = [rescale(i[name][at:at + PAD, :], rate) for rate, name, at in zip(
            rates, ("gxab", "gya", "gyb"), (2 * face, face, face))]
        o["near"][...] = jnp.concatenate([partners[0], partners[2], partners[1] + i["xab"][2 * face:, :]], axis=0)
    product(face, scale * q, i["stack"], o)


def six_columns(i, o):
    near = i["near"]
    rate = row(i["first"], 4)
    both = rescale(i["swapped"][0:PAD, :], rate), rescale(i["swapped"][PAD:2 * PAD, :], rate)
    o["six"][...] = ((near[0:PAD, :] + near[PAD:2 * PAD, :]) + near[2 * PAD:, :]) + (both[0] + both[1])
    return near[PAD:2 * PAD, :] + both[1]


def fourth_kernel(face, i, o):
    scale, *rates = (row(i["first"], k) for k in range(2, 6))
    sums = i["six"][...]
    if "whole" not in i:
        sums = sums + rescale(i["gxab"][2 * face:, :], rates[0])
    m0, m1 = row(sums, 0), row(sums, 1)
    alpha0 = m0 / m1
    ratio0 = alpha0 / scale
    square = ratio0 * ratio0
    m2, m3 = square * row(sums, 2), square * row(sums, 3)
    norm1 = m2 - m0
    curv1 = m1 - 2.0 * (m2 / alpha0) + m3
    beta1 = norm1 / m0
    alpha1 = norm1 / (curv1 - beta1 * norm1 / alpha0)
    r0, w0 = i["r0"][...], i["w0"][...]
    q = ratio0 * i["q"][...]
    b = q - square * assemble(face, i, [rate * rate for rate in rates])
    w1 = w0 - q
    s1 = alpha1 * (w1 + beta1 * w0)
    r2 = (r0 - alpha0 * w0) - s1
    z1 = (alpha1 / alpha0) * (b + beta1 * q)
    w2 = w1 - z1
    vec = alpha1 * w2
    cols = w2.shape[1]
    o["w2"][...] = vec
    o["s1"][...] = s1
    o["z1"][...] = z1
    o["known"][...] = stack_rows([norm1, alpha1, alpha0, beta1], cols)
    curv = product(face, vec, i["stack"], o)
    send_rows(face, stack_rows([
        half_dot(r2, r2), half_dot(r2, w2), half_dot(vec, vec), half_dot(vec, s1),
        half_dot(s1, s1), curv, half_dot(z1, vec), half_dot(s1, z1)], cols), PAD, o)


def four_kernel(face, i, o):
    near = i["dots"][...] + i["gxab"][2 * face:2 * face + PAD, :]
    o["part"][...] = near + (i["across"][...] + i["gyb"][face:face + PAD, :])


def ready_kernel(face, i, o):
    alpha1, alpha0, beta1 = (row(i["known"], k) for k in range(1, 4))
    r0 = i["r0"][...]
    r1 = r0 - alpha0 * i["w0"][...]
    p1 = r1 + beta1 * r0
    o["c3"][...] = assemble(face, i)
    o["r2"][...] = r1 - i["s1"][...]
    o["p1"][...] = p1
    o["m2"][...] = alpha0 * r0 + alpha1 * p1


def last_kernel(face, names, *refs):
    i = dict(zip(names, refs))
    mult_hbm, resid_hbm, mult_out, resid_out, sems = refs[len(names):]
    d = i["sum_near"][...] + i["sum_far"][...]
    rr, rw, ww, ws, ss, wc, sc, sz = (row(d, k) for k in range(8))
    norm1, alpha1 = row(i["known"], 0), row(i["known"], 1)
    beta2 = rr / norm1
    alpha2 = rr / (rw - beta2 * rr / alpha1)
    ratio = alpha2 / alpha1
    ratio2 = ratio * ratio
    norm3 = ratio2 * (ww + 2.0 * beta2 * ws + beta2 * beta2 * ss) - rr
    curv3 = rw - 2.0 * (ratio2 / alpha2) * (ww + beta2 * ws)
    curv3 = curv3 + ratio2 * (wc + 2.0 * beta2 * sc + beta2 * beta2 * sz)
    beta3 = norm3 / rr
    alpha3 = norm3 / (curv3 - beta3 * norm3 / alpha2)
    inverse1 = 1.0 / alpha1
    places, signs = face_places(face)
    copies = []
    for f in range(6):
        at = slice(f * face, (f + 1) * face)
        w2, s1 = i["w2"][at, :], i["s1"][at, :]
        p2 = i["r2"][at, :] + beta2 * i["p1"][at, :]
        s2 = w2 + beta2 * s1
        r3 = i["r2"][at, :] - ratio * s2
        w3 = w2 * inverse1 - ratio * (i["c3"][at, :] + beta2 * i["z1"][at, :])
        mult = i["m2"][at, :] + alpha2 * p2 + alpha3 * (r3 + beta3 * p2)
        resid = r3 - alpha3 * (w3 + (beta3 / alpha1) * s2)
        for k, (value, out, hbm) in enumerate(((mult, mult_out, mult_hbm), (resid, resid_out, resid_hbm))):
            out[f] = (signs[f] * value).T
            copy = pltpu.make_async_copy(out.at[f], hbm.at[:, pl.ds(places[f], face)], sems.at[2 * f + k])
            copy.start()
            copies.append(copy)
    for copy in copies:
        copy.wait()


def body(sizes, residual_in, schur, modes, coarse_inv):
    nx, ny, nz = sizes
    resid = residual_in[0, 0, 0]
    matrix = schur[0, 0, 0]
    loads, width = resid.shape
    face = width // 6
    n_modes = modes.shape[3]
    mode_rows = modes.reshape(n_modes, 1, width)
    coarse_rows = coarse_inv.reshape(n_modes, 1, nz * n_modes)
    small = (nx, ny, nz) == (2, 4, 4)

    def shift(x, axis, by):
        n = lax.axis_size(axis)
        return lax.ppermute(x, axis, [(k, (k + by) % n) for k in range(n)])

    def swap(x, axis, first):
        n = lax.axis_size(axis)
        side = lambda k: 1 if (k - first) % 2 == 0 else -1
        return lax.ppermute(x, axis, [(k, (k + side(k)) % n) for k in range(n)])

    def move(x, target):
        places = [(a, b) for a in range(nx) for b in range(ny)]
        pairs = [(a * ny + b, target(a, b)[0] * ny + target(a, b)[1]) for a, b in places]
        return lax.ppermute(x, ("gx", "gy"), pairs)

    def total(dots, scale):
        rate = lax.pmin(scale, ("gx", "gy")) / scale
        rates = jnp.concatenate([jnp.ones((2, loads), F32), rate * rate, rate * rate], axis=0)
        sums = lax.psum(dots[0:4] * rates, ("gx", "gy")) / rates
        return jnp.concatenate([sums, jnp.zeros((PAD - 4, loads), F32)], axis=0)

    vec = sds((width, loads))
    rows = sds((PAD, loads))
    stack_shape = sds((2 * width + 4 * PAD, width), BF16)
    flops = 2 * width * width * 2 * loads * 2

    def z_out(tiny, extra=0):
        return dict(y=sds((4 * face, loads)), za=sds((face + extra, loads)),
                    zb=sds((face + tiny * PAD + extra, loads)), t=sds((tiny * PAD, loads)),
                    t2=sds((tiny * PAD + PAD, loads)))

    def t_exchange(a, with_dots):
        got = dict(t=a["t"], y=a["y"])
        if small:
            got.update(gzb=swap(a["zb"], "gz", 1), gt2=shift(a["t2"], "gz", 2), gta=swap(a["t"], "gz", 0))
        else:
            got["g_all"] = lax.all_gather(a["t"][0:PAD], "gz", axis=0, tiled=True)
            if with_dots:
                got["d_all"] = lax.psum(a["t"][PAD:2 * PAD], "gz")
        return got

    def z_faces(a, v, t, modes=None):
        ins = dict(za=a["za"], zb=a["zb"], gzb=t["gzb"] if small else swap(a["zb"], "gz", 1),
                   gza=swap(a["za"], "gz", 0), mt=mt, amp=v["amp"])
        outs = dict(z=sds((2 * face, loads)))
        if modes is None:
            outs.update(mt_a=sds((face, 6 * PAD), BF16), mt_b=sds((face, 6 * PAD), BF16))
        else:
            ins.update(modes)
        return call(functools.partial(z_kernel, face), ins, outs, flops=Z_FLOPS)

    def value(stage, ins):
        extra = 0 if stage == 2 else PAD
        outs = dict(amp=sds((3 * PAD, loads)), xab=sds((2 * face + (PAD if small else extra), loads)),
                    ya=sds((face + extra, loads)), yb=sds((face + 2 * PAD, loads)))
        if stage == 0 and small:
            outs["c_all"] = sds((nz * PAD, 6 * nz * PAD), BF16)
        if stage == 2 and small:
            outs["six"] = rows
        if stage == 3:
            outs["dots"] = rows
        return call(functools.partial(value_kernel, face, stage), ins, outs, flops=2 * width * loads * 48)

    def x_exchange(v):
        got = dict(xab=v["xab"])
        if nx == 2:
            got["gxab"] = swap(v["xab"], "gx", 0)
        else:
            a, b, rest = v["xab"][:face], v["xab"][face:2 * face], v["xab"][2 * face:]
            got["gxab"] = jnp.concatenate([swap(a, "gx", 0), swap(b, "gx", 1), rest], axis=0)
        return got

    def y_exchange(v):
        gyb = swap(v["yb"], "gy", 1)
        return dict(ya=v["ya"], yb=v["yb"], gya=swap(v["ya"], "gy", 0), gyb=gyb)

    def xy_exchange(v):
        return dict(x_exchange(v), **y_exchange(v))

    hbm = pl.BlockSpec(memory_space=pltpu.HBM)
    vmem = pl.BlockSpec(memory_space=pltpu.VMEM)
    outs = dict(r0=vec, stack=stack_shape, mt=sds((width, 6 * PAD), BF16),
                c_own=sds((PAD, (4 if small else 1) * nz * PAD)), **z_out(3, PAD))
    res = pl.pallas_call(
        functools.partial(first_kernel, face, nz, n_modes, small),
        out_shape=list(outs.values()),
        in_specs=[hbm] * 4,
        out_specs=[vmem] * len(outs),
        scratch_shapes=[
            pltpu.VMEM(resid.shape, F32), pltpu.VMEM(matrix.shape, F32),
            pltpu.VMEM(mode_rows.shape, F32), pltpu.VMEM(coarse_rows.shape, F32),
            pltpu.SemaphoreType.DMA((9,)),
        ],
        compiler_params=pltpu.CompilerParams(vmem_limit_bytes=VMEM_LIMIT),
        cost_estimate=pl.CostEstimate(flops=flops, bytes_accessed=4 * matrix.size, transcendentals=0),
    )(*[pltpu.with_memory_space_constraint(x, pltpu.HBM) for x in (resid, matrix, mode_rows, coarse_rows)])
    a = dict(zip(outs, res))
    r0, mt, stack = a["r0"], a["mt"], a["stack"]
    ins = dict(t_exchange(a, True), mt=mt)
    if small:
        ins["c_own"] = a["c_own"]
    else:
        c_own = a["c_own"]
        ins["c_all"] = jnp.concatenate([
            c_own, swap(c_own, "gz", 0), swap(c_own, "gz", 1),
            lax.all_gather(c_own, "gz", axis=0, tiled=True)], axis=0)
    t = ins
    v = value(0, ins)
    column = dict(mt=mt, c_all=v["c_all"] if small else ins["c_all"])
    z = z_faces(a, v, t)
    got_modes = dict(mt_a=z["mt_a"], mt_b=z["mt_b"])
    x = dict(xy_exchange(v), z=z["z"])

    a = call(functools.partial(second_kernel, face), dict(x, stack=stack),
             dict(w0=vec, first=rows, **z_out(2)), flops=flops)
    w0, first = a["w0"], a["first"]
    t = t_exchange(a, True)
    v = value(1, dict(t, **column, first=first))
    x = dict(xy_exchange(v), z=z_faces(a, v, t, got_modes)["z"])

    near = dict(near=sds((3 * PAD, loads))) if small else {}
    a = call(functools.partial(third_kernel, face), dict(x, stack=stack, first=first),
             dict(q=vec, **near, **z_out(1)), flops=flops)
    q = a["q"]
    t = t_exchange(a, False)
    ins = dict(t, **column)
    if small:
        ins.update(first=first, near=a["near"], swapped=swap(a["near"][0:2 * PAD], "gy", 0))
        v = value(2, ins)
        sums = dict(six=v["six"])
    else:
        sums = dict(six=total(v["xab"][2 * face:], first[2:3]), whole=first)
        v = value(2, ins)
    x = dict(xy_exchange(v), z=z_faces(a, v, t, got_modes)["z"])

    a = call(functools.partial(fourth_kernel, face),
             dict(x, stack=stack, **sums, first=first, r0=r0, w0=w0, q=q),
             dict(w2=vec, s1=vec, z1=vec, known=rows, **z_out(2)), flops=flops)
    t = t_exchange(a, True)
    v = value(3, dict(t, **column))
    z = z_faces(a, v, t, got_modes)["z"]
    if small:
        x = x_exchange(v)
        across = move(v["dots"], lambda a, b: (1 - a, (b + (-1 if b % 2 == 0 else 1)) % ny))
        x.update(y_exchange(v))
        part = call(functools.partial(four_kernel, face),
                    dict(dots=v["dots"], across=across, gxab=x["gxab"], gyb=x["gyb"], z=z), dict(part=rows))["part"]
        sums = dict(sum_near=part, sum_far=swap(part, "gy", 0))
    else:
        x = xy_exchange(v)
        sums = dict(sum_near=lax.psum(v["dots"], ("gx", "gy")), sum_far=jnp.zeros((PAD, loads), F32))
    ready = call(functools.partial(ready_kernel, face),
                 dict(x, z=z, known=a["known"], s1=a["s1"], r0=r0, w0=w0),
                 {name: vec for name in ("c3", "r2", "p1", "m2")}, flops=10 * width * loads)
    ins = dict(sums, **ready, **{name: a[name] for name in ("known", "w2", "s1", "z1")})
    out = sds((loads, width))
    mult, final = pl.pallas_call(
        functools.partial(last_kernel, face, list(ins)),
        out_shape=[out, out],
        in_specs=[vmem] * len(ins),
        out_specs=[hbm, hbm],
        scratch_shapes=[pltpu.VMEM((6, loads, face), F32), pltpu.VMEM((6, loads, face), F32),
                        pltpu.SemaphoreType.DMA((12,))],
        compiler_params=pltpu.CompilerParams(vmem_limit_bytes=VMEM_LIMIT),
        cost_estimate=pl.CostEstimate(flops=20 * width * loads, bytes_accessed=9 * 4 * width * loads, transcendentals=0),
    )(*ins.values())
    return (mult[None, None, None], final[None, None, None])


def solution(mesh):
    spec = P("gx", "gy", "gz", None, None)
    sizes = tuple(mesh.shape[axis] for axis in ("gx", "gy", "gz"))
    return jax.shard_map(
        functools.partial(body, sizes),
        mesh=mesh,
        in_specs=(spec, spec, spec, P("gx", "gy", "gz", None)),
        out_specs=(spec, spec),
        check_vma=False,
    )
```
